32 devices in a mesh: space: 8 (over y, x, core), band: 4 (over z).
Axes of the slice: x: 2, y: 2, z: 4, core: 2. Of those that a mesh axis runs over, the one named last changes fastest.
Arguments:
- orbitals: float32 [32, 48, 32, 128], P('band', 'space'), may hold values from -18 to 18
- previous: float32 [32, 48, 32, 128], P('band', 'space'), may hold values from -18 to 18
- potential: float32 [48, 32, 128], P('space'), may hold values from -4 to 4
- projectors: bfloat16 [32, 9, 6, 32, 128], P('space'), may hold values from -0.1875 to 0.1875
- strengths: float32 [32, 9], replicated, may hold values from -3 to 3
- atom_planes: int32 [32], replicated, may hold values from 0 to 47, as said below
Outputs:
- filtered: bfloat16 [32, 48, 32, 128], P('band', 'space')
- margin: float32 [32, 32], P('space', 'band')
- projection: float32 [32, 32], P('space', 'band')
The draws below stay inside these ranges and needn't reach their ends.
Inputs may be any that keep to these rules, and one draw needn't show every extreme that they name: `atom_planes`: entry a is the first plane of atom a's box of 6 planes. In each aligned block of 4 entries (block s) every box starts at one of the planes s * 6 to s * 6 + 5, and in every block one atom starts at the first of these planes and another at the last.
All inputs are finite; a program needn't handle non-finite values.
Results may differ from the reference program's by a relative error of at most 0.0065.
Values may be sent and summed in bfloat16 or wider, within the bound.
No kernel may reach another device: no remote copies, remote signals or barrier semaphores. Data moves between devices by JAX's collectives and lax.ppermute only.
A program may use at most 192 MiB of HBM per device.

```python
import math
import jax
import jax.numpy as jnp
from jax import lax

CX = 6
NY = 32
NZ = 128
ATOM_DEV = 4
HALO = 6
BOX = 6
NPJ = 9
NX = 48
BANDS = 32
ATOMS = 32


def draw_atom_planes(key, part):
    slab_count = ATOMS // ATOM_DEV
    key_offsets = jax.random.fold_in(key, 11)
    key_first = jax.random.fold_in(key, 12)
    key_stride = jax.random.fold_in(key, 13)
    offsets = jax.random.randint(key_offsets, (slab_count, ATOM_DEV), 0, CX, dtype=jnp.int32)
    first = jax.random.randint(key_first, (slab_count, 1), 0, ATOM_DEV, dtype=jnp.int32)
    stride = jax.random.randint(key_stride, (slab_count, 1), 1, ATOM_DEV, dtype=jnp.int32)
    second = (first + stride) % ATOM_DEV
    column = jnp.arange(ATOM_DEV, dtype=jnp.int32)[None, :]
    offsets = jnp.where(column == first, 0, jnp.where(column == second, CX - 1, offsets))
    anchor = jnp.arange(slab_count, dtype=jnp.int32)[:, None] * CX
    return (anchor + offsets).reshape(-1).astype(jnp.int32)


def rough_values(key, shape):
    return jnp.clip(jax.random.normal(key, shape, jnp.float32), -3.0, 3.0)


def plane_envelope():
    planes = jnp.arange(NX, dtype=jnp.float32) / NX
    return 0.5 * jnp.exp(jnp.log(3.0) * planes)


def mixed_bands(key, salt, factor_low, factor_high):
    noise = rough_values(jax.random.fold_in(key, salt), (BANDS, NX, NY, NZ))
    shifts = jax.random.randint(jax.random.fold_in(key, salt + 1), (3,), 1, BANDS, dtype=jnp.int32)
    mixing = jax.random.uniform(jax.random.fold_in(key, salt + 2), (3,), jnp.float32, 0.2, 0.3)
    total = noise
    for index in range(3):
        total = total + mixing[index] * jnp.roll(noise, shifts[index], axis=0)
    factors = jax.random.uniform(jax.random.fold_in(key, salt + 3), (BANDS,), jnp.float32, factor_low, factor_high)
    envelope = plane_envelope()
    return factors[:, None, None, None] * envelope[None, :, None, None] * total


def draw_orbitals(key, part):
    return mixed_bands(key, 51, 0.6, 1.4)


def draw_previous(key, part):
    return mixed_bands(key, 61, 0.3, 0.8)


def shard_levels(rng, dims, shards, smallest, top_value):
    gain, own = 1.0, jax.random.fold_in(rng, 6)
    for dim, blocks in shards:
        heights = jnp.exp(jax.random.uniform(jax.random.fold_in(own, dim), (blocks,), jnp.float32, smallest / len(shards), top_value / len(shards)))
        gain = gain * jnp.repeat(heights, dims[dim] // blocks).reshape([-1 if axis == dim else 1 for axis in range(len(dims))])
    return gain


def centred(rng, extent, scale, most, split=(), kind=jnp.bfloat16):
    result = scale * jax.random.normal(rng, extent, jnp.float32)
    if split:
        result = result * shard_levels(rng, extent, split, -0.22, 0.18)
    return jnp.clip(result, -most, most).astype(kind)


def setup_inputs(seed: int = 0) -> dict:
    keys = jax.random.split(jax.random.key(seed), 7)
    return {
        "orbitals": draw_orbitals(jax.random.fold_in(keys[6], 71), 0),
        "previous": draw_previous(jax.random.fold_in(keys[6], 71), 0),
        "potential": centred(keys[2], (NX, NY, NZ), 1.0, 4.0, ((0, 8),), jnp.float32),
        "projectors": centred(keys[3], (ATOMS, NPJ, BOX, NY, NZ), (0.4 / (BOX * NY * NZ) ** 0.25), 0.1875, ((0, 8),)),
        "strengths": jnp.clip(jax.random.uniform(keys[4], (ATOMS, NPJ), jnp.float32, -3.0, 3.0), -3.0, 3.0),
        "atom_planes": draw_atom_planes(jax.random.fold_in(keys[6], 71), 0),
    }


stencil_weights = (-5369.0 / 1800.0, 12.0 / 7.0, -15.0 / 56.0, 10.0 / 189.0, -1.0 / 112.0, 2.0 / 1925.0, -1.0 / 16632.0)
center = 5.5
halfwidth = 5.5


def laplace_axis(field, axis):
    total = stencil_weights[0] * field
    for offset in range(1, HALO + 1):
        total = total + stencil_weights[offset] * (jnp.roll(field, offset, axis) + jnp.roll(field, -offset, axis))
    return total


def reference(orbitals, previous, potential, projectors, strengths, atom_planes):
    block = math.gcd(BANDS, 32)
    count = BANDS // block
    projector_values = projectors.astype(jnp.float32)

    def filter_block(block_pair):
        psi_block, prev_block = block_pair
        kinetic = -0.5 * (laplace_axis(psi_block, 1) + laplace_axis(psi_block, 2) + laplace_axis(psi_block, 3))

        def per_atom(accumulated, inputs):
            first_plane, values, scales = inputs
            planes = ((first_plane + jnp.arange(BOX, dtype=jnp.int32)) % NX).astype(jnp.int32)
            box_values = jnp.take(psi_block, planes, axis=1)
            coefficients = jnp.einsum("jpyz,bpyz->jb", values, box_values, precision=lax.Precision.HIGHEST)
            added = jnp.einsum("jpyz,jb->bpyz", values, coefficients * scales[:, None], precision=lax.Precision.HIGHEST)
            return accumulated.at[:, planes].add(added), None

        projected, unused = lax.scan(per_atom, jnp.zeros_like(psi_block), (atom_planes, projector_values, strengths))
        hamil = kinetic + potential[None] * psi_block + projected
        return ((2.0 / halfwidth) * (hamil - center * psi_block) - prev_block).astype(jnp.bfloat16)

    filtered = lax.map(filter_block, (orbitals.reshape(count, block, NX, NY, NZ), previous.reshape(count, block, NX, NY, NZ)))
    filtered = filtered.reshape(BANDS, NX, NY, NZ)
    scale = 1.0 / (NX * NY * NZ)
    rows = filtered.reshape(BANDS, -1)
    panel = orbitals.astype(jnp.bfloat16).reshape(BANDS, -1)
    margin = jnp.dot(rows, rows.T, preferred_element_type=jnp.float32) * scale
    projection = jnp.dot(rows, panel.T, preferred_element_type=jnp.float32) * scale
    return filtered, margin, projection
```

```python
import jax
import jax.numpy as jnp
import numpy as np
from jax import lax
from jax.experimental import pallas as pl
from jax.experimental.pallas import tpu as pltpu
from jax.sharding import PartitionSpec as P

HALO = 6
BOX = 6
NPJ = 9
HALF = 16

stencil_weights = (
    -5369.0 / 1800.0,
    12.0 / 7.0,
    -15.0 / 56.0,
    10.0 / 189.0,
    -1.0 / 112.0,
    2.0 / 1925.0,
    -1.0 / 16632.0,
)
center = 5.5
halfwidth = 5.5
outer = 2.0 / halfwidth
kinetic_weights = [-0.5 * outer * w for w in stencil_weights]

F32 = jnp.float32
BF16 = jnp.bfloat16


def params(vmem=48 * 2**20):
    return pltpu.CompilerParams(vmem_limit_bytes=vmem)


def circulant(n):
    c = np.zeros((n, n), np.float64)
    for i in range(n):
        c[i, i] += kinetic_weights[0]
        for m in range(1, HALO + 1):
            c[i, (i + m) % n] += kinetic_weights[m]
            c[i, (i - m) % n] += kinetic_weights[m]
    return c


def split_hi_lo(m):
    hi = np.asarray(m, np.float32).astype(jnp.bfloat16)
    lo = (m - hi.astype(np.float64)).astype(np.float32).astype(jnp.bfloat16)
    return hi, lo


def dot(a, b, dims=((1,), (0,))):
    return lax.dot_general(a, b, (dims, ((), ())), preferred_element_type=F32)


def local_kernel(psi_ref, prev_ref, pot_ref, cz_ref, cy_ref, g_ref):
    bands, planes, ny, nz = psi_ref.shape
    rows = bands * ny
    for x in range(planes):
        psi3 = psi_ref[:, x]
        psi = psi3.reshape(rows, nz)
        hi = psi.astype(BF16)
        lo = (psi - hi.astype(F32)).astype(BF16)
        both = jnp.concatenate([hi, lo], axis=1)
        along_z = dot(both, cz_ref[0 : 2 * nz]) + dot(hi, cz_ref[2 * nz : 3 * nz])
        pair = dot(cy_ref[0], both)
        along_y = pair[:, :nz] + pair[:, nz:] + dot(cy_ref[1], hi)
        total = (along_z + along_y).reshape(bands, ny, nz)
        total = total + (outer * pot_ref[x] + (kinetic_weights[0] - outer * center))[None] * psi3
        for m in range(1, HALO + 1):
            if x + m < planes:
                total = total + kinetic_weights[m] * psi_ref[:, x + m]
            if x - m >= 0:
                total = total + kinetic_weights[m] * psi_ref[:, x - m]
        g_ref[x] = total - prev_ref[:, x]


def projector_kernel(offs_ref, own_ref, upper_ref, proj_ref, s_ref, near_ref, next_ref, ext, acc):
    planes, bands, ny, nz = own_ref.shape
    atoms, npj = proj_ref.shape[:2]
    ext[0:planes] = own_ref[...]
    ext[planes : 2 * planes] = upper_ref[...]
    acc[...] = jnp.zeros_like(acc)
    rows, cols = bands * HALF, npj * HALF
    row_y = lax.broadcasted_iota(jnp.int32, (rows, cols), 0) % HALF
    col_y = lax.broadcasted_iota(jnp.int32, (rows, cols), 1) % HALF
    mask = jnp.where(row_y == col_y, 1.0, 0.0).astype(F32)
    gi = lax.broadcasted_iota(jnp.int32, (cols, cols), 0) // HALF
    gj = lax.broadcasted_iota(jnp.int32, (cols, cols), 1) // HALF
    group = jnp.where(gi == gj, 1.0, 0.0).astype(BF16)
    halves = [slice(h * HALF, (h + 1) * HALF) for h in range(ny // HALF)]

    def table(a, sl):
        return jnp.concatenate(
            [proj_ref[a, :, p, sl, :].reshape(cols, nz) for p in range(BOX)], axis=1
        )

    parts = []
    for a in range(atoms):
        start = offs_ref[a]
        total = None
        for sl in halves:
            left = jnp.concatenate(
                [ext[start + p, :, sl, :].reshape(rows, nz) for p in range(BOX)], axis=1
            )
            d = dot(left, table(a, sl), ((1,), (1,)))
            total = d if total is None else total + d
        parts.append((total * mask).reshape(bands, HALF, cols).sum(axis=1))
    e = jnp.concatenate(parts, axis=0)
    e_hi = e.astype(BF16)
    e_lo = (e - e_hi.astype(F32)).astype(BF16)
    coef = dot(e_hi, group) + dot(e_lo, group)
    for a in range(atoms):
        start = offs_ref[a]
        w = coef[a * bands : (a + 1) * bands] * s_ref[a : a + 1, :]
        full = jnp.broadcast_to(w[:, None, :], (bands, HALF, cols)).reshape(rows, cols) * mask
        full = full.astype(BF16)
        for sl in halves:
            out = dot(full, table(a, sl))
            for p in range(BOX):
                acc[start + p, :, sl, :] += out[:, p * nz : (p + 1) * nz].reshape(bands, HALF, nz)
    near_ref[...] = acc[0:planes]
    next_ref[...] = acc[planes : planes + BOX - 1].astype(BF16)


def halo_kernel(g_ref, near_ref, upper_ref, lower_ref, out_ref):
    planes = g_ref.shape[0]
    for x in range(planes):
        total = g_ref[x] + near_ref[x]
        for m in range(1, HALO + 1):
            if x + m >= planes:
                total = total + kinetic_weights[m] * upper_ref[x + m - planes].astype(F32)
            if x - m < 0:
                total = total + kinetic_weights[m] * lower_ref[x - m + planes].astype(F32)
        out_ref[x] = total


def finish_kernel(g_ref, arrived_ref, out_ref):
    planes = g_ref.shape[0]
    reach = arrived_ref.shape[0]
    for x in range(planes):
        total = g_ref[x]
        if x < reach:
            total = total + arrived_ref[x].astype(F32)
        out_ref[:, x] = total.astype(BF16)


def shards(orbitals, previous, potential, projectors, strengths, atom_planes):
    bands, planes, ny, nz = orbitals.shape
    n_space = lax.axis_size("space")
    n_band = lax.axis_size("band")
    atoms = projectors.shape[0]
    me = lax.axis_index("space")
    forward = [(i, (i + 1) % n_space) for i in range(n_space)]
    backward = [(target, source) for source, target in forward]

    psi16 = orbitals.astype(BF16)
    own = jnp.transpose(psi16, (1, 0, 2, 3))
    upper = lax.ppermute(own, "space", backward)
    lower = lax.ppermute(own, "space", forward)

    def to_quarters(block):
        cut = block.reshape(bands, n_band, planes * ny // n_band, nz)
        return lax.all_to_all(jnp.transpose(cut, (1, 0, 2, 3)), "band", 0, 0)

    panel = to_quarters(psi16)

    cz = circulant(nz)
    cz_hi, cz_lo = split_hi_lo(cz)
    cz_const = jnp.asarray(np.concatenate([cz_hi, cz_hi, cz_lo], axis=0))
    cy = np.kron(np.eye(bands), circulant(ny))
    cy_const = jnp.asarray(np.stack(split_hi_lo(cy)))
    shape = (planes, bands, ny, nz)
    g = pl.pallas_call(
        local_kernel,
        out_shape=jax.ShapeDtypeStruct(shape, F32),
        compiler_params=params(),
        name="local_part",
    )(orbitals, previous, potential, cz_const, cy_const)

    own_start = me * atoms
    offs = lax.dynamic_slice_in_dim(atom_planes, own_start, atoms, 0) - me * planes
    s = lax.dynamic_slice_in_dim(strengths, own_start, atoms, 0) * outer
    s_wide = jnp.repeat(s, HALF, axis=1)
    vm = pl.BlockSpec(memory_space=pltpu.VMEM)
    near, beyond = pl.pallas_call(
        projector_kernel,
        out_shape=(
            jax.ShapeDtypeStruct(shape, F32),
            jax.ShapeDtypeStruct((BOX - 1, bands, ny, nz), BF16),
        ),
        in_specs=[pl.BlockSpec(memory_space=pltpu.SMEM), vm, vm, vm, vm],
        out_specs=(vm, vm),
        scratch_shapes=[
            pltpu.VMEM((2 * planes, bands, ny, nz), BF16),
            pltpu.VMEM((2 * planes, bands, ny, nz), F32),
        ],
        compiler_params=params(),
        name="projector_part",
    )(offs, own, upper, projectors, s_wide)
    arrived = lax.ppermute(beyond, "space", forward)
    g = pl.pallas_call(
        halo_kernel,
        out_shape=jax.ShapeDtypeStruct(shape, F32),
        compiler_params=params(),
        name="halo_part",
    )(g, near, upper, lower)
    filtered = pl.pallas_call(
        finish_kernel,
        out_shape=jax.ShapeDtypeStruct((bands, planes, ny, nz), BF16),
        compiler_params=params(),
        name="finish",
    )(g, arrived)
    mine = to_quarters(filtered)
    total_bands = n_band * bands
    left = mine.reshape(total_bands, -1)
    right = jnp.concatenate([left, panel.reshape(total_bands, -1)], axis=0)
    scale = 1.0 / (planes * n_space * ny * nz)
    products = dot(left, right, ((1,), (1,))) * scale
    out_rows = total_bands // n_space
    pieces = products.reshape(n_space, out_rows, 2, n_band, bands)
    pieces = jnp.transpose(pieces, (0, 3, 1, 2, 4)).reshape(n_space * n_band, out_rows, 2 * bands)
    got = lax.all_to_all(pieces, ("space", "band"), 0, 0)
    share = got.sum(axis=0)
    return filtered, share[:, :bands], share[:, bands:]


def solution(mesh):
    in_specs = (
        P("band", "space", None, None),
        P("band", "space", None, None),
        P("space", None, None),
        P("space", None, None, None, None),
        P(),
        P(),
    )
    out_specs = (P("band", "space", None, None), P("space", "band"), P("space", "band"))
    return jax.shard_map(shards, mesh=mesh, in_specs=in_specs, out_specs=out_specs, check_vma=False)
```

```python
from functools import partial

import jax
import jax.numpy as jnp
import numpy as np
from jax import lax
from jax.experimental import pallas as pl
from jax.experimental.pallas import tpu as pltpu
from jax.sharding import PartitionSpec as P

HALO = 6
BOX = 6
NPJ = 9
HALF = 16

stencil_weights = (
    -5369.0 / 1800.0,
    12.0 / 7.0,
    -15.0 / 56.0,
    10.0 / 189.0,
    -1.0 / 112.0,
    2.0 / 1925.0,
    -1.0 / 16632.0,
)
center = 5.5
halfwidth = 5.5
outer = 2.0 / halfwidth
kinetic_weights = [-0.5 * outer * w for w in stencil_weights]

F32 = jnp.float32
BF16 = jnp.bfloat16


def params(vmem=48 * 2**20):
    return pltpu.CompilerParams(vmem_limit_bytes=vmem)


def circulant(n):
    c = np.zeros((n, n), np.float64)
    for i in range(n):
        c[i, i] += kinetic_weights[0]
        for m in range(1, HALO + 1):
            c[i, (i + m) % n] += kinetic_weights[m]
            c[i, (i - m) % n] += kinetic_weights[m]
    return c


def split_hi_lo(m):
    hi = np.asarray(m, np.float32).astype(jnp.bfloat16)
    lo = (m - hi.astype(np.float64)).astype(np.float32).astype(jnp.bfloat16)
    return hi, lo


def dot(a, b, dims=((1,), (0,))):
    return lax.dot_general(a, b, (dims, ((), ())), preferred_element_type=F32)


def plane_rows(x, ny):
    return slice(x * ny, (x + 1) * ny)


def pieces_of(ref, index, count, rows, outs):
    for shift, out in enumerate(outs):
        quarter = lax.rem(index + shift, count)
        begin = pl.multiple_of(quarter * rows, 8)
        out[...] = ref[:, pl.ds(begin, rows), :].astype(out.dtype)


def cast_kernel(count, psi_ref, half_ref, *outs):
    half_ref[...] = psi_ref[...].astype(BF16)
    rows = psi_ref.shape[1] // count
    pieces_of(psi_ref, lax.axis_index("band"), count, rows, outs)


def local_kernel(planes, psi_ref, prev_ref, pot_ref, cz_ref, cy_ref, g_ref):
    bands, cells, nz = psi_ref.shape
    ny = cells // planes
    rows = bands * ny
    for x in range(planes):
        here = plane_rows(x, ny)
        psi3 = psi_ref[:, here]
        psi = psi3.reshape(rows, nz)
        hi = psi.astype(BF16)
        lo = (psi - hi.astype(F32)).astype(BF16)
        both = jnp.concatenate([hi, lo], axis=1)
        along_z = dot(both, cz_ref[0 : 2 * nz]) + dot(hi, cz_ref[2 * nz : 3 * nz])
        pair = dot(cy_ref[0], both)
        along_y = pair[:, :nz] + pair[:, nz:] + dot(cy_ref[1], hi)
        total = (along_z + along_y).reshape(bands, ny, nz)
        site = outer * pot_ref[here] + (kinetic_weights[0] - outer * center)
        total = total + site[None] * psi3
        for m in range(1, HALO + 1):
            if x + m < planes:
                total = total + kinetic_weights[m] * psi_ref[:, plane_rows(x + m, ny)]
            if x - m >= 0:
                total = total + kinetic_weights[m] * psi_ref[:, plane_rows(x - m, ny)]
        g_ref[:, here] = total - prev_ref[:, here]


def projector_kernel(
    planes, first_ref, strength_ref, own_ref, upper_ref, proj_ref, near_ref, next_ref, ext, acc
):
    bands, cells, nz = own_ref.shape
    ny = cells // planes
    atoms, npj = proj_ref.shape[:2]
    me = lax.axis_index("space")
    for x in range(planes):
        ext[x] = own_ref[:, plane_rows(x, ny)]
        ext[planes + x] = upper_ref[:, plane_rows(x, ny)]
    acc[...] = jnp.zeros_like(acc)
    rows, cols = bands * HALF, npj * HALF
    row_y = lax.broadcasted_iota(jnp.int32, (rows, cols), 0) % HALF
    col_y = lax.broadcasted_iota(jnp.int32, (rows, cols), 1) % HALF
    mask = jnp.where(row_y == col_y, 1.0, 0.0).astype(F32)
    gi = lax.broadcasted_iota(jnp.int32, (cols, cols), 0) // HALF
    gj = lax.broadcasted_iota(jnp.int32, (cols, cols), 1) // HALF
    group = jnp.where(gi == gj, 1.0, 0.0).astype(BF16)
    owner = lax.broadcasted_iota(jnp.int32, (1, cols), 1) // HALF
    halves = [slice(h * HALF, (h + 1) * HALF) for h in range(ny // HALF)]
    starts = [first_ref[me * atoms + a] - me * planes for a in range(atoms)]

    def table(a, sl):
        return jnp.concatenate(
            [proj_ref[a, :, p, sl, :].reshape(cols, nz) for p in range(BOX)], axis=1
        )

    parts = []
    for a in range(atoms):
        total = None
        for sl in halves:
            left = jnp.concatenate(
                [ext[starts[a] + p, :, sl, :].reshape(rows, nz) for p in range(BOX)], axis=1
            )
            d = dot(left, table(a, sl), ((1,), (1,)))
            total = d if total is None else total + d
        parts.append((total * mask).reshape(bands, HALF, cols).sum(axis=1))
    e = jnp.concatenate(parts, axis=0)
    e_hi = e.astype(BF16)
    e_lo = (e - e_hi.astype(F32)).astype(BF16)
    coef = dot(e_hi, group) + dot(e_lo, group)
    for a in range(atoms):
        scale = jnp.zeros((1, cols), F32)
        for j in range(npj):
            scale = jnp.where(owner == j, outer * strength_ref[me * atoms + a, j], scale)
        w = coef[a * bands : (a + 1) * bands] * scale
        full = jnp.broadcast_to(w[:, None, :], (bands, HALF, cols)).reshape(rows, cols) * mask
        full = full.astype(BF16)
        for sl in halves:
            out = dot(full, table(a, sl))
            for p in range(BOX):
                acc[starts[a] + p, :, sl, :] += out[:, p * nz : (p + 1) * nz].reshape(
                    bands, HALF, nz
                )
    for x in range(planes):
        near_ref[:, plane_rows(x, ny)] = acc[x]
    for x in range(BOX - 1):
        next_ref[:, plane_rows(x, ny)] = acc[planes + x].astype(BF16)


def halo_kernel(planes, g_ref, near_ref, upper_ref, lower_ref, out_ref):
    ny = g_ref.shape[1] // planes
    for x in range(planes):
        here = plane_rows(x, ny)
        total = g_ref[:, here] + near_ref[:, here]
        for m in range(1, HALO + 1):
            if x + m >= planes:
                there = plane_rows(x + m - planes, ny)
                total = total + kinetic_weights[m] * upper_ref[:, there].astype(F32)
            if x - m < 0:
                there = plane_rows(x - m + planes, ny)
                total = total + kinetic_weights[m] * lower_ref[:, there].astype(F32)
        out_ref[:, here] = total


def finish_kernel(count, g_ref, arrived_ref, out_ref, *rest):
    outs, total = rest[:-1], rest[-1]
    reach = arrived_ref.shape[1]
    total[:, :reach] = g_ref[:, :reach] + arrived_ref[...].astype(F32)
    total[:, reach:] = g_ref[:, reach:]
    out_ref[...] = total[...].astype(BF16)
    rows = g_ref.shape[1] // count
    pieces_of(total, lax.axis_index("band"), count, rows, outs)


def split_kernel(count, prod_ref, *outs):
    bands = prod_ref.shape[0] // count
    me = lax.axis_index("band")
    for back, out in enumerate(outs):
        for j in range(count):
            shift = lax.rem(me - j + count, count)
            rows = pl.ds(pl.multiple_of(shift * bands, 8), bands)
            block = prod_ref[rows, :]
            cols = [block[:, (h * count + back) * bands : (h * count + back + 1) * bands] for h in (0, 1)]
            out[j * bands : (j + 1) * bands, :] = jnp.concatenate(cols, axis=1)


def sum_kernel(count, *refs):
    parts, outs, held = refs[:-count - 1], refs[-count - 1 : -1], refs[-1]
    total = parts[0][...]
    for part in parts[1:]:
        total = total + part[...]
    rows = total.shape[0] // count
    for i in range(count):
        held[i] = total[i * rows : (i + 1) * rows]
    me = lax.axis_index("space")
    for shift, out in enumerate(outs):
        out[...] = held[lax.rem(me + shift, count)]


def last_kernel(*refs):
    parts, outs = refs[:-2], refs[-2:]
    total = parts[0][...]
    for part in parts[1:]:
        total = total + part[...]
    bands = outs[0].shape[1]
    outs[0][...] = total[:, :bands]
    outs[1][...] = total[:, bands:]


def cyclic(value, axis, steps):
    count = lax.axis_size(axis)
    return lax.ppermute(value, axis, [(i, (i + steps) % count) for i in range(count)])


def struct(shape, kind=F32):
    return jax.ShapeDtypeStruct(shape, kind)


def call(kernel, name, out_shape, args, **extra):
    return pl.pallas_call(
        kernel, out_shape=out_shape, compiler_params=params(), name=name, **extra
    )(*args)


def shards(orbitals, previous, potential, projectors, strengths, atom_planes):
    bands, planes, ny, nz = orbitals.shape
    n_space = lax.axis_size("space")
    n_band = lax.axis_size("band")
    cells = planes * ny
    whole = (bands, cells, nz)
    quarter = (bands, cells // n_band, nz)
    psi = orbitals.reshape(whole)
    prev = previous.reshape(whole)
    pot = potential.reshape(cells, nz)

    half, *panel = call(
        partial(cast_kernel, n_band),
        "cast",
        (struct(whole, BF16),) + (struct(quarter, BF16),) * n_band,
        (psi,),
    )
    upper = cyclic(half, "space", -1)
    lower = cyclic(half, "space", 1)
    panel = [cyclic(piece, "band", shift) if shift else piece for shift, piece in enumerate(panel)]

    cz_hi, cz_lo = split_hi_lo(circulant(nz))
    cz = jnp.asarray(np.concatenate([cz_hi, cz_hi, cz_lo], axis=0))
    cy = jnp.asarray(np.stack(split_hi_lo(np.kron(np.eye(bands), circulant(ny)))))
    g = call(partial(local_kernel, planes), "local_part", struct(whole), (psi, prev, pot, cz, cy))
    upper, g = lax.optimization_barrier((upper, g))

    vm = pl.BlockSpec(memory_space=pltpu.VMEM)
    sm = pl.BlockSpec(memory_space=pltpu.SMEM)
    near, beyond = call(
        partial(projector_kernel, planes),
        "projector_part",
        (struct(whole), struct((bands, (BOX - 1) * ny, nz), BF16)),
        (atom_planes, strengths, half, upper, projectors),
        in_specs=[sm, sm, vm, vm, vm],
        out_specs=(vm, vm),
        scratch_shapes=[
            pltpu.VMEM((2 * planes, bands, ny, nz), BF16),
            pltpu.VMEM((2 * planes, bands, ny, nz), F32),
        ],
    )
    arrived = cyclic(beyond, "space", 1)
    g = call(partial(halo_kernel, planes), "halo_part", struct(whole), (g, near, upper, lower))
    filtered, *mine = call(
        partial(finish_kernel, n_band),
        "finish",
        (struct(whole, BF16),) + (struct(quarter, BF16),) * n_band,
        (g, arrived),
        scratch_shapes=[pltpu.VMEM(whole, F32)],
    )
    mine = [cyclic(piece, "band", shift) if shift else piece for shift, piece in enumerate(mine)]
    total_bands = n_band * bands
    left = jnp.concatenate(mine, axis=0).reshape(total_bands, -1)
    right = jnp.concatenate([left, jnp.concatenate(panel, axis=0).reshape(total_bands, -1)], axis=0)
    products = dot(left, right, ((1,), (1,))) * (1.0 / (cells * n_space * nz))
    blocks = call(
        partial(split_kernel, n_band),
        "split",
        (struct((total_bands, 2 * bands)),) * n_band,
        (products,),
    )
    blocks = [cyclic(b, "band", -shift) if shift else b for shift, b in enumerate(blocks)]
    out_rows = total_bands // n_space
    shares = call(
        partial(sum_kernel, n_space),
        "band_sum",
        (struct((out_rows, 2 * bands)),) * n_space,
        blocks,
        scratch_shapes=[pltpu.VMEM((n_space, out_rows, 2 * bands), F32)],
    )
    shares = [cyclic(b, "space", shift) if shift else b for shift, b in enumerate(shares)]
    margin, projection = call(
        last_kernel, "space_sum", (struct((out_rows, bands)), struct((out_rows, bands))), shares
    )
    return filtered.reshape(orbitals.shape), margin, projection


def solution(mesh):
    in_specs = (
        P("band", "space", None, None),
        P("band", "space", None, None),
        P("space", None, None),
        P("space", None, None, None, None),
        P(),
        P(),
    )
    out_specs = (P("band", "space", None, None), P("space", "band"), P("space", "band"))
    return jax.shard_map(shards, mesh=mesh, in_specs=in_specs, out_specs=out_specs, check_vma=False)
```

```python
from functools import partial

import jax
import jax.numpy as jnp
from jax import lax
from jax.experimental import pallas as pl
from jax.experimental.pallas import tpu as pltpu
from jax.sharding import PartitionSpec as P

HALO = 6
BOX = 6
NPJ = 9
HALF = 16

stencil_weights = (
    -5369.0 / 1800.0,
    12.0 / 7.0,
    -15.0 / 56.0,
    10.0 / 189.0,
    -1.0 / 112.0,
    2.0 / 1925.0,
    -1.0 / 16632.0,
)
center = 5.5
halfwidth = 5.5
outer = 2.0 / halfwidth
kinetic_weights = [-0.5 * outer * w for w in stencil_weights]

F32 = jnp.float32
BF16 = jnp.bfloat16


def params(vmem):
    return pltpu.CompilerParams(vmem_limit_bytes=vmem)


def circulant(n, blocks):
    size = n * blocks
    row = lax.broadcasted_iota(jnp.int32, (size, size), 0)
    col = lax.broadcasted_iota(jnp.int32, (size, size), 1)
    ahead = jnp.bitwise_and(col - row, n - 1)
    reach = jnp.minimum(ahead, n - ahead)
    value = jnp.zeros((size, size), F32)
    for m, weight in enumerate(kinetic_weights):
        value = jnp.where(reach == m, weight, value)
    value = jnp.where(row // n == col // n, value, 0.0)
    hi = value.astype(BF16)
    return hi, (value - hi.astype(F32)).astype(BF16)


def dot(a, b, dims=((1,), (0,))):
    return lax.dot_general(a, b, (dims, ((), ())), preferred_element_type=F32)


def plane_rows(x, ny):
    return slice(x * ny, (x + 1) * ny)


def partners(count):
    return [0, *range(count // 2, count), *range(1, count // 2)]


def pieces_of(ref, index, count, rows, outs):
    for bits, out in zip(partners(count), outs):
        quarter = jnp.bitwise_xor(index, bits)
        begin = pl.multiple_of(quarter * rows, 8)
        out[...] = ref[:, pl.ds(begin, rows), :].astype(out.dtype)


def cast_kernel(count, psi_ref, half_ref, *outs):
    half_ref[...] = psi_ref[...].astype(BF16)
    rows = psi_ref.shape[1] // count
    pieces_of(psi_ref, lax.axis_index("band"), count, rows, outs)


def local_kernel(planes, psi_ref, prev_hbm, pot_hbm, g_ref, half_ref, prev_ref, pot_ref, sems):
    copies = [
        pltpu.make_async_copy(prev_hbm, prev_ref, sems.at[0]),
        pltpu.make_async_copy(pot_hbm, pot_ref, sems.at[1]),
    ]
    for copy in copies:
        copy.start()
    half_ref[...] = psi_ref[...].astype(BF16)
    bands, cells, nz = psi_ref.shape
    ny = cells // planes
    rows = bands * ny
    cz_hi, cz_lo = circulant(nz, 1)
    cz_twice = jnp.concatenate([cz_hi, cz_hi], axis=0)
    cy_hi, cy_lo = circulant(ny, bands)
    for copy in copies:
        copy.wait()
    for x in range(planes):
        here = plane_rows(x, ny)
        psi3 = psi_ref[:, here]
        psi = psi3.reshape(rows, nz)
        hi = psi.astype(BF16)
        lo = (psi - hi.astype(F32)).astype(BF16)
        both = jnp.concatenate([hi, lo], axis=1)
        along_z = dot(both, cz_twice) + dot(hi, cz_lo)
        pair = dot(cy_hi, both)
        along_y = pair[:, :nz] + pair[:, nz:] + dot(cy_lo, hi)
        total = (along_z + along_y).reshape(bands, ny, nz)
        site = outer * pot_ref[here] + (kinetic_weights[0] - outer * center)
        total = total + site[None] * psi3
        for m in range(1, HALO + 1):
            if x + m < planes:
                total = total + kinetic_weights[m] * psi_ref[:, plane_rows(x + m, ny)]
            if x - m >= 0:
                total = total + kinetic_weights[m] * psi_ref[:, plane_rows(x - m, ny)]
        g_ref[:, here] = total - prev_ref[:, here]


def projector_kernel(
    planes, first_ref, strength_ref, own_ref, upper_ref, proj_ref, near_ref, next_ref, ext, acc
):
    bands, cells, nz = own_ref.shape
    ny = cells // planes
    atoms, npj = proj_ref.shape[:2]
    me = lax.axis_index("space")
    for x in range(planes):
        ext[x] = own_ref[:, plane_rows(x, ny)]
        ext[planes + x] = upper_ref[:, plane_rows(x, ny)]
    acc[...] = jnp.zeros_like(acc)
    rows, cols = bands * HALF, npj * HALF
    row_y = lax.broadcasted_iota(jnp.int32, (rows, cols), 0) % HALF
    col_y = lax.broadcasted_iota(jnp.int32, (rows, cols), 1) % HALF
    mask = jnp.where(row_y == col_y, 1.0, 0.0).astype(F32)
    gi = lax.broadcasted_iota(jnp.int32, (cols, cols), 0) // HALF
    gj = lax.broadcasted_iota(jnp.int32, (cols, cols), 1) // HALF
    group = jnp.where(gi == gj, 1.0, 0.0).astype(BF16)
    owner = lax.broadcasted_iota(jnp.int32, (1, cols), 1) // HALF
    halves = [slice(h * HALF, (h + 1) * HALF) for h in range(ny // HALF)]
    starts = [first_ref[me * atoms + a] - me * planes for a in range(atoms)]

    def table(a, sl):
        return jnp.concatenate(
            [proj_ref[a, :, p, sl, :].reshape(cols, nz) for p in range(BOX)], axis=1
        )

    parts = []
    for a in range(atoms):
        total = None
        for sl in halves:
            left = jnp.concatenate(
                [ext[starts[a] + p, :, sl, :].reshape(rows, nz) for p in range(BOX)], axis=1
            )
            d = dot(left, table(a, sl), ((1,), (1,)))
            total = d if total is None else total + d
        parts.append((total * mask).reshape(bands, HALF, cols).sum(axis=1))
    e = jnp.concatenate(parts, axis=0)
    e_hi = e.astype(BF16)
    e_lo = (e - e_hi.astype(F32)).astype(BF16)
    coef = dot(e_hi, group) + dot(e_lo, group)
    for a in range(atoms):
        scale = jnp.zeros((1, cols), F32)
        for j in range(npj):
            scale = jnp.where(owner == j, outer * strength_ref[j, me * atoms + a], scale)
        w = coef[a * bands : (a + 1) * bands] * scale
        full = jnp.broadcast_to(w[:, None, :], (bands, HALF, cols)).reshape(rows, cols) * mask
        full = full.astype(BF16)
        for sl in halves:
            out = dot(full, table(a, sl))
            for p in range(BOX):
                acc[starts[a] + p, :, sl, :] += out[:, p * nz : (p + 1) * nz].reshape(
                    bands, HALF, nz
                )
    for x in range(planes):
        near_ref[:, plane_rows(x, ny)] = acc[x]
    for x in range(BOX - 1):
        next_ref[:, plane_rows(x, ny)] = acc[planes + x].astype(BF16)


def halo_kernel(planes, g_ref, near_ref, upper_ref, lower_ref, out_ref):
    ny = g_ref.shape[1] // planes
    for x in range(planes):
        here = plane_rows(x, ny)
        total = g_ref[:, here] + near_ref[:, here]
        for m in range(1, HALO + 1):
            if x + m >= planes:
                there = plane_rows(x + m - planes, ny)
                total = total + kinetic_weights[m] * upper_ref[:, there].astype(F32)
            if x - m < 0:
                there = plane_rows(x - m + planes, ny)
                total = total + kinetic_weights[m] * lower_ref[:, there].astype(F32)
        out_ref[:, here] = total


def finish_kernel(count, g_ref, arrived_ref, out_ref, *rest):
    outs, total = rest[:-1], rest[-1]
    reach = arrived_ref.shape[1]
    total[:, :reach] = g_ref[:, :reach] + arrived_ref[...].astype(F32)
    total[:, reach:] = g_ref[:, reach:]
    out_ref[...] = total[...].astype(BF16)
    rows = g_ref.shape[1] // count
    pieces_of(total, lax.axis_index("band"), count, rows, outs)


def split_kernel(n_space, n_band, prod_ref, out_ref, held):
    bands = prod_ref.shape[0] // n_band
    me = lax.axis_index("band")
    for p, bits in enumerate(partners(n_band)):
        begin = pl.multiple_of(jnp.bitwise_xor(me, bits) * bands, 8)
        held[pl.ds(begin, bands), :] = prod_ref[p * bands : (p + 1) * bands]
    rows = held.shape[0] // n_space
    for p, bits in enumerate(partners(n_band)):
        cols = [slice((h * n_band + p) * bands, (h * n_band + p + 1) * bands) for h in (0, 1)]
        pair = jnp.concatenate([held[:, c] for c in cols], axis=1)
        owner = jnp.bitwise_xor(me, bits)
        for i in range(n_space):
            out_ref[i * n_band + owner] = pair[i * rows : (i + 1) * rows]


def last_kernel(got_ref, margin_ref, projection_ref):
    total = got_ref[...].sum(axis=0)
    bands = margin_ref.shape[1]
    margin_ref[...] = total[:, :bands]
    projection_ref[...] = total[:, bands:]


def cyclic(value, axis, steps):
    count = lax.axis_size(axis)
    return lax.ppermute(value, axis, [(i, (i + steps) % count) for i in range(count)])


def mirrored(value, axis, bits):
    count = lax.axis_size(axis)
    return lax.ppermute(value, axis, [(i, i ^ bits) for i in range(count)])


def exchanged(pieces):
    offsets = partners(len(pieces))
    return [mirrored(p, "band", bits) if bits else p for bits, p in zip(offsets, pieces)]


def struct(shape, kind=F32):
    return jax.ShapeDtypeStruct(shape, kind)


def call(kernel, name, out_shape, args, vmem=48, **extra):
    return pl.pallas_call(
        kernel, out_shape=out_shape, compiler_params=params(vmem * 2**20), name=name, **extra
    )(*args)


def shards(orbitals, previous, potential, projectors, strengths, atom_planes):
    bands, planes, ny, nz = orbitals.shape
    n_space = lax.axis_size("space")
    n_band = lax.axis_size("band")
    cells = planes * ny
    whole = (bands, cells, nz)
    quarter = (bands, cells // n_band, nz)
    psi = orbitals.reshape(whole)
    prev = previous.reshape(whole)
    pot = potential.reshape(cells, nz)

    vm = pl.BlockSpec(memory_space=pltpu.VMEM)
    sm = pl.BlockSpec(memory_space=pltpu.SMEM)
    anywhere = pl.BlockSpec(memory_space=pl.ANY)

    half, *panel = call(
        partial(cast_kernel, n_band),
        "cast",
        (struct(whole, BF16),) + (struct(quarter, BF16),) * n_band,
        (psi,),
    )
    upper = cyclic(half, "space", -1)
    panel = exchanged(panel)

    g, again = call(
        partial(local_kernel, planes),
        "local_part",
        (struct(whole), struct(whole, BF16)),
        (psi, prev, pot),
        vmem=58,
        in_specs=[vm, anywhere, anywhere],
        out_specs=(vm, vm),
        scratch_shapes=[
            pltpu.VMEM(whole, F32),
            pltpu.VMEM(pot.shape, F32),
            pltpu.SemaphoreType.DMA((2,)),
        ],
    )
    lower = cyclic(again, "space", 1)
    upper, g = lax.optimization_barrier((upper, g))

    near, beyond = call(
        partial(projector_kernel, planes),
        "projector_part",
        (struct(whole), struct((bands, (BOX - 1) * ny, nz), BF16)),
        (atom_planes, strengths.T, half, upper, projectors),
        in_specs=[sm, sm, vm, vm, vm],
        out_specs=(vm, vm),
        scratch_shapes=[
            pltpu.VMEM((2 * planes, bands, ny, nz), BF16),
            pltpu.VMEM((2 * planes, bands, ny, nz), F32),
        ],
    )
    arrived = cyclic(beyond, "space", 1)
    g = call(partial(halo_kernel, planes), "halo_part", struct(whole), (g, near, upper, lower))
    filtered, *mine = call(
        partial(finish_kernel, n_band),
        "finish",
        (struct(whole, BF16),) + (struct(quarter, BF16),) * n_band,
        (g, arrived),
        scratch_shapes=[pltpu.VMEM(whole, F32)],
    )
    mine = exchanged(mine)
    total_bands = n_band * bands
    left = jnp.concatenate(mine, axis=0).reshape(total_bands, -1)
    right = jnp.concatenate([left, jnp.concatenate(panel, axis=0).reshape(total_bands, -1)], axis=0)
    products = dot(left, right, ((1,), (1,))) * (1.0 / (cells * n_space * nz))
    out_rows = total_bands // n_space
    pieces = call(
        partial(split_kernel, n_space, n_band),
        "split",
        struct((n_space * n_band, out_rows, 2 * bands)),
        (products,),
        scratch_shapes=[pltpu.VMEM(products.shape, F32)],
    )
    got = lax.all_to_all(pieces, ("space", "band"), 0, 0)
    margin, projection = call(
        last_kernel, "last_sum", (struct((out_rows, bands)), struct((out_rows, bands))), (got,)
    )
    return filtered.reshape(orbitals.shape), margin, projection


def solution(mesh):
    in_specs = (
        P("band", "space", None, None),
        P("band", "space", None, None),
        P("space", None, None),
        P("space", None, None, None, None),
        P(),
        P(),
    )
    out_specs = (P("band", "space", None, None), P("space", "band"), P("space", "band"))
    return jax.shard_map(shards, mesh=mesh, in_specs=in_specs, out_specs=out_specs, check_vma=False)
```

```python
from functools import partial

import jax
import jax.numpy as jnp
from jax import lax
from jax.experimental import pallas as pl
from jax.experimental.pallas import tpu as pltpu
from jax.sharding import PartitionSpec as P

HALO = 6
BOX = 6
NPJ = 9
HALF = 16

stencil_weights = (
    -5369.0 / 1800.0,
    12.0 / 7.0,
    -15.0 / 56.0,
    10.0 / 189.0,
    -1.0 / 112.0,
    2.0 / 1925.0,
    -1.0 / 16632.0,
)
center = 5.5
halfwidth = 5.5
outer = 2.0 / halfwidth
kinetic_weights = [-0.5 * outer * w for w in stencil_weights]

F32 = jnp.float32
BF16 = jnp.bfloat16


def params(vmem):
    return pltpu.CompilerParams(vmem_limit_bytes=vmem)


def circulant(n, blocks):
    size = n * blocks
    row = lax.broadcasted_iota(jnp.int32, (size, size), 0)
    col = lax.broadcasted_iota(jnp.int32, (size, size), 1)
    ahead = jnp.bitwise_and(col - row, n - 1)
    reach = jnp.minimum(ahead, n - ahead)
    value = jnp.zeros((size, size), F32)
    for m, weight in enumerate(kinetic_weights):
        value = jnp.where(reach == m, weight, value)
    value = jnp.where(jnp.bitwise_xor(row, col) < n, value, 0.0)
    hi = value.astype(BF16)
    return hi, (value - hi.astype(F32)).astype(BF16)


def dot(a, b, dims=((1,), (0,))):
    return lax.dot_general(a, b, (dims, ((), ())), preferred_element_type=F32)


def plane_rows(x, ny):
    return slice(x * ny, (x + 1) * ny)


def partners(count):
    return [0, *range(count // 2, count), *range(1, count // 2)]


def pieces_of(ref, index, count, rows, outs):
    for bits, out in zip(partners(count), outs):
        quarter = jnp.bitwise_xor(index, bits)
        begin = pl.multiple_of(quarter * rows, 8)
        out[...] = ref[:, pl.ds(begin, rows), :].astype(out.dtype)


def cast_kernel(count, psi_ref, half_ref, *outs):
    half_ref[...] = psi_ref[...].astype(BF16)
    rows = psi_ref.shape[1] // count
    pieces_of(psi_ref, lax.axis_index("band"), count, rows, outs)


def local_kernel(planes, psi_ref, prev_hbm, pot_hbm, g_ref, half_ref, prev_ref, pot_ref, sems):
    copies = [
        pltpu.make_async_copy(prev_hbm, prev_ref, sems.at[0]),
        pltpu.make_async_copy(pot_hbm, pot_ref, sems.at[1]),
    ]
    for copy in copies:
        copy.start()
    half_ref[...] = psi_ref[...].astype(BF16)
    bands, cells, nz = psi_ref.shape
    ny = cells // planes
    rows = bands * ny
    cz_hi, cz_lo = circulant(nz, 1)
    cz_twice = jnp.concatenate([cz_hi, cz_hi], axis=0)
    cy_hi, cy_lo = circulant(ny, bands)
    for copy in copies:
        copy.wait()
    for x in range(planes):
        here = plane_rows(x, ny)
        psi3 = psi_ref[:, here]
        psi = psi3.reshape(rows, nz)
        hi = psi.astype(BF16)
        lo = (psi - hi.astype(F32)).astype(BF16)
        both = jnp.concatenate([hi, lo], axis=1)
        along_z = dot(both, cz_twice) + dot(hi, cz_lo)
        pair = dot(cy_hi, both)
        along_y = pair[:, :nz] + pair[:, nz:] + dot(cy_lo, hi)
        total = (along_z + along_y).reshape(bands, ny, nz)
        site = outer * pot_ref[here] + (kinetic_weights[0] - outer * center)
        total = total + site[None] * psi3
        for m in range(1, HALO + 1):
            if x + m < planes:
                total = total + kinetic_weights[m] * psi_ref[:, plane_rows(x + m, ny)]
            if x - m >= 0:
                total = total + kinetic_weights[m] * psi_ref[:, plane_rows(x - m, ny)]
        g_ref[:, here] = total - prev_ref[:, here]


def same_cell(rows, cols):
    row = lax.broadcasted_iota(jnp.int32, (rows, cols), 0)
    col = lax.broadcasted_iota(jnp.int32, (rows, cols), 1)
    return jnp.where(jnp.bitwise_and(row - col, HALF - 1) == 0, 1.0, 0.0).astype(F32)


def table(proj_ref, a, p):
    npj, ny, nz = proj_ref.shape[1], proj_ref.shape[3], proj_ref.shape[4]
    halves = [
        proj_ref[a, :, p, h * HALF : (h + 1) * HALF, :].reshape(npj * HALF, nz)
        for h in range(ny // HALF)
    ]
    return jnp.concatenate(halves, axis=1)


def spread_weights(w_ref, bands, atoms, mask):
    cols = mask.shape[1]
    out = []
    for a in range(atoms):
        w = w_ref[a * bands : (a + 1) * bands]
        full = jnp.broadcast_to(w[:, None, :], (bands, HALF, cols)).reshape(bands * HALF, cols)
        out.append((full * mask).astype(BF16))
    return out


def spread_plane(weights, proj_ref, plane_of, valid):
    total = None
    for a, w in enumerate(weights):
        p = jnp.clip(plane_of[a], 0, BOX - 1)
        term = dot(w, table(proj_ref, a, p)) * jnp.where(valid[a], 1.0, 0.0)
        total = term if total is None else total + term
    nz = proj_ref.shape[4]
    rows = total.shape[0]
    return [
        total[:, h * nz : (h + 1) * nz].reshape(rows // HALF, HALF, nz)
        for h in range(total.shape[1] // nz)
    ]


def coefficient_kernel(
    planes, first_ref, strength_ref, own_ref, upper_ref, proj_ref, w_ref, next_ref, ext
):
    bands, cells, nz = own_ref.shape
    ny = cells // planes
    atoms, npj = proj_ref.shape[:2]
    me = lax.axis_index("space")
    for x in range(planes):
        ext[x] = own_ref[:, plane_rows(x, ny)]
        if x < BOX - 1:
            ext[planes + x] = upper_ref[:, plane_rows(x, ny)]
    rows, cols = bands * HALF, npj * HALF
    mask = same_cell(rows, cols)
    gi = lax.broadcasted_iota(jnp.int32, (cols, cols), 0)
    gj = lax.broadcasted_iota(jnp.int32, (cols, cols), 1)
    group = jnp.where(jnp.bitwise_xor(gi, gj) < HALF, 1.0, 0.0).astype(BF16)
    owner = lax.broadcasted_iota(jnp.int32, (1, cols), 1)
    starts = [first_ref[me * atoms + a] - me * planes for a in range(atoms)]
    halves = range(ny // HALF)

    parts = []
    for a in range(atoms):
        left = [
            ext[starts[a] + p, :, h * HALF : (h + 1) * HALF, :].reshape(rows, nz)
            for p in range(BOX)
            for h in halves
        ]
        right = [table(proj_ref, a, p) for p in range(BOX)]
        d = dot(jnp.concatenate(left, axis=1), jnp.concatenate(right, axis=1), ((1,), (1,)))
        parts.append((d * mask).reshape(bands, HALF, cols).sum(axis=1))
    e = jnp.concatenate(parts, axis=0)
    e_hi = e.astype(BF16)
    e_lo = (e - e_hi.astype(F32)).astype(BF16)
    coef = dot(e_hi, group) + dot(e_lo, group)
    for a in range(atoms):
        scale = jnp.zeros((1, cols), F32)
        for j in range(npj):
            scale = jnp.where(owner >= j * HALF, outer * strength_ref[j, me * atoms + a], scale)
        w_ref[a * bands : (a + 1) * bands] = coef[a * bands : (a + 1) * bands] * scale
    weights = spread_weights(w_ref, bands, atoms, mask)
    for q in range(BOX - 1):
        blocks = spread_plane(
            weights, proj_ref, [planes + q - s for s in starts], [planes + q - s < BOX for s in starts]
        )
        for h in halves:
            begin = q * ny + h * HALF
            next_ref[:, begin : begin + HALF] = blocks[h].astype(BF16)


def near_kernel(planes, first_ref, w_ref, g_ref, upper_ref, lower_ref, proj_ref, out_ref):
    bands, cells, nz = g_ref.shape
    ny = cells // planes
    atoms, npj = proj_ref.shape[:2]
    me = lax.axis_index("space")
    starts = [first_ref[me * atoms + a] - me * planes for a in range(atoms)]
    weights = spread_weights(w_ref, bands, atoms, same_cell(bands * HALF, npj * HALF))
    for x in range(planes):
        blocks = spread_plane(
            weights, proj_ref, [x - s for s in starts], [jnp.logical_and(x >= s, x - s < BOX) for s in starts]
        )
        for h, block in enumerate(blocks):
            def here(plane):
                return slice(plane * ny + h * HALF, plane * ny + (h + 1) * HALF)

            total = g_ref[:, here(x)] + block
            for m in range(1, HALO + 1):
                if x + m >= planes:
                    there = here(x + m - planes)
                    total = total + kinetic_weights[m] * upper_ref[:, there].astype(F32)
                if x - m < 0:
                    there = here(x - m + planes)
                    total = total + kinetic_weights[m] * lower_ref[:, there].astype(F32)
            out_ref[:, here(x)] = total


def with_arrived(g_ref, arrived_ref, total):
    reach = arrived_ref.shape[1]
    total[:, :reach] = g_ref[:, :reach] + arrived_ref[...].astype(F32)
    total[:, reach:] = g_ref[:, reach:]


def finish_kernel(count, g_ref, arrived_ref, *rest):
    outs, total = rest[:-1], rest[-1]
    with_arrived(g_ref, arrived_ref, total)
    rows = g_ref.shape[1] // count
    pieces_of(total, lax.axis_index("band"), count, rows, outs)


def output_kernel(g_ref, arrived_ref, out_ref):
    reach = arrived_ref.shape[1]
    out_ref[:, :reach] = (g_ref[:, :reach] + arrived_ref[...].astype(F32)).astype(BF16)
    out_ref[:, reach:] = g_ref[:, reach:].astype(BF16)


def split_kernel(n_space, n_band, prod_ref, out_ref, held):
    bands = prod_ref.shape[0] // n_band
    me = lax.axis_index("band")
    for p, bits in enumerate(partners(n_band)):
        begin = pl.multiple_of(jnp.bitwise_xor(me, bits) * bands, 8)
        held[pl.ds(begin, bands), :] = prod_ref[p * bands : (p + 1) * bands]
    rows = held.shape[0] // n_space
    for p, bits in enumerate(partners(n_band)):
        cols = [slice((h * n_band + p) * bands, (h * n_band + p + 1) * bands) for h in (0, 1)]
        pair = jnp.concatenate([held[:, c] for c in cols], axis=1)
        owner = jnp.bitwise_xor(me, bits)
        for i in range(n_space):
            out_ref[i * n_band + owner] = pair[i * rows : (i + 1) * rows]


def last_kernel(got_ref, margin_ref, projection_ref):
    total = got_ref[...].sum(axis=0)
    bands = margin_ref.shape[1]
    margin_ref[...] = total[:, :bands]
    projection_ref[...] = total[:, bands:]


def cyclic(value, axis, steps):
    count = lax.axis_size(axis)
    return lax.ppermute(value, axis, [(i, (i + steps) % count) for i in range(count)])


def mirrored(value, axis, bits):
    count = lax.axis_size(axis)
    return lax.ppermute(value, axis, [(i, i ^ bits) for i in range(count)])


def exchanged(pieces):
    offsets = partners(len(pieces))
    return [mirrored(p, "band", bits) if bits else p for bits, p in zip(offsets, pieces)]


def struct(shape, kind=F32):
    return jax.ShapeDtypeStruct(shape, kind)


def call(kernel, name, out_shape, args, vmem=48, **extra):
    return pl.pallas_call(
        kernel, out_shape=out_shape, compiler_params=params(vmem * 2**20), name=name, **extra
    )(*args)


def shards(orbitals, previous, potential, projectors, strengths, atom_planes):
    bands, planes, ny, nz = orbitals.shape
    n_space = lax.axis_size("space")
    n_band = lax.axis_size("band")
    cells = planes * ny
    whole = (bands, cells, nz)
    quarter = (bands, cells // n_band, nz)
    psi = orbitals.reshape(whole)
    prev = previous.reshape(whole)
    pot = potential.reshape(cells, nz)

    vm = pl.BlockSpec(memory_space=pltpu.VMEM)
    sm = pl.BlockSpec(memory_space=pltpu.SMEM)
    anywhere = pl.BlockSpec(memory_space=pl.ANY)

    half, *panel = call(
        partial(cast_kernel, n_band),
        "cast",
        (struct(whole, BF16),) + (struct(quarter, BF16),) * n_band,
        (psi,),
    )
    upper = cyclic(half, "space", -1)
    panel = exchanged(panel)

    g, again = call(
        partial(local_kernel, planes),
        "local_part",
        (struct(whole), struct(whole, BF16)),
        (psi, prev, pot),
        vmem=58,
        in_specs=[vm, anywhere, anywhere],
        out_specs=(vm, vm),
        scratch_shapes=[
            pltpu.VMEM(whole, F32),
            pltpu.VMEM(pot.shape, F32),
            pltpu.SemaphoreType.DMA((2,)),
        ],
    )
    lower = cyclic(again, "space", 1)
    upper, g = lax.optimization_barrier((upper, g))

    w, beyond = call(
        partial(coefficient_kernel, planes),
        "coefficients",
        (
            struct((projectors.shape[0] * bands, projectors.shape[1] * HALF)),
            struct((bands, (BOX - 1) * ny, nz), BF16),
        ),
        (atom_planes, strengths.T, half, upper, projectors),
        in_specs=[sm, sm, vm, vm, vm],
        out_specs=(vm, vm),
        scratch_shapes=[pltpu.VMEM((planes + BOX - 1, bands, ny, nz), BF16)],
    )
    arrived = cyclic(beyond, "space", 1)
    g = call(
        partial(near_kernel, planes),
        "near_part",
        struct(whole),
        (atom_planes, w, g, upper, lower, projectors),
        in_specs=[sm, vm, vm, vm, vm, vm],
        out_specs=vm,
        cost_estimate=pl.CostEstimate(flops=2 * 10**10, bytes_accessed=4 * 2**20, transcendentals=0),
    )
    mine = call(
        partial(finish_kernel, n_band),
        "finish",
        (struct(quarter, BF16),) * n_band,
        (g, arrived),
        scratch_shapes=[pltpu.VMEM(whole, F32)],
    )
    filtered = call(output_kernel, "output", struct(whole, BF16), (g, arrived))
    mine = exchanged(mine)
    total_bands = n_band * bands
    left = jnp.concatenate(mine, axis=0).reshape(total_bands, -1)
    right = jnp.concatenate([left, jnp.concatenate(panel, axis=0).reshape(total_bands, -1)], axis=0)
    products = dot(left, right, ((1,), (1,))) * (1.0 / (cells * n_space * nz))
    out_rows = total_bands // n_space
    pieces = call(
        partial(split_kernel, n_space, n_band),
        "split",
        struct((n_space * n_band, out_rows, 2 * bands)),
        (products,),
        scratch_shapes=[pltpu.VMEM(products.shape, F32)],
    )
    got = lax.all_to_all(pieces, ("space", "band"), 0, 0)
    margin, projection = call(
        last_kernel, "last_sum", (struct((out_rows, bands)), struct((out_rows, bands))), (got,)
    )
    return filtered.reshape(orbitals.shape), margin, projection


def solution(mesh):
    in_specs = (
        P("band", "space", None, None),
        P("band", "space", None, None),
        P("space", None, None),
        P("space", None, None, None, None),
        P(),
        P(),
    )
    out_specs = (P("band", "space", None, None), P("space", "band"), P("space", "band"))
    return jax.shard_map(shards, mesh=mesh, in_specs=in_specs, out_specs=out_specs, check_vma=False)
```

```python
from functools import partial

import jax
import jax.numpy as jnp
from jax import lax
from jax.experimental import pallas as pl
from jax.experimental.pallas import tpu as pltpu
from jax.sharding import PartitionSpec as P

HALO = 6
BOX = 6
NPJ = 9
HALF = 16

stencil_weights = (
    -5369.0 / 1800.0,
    12.0 / 7.0,
    -15.0 / 56.0,
    10.0 / 189.0,
    -1.0 / 112.0,
    2.0 / 1925.0,
    -1.0 / 16632.0,
)
center = 5.5
halfwidth = 5.5
outer = 2.0 / halfwidth
kinetic_weights = [-0.5 * outer * w for w in stencil_weights]

F32 = jnp.float32
BF16 = jnp.bfloat16


def params(vmem):
    return pltpu.CompilerParams(vmem_limit_bytes=vmem)


def circulant(n, blocks):
    size = n * blocks
    row = lax.broadcasted_iota(jnp.int32, (size, size), 0)
    col = lax.broadcasted_iota(jnp.int32, (size, size), 1)
    ahead = jnp.bitwise_and(col - row, n - 1)
    reach = jnp.minimum(ahead, n - ahead)
    value = jnp.zeros((size, size), F32)
    for m, weight in enumerate(kinetic_weights):
        value = jnp.where(reach == m, weight, value)
    value = jnp.where(jnp.bitwise_xor(row, col) < n, value, 0.0)
    hi = value.astype(BF16)
    return hi, (value - hi.astype(F32)).astype(BF16)


def dot(a, b, dims=((1,), (0,))):
    return lax.dot_general(a, b, (dims, ((), ())), preferred_element_type=F32)


def plane_rows(x, ny):
    return slice(x * ny, (x + 1) * ny)


def partners(count):
    return [0, *range(count // 2, count), *range(1, count // 2)]


def pieces_of(ref, index, count, rows, outs):
    for bits, out in zip(partners(count), outs):
        quarter = jnp.bitwise_xor(index, bits)
        begin = pl.multiple_of(quarter * rows, 8)
        out[...] = ref[:, pl.ds(begin, rows), :].astype(out.dtype)


def cast_kernel(count, psi_ref, half_ref, *outs):
    half_ref[...] = psi_ref[...].astype(BF16)
    rows = psi_ref.shape[1] // count
    pieces_of(psi_ref, lax.axis_index("band"), count, rows, outs)


def yz_part(psi, cz, cy):
    bands, ny, nz = psi.shape
    flat = psi.reshape(bands * ny, nz)
    hi = flat.astype(BF16)
    lo = (flat - hi.astype(F32)).astype(BF16)
    both = jnp.concatenate([hi, lo], axis=1)
    along_z = dot(both, cz[0]) + dot(hi, cz[1])
    size = cy[0].shape[0]
    along_y = []
    for begin in range(0, bands * ny, size):
        pair = dot(cy[0], both[begin : begin + size])
        along_y.append(pair[:, :nz] + pair[:, nz:] + dot(cy[1], hi[begin : begin + size]))
    return (along_z + jnp.concatenate(along_y, axis=0)).reshape(bands, ny, nz)


def same_cell(rows, cols):
    row = lax.broadcasted_iota(jnp.int32, (rows, cols), 0)
    col = lax.broadcasted_iota(jnp.int32, (rows, cols), 1)
    return jnp.where(jnp.bitwise_and(row - col, HALF - 1) == 0, 1.0, 0.0).astype(F32)


def table(proj_ref, a, p):
    npj, ny, nz = proj_ref.shape[1], proj_ref.shape[3], proj_ref.shape[4]
    halves = [
        proj_ref[a, :, p, h * HALF : (h + 1) * HALF, :].reshape(npj * HALF, nz)
        for h in range(ny // HALF)
    ]
    return jnp.concatenate(halves, axis=1)


def spread_weights(w_ref, bands, atoms, mask):
    cols = mask.shape[1]
    out = []
    for a in range(atoms):
        w = w_ref[a * bands : (a + 1) * bands]
        full = jnp.broadcast_to(w[:, None, :], (bands, HALF, cols)).reshape(bands * HALF, cols)
        out.append((full * mask).astype(BF16))
    return out


def spread_plane(weights, proj_ref, plane_of, valid):
    total = None
    for a, w in enumerate(weights):
        p = jnp.clip(plane_of[a], 0, BOX - 1)
        term = dot(w, table(proj_ref, a, p)) * jnp.where(valid[a], 1.0, 0.0)
        total = term if total is None else total + term
    nz = proj_ref.shape[4]
    rows = total.shape[0]
    return [
        total[:, h * nz : (h + 1) * nz].reshape(rows // HALF, HALF, nz)
        for h in range(total.shape[1] // nz)
    ]


def coefficient_kernel(
    planes, first_ref, strength_ref, own_ref, upper_ref, proj_ref, w_ref, next_ref, ext
):
    bands, cells, nz = own_ref.shape
    ny = cells // planes
    atoms, npj = proj_ref.shape[:2]
    me = lax.axis_index("space")
    for x in range(planes):
        ext[x] = own_ref[:, plane_rows(x, ny)]
        if x < BOX - 1:
            ext[planes + x] = upper_ref[:, plane_rows(x, ny)]
    rows, cols = bands * HALF, npj * HALF
    mask = same_cell(rows, cols)
    gi = lax.broadcasted_iota(jnp.int32, (cols, cols), 0)
    gj = lax.broadcasted_iota(jnp.int32, (cols, cols), 1)
    group = jnp.where(jnp.bitwise_xor(gi, gj) < HALF, 1.0, 0.0).astype(BF16)
    owner = lax.broadcasted_iota(jnp.int32, (1, cols), 1)
    starts = [first_ref[me * atoms + a] - me * planes for a in range(atoms)]
    halves = range(ny // HALF)

    parts = []
    for a in range(atoms):
        left = [
            ext[starts[a] + p, :, h * HALF : (h + 1) * HALF, :].reshape(rows, nz)
            for p in range(BOX)
            for h in halves
        ]
        right = [table(proj_ref, a, p) for p in range(BOX)]
        d = dot(jnp.concatenate(left, axis=1), jnp.concatenate(right, axis=1), ((1,), (1,)))
        parts.append((d * mask).reshape(bands, HALF, cols).sum(axis=1))
    e = jnp.concatenate(parts, axis=0)
    e_hi = e.astype(BF16)
    e_lo = (e - e_hi.astype(F32)).astype(BF16)
    coef = dot(e_hi, group) + dot(e_lo, group)
    for a in range(atoms):
        scale = jnp.zeros((1, cols), F32)
        for j in range(npj):
            scale = jnp.where(owner >= j * HALF, outer * strength_ref[j, me * atoms + a], scale)
        w_ref[a * bands : (a + 1) * bands] = coef[a * bands : (a + 1) * bands] * scale
    weights = spread_weights(w_ref, bands, atoms, mask)
    for q in range(BOX - 1):
        blocks = spread_plane(
            weights, proj_ref, [planes + q - s for s in starts], [planes + q - s < BOX for s in starts]
        )
        for h in halves:
            begin = q * ny + h * HALF
            next_ref[:, begin : begin + HALF] = blocks[h].astype(BF16)


def local_kernel(planes, psi_ref, g_ref, half_ref):
    half_ref[...] = psi_ref[...].astype(BF16)
    bands, cells, nz = psi_ref.shape
    ny = cells // planes
    cz_hi, cz_lo = circulant(nz, 1)
    cz = (jnp.concatenate([cz_hi, cz_hi], axis=0), cz_lo)
    cy = circulant(ny, bands // 2)
    for x in range(planes):
        here = plane_rows(x, ny)
        psi = psi_ref[:, here]
        total = yz_part(psi, cz, cy) + (kinetic_weights[0] - outer * center) * psi
        for m in range(1, HALO + 1):
            for target in (x + m, x - m):
                if 0 <= target < planes:
                    total = total + kinetic_weights[m] * psi_ref[:, plane_rows(target, ny)]
        g_ref[:, here] = total


def near_kernel(
    planes, first_ref, g_ref, psi_ref, prev_ref, pot_ref, w_ref, upper_ref, lower_ref, proj_ref, out_ref
):
    bands, cells, nz = psi_ref.shape
    ny = cells // planes
    atoms, npj = proj_ref.shape[:2]
    me = lax.axis_index("space")
    starts = [first_ref[me * atoms + a] - me * planes for a in range(atoms)]
    weights = spread_weights(w_ref, bands, atoms, same_cell(bands * HALF, npj * HALF))
    for x in range(planes):
        blocks = spread_plane(
            weights, proj_ref, [x - s for s in starts], [jnp.logical_and(x >= s, x - s < BOX) for s in starts]
        )
        here = plane_rows(x, ny)
        total = g_ref[:, here] + jnp.concatenate(blocks, axis=1)
        total = total + (outer * pot_ref[here])[None] * psi_ref[:, here] - prev_ref[:, here]
        for m in range(1, HALO + 1):
            if x + m >= planes:
                there = plane_rows(x + m - planes, ny)
                total = total + kinetic_weights[m] * upper_ref[:, there].astype(F32)
            if x - m < 0:
                there = plane_rows(x - m + planes, ny)
                total = total + kinetic_weights[m] * lower_ref[:, there].astype(F32)
        out_ref[:, here] = total


def with_arrived(g_ref, arrived_ref, total):
    reach = arrived_ref.shape[1]
    total[:, :reach] = g_ref[:, :reach] + arrived_ref[...].astype(F32)
    total[:, reach:] = g_ref[:, reach:]


def finish_kernel(count, g_ref, arrived_ref, *rest):
    outs, total = rest[:-1], rest[-1]
    with_arrived(g_ref, arrived_ref, total)
    rows = g_ref.shape[1] // count
    pieces_of(total, lax.axis_index("band"), count, rows, outs)


def output_kernel(g_ref, arrived_ref, *rest):
    pieces, (out_ref, panel_ref) = rest[:-2], rest[-2:]
    reach = arrived_ref.shape[1]
    out_ref[:, :reach] = (g_ref[:, :reach] + arrived_ref[...].astype(F32)).astype(BF16)
    out_ref[:, reach:] = g_ref[:, reach:].astype(BF16)
    bands = g_ref.shape[0]
    for p, piece in enumerate(pieces):
        panel_ref[p * bands : (p + 1) * bands] = piece[...]


def split_kernel(n_space, n_band, prod_ref, out_ref, held):
    bands = prod_ref.shape[0] // n_band
    me = lax.axis_index("band")
    for p, bits in enumerate(partners(n_band)):
        begin = pl.multiple_of(jnp.bitwise_xor(me, bits) * bands, 8)
        held[pl.ds(begin, bands), :] = prod_ref[p * bands : (p + 1) * bands]
    rows = held.shape[0] // n_space
    for p, bits in enumerate(partners(n_band)):
        cols = [slice((h * n_band + p) * bands, (h * n_band + p + 1) * bands) for h in (0, 1)]
        pair = jnp.concatenate([held[:, c] for c in cols], axis=1)
        owner = jnp.bitwise_xor(me, bits)
        for i in range(n_space):
            out_ref[i * n_band + owner] = pair[i * rows : (i + 1) * rows]


def last_kernel(got_ref, margin_ref, projection_ref):
    total = got_ref[...].sum(axis=0)
    bands = margin_ref.shape[1]
    margin_ref[...] = total[:, :bands]
    projection_ref[...] = total[:, bands:]


def cyclic(value, axis, steps):
    count = lax.axis_size(axis)
    return lax.ppermute(value, axis, [(i, (i + steps) % count) for i in range(count)])


def mirrored(value, axis, bits):
    count = lax.axis_size(axis)
    return lax.ppermute(value, axis, [(i, i ^ bits) for i in range(count)])


def exchanged(pieces):
    offsets = partners(len(pieces))
    return [mirrored(p, "band", bits) if bits else p for bits, p in zip(offsets, pieces)]


def struct(shape, kind=F32):
    return jax.ShapeDtypeStruct(shape, kind)


def call(kernel, name, out_shape, args, vmem=48, **extra):
    return pl.pallas_call(
        kernel, out_shape=out_shape, compiler_params=params(vmem * 2**20), name=name, **extra
    )(*args)


def shards(orbitals, previous, potential, projectors, strengths, atom_planes):
    bands, planes, ny, nz = orbitals.shape
    n_space = lax.axis_size("space")
    n_band = lax.axis_size("band")
    cells = planes * ny
    whole = (bands, cells, nz)
    quarter = (bands, cells // n_band, nz)
    psi = orbitals.reshape(whole)
    prev = previous.reshape(whole)
    pot = potential.reshape(cells, nz)

    vm = pl.BlockSpec(memory_space=pltpu.VMEM)
    sm = pl.BlockSpec(memory_space=pltpu.SMEM)
    anywhere = pl.BlockSpec(memory_space=pl.ANY)

    half, *panel = call(
        partial(cast_kernel, n_band),
        "cast",
        (struct(whole, BF16),) + (struct(quarter, BF16),) * n_band,
        (psi,),
    )
    upper = cyclic(half, "space", -1)
    panel = exchanged(panel)

    g, again = call(
        partial(local_kernel, planes),
        "local_part",
        (struct(whole), struct(whole, BF16)),
        (psi,),
        cost_estimate=pl.CostEstimate(flops=10**9, bytes_accessed=2**20, transcendentals=0),
    )
    lower = cyclic(again, "space", 1)
    upper, g = lax.optimization_barrier((upper, g))
    w, beyond = call(
        partial(coefficient_kernel, planes),
        "coefficients",
        (
            struct((projectors.shape[0] * bands, projectors.shape[1] * HALF)),
            struct((bands, (BOX - 1) * ny, nz), BF16),
        ),
        (atom_planes, strengths.T, half, upper, projectors),
        in_specs=[sm, sm, vm, vm, vm],
        out_specs=(vm, vm),
        scratch_shapes=[pltpu.VMEM((planes + BOX - 1, bands, ny, nz), BF16)],
    )
    arrived = cyclic(beyond, "space", 1)
    g = call(
        partial(near_kernel, planes),
        "near_part",
        struct(whole),
        (atom_planes, g, psi, prev, pot, w, upper, lower, projectors),
        in_specs=[sm] + [vm] * 8,
        out_specs=vm,
        cost_estimate=pl.CostEstimate(flops=2 * 10**10, bytes_accessed=4 * 2**20, transcendentals=0),
    )
    mine = call(
        partial(finish_kernel, n_band),
        "finish",
        (struct(quarter, BF16),) * n_band,
        (g, arrived),
        scratch_shapes=[pltpu.VMEM(whole, F32)],
    )
    mine = exchanged(mine)
    total_bands = n_band * bands
    filtered, panels = call(
        output_kernel,
        "output",
        (struct(whole, BF16), struct((total_bands, *quarter[1:]), BF16)),
        (g, arrived, *panel),
    )
    left = jnp.concatenate(mine, axis=0).reshape(total_bands, -1)
    right = jnp.concatenate([left, panels.reshape(total_bands, -1)], axis=0)
    products = dot(left, right, ((1,), (1,))) * (1.0 / (cells * n_space * nz))
    out_rows = total_bands // n_space
    pieces = call(
        partial(split_kernel, n_space, n_band),
        "split",
        struct((n_space * n_band, out_rows, 2 * bands)),
        (products,),
        scratch_shapes=[pltpu.VMEM(products.shape, F32)],
    )
    got = lax.all_to_all(pieces, ("space", "band"), 0, 0)
    margin, projection = call(
        last_kernel, "last_sum", (struct((out_rows, bands)), struct((out_rows, bands))), (got,)
    )
    return filtered.reshape(orbitals.shape), margin, projection


def solution(mesh):
    in_specs = (
        P("band", "space", None, None),
        P("band", "space", None, None),
        P("space", None, None),
        P("space", None, None, None, None),
        P(),
        P(),
    )
    out_specs = (P("band", "space", None, None), P("space", "band"), P("space", "band"))
    return jax.shard_map(shards, mesh=mesh, in_specs=in_specs, out_specs=out_specs, check_vma=False)
```

```python
from functools import partial

import jax
import jax.numpy as jnp
from jax import lax
from jax.experimental import pallas as pl
from jax.experimental.pallas import tpu as pltpu
from jax.sharding import PartitionSpec as P

HALO = 6
BOX = 6
NPJ = 9
HALF = 16

stencil_weights = (
    -5369.0 / 1800.0,
    12.0 / 7.0,
    -15.0 / 56.0,
    10.0 / 189.0,
    -1.0 / 112.0,
    2.0 / 1925.0,
    -1.0 / 16632.0,
)
center = 5.5
halfwidth = 5.5
outer = 2.0 / halfwidth
kinetic_weights = [-0.5 * outer * w for w in stencil_weights]

F32 = jnp.float32
BF16 = jnp.bfloat16


def params(vmem):
    return pltpu.CompilerParams(vmem_limit_bytes=vmem)


def circulant(n, blocks):
    size = n * blocks
    row = lax.broadcasted_iota(jnp.int32, (size, size), 0)
    col = lax.broadcasted_iota(jnp.int32, (size, size), 1)
    ahead = jnp.bitwise_and(col - row, n - 1)
    reach = jnp.minimum(ahead, n - ahead)
    value = jnp.zeros((size, size), F32)
    for m, weight in enumerate(kinetic_weights):
        value = jnp.where(reach == m, weight, value)
    value = jnp.where(jnp.bitwise_xor(row, col) < n, value, 0.0)
    hi = value.astype(BF16)
    return hi, (value - hi.astype(F32)).astype(BF16)


def dot(a, b, dims=((1,), (0,))):
    return lax.dot_general(a, b, (dims, ((), ())), preferred_element_type=F32)


def plane_rows(x, ny):
    return slice(x * ny, (x + 1) * ny)


def partners(count):
    return [0, *reversed(range(1, count))]


def pieces_of(ref, index, count, rows, outs):
    for bits, out in zip(partners(count), outs):
        quarter = jnp.bitwise_xor(index, bits)
        begin = pl.multiple_of(quarter * rows, 8)
        out[...] = ref[:, pl.ds(begin, rows), :].astype(out.dtype)


def cast_kernel(count, psi_ref, half_ref, *outs):
    half_ref[...] = psi_ref[...].astype(BF16)
    rows = psi_ref.shape[1] // count
    pieces_of(psi_ref, lax.axis_index("band"), count, rows, outs)


def yz_part(psi, cz, cy):
    bands, ny, nz = psi.shape
    flat = psi.reshape(bands * ny, nz)
    hi = flat.astype(BF16)
    lo = (flat - hi.astype(F32)).astype(BF16)
    both = jnp.concatenate([hi, lo], axis=1)
    along_z = dot(both, cz[0]) + dot(hi, cz[1])
    size = cy[0].shape[0]
    along_y = []
    for begin in range(0, bands * ny, size):
        pair = dot(cy[0], both[begin : begin + size])
        along_y.append(pair[:, :nz] + pair[:, nz:] + dot(cy[1], hi[begin : begin + size]))
    return (along_z + jnp.concatenate(along_y, axis=0)).reshape(bands, ny, nz)


def same_cell(rows, cols):
    row = lax.broadcasted_iota(jnp.int32, (rows, cols), 0)
    col = lax.broadcasted_iota(jnp.int32, (rows, cols), 1)
    return jnp.where(jnp.bitwise_and(row - col, HALF - 1) == 0, 1.0, 0.0).astype(F32)


def table(proj_ref, a, p):
    npj, ny, nz = proj_ref.shape[1], proj_ref.shape[3], proj_ref.shape[4]
    halves = [
        proj_ref[a, :, p, h * HALF : (h + 1) * HALF, :].reshape(npj * HALF, nz)
        for h in range(ny // HALF)
    ]
    return jnp.concatenate(halves, axis=1)


def spread_weights(w_ref, bands, atoms, mask):
    cols = mask.shape[1]
    out = []
    for a in range(atoms):
        w = w_ref[a * bands : (a + 1) * bands]
        full = jnp.broadcast_to(w[:, None, :], (bands, HALF, cols)).reshape(bands * HALF, cols)
        out.append((full * mask).astype(BF16))
    return out


def spread_plane(weights, proj_ref, plane_of, valid):
    total = None
    for a, w in enumerate(weights):
        p = jnp.clip(plane_of[a], 0, BOX - 1)
        term = dot(w, table(proj_ref, a, p)) * jnp.where(valid[a], 1.0, 0.0)
        total = term if total is None else total + term
    nz = proj_ref.shape[4]
    rows = total.shape[0]
    return [
        total[:, h * nz : (h + 1) * nz].reshape(rows // HALF, HALF, nz)
        for h in range(total.shape[1] // nz)
    ]


def coefficient_kernel(
    planes, first_ref, strength_ref, own_ref, upper_ref, proj_ref, w_ref, next_ref, ext
):
    bands, cells, nz = own_ref.shape
    ny = cells // planes
    atoms, npj = proj_ref.shape[:2]
    me = lax.axis_index("space")
    for x in range(planes):
        ext[x] = own_ref[:, plane_rows(x, ny)]
        if x < BOX - 1:
            ext[planes + x] = upper_ref[:, plane_rows(x, ny)]
    rows, cols = bands * HALF, npj * HALF
    mask = same_cell(rows, cols)
    gi = lax.broadcasted_iota(jnp.int32, (cols, cols), 0)
    gj = lax.broadcasted_iota(jnp.int32, (cols, cols), 1)
    group = jnp.where(jnp.bitwise_xor(gi, gj) < HALF, 1.0, 0.0).astype(BF16)
    owner = lax.broadcasted_iota(jnp.int32, (1, cols), 1)
    starts = [first_ref[me * atoms + a] - me * planes for a in range(atoms)]
    halves = range(ny // HALF)

    parts = []
    for a in range(atoms):
        left = [
            ext[starts[a] + p, :, h * HALF : (h + 1) * HALF, :].reshape(rows, nz)
            for p in range(BOX)
            for h in halves
        ]
        right = [table(proj_ref, a, p) for p in range(BOX)]
        d = dot(jnp.concatenate(left, axis=1), jnp.concatenate(right, axis=1), ((1,), (1,)))
        parts.append((d * mask).reshape(bands, HALF, cols).sum(axis=1))
    e = jnp.concatenate(parts, axis=0)
    e_hi = e.astype(BF16)
    e_lo = (e - e_hi.astype(F32)).astype(BF16)
    coef = dot(e_hi, group) + dot(e_lo, group)
    for a in range(atoms):
        scale = jnp.zeros((1, cols), F32)
        for j in range(npj):
            scale = jnp.where(owner >= j * HALF, outer * strength_ref[j, me * atoms + a], scale)
        w_ref[a * bands : (a + 1) * bands] = coef[a * bands : (a + 1) * bands] * scale
    weights = spread_weights(w_ref, bands, atoms, mask)
    for q in range(BOX - 1):
        blocks = spread_plane(
            weights, proj_ref, [planes + q - s for s in starts], [planes + q - s < BOX for s in starts]
        )
        for h in halves:
            begin = q * ny + h * HALF
            next_ref[:, begin : begin + HALF] = blocks[h].astype(BF16)


def again_kernel(half_ref, *refs):
    refs[-1][...] = half_ref[...]


def near_kernel(planes, unused, first_ref, *refs):
    near_body(planes, first_ref, *refs[unused:])


def near_body(
    planes, first_ref, psi_ref, prev_ref, pot_ref, w_ref, upper_ref, lower_ref, proj_ref, out_ref
):
    bands, cells, nz = psi_ref.shape
    ny = cells // planes
    atoms, npj = proj_ref.shape[:2]
    me = lax.axis_index("space")
    starts = [first_ref[me * atoms + a] - me * planes for a in range(atoms)]
    weights = spread_weights(w_ref, bands, atoms, same_cell(bands * HALF, npj * HALF))
    cz_hi, cz_lo = circulant(nz, 1)
    cz = (jnp.concatenate([cz_hi, cz_hi], axis=0), cz_lo)
    cy = circulant(ny, bands // 2)
    for x in range(planes):
        blocks = spread_plane(
            weights, proj_ref, [x - s for s in starts], [jnp.logical_and(x >= s, x - s < BOX) for s in starts]
        )
        here = plane_rows(x, ny)
        psi = psi_ref[:, here]
        total = yz_part(psi, cz, cy) + jnp.concatenate(blocks, axis=1)
        site = outer * pot_ref[here] + (kinetic_weights[0] - outer * center)
        total = total + site[None] * psi - prev_ref[:, here]
        for m in range(1, HALO + 1):
            for target in (x + m, x - m):
                if target >= planes:
                    value = upper_ref[:, plane_rows(target - planes, ny)].astype(F32)
                elif target < 0:
                    value = lower_ref[:, plane_rows(target + planes, ny)].astype(F32)
                else:
                    value = psi_ref[:, plane_rows(target, ny)]
                total = total + kinetic_weights[m] * value
        out_ref[:, here] = total


def with_arrived(g_ref, arrived_ref, total):
    reach = arrived_ref.shape[1]
    total[:, :reach] = g_ref[:, :reach] + arrived_ref[...].astype(F32)
    total[:, reach:] = g_ref[:, reach:]


def finish_kernel(count, g_ref, arrived_ref, *rest):
    outs, total = rest[:-1], rest[-1]
    with_arrived(g_ref, arrived_ref, total)
    rows = g_ref.shape[1] // count
    pieces_of(total, lax.axis_index("band"), count, rows, outs)


def output_kernel(g_ref, arrived_ref, *rest):
    pieces, (out_ref, panel_ref) = rest[:-2], rest[-2:]
    reach = arrived_ref.shape[1]
    out_ref[:, :reach] = (g_ref[:, :reach] + arrived_ref[...].astype(F32)).astype(BF16)
    out_ref[:, reach:] = g_ref[:, reach:].astype(BF16)
    bands = g_ref.shape[0]
    for p, piece in enumerate(pieces):
        panel_ref[p * bands : (p + 1) * bands] = piece[...]


def split_kernel(n_space, n_band, prod_ref, out_ref, held):
    bands = prod_ref.shape[0] // n_band
    me = lax.axis_index("band")
    for p, bits in enumerate(partners(n_band)):
        begin = pl.multiple_of(jnp.bitwise_xor(me, bits) * bands, 8)
        held[pl.ds(begin, bands), :] = prod_ref[p * bands : (p + 1) * bands]
    rows = held.shape[0] // n_space
    for p, bits in enumerate(partners(n_band)):
        cols = [slice((h * n_band + p) * bands, (h * n_band + p + 1) * bands) for h in (0, 1)]
        pair = jnp.concatenate([held[:, c] for c in cols], axis=1)
        owner = jnp.bitwise_xor(me, bits)
        for i in range(n_space):
            out_ref[i * n_band + owner] = pair[i * rows : (i + 1) * rows]


def last_kernel(got_ref, margin_ref, projection_ref):
    total = got_ref[...].sum(axis=0)
    bands = margin_ref.shape[1]
    margin_ref[...] = total[:, :bands]
    projection_ref[...] = total[:, bands:]


def cyclic(value, axis, steps):
    count = lax.axis_size(axis)
    return lax.ppermute(value, axis, [(i, (i + steps) % count) for i in range(count)])


def mirrored(value, axis, bits):
    count = lax.axis_size(axis)
    return lax.ppermute(value, axis, [(i, i ^ bits) for i in range(count)])


def exchanged(pieces):
    offsets = partners(len(pieces))
    return [mirrored(p, "band", bits) if bits else p for bits, p in zip(offsets, pieces)]


def struct(shape, kind=F32):
    return jax.ShapeDtypeStruct(shape, kind)


def call(kernel, name, out_shape, args, vmem=48, **extra):
    return pl.pallas_call(
        kernel, out_shape=out_shape, compiler_params=params(vmem * 2**20), name=name, **extra
    )(*args)


def shards(orbitals, previous, potential, projectors, strengths, atom_planes):
    bands, planes, ny, nz = orbitals.shape
    n_space = lax.axis_size("space")
    n_band = lax.axis_size("band")
    cells = planes * ny
    whole = (bands, cells, nz)
    quarter = (bands, cells // n_band, nz)
    psi = orbitals.reshape(whole)
    prev = previous.reshape(whole)
    pot = potential.reshape(cells, nz)

    vm = pl.BlockSpec(memory_space=pltpu.VMEM)
    sm = pl.BlockSpec(memory_space=pltpu.SMEM)
    anywhere = pl.BlockSpec(memory_space=pl.ANY)

    half, *panel = call(
        partial(cast_kernel, n_band),
        "cast",
        (struct(whole, BF16),) + (struct(quarter, BF16),) * n_band,
        (psi,),
    )
    upper = cyclic(half, "space", -1)
    panel = exchanged(panel)

    again = call(
        again_kernel,
        "again",
        struct(whole, BF16),
        (half, panel[3]),
        in_specs=[vm] + [anywhere] * 1,
        out_specs=vm,
        cost_estimate=pl.CostEstimate(flops=10**9, bytes_accessed=2**20, transcendentals=0),
    )
    lower = cyclic(again, "space", 1)
    w, beyond = call(
        partial(coefficient_kernel, planes),
        "coefficients",
        (
            struct((projectors.shape[0] * bands, projectors.shape[1] * HALF)),
            struct((bands, (BOX - 1) * ny, nz), BF16),
        ),
        (atom_planes, strengths.T, half, upper, projectors),
        in_specs=[sm, sm, vm, vm, vm],
        out_specs=(vm, vm),
        scratch_shapes=[pltpu.VMEM((planes + BOX - 1, bands, ny, nz), BF16)],
        cost_estimate=pl.CostEstimate(flops=10**10, bytes_accessed=2**20, transcendentals=0),
    )
    arrived = cyclic(beyond, "space", 1)
    g = call(
        partial(near_kernel, planes, 1),
        "near_part",
        struct(whole),
        (atom_planes, panel[2], psi, prev, pot, w, upper, lower, projectors),
        in_specs=[sm] + [anywhere] * 1 + [vm] * 7,
        out_specs=vm,
        cost_estimate=pl.CostEstimate(flops=2*10**10, bytes_accessed=4 * 2**20, transcendentals=0),
    )
    mine = call(
        partial(finish_kernel, n_band),
        "finish",
        (struct(quarter, BF16),) * n_band,
        (g, arrived),
        scratch_shapes=[pltpu.VMEM(whole, F32)],
    )
    mine = exchanged(mine)
    total_bands = n_band * bands
    filtered, panels = call(
        output_kernel,
        "output",
        (struct(whole, BF16), struct((total_bands, *quarter[1:]), BF16)),
        (g, arrived, *panel),
    )
    left = jnp.concatenate(mine, axis=0).reshape(total_bands, -1)
    right = jnp.concatenate([left, panels.reshape(total_bands, -1)], axis=0)
    products = dot(left, right, ((1,), (1,))) * (1.0 / (cells * n_space * nz))
    out_rows = total_bands // n_space
    pieces = call(
        partial(split_kernel, n_space, n_band),
        "split",
        struct((n_space * n_band, out_rows, 2 * bands)),
        (products,),
        scratch_shapes=[pltpu.VMEM(products.shape, F32)],
    )
    got = lax.all_to_all(pieces, ("space", "band"), 0, 0)
    margin, projection = call(
        last_kernel, "last_sum", (struct((out_rows, bands)), struct((out_rows, bands))), (got,)
    )
    return filtered.reshape(orbitals.shape), margin, projection


def solution(mesh):
    in_specs = (
        P("band", "space", None, None),
        P("band", "space", None, None),
        P("space", None, None),
        P("space", None, None, None, None),
        P(),
        P(),
    )
    out_specs = (P("band", "space", None, None), P("space", "band"), P("space", "band"))
    return jax.shard_map(shards, mesh=mesh, in_specs=in_specs, out_specs=out_specs, check_vma=False)
```

```python
from functools import partial

import jax
import jax.numpy as jnp
from jax import lax
from jax.experimental import pallas as pl
from jax.experimental.pallas import tpu as pltpu
from jax.sharding import PartitionSpec as P

HALO = 6
BOX = 6
NPJ = 9
HALF = 16

stencil_weights = (
    -5369.0 / 1800.0,
    12.0 / 7.0,
    -15.0 / 56.0,
    10.0 / 189.0,
    -1.0 / 112.0,
    2.0 / 1925.0,
    -1.0 / 16632.0,
)
center = 5.5
halfwidth = 5.5
outer = 2.0 / halfwidth
kinetic_weights = [-0.5 * outer * w for w in stencil_weights]

F32 = jnp.float32
BF16 = jnp.bfloat16


def params(vmem):
    return pltpu.CompilerParams(vmem_limit_bytes=vmem)


def circulant(n, blocks):
    size = n * blocks
    row = lax.broadcasted_iota(jnp.int32, (size, size), 0)
    col = lax.broadcasted_iota(jnp.int32, (size, size), 1)
    ahead = jnp.bitwise_and(col - row, n - 1)
    reach = jnp.minimum(ahead, n - ahead)
    value = jnp.zeros((size, size), F32)
    for m, weight in enumerate(kinetic_weights):
        value = jnp.where(reach == m, weight, value)
    value = jnp.where(jnp.bitwise_xor(row, col) < n, value, 0.0)
    hi = value.astype(BF16)
    return hi, (value - hi.astype(F32)).astype(BF16)


def dot(a, b, dims=((1,), (0,))):
    return lax.dot_general(a, b, (dims, ((), ())), preferred_element_type=F32)


def plane_rows(x, ny):
    return slice(x * ny, (x + 1) * ny)


def partners(count):
    return range(count)


def pieces_of(ref, index, count, rows, outs):
    for bits, out in zip(partners(count), outs):
        quarter = jnp.bitwise_xor(index, bits)
        begin = pl.multiple_of(quarter * rows, 8)
        out[...] = ref[:, pl.ds(begin, rows), :].astype(out.dtype)


def cast_kernel(count, psi_ref, half_ref, *outs):
    half_ref[...] = psi_ref[...].astype(BF16)
    rows = psi_ref.shape[1] // count
    pieces_of(psi_ref, lax.axis_index("band"), count, rows, outs)


def yz_part(psi, cz, cy):
    bands, ny, nz = psi.shape
    flat = psi.reshape(bands * ny, nz)
    hi = flat.astype(BF16)
    lo = (flat - hi.astype(F32)).astype(BF16)
    both = jnp.concatenate([hi, lo], axis=1)
    along_z = dot(both, cz[0]) + dot(hi, cz[1])
    size = cy[0].shape[0]
    along_y = []
    for begin in range(0, bands * ny, size):
        pair = dot(cy[0], both[begin : begin + size])
        along_y.append(pair[:, :nz] + pair[:, nz:] + dot(cy[1], hi[begin : begin + size]))
    return (along_z + jnp.concatenate(along_y, axis=0)).reshape(bands, ny, nz)


def same_cell(rows, cols):
    row = lax.broadcasted_iota(jnp.int32, (rows, cols), 0)
    col = lax.broadcasted_iota(jnp.int32, (rows, cols), 1)
    return jnp.where(jnp.bitwise_and(row - col, HALF - 1) == 0, 1.0, 0.0).astype(F32)


def table(proj_ref, a, p):
    npj, ny, nz = proj_ref.shape[1], proj_ref.shape[3], proj_ref.shape[4]
    halves = [
        proj_ref[a, :, p, h * HALF : (h + 1) * HALF, :].reshape(npj * HALF, nz)
        for h in range(ny // HALF)
    ]
    return jnp.concatenate(halves, axis=1)


def spread_weights(w_ref, bands, atoms, mask):
    cols = mask.shape[1]
    out = []
    for a in range(atoms):
        w = w_ref[a * bands : (a + 1) * bands]
        full = jnp.broadcast_to(w[:, None, :], (bands, HALF, cols)).reshape(bands * HALF, cols)
        out.append((full * mask).astype(BF16))
    return out


def spread_plane(weights, proj_ref, plane_of, valid):
    total = None
    for a, w in enumerate(weights):
        p = jnp.clip(plane_of[a], 0, BOX - 1)
        term = dot(w, table(proj_ref, a, p)) * jnp.where(valid[a], 1.0, 0.0)
        total = term if total is None else total + term
    nz = proj_ref.shape[4]
    rows = total.shape[0]
    return [
        total[:, h * nz : (h + 1) * nz].reshape(rows // HALF, HALF, nz)
        for h in range(total.shape[1] // nz)
    ]


def coefficient_kernel(
    planes, first_ref, strength_ref, own_ref, upper_ref, proj_ref, ahead_ref, w_ref, next_ref, ext
):
    bands, cells, nz = own_ref.shape
    ny = cells // planes
    atoms, npj = proj_ref.shape[:2]
    me = lax.axis_index("space")
    for x in range(planes):
        ext[x] = own_ref[:, plane_rows(x, ny)]
        if x < BOX - 1:
            ext[planes + x] = upper_ref[:, plane_rows(x, ny)]
    rows, cols = bands * HALF, npj * HALF
    mask = same_cell(rows, cols)
    gi = lax.broadcasted_iota(jnp.int32, (cols, cols), 0)
    gj = lax.broadcasted_iota(jnp.int32, (cols, cols), 1)
    group = jnp.where(jnp.bitwise_xor(gi, gj) < HALF, 1.0, 0.0).astype(BF16)
    owner = lax.broadcasted_iota(jnp.int32, (1, cols), 1)
    starts = [first_ref[me * atoms + a] - me * planes for a in range(atoms)]
    halves = range(ny // HALF)

    parts = []
    for a in range(atoms):
        left = [
            ext[starts[a] + p, :, h * HALF : (h + 1) * HALF, :].reshape(rows, nz)
            for p in range(BOX)
            for h in halves
        ]
        right = [table(proj_ref, a, p) for p in range(BOX)]
        d = dot(jnp.concatenate(left, axis=1), jnp.concatenate(right, axis=1), ((1,), (1,)))
        parts.append((d * mask).reshape(bands, HALF, cols).sum(axis=1))
    e = jnp.concatenate(parts, axis=0)
    e_hi = e.astype(BF16)
    e_lo = (e - e_hi.astype(F32)).astype(BF16)
    coef = dot(e_hi, group) + dot(e_lo, group)
    for a in range(atoms):
        scale = jnp.zeros((1, cols), F32)
        for j in range(npj):
            scale = jnp.where(owner >= j * HALF, outer * strength_ref[j, me * atoms + a], scale)
        w_ref[a * bands : (a + 1) * bands] = coef[a * bands : (a + 1) * bands] * scale
    weights = spread_weights(w_ref, bands, atoms, mask)
    for q in range(BOX - 1):
        blocks = spread_plane(
            weights, proj_ref, [planes + q - s for s in starts], [planes + q - s < BOX for s in starts]
        )
        for h in halves:
            begin = q * ny + h * HALF
            block = blocks[h] + ahead_ref[:, begin : begin + HALF]
            next_ref[:, begin : begin + HALF] = block.astype(BF16)
    rest = slice((BOX - 1) * ny, planes * ny)
    next_ref[:, rest] = ahead_ref[:, rest].astype(BF16)


def ahead_kernel(planes, psi_ref, out_ref):
    ny = psi_ref.shape[1] // planes
    for x in range(planes):
        total = None
        for m in range(x + 1, HALO + 1):
            term = kinetic_weights[m] * psi_ref[:, plane_rows(planes + x - m, ny)]
            total = term if total is None else total + term
        out_ref[:, plane_rows(x, ny)] = total


def near_kernel(
    planes, first_ref, psi_ref, prev_ref, pot_ref, w_ref, upper_ref, proj_ref, out_ref
):
    bands, cells, nz = psi_ref.shape
    ny = cells // planes
    atoms, npj = proj_ref.shape[:2]
    me = lax.axis_index("space")
    starts = [first_ref[me * atoms + a] - me * planes for a in range(atoms)]
    weights = spread_weights(w_ref, bands, atoms, same_cell(bands * HALF, npj * HALF))
    cz_hi, cz_lo = circulant(nz, 1)
    cz = (jnp.concatenate([cz_hi, cz_hi], axis=0), cz_lo)
    cy = circulant(ny, bands // 2)
    for x in range(planes):
        blocks = spread_plane(
            weights, proj_ref, [x - s for s in starts], [jnp.logical_and(x >= s, x - s < BOX) for s in starts]
        )
        here = plane_rows(x, ny)
        psi = psi_ref[:, here]
        total = yz_part(psi, cz, cy) + jnp.concatenate(blocks, axis=1)
        site = outer * pot_ref[here] + (kinetic_weights[0] - outer * center)
        total = total + site[None] * psi - prev_ref[:, here]
        for m in range(1, HALO + 1):
            for target in (x + m, x - m):
                if target >= planes:
                    value = upper_ref[:, plane_rows(target - planes, ny)].astype(F32)
                elif target >= 0:
                    value = psi_ref[:, plane_rows(target, ny)]
                else:
                    continue
                total = total + kinetic_weights[m] * value
        out_ref[:, here] = total


def finish_kernel(count, g_ref, arrived_ref, *rest):
    outs, total = rest[:-1], rest[-1]
    total[...] = g_ref[...] + arrived_ref[...].astype(F32)
    rows = g_ref.shape[1] // count
    pieces_of(total, lax.axis_index("band"), count, rows, outs)


def output_kernel(g_ref, arrived_ref, *rest):
    pieces, (out_ref, panel_ref) = rest[:-2], rest[-2:]
    out_ref[...] = (g_ref[...] + arrived_ref[...].astype(F32)).astype(BF16)
    bands = g_ref.shape[0]
    for p, piece in enumerate(pieces):
        panel_ref[p * bands : (p + 1) * bands] = piece[...]


def split_kernel(n_space, n_band, prod_ref, out_ref, held):
    bands = prod_ref.shape[0] // n_band
    me = lax.axis_index("band")
    for p, bits in enumerate(partners(n_band)):
        begin = pl.multiple_of(jnp.bitwise_xor(me, bits) * bands, 8)
        held[pl.ds(begin, bands), :] = prod_ref[p * bands : (p + 1) * bands]
    rows = held.shape[0] // n_space
    for p, bits in enumerate(partners(n_band)):
        cols = [slice((h * n_band + p) * bands, (h * n_band + p + 1) * bands) for h in (0, 1)]
        pair = jnp.concatenate([held[:, c] for c in cols], axis=1)
        owner = jnp.bitwise_xor(me, bits)
        for i in range(n_space):
            out_ref[i * n_band + owner] = pair[i * rows : (i + 1) * rows]


def last_kernel(got_ref, margin_ref, projection_ref):
    total = got_ref[...].sum(axis=0)
    bands = margin_ref.shape[1]
    margin_ref[...] = total[:, :bands]
    projection_ref[...] = total[:, bands:]


def cyclic(value, axis, steps):
    count = lax.axis_size(axis)
    return lax.ppermute(value, axis, [(i, (i + steps) % count) for i in range(count)])


def mirrored(value, axis, bits):
    count = lax.axis_size(axis)
    return lax.ppermute(value, axis, [(i, i ^ bits) for i in range(count)])


def exchanged(pieces):
    offsets = partners(len(pieces))
    return [mirrored(p, "band", bits) if bits else p for bits, p in zip(offsets, pieces)]


def struct(shape, kind=F32):
    return jax.ShapeDtypeStruct(shape, kind)


def call(kernel, name, out_shape, args, vmem=48, **extra):
    return pl.pallas_call(
        kernel, out_shape=out_shape, compiler_params=params(vmem * 2**20), name=name, **extra
    )(*args)


def shards(orbitals, previous, potential, projectors, strengths, atom_planes):
    bands, planes, ny, nz = orbitals.shape
    n_space = lax.axis_size("space")
    n_band = lax.axis_size("band")
    cells = planes * ny
    whole = (bands, cells, nz)
    quarter = (bands, cells // n_band, nz)
    psi = orbitals.reshape(whole)
    prev = previous.reshape(whole)
    pot = potential.reshape(cells, nz)

    vm = pl.BlockSpec(memory_space=pltpu.VMEM)
    sm = pl.BlockSpec(memory_space=pltpu.SMEM)
    anywhere = pl.BlockSpec(memory_space=pl.ANY)

    half, *panel = call(
        partial(cast_kernel, n_band),
        "cast",
        (struct(whole, BF16),) + (struct(quarter, BF16),) * n_band,
        (psi,),
    )
    upper = cyclic(half, "space", -1)
    panel = exchanged(panel)

    ahead = call(
        partial(ahead_kernel, planes),
        "ahead",
        struct(whole),
        (psi,),
        cost_estimate=pl.CostEstimate(flops=10**9, bytes_accessed=2**20, transcendentals=0),
    )
    w, beyond = call(
        partial(coefficient_kernel, planes),
        "coefficients",
        (
            struct((projectors.shape[0] * bands, projectors.shape[1] * HALF)),
            struct(whole, BF16),
        ),
        (atom_planes, strengths.T, half, upper, projectors, ahead),
        in_specs=[sm, sm, vm, vm, vm, vm],
        out_specs=(vm, vm),
        scratch_shapes=[pltpu.VMEM((planes + BOX - 1, bands, ny, nz), BF16)],
    )
    arrived = cyclic(beyond, "space", 1)
    g = call(
        partial(near_kernel, planes),
        "near_part",
        struct(whole),
        (atom_planes, psi, prev, pot, w, upper, projectors),
        in_specs=[sm] + [vm] * 6,
        out_specs=vm,
        cost_estimate=pl.CostEstimate(flops=2 * 10**10, bytes_accessed=4 * 2**20, transcendentals=0),
    )
    mine = call(
        partial(finish_kernel, n_band),
        "finish",
        (struct(quarter, BF16),) * n_band,
        (g, arrived),
        scratch_shapes=[pltpu.VMEM(whole, F32)],
    )
    mine = exchanged(mine)
    total_bands = n_band * bands
    filtered, panels = call(
        output_kernel,
        "output",
        (struct(whole, BF16), struct((total_bands, *quarter[1:]), BF16)),
        (g, arrived, *panel),
    )
    left = jnp.concatenate(mine, axis=0).reshape(total_bands, -1)
    right = jnp.concatenate([left, panels.reshape(total_bands, -1)], axis=0)
    products = dot(left, right, ((1,), (1,))) * (1.0 / (cells * n_space * nz))
    out_rows = total_bands // n_space
    pieces = call(
        partial(split_kernel, n_space, n_band),
        "split",
        struct((n_space * n_band, out_rows, 2 * bands)),
        (products,),
        scratch_shapes=[pltpu.VMEM(products.shape, F32)],
    )
    got = lax.all_to_all(pieces, ("space", "band"), 0, 0)
    margin, projection = call(
        last_kernel, "last_sum", (struct((out_rows, bands)), struct((out_rows, bands))), (got,)
    )
    return filtered.reshape(orbitals.shape), margin, projection


def solution(mesh):
    in_specs = (
        P("band", "space", None, None),
        P("band", "space", None, None),
        P("space", None, None),
        P("space", None, None, None, None),
        P(),
        P(),
    )
    out_specs = (P("band", "space", None, None), P("space", "band"), P("space", "band"))
    return jax.shard_map(shards, mesh=mesh, in_specs=in_specs, out_specs=out_specs, check_vma=False)
```

```python
from functools import partial

import jax
import jax.numpy as jnp
from jax import lax
from jax.experimental import pallas as pl
from jax.experimental.pallas import tpu as pltpu
from jax.sharding import PartitionSpec as P

HALO = 6
BOX = 6
NPJ = 9
HALF = 16

stencil_weights = (
    -5369.0 / 1800.0,
    12.0 / 7.0,
    -15.0 / 56.0,
    10.0 / 189.0,
    -1.0 / 112.0,
    2.0 / 1925.0,
    -1.0 / 16632.0,
)
center = 5.5
halfwidth = 5.5
outer = 2.0 / halfwidth
kinetic_weights = [-0.5 * outer * w for w in stencil_weights]

F32 = jnp.float32
BF16 = jnp.bfloat16


def params(vmem):
    return pltpu.CompilerParams(vmem_limit_bytes=vmem)


def circulant(n, blocks):
    size = n * blocks
    row = lax.broadcasted_iota(jnp.int32, (size, size), 0)
    col = lax.broadcasted_iota(jnp.int32, (size, size), 1)
    ahead = jnp.bitwise_and(col - row, n - 1)
    reach = jnp.minimum(ahead, n - ahead)
    value = jnp.zeros((size, size), F32)
    for m, weight in enumerate(kinetic_weights):
        value = jnp.where(reach == m, weight, value)
    value = jnp.where(jnp.bitwise_xor(row, col) < n, value, 0.0)
    hi = value.astype(BF16)
    return hi, (value - hi.astype(F32)).astype(BF16)


def dot(a, b, dims=((1,), (0,))):
    return lax.dot_general(a, b, (dims, ((), ())), preferred_element_type=F32)


def plane_rows(x, ny):
    return slice(x * ny, (x + 1) * ny)


def partners(count):
    return range(count)


def pieces_of(ref, index, count, rows, outs):
    for bits, out in zip(partners(count), outs):
        quarter = jnp.bitwise_xor(index, bits)
        begin = pl.multiple_of(quarter * rows, 8)
        out[...] = ref[:, pl.ds(begin, rows), :].astype(out.dtype)


def cast_kernel(count, psi_ref, up_ref, *outs):
    up_ref[...] = psi_ref[:, : up_ref.shape[1]].astype(BF16)
    rows = psi_ref.shape[1] // count
    pieces_of(psi_ref, lax.axis_index("band"), count, rows, outs)


def yz_part(psi, cz, cy):
    bands, ny, nz = psi.shape
    flat = psi.reshape(bands * ny, nz)
    hi = flat.astype(BF16)
    lo = (flat - hi.astype(F32)).astype(BF16)
    both = jnp.concatenate([hi, lo], axis=1)
    along_z = dot(both, cz[0]) + dot(hi, cz[1])
    size = cy[0].shape[0]
    along_y = []
    for begin in range(0, bands * ny, size):
        pair = dot(cy[0], both[begin : begin + size])
        along_y.append(pair[:, :nz] + pair[:, nz:] + dot(cy[1], hi[begin : begin + size]))
    return (along_z + jnp.concatenate(along_y, axis=0)).reshape(bands, ny, nz)


def same_cell(rows, cols):
    row = lax.broadcasted_iota(jnp.int32, (rows, cols), 0)
    col = lax.broadcasted_iota(jnp.int32, (rows, cols), 1)
    return jnp.where(jnp.bitwise_and(row - col, HALF - 1) == 0, 1.0, 0.0).astype(F32)


def table(proj_ref, a, p):
    npj, ny, nz = proj_ref.shape[1], proj_ref.shape[3], proj_ref.shape[4]
    halves = [
        proj_ref[a, :, p, h * HALF : (h + 1) * HALF, :].reshape(npj * HALF, nz)
        for h in range(ny // HALF)
    ]
    return jnp.concatenate(halves, axis=1)


def spread_plane(weights, proj_ref, plane_of, valid):
    total = None
    for a, w in enumerate(weights):
        p = jnp.clip(plane_of[a], 0, BOX - 1)
        term = dot(w, table(proj_ref, a, p)) * jnp.where(valid[a], 1.0, 0.0)
        total = term if total is None else total + term
    nz = proj_ref.shape[4]
    rows = total.shape[0]
    halves = [
        total[:, h * nz : (h + 1) * nz].reshape(rows // HALF, HALF, nz)
        for h in range(total.shape[1] // nz)
    ]
    return jnp.concatenate(halves, axis=1)


def turned(plane):
    bands, ny, nz = plane.shape
    plane = plane.astype(BF16)
    parts = [
        jnp.transpose(plane[:, h * HALF : (h + 1) * HALF].reshape(bands * HALF, nz))
        for h in range(ny // HALF)
    ]
    return jnp.concatenate(parts, axis=0)


def ahead_kernel(planes, psi_ref, ahead_ref, edge_ref, turned_ref):
    ny = psi_ref.shape[1] // planes
    for x in range(planes - 1):
        total = None
        for m in range(x + 1, HALO + 1):
            term = kinetic_weights[m] * psi_ref[:, plane_rows(planes + x - m, ny)]
            total = term if total is None else total + term
        ahead_ref[:, plane_rows(x, ny)] = total
    edge_ref[...] = psi_ref[:, plane_rows(planes - 1, ny)].astype(BF16)
    for x in range(planes):
        turned_ref[x] = turned(psi_ref[:, plane_rows(x, ny)])


def coefficient_kernel(
    planes,
    first_ref,
    strength_ref,
    turned_ref,
    upper_ref,
    proj_ref,
    ahead_ref,
    edge_ref,
    w_ref,
    next_ref,
    edge_again_ref,
    ext,
):
    bands, cells, nz = upper_ref.shape
    reach = BOX - 1
    ny = cells // reach
    atoms, npj = proj_ref.shape[:2]
    me = lax.axis_index("space")
    edge_again_ref[...] = edge_ref[...]
    ext[0:planes] = turned_ref[...]
    for x in range(reach):
        ext[planes + x] = turned(upper_ref[:, plane_rows(x, ny)])
    rows, cols = npj * HALF, bands * HALF
    mask = same_cell(rows, cols)
    gi = lax.broadcasted_iota(jnp.int32, (cols, cols), 0)
    gj = lax.broadcasted_iota(jnp.int32, (cols, cols), 1)
    group = jnp.where(jnp.bitwise_xor(gi, gj) < HALF, 1.0, 0.0).astype(BF16)
    starts = [first_ref[me * atoms + a] - me * planes for a in range(atoms)]

    parts = []
    for a in range(atoms):
        left = jnp.concatenate([table(proj_ref, a, p) for p in range(BOX)], axis=1)
        right = jnp.concatenate([ext[starts[a] + p] for p in range(BOX)], axis=0)
        d = dot(left, right) * mask
        parts.append(d.reshape(npj, HALF, cols).sum(axis=1))
    e = jnp.concatenate(parts, axis=0)
    e_hi = e.astype(BF16)
    e_lo = (e - e_hi.astype(F32)).astype(BF16)
    coef = dot(e_hi, group) + dot(e_lo, group)
    weights = []
    for a in range(atoms):
        scaled = [
            coef[a * npj + j : a * npj + j + 1] * (outer * strength_ref[j, me * atoms + a])
            for j in range(npj)
        ]
        full = jnp.concatenate([jnp.broadcast_to(s, (HALF, cols)) for s in scaled], axis=0)
        weights.append(jnp.transpose((full * mask)).astype(BF16))
        w_ref[a] = weights[a]
    for q in range(reach):
        block = spread_plane(
            weights, proj_ref, [planes + q - s for s in starts], [planes + q - s < BOX for s in starts]
        )
        here = plane_rows(q, ny)
        next_ref[:, here] = (block + ahead_ref[:, here]).astype(BF16)


def near_kernel(
    planes, first_ref, psi_ref, prev_ref, pot_ref, w_ref, upper_ref, proj_ref, out_ref
):
    bands, cells, nz = psi_ref.shape
    ny = cells // planes
    atoms, npj = proj_ref.shape[:2]
    me = lax.axis_index("space")
    starts = [first_ref[me * atoms + a] - me * planes for a in range(atoms)]
    weights = [w_ref[a] for a in range(atoms)]
    cz_hi, cz_lo = circulant(nz, 1)
    cz = (jnp.concatenate([cz_hi, cz_hi], axis=0), cz_lo)
    cy = circulant(ny, bands // 2)
    for x in range(planes):
        block = spread_plane(
            weights, proj_ref, [x - s for s in starts], [jnp.logical_and(x >= s, x - s < BOX) for s in starts]
        )
        here = plane_rows(x, ny)
        psi = psi_ref[:, here]
        total = yz_part(psi, cz, cy) + block
        site = outer * pot_ref[here] + (kinetic_weights[0] - outer * center)
        total = total + site[None] * psi - prev_ref[:, here]
        for m in range(1, HALO + 1):
            for target in (x + m, x - m):
                if 0 <= target < planes:
                    total = total + kinetic_weights[m] * psi_ref[:, plane_rows(target, ny)]
                elif planes <= target < planes + BOX - 1:
                    value = upper_ref[:, plane_rows(target - planes, ny)].astype(F32)
                    total = total + kinetic_weights[m] * value
        out_ref[:, here] = total


def complete(g_ref, arrived_ref, below_ref, above_ref, out_ref):
    cut = arrived_ref.shape[1]
    out_ref[:, :cut] = (g_ref[:, :cut] + arrived_ref[...].astype(F32)).astype(out_ref.dtype)
    edges = below_ref[...].astype(F32) + above_ref[...].astype(F32)
    out_ref[:, cut:] = (g_ref[:, cut:] + kinetic_weights[HALO] * edges).astype(out_ref.dtype)


def finish_kernel(count, g_ref, arrived_ref, below_ref, above_ref, *rest):
    outs, total = rest[:-1], rest[-1]
    complete(g_ref, arrived_ref, below_ref, above_ref, total)
    rows = g_ref.shape[1] // count
    pieces_of(total, lax.axis_index("band"), count, rows, outs)


def output_kernel(g_ref, arrived_ref, below_ref, above_ref, *rest):
    pieces, (out_ref, panel_ref) = rest[:-2], rest[-2:]
    complete(g_ref, arrived_ref, below_ref, above_ref, out_ref)
    bands = g_ref.shape[0]
    for p, piece in enumerate(reversed(pieces)):
        panel_ref[p * bands : (p + 1) * bands] = piece[...]


def split_kernel(n_space, n_band, prod_ref, out_ref, held):
    bands = prod_ref.shape[0] // n_band
    me = lax.axis_index("band")
    for p, bits in enumerate(partners(n_band)):
        begin = pl.multiple_of(jnp.bitwise_xor(me, bits) * bands, 8)
        held[pl.ds(begin, bands), :] = prod_ref[p * bands : (p + 1) * bands]
    rows = held.shape[0] // n_space
    for p, bits in enumerate(partners(n_band)):
        cols = [slice((h * n_band + p) * bands, (h * n_band + p + 1) * bands) for h in (0, 1)]
        pair = jnp.concatenate([held[:, c] for c in cols], axis=1)
        owner = jnp.bitwise_xor(me, bits)
        for i in range(n_space):
            out_ref[i * n_band + owner] = pair[i * rows : (i + 1) * rows]


def last_kernel(got_ref, margin_ref, projection_ref):
    total = got_ref[...].sum(axis=0)
    bands = margin_ref.shape[1]
    margin_ref[...] = total[:, :bands]
    projection_ref[...] = total[:, bands:]


def cyclic(value, axis, steps):
    count = lax.axis_size(axis)
    return lax.ppermute(value, axis, [(i, (i + steps) % count) for i in range(count)])


def mirrored(value, axis, bits):
    count = lax.axis_size(axis)
    return lax.ppermute(value, axis, [(i, i ^ bits) for i in range(count)])


def exchanged(pieces):
    offsets = partners(len(pieces))
    return [mirrored(p, "band", bits) if bits else p for bits, p in zip(offsets, pieces)]


def struct(shape, kind=F32):
    return jax.ShapeDtypeStruct(shape, kind)


def call(kernel, name, out_shape, args, vmem=48, **extra):
    return pl.pallas_call(
        kernel, out_shape=out_shape, compiler_params=params(vmem * 2**20), name=name, **extra
    )(*args)


def shards(orbitals, previous, potential, projectors, strengths, atom_planes):
    bands, planes, ny, nz = orbitals.shape
    n_space = lax.axis_size("space")
    n_band = lax.axis_size("band")
    cells = planes * ny
    whole = (bands, cells, nz)
    quarter = (bands, cells // n_band, nz)
    psi = orbitals.reshape(whole)
    prev = previous.reshape(whole)
    pot = potential.reshape(cells, nz)

    vm = pl.BlockSpec(memory_space=pltpu.VMEM)
    sm = pl.BlockSpec(memory_space=pltpu.SMEM)
    anywhere = pl.BlockSpec(memory_space=pl.ANY)

    most = (bands, (planes - 1) * ny, nz)
    plane = (bands, ny, nz)
    up, *panel = call(
        partial(cast_kernel, n_band),
        "cast",
        (struct(most, BF16),) + (struct(quarter, BF16),) * n_band,
        (psi,),
    )
    upper = cyclic(up, "space", -1)
    panel = exchanged(panel)
    ahead, edge, own = call(
        partial(ahead_kernel, planes),
        "ahead",
        (struct(most), struct(plane, BF16), struct((planes, ny // HALF * nz, bands * HALF), BF16)),
        (psi,),
        cost_estimate=pl.CostEstimate(flops=10**9, bytes_accessed=2**20, transcendentals=0),
    )
    below = cyclic(edge, "space", 1)
    atoms, npj = projectors.shape[:2]
    w, beyond, edge = call(
        partial(coefficient_kernel, planes),
        "coefficients",
        (struct((atoms, bands * HALF, npj * HALF), BF16), struct(most, BF16), struct(plane, BF16)),
        (atom_planes, strengths.T, own, upper, projectors, ahead, edge),
        in_specs=[sm, sm] + [vm] * 5,
        out_specs=(vm, vm, vm),
        scratch_shapes=[pltpu.VMEM((planes + BOX - 1, *own.shape[1:]), BF16)],
    )
    arrived = cyclic(beyond, "space", 1)
    above = cyclic(edge, "space", -1)
    g = call(
        partial(near_kernel, planes),
        "near_part",
        struct(whole),
        (atom_planes, psi, prev, pot, w, upper, projectors),
        in_specs=[sm] + [vm] * 6,
        out_specs=vm,
        cost_estimate=pl.CostEstimate(flops=2 * 10**10, bytes_accessed=4 * 2**20, transcendentals=0),
    )
    mine = call(
        partial(finish_kernel, n_band),
        "finish",
        (struct(quarter, BF16),) * n_band,
        (g, arrived, below, above),
        scratch_shapes=[pltpu.VMEM(whole, F32)],
    )
    mine = exchanged(mine)
    total_bands = n_band * bands
    filtered, panels = call(
        output_kernel,
        "output",
        (struct(whole, BF16), struct((total_bands, *quarter[1:]), BF16)),
        (g, arrived, below, above, *reversed(panel)),
    )
    left = jnp.concatenate(mine, axis=0).reshape(total_bands, -1)
    right = jnp.concatenate([left, panels.reshape(total_bands, -1)], axis=0)
    products = dot(left, right, ((1,), (1,))) * (1.0 / (cells * n_space * nz))
    out_rows = total_bands // n_space
    pieces = call(
        partial(split_kernel, n_space, n_band),
        "split",
        struct((n_space * n_band, out_rows, 2 * bands)),
        (products,),
        scratch_shapes=[pltpu.VMEM(products.shape, F32)],
    )
    got = lax.all_to_all(pieces, ("space", "band"), 0, 0)
    margin, projection = call(
        last_kernel, "last_sum", (struct((out_rows, bands)), struct((out_rows, bands))), (got,)
    )
    return filtered.reshape(orbitals.shape), margin, projection


def solution(mesh):
    in_specs = (
        P("band", "space", None, None),
        P("band", "space", None, None),
        P("space", None, None),
        P("space", None, None, None, None),
        P(),
        P(),
    )
    out_specs = (P("band", "space", None, None), P("space", "band"), P("space", "band"))
    return jax.shard_map(shards, mesh=mesh, in_specs=in_specs, out_specs=out_specs, check_vma=False)
```

```python
from functools import partial

import jax
import jax.numpy as jnp
from jax import lax
from jax.experimental import pallas as pl
from jax.experimental.pallas import tpu as pltpu
from jax.sharding import PartitionSpec as P

HALO = 6
BOX = 6
NPJ = 9
HALF = 16

stencil_weights = (
    -5369.0 / 1800.0,
    12.0 / 7.0,
    -15.0 / 56.0,
    10.0 / 189.0,
    -1.0 / 112.0,
    2.0 / 1925.0,
    -1.0 / 16632.0,
)
center = 5.5
halfwidth = 5.5
outer = 2.0 / halfwidth
kinetic_weights = [-0.5 * outer * w for w in stencil_weights]

F32 = jnp.float32
BF16 = jnp.bfloat16


def params(vmem):
    return pltpu.CompilerParams(vmem_limit_bytes=vmem)


def circulant(n, blocks):
    size = n * blocks
    row = lax.broadcasted_iota(jnp.int32, (size, size), 0)
    col = lax.broadcasted_iota(jnp.int32, (size, size), 1)
    ahead = jnp.bitwise_and(col - row, n - 1)
    reach = jnp.minimum(ahead, n - ahead)
    value = jnp.zeros((size, size), F32)
    for m, weight in enumerate(kinetic_weights):
        value = jnp.where(reach == m, weight, value)
    value = jnp.where(jnp.bitwise_xor(row, col) < n, value, 0.0)
    hi = value.astype(BF16)
    return hi, (value - hi.astype(F32)).astype(BF16)


def dot(a, b, dims=((1,), (0,))):
    return lax.dot_general(a, b, (dims, ((), ())), preferred_element_type=F32)


def plane_rows(x, ny):
    return slice(x * ny, (x + 1) * ny)


def partners(count):
    return [0, *reversed(range(1, count))]


def pieces_of(ref, index, count, rows, outs):
    for bits, out in zip(partners(count), outs):
        quarter = jnp.bitwise_xor(index, bits)
        begin = pl.multiple_of(quarter * rows, 8)
        out[...] = ref[:, pl.ds(begin, rows), :].astype(out.dtype)


def cast_kernel(count, psi_ref, half_ref, *outs):
    half_ref[...] = psi_ref[...].astype(BF16)
    rows = psi_ref.shape[1] // count
    pieces_of(psi_ref, lax.axis_index("band"), count, rows, outs)


def yz_part(psi, cz, cy):
    bands, ny, nz = psi.shape
    flat = psi.reshape(bands * ny, nz)
    hi = flat.astype(BF16)
    lo = (flat - hi.astype(F32)).astype(BF16)
    both = jnp.concatenate([hi, lo], axis=1)
    along_z = dot(both, cz[0]) + dot(hi, cz[1])
    size = cy[0].shape[0]
    along_y = []
    for begin in range(0, bands * ny, size):
        pair = dot(cy[0], both[begin : begin + size])
        along_y.append(pair[:, :nz] + pair[:, nz:] + dot(cy[1], hi[begin : begin + size]))
    return (along_z + jnp.concatenate(along_y, axis=0)).reshape(bands, ny, nz)


def same_cell(rows, cols):
    row = lax.broadcasted_iota(jnp.int32, (rows, cols), 0)
    col = lax.broadcasted_iota(jnp.int32, (rows, cols), 1)
    return jnp.where(jnp.bitwise_and(row - col, HALF - 1) == 0, 1.0, 0.0).astype(F32)


def table(proj_ref, a, p):
    npj, ny, nz = proj_ref.shape[1], proj_ref.shape[3], proj_ref.shape[4]
    halves = [
        proj_ref[a, :, p, h * HALF : (h + 1) * HALF, :].reshape(npj * HALF, nz)
        for h in range(ny // HALF)
    ]
    return jnp.concatenate(halves, axis=1)


def spread_plane(weights, proj_ref, plane_of, valid):
    total = None
    for a, w in enumerate(weights):
        p = jnp.clip(plane_of[a], 0, BOX - 1)
        term = dot(w, table(proj_ref, a, p)) * jnp.where(valid[a], 1.0, 0.0)
        total = term if total is None else total + term
    nz = proj_ref.shape[4]
    rows = total.shape[0]
    halves = [
        total[:, h * nz : (h + 1) * nz].reshape(rows // HALF, HALF, nz)
        for h in range(total.shape[1] // nz)
    ]
    return jnp.concatenate(halves, axis=1)


def local_kernel(planes, psi_ref, g_ref, ahead_ref, edge_ref):
    bands, cells, nz = psi_ref.shape
    ny = cells // planes
    edge_ref[...] = psi_ref[:, plane_rows(planes - 1, ny)].astype(BF16)
    for x in range(planes - 1):
        total = None
        for m in range(x + 1, HALO + 1):
            term = kinetic_weights[m] * psi_ref[:, plane_rows(planes + x - m, ny)]
            total = term if total is None else total + term
        ahead_ref[:, plane_rows(x, ny)] = total
    cz_hi, cz_lo = circulant(nz, 1)
    cz = (jnp.concatenate([cz_hi, cz_hi], axis=0), cz_lo)
    cy = circulant(ny, bands // 2)
    for x in range(planes):
        here = plane_rows(x, ny)
        psi = psi_ref[:, here]
        total = yz_part(psi, cz, cy) + (kinetic_weights[0] - outer * center) * psi
        for m in range(1, HALO + 1):
            for target in (x + m, x - m):
                if 0 <= target < planes:
                    total = total + kinetic_weights[m] * psi_ref[:, plane_rows(target, ny)]
        g_ref[:, here] = total


def coefficient_kernel(
    planes, first_ref, strength_ref, own_ref, upper_ref, proj_ref, ahead_ref, w_ref, next_ref, ext
):
    bands, cells, nz = own_ref.shape
    reach = BOX - 1
    ny = cells // planes
    atoms, npj = proj_ref.shape[:2]
    me = lax.axis_index("space")
    for x in range(planes):
        ext[x] = own_ref[:, plane_rows(x, ny)]
        if x < reach:
            ext[planes + x] = upper_ref[:, plane_rows(x, ny)]
    rows, cols = bands * HALF, npj * HALF
    mask = same_cell(rows, cols)
    gi = lax.broadcasted_iota(jnp.int32, (cols, cols), 0)
    gj = lax.broadcasted_iota(jnp.int32, (cols, cols), 1)
    group = jnp.where(jnp.bitwise_xor(gi, gj) < HALF, 1.0, 0.0).astype(BF16)
    owner = lax.broadcasted_iota(jnp.int32, (1, cols), 1)
    starts = [first_ref[me * atoms + a] - me * planes for a in range(atoms)]
    halves = range(ny // HALF)
    parts = []
    for a in range(atoms):
        left = [
            ext[starts[a] + p, :, h * HALF : (h + 1) * HALF, :].reshape(rows, nz)
            for p in range(BOX)
            for h in halves
        ]
        right = [table(proj_ref, a, p) for p in range(BOX)]
        d = dot(jnp.concatenate(left, axis=1), jnp.concatenate(right, axis=1), ((1,), (1,)))
        parts.append((d * mask).reshape(bands, HALF, cols).sum(axis=1))
    e = jnp.concatenate(parts, axis=0)
    e_hi = e.astype(BF16)
    e_lo = (e - e_hi.astype(F32)).astype(BF16)
    coef = dot(e_hi, group) + dot(e_lo, group)
    weights = []
    for a in range(atoms):
        scale = jnp.zeros((1, cols), F32)
        for j in range(npj):
            scale = jnp.where(owner >= j * HALF, outer * strength_ref[j, me * atoms + a], scale)
        w = coef[a * bands : (a + 1) * bands] * scale
        full = jnp.broadcast_to(w[:, None, :], (bands, HALF, cols)).reshape(rows, cols) * mask
        weights.append(full.astype(BF16))
        w_ref[a] = weights[a]
    for q in range(reach):
        block = spread_plane(
            weights, proj_ref, [planes + q - s for s in starts], [planes + q - s < BOX for s in starts]
        )
        here = plane_rows(q, ny)
        next_ref[:, here] = (block + ahead_ref[:, here]).astype(BF16)


def near_kernel(planes, unused, first_ref, *refs):
    g_ref, psi_ref, prev_ref, pot_ref, w_ref, upper_ref, proj_ref, out_ref = refs[unused:]
    bands, cells, nz = psi_ref.shape
    ny = cells // planes
    atoms = proj_ref.shape[0]
    me = lax.axis_index("space")
    starts = [first_ref[me * atoms + a] - me * planes for a in range(atoms)]
    weights = [w_ref[a] for a in range(atoms)]
    for x in range(planes):
        block = spread_plane(
            weights, proj_ref, [x - s for s in starts], [jnp.logical_and(x >= s, x - s < BOX) for s in starts]
        )
        here = plane_rows(x, ny)
        total = g_ref[:, here] + block
        total = total + (outer * pot_ref[here])[None] * psi_ref[:, here] - prev_ref[:, here]
        for m in range(planes - x, HALO + 1):
            value = upper_ref[:, plane_rows(x + m - planes, ny)].astype(F32)
            total = total + kinetic_weights[m] * value
        out_ref[:, here] = total


def complete(g_ref, arrived_ref, below_ref, out_ref):
    cut = arrived_ref.shape[1]
    out_ref[:, :cut] = (g_ref[:, :cut] + arrived_ref[...].astype(F32)).astype(out_ref.dtype)
    edge = kinetic_weights[HALO] * below_ref[...].astype(F32)
    out_ref[:, cut:] = (g_ref[:, cut:] + edge).astype(out_ref.dtype)


def finish_kernel(count, g_ref, arrived_ref, below_ref, *rest):
    outs, total = rest[:-1], rest[-1]
    complete(g_ref, arrived_ref, below_ref, total)
    rows = g_ref.shape[1] // count
    pieces_of(total, lax.axis_index("band"), count, rows, outs)


def output_kernel(g_ref, arrived_ref, below_ref, *rest):
    pieces, (out_ref, panel_ref) = rest[:-2], rest[-2:]
    complete(g_ref, arrived_ref, below_ref, out_ref)
    bands = g_ref.shape[0]
    for p, piece in enumerate(reversed(pieces)):
        panel_ref[p * bands : (p + 1) * bands] = piece[...]


def split_kernel(n_space, n_band, prod_ref, out_ref, held):
    bands = prod_ref.shape[0] // n_band
    me = lax.axis_index("band")
    for p, bits in enumerate(partners(n_band)):
        begin = pl.multiple_of(jnp.bitwise_xor(me, bits) * bands, 8)
        held[pl.ds(begin, bands), :] = prod_ref[p * bands : (p + 1) * bands]
    rows = held.shape[0] // n_space
    for p, bits in enumerate(partners(n_band)):
        cols = [slice((h * n_band + p) * bands, (h * n_band + p + 1) * bands) for h in (0, 1)]
        pair = jnp.concatenate([held[:, c] for c in cols], axis=1)
        owner = jnp.bitwise_xor(me, bits)
        for i in range(n_space):
            out_ref[i * n_band + owner] = pair[i * rows : (i + 1) * rows]


def last_kernel(got_ref, margin_ref, projection_ref):
    total = got_ref[...].sum(axis=0)
    bands = margin_ref.shape[1]
    margin_ref[...] = total[:, :bands]
    projection_ref[...] = total[:, bands:]


def cyclic(value, axis, steps):
    count = lax.axis_size(axis)
    return lax.ppermute(value, axis, [(i, (i + steps) % count) for i in range(count)])


def mirrored(value, axis, bits):
    count = lax.axis_size(axis)
    return lax.ppermute(value, axis, [(i, i ^ bits) for i in range(count)])


def exchanged(pieces):
    offsets = partners(len(pieces))
    return [mirrored(p, "band", bits) if bits else p for bits, p in zip(offsets, pieces)]


def struct(shape, kind=F32):
    return jax.ShapeDtypeStruct(shape, kind)


def call(kernel, name, out_shape, args, vmem=48, **extra):
    return pl.pallas_call(
        kernel, out_shape=out_shape, compiler_params=params(vmem * 2**20), name=name, **extra
    )(*args)


def shards(orbitals, previous, potential, projectors, strengths, atom_planes):
    bands, planes, ny, nz = orbitals.shape
    n_space = lax.axis_size("space")
    n_band = lax.axis_size("band")
    cells = planes * ny
    whole = (bands, cells, nz)
    quarter = (bands, cells // n_band, nz)
    psi = orbitals.reshape(whole)
    prev = previous.reshape(whole)
    pot = potential.reshape(cells, nz)

    vm = pl.BlockSpec(memory_space=pltpu.VMEM)
    sm = pl.BlockSpec(memory_space=pltpu.SMEM)
    anywhere = pl.BlockSpec(memory_space=pl.ANY)

    most = (bands, (planes - 1) * ny, nz)
    plane = (bands, ny, nz)
    half, *panel = call(
        partial(cast_kernel, n_band),
        "cast",
        (struct(whole, BF16),) + (struct(quarter, BF16),) * n_band,
        (psi,),
    )
    upper = cyclic(half, "space", -1)
    panel = exchanged(panel)
    g, ahead, edge = call(
        partial(local_kernel, planes),
        "local_part",
        (struct(whole), struct(most), struct(plane, BF16)),
        (psi,),
        cost_estimate=pl.CostEstimate(flops=10**9, bytes_accessed=2**20, transcendentals=0),
    )
    below = cyclic(edge, "space", 1)
    atoms, npj = projectors.shape[:2]
    w, beyond = call(
        partial(coefficient_kernel, planes),
        "coefficients",
        (struct((atoms, bands * HALF, npj * HALF), BF16), struct(most, BF16)),
        (atom_planes, strengths.T, half, upper, projectors, ahead),
        in_specs=[sm, sm] + [vm] * 4,
        out_specs=(vm, vm),
        scratch_shapes=[pltpu.VMEM((planes + BOX - 1, bands, ny, nz), BF16)],
    )
    arrived = cyclic(beyond, "space", 1)
    g = call(
        partial(near_kernel, planes, 1),
        "near_part",
        struct(whole),
        (atom_planes, panel[1], g, psi, prev, pot, w, upper, projectors),
        in_specs=[sm] + [anywhere] * 1 + [vm] * 7,
        out_specs=vm,
        cost_estimate=pl.CostEstimate(flops=2*10**10, bytes_accessed=4 * 2**20, transcendentals=0),
    )
    mine = call(
        partial(finish_kernel, n_band),
        "finish",
        (struct(quarter, BF16),) * n_band,
        (g, arrived, below),
        scratch_shapes=[pltpu.VMEM(whole, F32)],
    )
    mine = exchanged(mine)
    total_bands = n_band * bands
    filtered, panels = call(
        output_kernel,
        "output",
        (struct(whole, BF16), struct((total_bands, *quarter[1:]), BF16)),
        (g, arrived, below, *reversed(panel)),
    )
    left = jnp.concatenate(mine, axis=0).reshape(total_bands, -1)
    right = jnp.concatenate([left, panels.reshape(total_bands, -1)], axis=0)
    products = dot(left, right, ((1,), (1,))) * (1.0 / (cells * n_space * nz))
    out_rows = total_bands // n_space
    pieces = call(
        partial(split_kernel, n_space, n_band),
        "split",
        struct((n_space * n_band, out_rows, 2 * bands)),
        (products,),
        scratch_shapes=[pltpu.VMEM(products.shape, F32)],
    )
    got = lax.all_to_all(pieces, ("space", "band"), 0, 0)
    margin, projection = call(
        last_kernel, "last_sum", (struct((out_rows, bands)), struct((out_rows, bands))), (got,)
    )
    return filtered.reshape(orbitals.shape), margin, projection


def solution(mesh):
    in_specs = (
        P("band", "space", None, None),
        P("band", "space", None, None),
        P("space", None, None),
        P("space", None, None, None, None),
        P(),
        P(),
    )
    out_specs = (P("band", "space", None, None), P("space", "band"), P("space", "band"))
    return jax.shard_map(shards, mesh=mesh, in_specs=in_specs, out_specs=out_specs, check_vma=False)
```

```python
from functools import partial

import jax
import jax.numpy as jnp
from jax import lax
from jax.experimental import pallas as pl
from jax.experimental.pallas import tpu as pltpu
from jax.sharding import PartitionSpec as P

HALO = 6
BOX = 6
NPJ = 9
HALF = 16

stencil_weights = (
    -5369.0 / 1800.0,
    12.0 / 7.0,
    -15.0 / 56.0,
    10.0 / 189.0,
    -1.0 / 112.0,
    2.0 / 1925.0,
    -1.0 / 16632.0,
)
center = 5.5
halfwidth = 5.5
outer = 2.0 / halfwidth
kinetic_weights = [-0.5 * outer * w for w in stencil_weights]

F32 = jnp.float32
BF16 = jnp.bfloat16


def params(vmem):
    return pltpu.CompilerParams(vmem_limit_bytes=vmem)


def circulant(n, blocks):
    size = n * blocks
    row = lax.broadcasted_iota(jnp.int32, (size, size), 0)
    col = lax.broadcasted_iota(jnp.int32, (size, size), 1)
    ahead = jnp.bitwise_and(col - row, n - 1)
    reach = jnp.minimum(ahead, n - ahead)
    value = jnp.zeros((size, size), F32)
    for m, weight in enumerate(kinetic_weights):
        value = jnp.where(reach == m, weight, value)
    value = jnp.where(jnp.bitwise_xor(row, col) < n, value, 0.0)
    hi = value.astype(BF16)
    return hi, (value - hi.astype(F32)).astype(BF16)


def dot(a, b, dims=((1,), (0,))):
    return lax.dot_general(a, b, (dims, ((), ())), preferred_element_type=F32)


def plane_rows(x, ny):
    return slice(x * ny, (x + 1) * ny)


def partners(count):
    return [0, *reversed(range(1, count))]


def pieces_of(ref, index, count, rows, outs):
    for bits, out in zip(partners(count), outs):
        quarter = jnp.bitwise_xor(index, bits)
        begin = pl.multiple_of(quarter * rows, 8)
        out[...] = ref[:, pl.ds(begin, rows), :].astype(out.dtype)


def cast_kernel(count, psi_ref, half_ref, *outs):
    half_ref[...] = psi_ref[...].astype(BF16)
    rows = psi_ref.shape[1] // count
    pieces_of(psi_ref, lax.axis_index("band"), count, rows, outs)


def yz_part(psi, cz, cy):
    bands, ny, nz = psi.shape
    flat = psi.reshape(bands * ny, nz)
    hi = flat.astype(BF16)
    lo = (flat - hi.astype(F32)).astype(BF16)
    both = jnp.concatenate([hi, lo], axis=1)
    along_z = dot(both, cz[0]) + dot(hi, cz[1])
    size = cy[0].shape[0]
    along_y = []
    for begin in range(0, bands * ny, size):
        pair = dot(cy[0], both[begin : begin + size])
        along_y.append(pair[:, :nz] + pair[:, nz:] + dot(cy[1], hi[begin : begin + size]))
    return (along_z + jnp.concatenate(along_y, axis=0)).reshape(bands, ny, nz)


def same_cell(rows, cols):
    row = lax.broadcasted_iota(jnp.int32, (rows, cols), 0)
    col = lax.broadcasted_iota(jnp.int32, (rows, cols), 1)
    return jnp.where(jnp.bitwise_and(row - col, HALF - 1) == 0, 1.0, 0.0).astype(F32)


def table(proj_ref, a, p):
    npj, ny, nz = proj_ref.shape[1], proj_ref.shape[3], proj_ref.shape[4]
    halves = [
        proj_ref[a, :, p, h * HALF : (h + 1) * HALF, :].reshape(npj * HALF, nz)
        for h in range(ny // HALF)
    ]
    return jnp.concatenate(halves, axis=1)


def spread_plane(weights, proj_ref, plane_of, valid):
    tables = []
    for a in range(proj_ref.shape[0]):
        part = table(proj_ref, a, jnp.clip(plane_of[a], 0, BOX - 1))
        tables.append(part * jnp.where(valid[a], 1.0, 0.0).astype(BF16))
    total = dot(weights, jnp.concatenate(tables, axis=0))
    nz = proj_ref.shape[4]
    rows = total.shape[0]
    halves = [
        total[:, h * nz : (h + 1) * nz].reshape(rows // HALF, HALF, nz)
        for h in range(total.shape[1] // nz)
    ]
    return jnp.concatenate(halves, axis=1)


def local_kernel(planes, psi_ref, g_ref, ahead_ref, edge_ref):
    bands, cells, nz = psi_ref.shape
    ny = cells // planes
    edge_ref[...] = psi_ref[:, plane_rows(planes - 1, ny)].astype(BF16)
    for x in range(planes - 1):
        total = None
        for m in range(x + 1, HALO + 1):
            term = kinetic_weights[m] * psi_ref[:, plane_rows(planes + x - m, ny)]
            total = term if total is None else total + term
        ahead_ref[:, plane_rows(x, ny)] = total
    cz_hi, cz_lo = circulant(nz, 1)
    cz = (jnp.concatenate([cz_hi, cz_hi], axis=0), cz_lo)
    cy = circulant(ny, bands // 2)
    for x in range(planes):
        here = plane_rows(x, ny)
        psi = psi_ref[:, here]
        total = yz_part(psi, cz, cy) + (kinetic_weights[0] - outer * center) * psi
        for m in range(1, HALO + 1):
            for target in (x + m, x - m):
                if 0 <= target < planes:
                    total = total + kinetic_weights[m] * psi_ref[:, plane_rows(target, ny)]
        g_ref[:, here] = total


def coefficient_kernel(
    planes, first_ref, strength_ref, own_ref, upper_ref, proj_ref, ahead_ref, w_ref, next_ref, ext
):
    bands, cells, nz = own_ref.shape
    reach = BOX - 1
    ny = cells // planes
    atoms, npj = proj_ref.shape[:2]
    me = lax.axis_index("space")
    for x in range(planes):
        ext[x] = own_ref[:, plane_rows(x, ny)]
        if x < reach:
            ext[planes + x] = upper_ref[:, plane_rows(x, ny)]
    rows, cols = bands * HALF, npj * HALF
    mask = same_cell(rows, cols)
    gi = lax.broadcasted_iota(jnp.int32, (cols, cols), 0)
    gj = lax.broadcasted_iota(jnp.int32, (cols, cols), 1)
    group = jnp.where(jnp.bitwise_xor(gi, gj) < HALF, 1.0, 0.0).astype(BF16)
    owner = lax.broadcasted_iota(jnp.int32, (1, cols), 1)
    starts = [first_ref[me * atoms + a] - me * planes for a in range(atoms)]
    halves = range(ny // HALF)
    parts = []
    for a in range(atoms):
        left = [
            ext[starts[a] + p, :, h * HALF : (h + 1) * HALF, :].reshape(rows, nz)
            for p in range(BOX)
            for h in halves
        ]
        right = [table(proj_ref, a, p) for p in range(BOX)]
        d = dot(jnp.concatenate(left, axis=1), jnp.concatenate(right, axis=1), ((1,), (1,)))
        parts.append((d * mask).reshape(bands, HALF, cols).sum(axis=1))
    e = jnp.concatenate(parts, axis=0)
    e_hi = e.astype(BF16)
    e_lo = (e - e_hi.astype(F32)).astype(BF16)
    coef = dot(e_hi, group) + dot(e_lo, group)
    scaled = []
    for a in range(atoms):
        scale = jnp.zeros((1, cols), F32)
        for j in range(npj):
            scale = jnp.where(owner >= j * HALF, outer * strength_ref[j, me * atoms + a], scale)
        scaled.append(coef[a * bands : (a + 1) * bands] * scale)
    w = jnp.concatenate(scaled, axis=1)
    full = jnp.broadcast_to(w[:, None, :], (bands, HALF, atoms * cols)).reshape(rows, atoms * cols)
    weights = (full * same_cell(rows, atoms * cols)).astype(BF16)
    w_ref[...] = weights
    for q in range(reach):
        block = spread_plane(
            weights, proj_ref, [planes + q - s for s in starts], [planes + q - s < BOX for s in starts]
        )
        here = plane_rows(q, ny)
        next_ref[:, here] = (block + ahead_ref[:, here]).astype(BF16)


def near_kernel(planes, unused, first_ref, *refs):
    g_ref, psi_ref, prev_ref, pot_ref, w_ref, upper_ref, proj_ref, out_ref = refs[unused:]
    bands, cells, nz = psi_ref.shape
    ny = cells // planes
    atoms = proj_ref.shape[0]
    me = lax.axis_index("space")
    starts = [first_ref[me * atoms + a] - me * planes for a in range(atoms)]
    weights = w_ref[...]
    for x in range(planes):
        block = spread_plane(
            weights, proj_ref, [x - s for s in starts], [jnp.logical_and(x >= s, x - s < BOX) for s in starts]
        )
        here = plane_rows(x, ny)
        total = g_ref[:, here] + block
        total = total + (outer * pot_ref[here])[None] * psi_ref[:, here] - prev_ref[:, here]
        for m in range(planes - x, HALO + 1):
            value = upper_ref[:, plane_rows(x + m - planes, ny)].astype(F32)
            total = total + kinetic_weights[m] * value
        out_ref[:, here] = total


def complete(g_ref, arrived_ref, below_ref, out_ref):
    cut = arrived_ref.shape[1]
    out_ref[:, :cut] = (g_ref[:, :cut] + arrived_ref[...].astype(F32)).astype(out_ref.dtype)
    edge = kinetic_weights[HALO] * below_ref[...].astype(F32)
    out_ref[:, cut:] = (g_ref[:, cut:] + edge).astype(out_ref.dtype)


def finish_kernel(count, g_ref, arrived_ref, below_ref, *rest):
    outs, total = rest[:-1], rest[-1]
    complete(g_ref, arrived_ref, below_ref, total)
    rows = g_ref.shape[1] // count
    pieces_of(total, lax.axis_index("band"), count, rows, outs)


def output_kernel(g_ref, arrived_ref, below_ref, *rest):
    pieces, (out_ref, panel_ref) = rest[:-2], rest[-2:]
    complete(g_ref, arrived_ref, below_ref, out_ref)
    bands = g_ref.shape[0]
    for p, piece in enumerate(reversed(pieces)):
        panel_ref[p * bands : (p + 1) * bands] = piece[...]


def split_kernel(n_space, n_band, prod_ref, out_ref, held, pair):
    bands = prod_ref.shape[0] // n_band
    me = lax.axis_index("band")
    for p, bits in enumerate(partners(n_band)):
        begin = pl.multiple_of(jnp.bitwise_xor(me, bits) * bands, 8)
        held[pl.ds(begin, bands), :] = prod_ref[p * bands : (p + 1) * bands]
    rows = held.shape[0] // n_space
    for p, bits in enumerate(partners(n_band)):
        cols = [slice((h * n_band + p) * bands, (h * n_band + p + 1) * bands) for h in (0, 1)]
        pair[p] = jnp.concatenate([held[:, c] for c in cols], axis=1)
        owner = jnp.bitwise_xor(me, bits)
        lines = [pair[p, pl.ds(r, n_space, stride=rows), :] for r in range(rows)]
        packed = jnp.concatenate(lines, axis=1)
        for i in range(n_space):
            out_ref[i * n_band + owner] = packed[i : i + 1]


def last_kernel(got_ref, margin_ref, projection_ref):
    total = got_ref[...].sum(axis=0)
    rows, bands = margin_ref.shape
    for r in range(rows):
        begin = 2 * r * bands
        margin_ref[r : r + 1] = total[:, begin : begin + bands]
        projection_ref[r : r + 1] = total[:, begin + bands : begin + 2 * bands]


def cyclic(value, axis, steps):
    count = lax.axis_size(axis)
    return lax.ppermute(value, axis, [(i, (i + steps) % count) for i in range(count)])


def mirrored(value, axis, bits):
    count = lax.axis_size(axis)
    return lax.ppermute(value, axis, [(i, i ^ bits) for i in range(count)])


def exchanged(pieces):
    offsets = partners(len(pieces))
    return [mirrored(p, "band", bits) if bits else p for bits, p in zip(offsets, pieces)]


def struct(shape, kind=F32):
    return jax.ShapeDtypeStruct(shape, kind)


def call(kernel, name, out_shape, args, vmem=48, **extra):
    return pl.pallas_call(
        kernel, out_shape=out_shape, compiler_params=params(vmem * 2**20), name=name, **extra
    )(*args)


def shards(orbitals, previous, potential, projectors, strengths, atom_planes):
    bands, planes, ny, nz = orbitals.shape
    n_space = lax.axis_size("space")
    n_band = lax.axis_size("band")
    cells = planes * ny
    whole = (bands, cells, nz)
    quarter = (bands, cells // n_band, nz)
    psi = orbitals.reshape(whole)
    prev = previous.reshape(whole)
    pot = potential.reshape(cells, nz)

    vm = pl.BlockSpec(memory_space=pltpu.VMEM)
    sm = pl.BlockSpec(memory_space=pltpu.SMEM)
    anywhere = pl.BlockSpec(memory_space=pl.ANY)

    most = (bands, (planes - 1) * ny, nz)
    plane = (bands, ny, nz)
    half, *panel = call(
        partial(cast_kernel, n_band),
        "cast",
        (struct(whole, BF16),) + (struct(quarter, BF16),) * n_band,
        (psi,),
    )
    upper = cyclic(half, "space", -1)
    panel = exchanged(panel)
    g, ahead, edge = call(
        partial(local_kernel, planes),
        "local_part",
        (struct(whole), struct(most), struct(plane, BF16)),
        (psi,),
        cost_estimate=pl.CostEstimate(flops=10**9, bytes_accessed=2**20, transcendentals=0),
    )
    below = cyclic(edge, "space", 1)
    atoms, npj = projectors.shape[:2]
    w, beyond = call(
        partial(coefficient_kernel, planes),
        "coefficients",
        (struct((bands * HALF, atoms * npj * HALF), BF16), struct(most, BF16)),
        (atom_planes, strengths.T, half, upper, projectors, ahead),
        in_specs=[sm, sm] + [vm] * 4,
        out_specs=(vm, vm),
        scratch_shapes=[pltpu.VMEM((planes + BOX - 1, bands, ny, nz), BF16)],
    )
    arrived = cyclic(beyond, "space", 1)
    g = call(
        partial(near_kernel, planes, 1),
        "near_part",
        struct(whole),
        (atom_planes, panel[1], g, psi, prev, pot, w, upper, projectors),
        in_specs=[sm] + [anywhere] * 1 + [vm] * 7,
        out_specs=vm,
        cost_estimate=pl.CostEstimate(flops=2*10**10, bytes_accessed=4 * 2**20, transcendentals=0),
    )
    mine = call(
        partial(finish_kernel, n_band),
        "finish",
        (struct(quarter, BF16),) * n_band,
        (g, arrived, below),
        scratch_shapes=[pltpu.VMEM(whole, F32)],
    )
    mine = exchanged(mine)
    total_bands = n_band * bands
    filtered, panels = call(
        output_kernel,
        "output",
        (struct(whole, BF16), struct((total_bands, *quarter[1:]), BF16)),
        (g, arrived, below, *reversed(panel)),
    )
    left = jnp.concatenate(mine, axis=0).reshape(total_bands, -1)
    right = jnp.concatenate([left, panels.reshape(total_bands, -1)], axis=0)
    products = dot(left, right, ((1,), (1,))) * (1.0 / (cells * n_space * nz))
    out_rows = total_bands // n_space
    pieces = call(
        partial(split_kernel, n_space, n_band),
        "split",
        struct((n_space * n_band, 1, out_rows * 2 * bands)),
        (products,),
        scratch_shapes=[
            pltpu.VMEM(products.shape, F32),
            pltpu.VMEM((n_band, total_bands, 2 * bands), F32),
        ],
    )
    got = lax.all_to_all(pieces, ("space", "band"), 0, 0)
    margin, projection = call(
        last_kernel, "last_sum", (struct((out_rows, bands)), struct((out_rows, bands))), (got,)
    )
    return filtered.reshape(orbitals.shape), margin, projection


def solution(mesh):
    in_specs = (
        P("band", "space", None, None),
        P("band", "space", None, None),
        P("space", None, None),
        P("space", None, None, None, None),
        P(),
        P(),
    )
    out_specs = (P("band", "space", None, None), P("space", "band"), P("space", "band"))
    return jax.shard_map(shards, mesh=mesh, in_specs=in_specs, out_specs=out_specs, check_vma=False)
```

```python
from functools import partial

import jax
import jax.numpy as jnp
from jax import lax
from jax.experimental import pallas as pl
from jax.experimental.pallas import tpu as pltpu
from jax.sharding import PartitionSpec as P

HALO = 6
BOX = 6
NPJ = 9
HALF = 16

stencil_weights = (
    -5369.0 / 1800.0,
    12.0 / 7.0,
    -15.0 / 56.0,
    10.0 / 189.0,
    -1.0 / 112.0,
    2.0 / 1925.0,
    -1.0 / 16632.0,
)
center = 5.5
halfwidth = 5.5
outer = 2.0 / halfwidth
kinetic_weights = [-0.5 * outer * w for w in stencil_weights]

F32 = jnp.float32
BF16 = jnp.bfloat16


def params(vmem):
    return pltpu.CompilerParams(vmem_limit_bytes=vmem)


def circulant(n, blocks):
    size = n * blocks
    row = lax.broadcasted_iota(jnp.int32, (size, size), 0)
    col = lax.broadcasted_iota(jnp.int32, (size, size), 1)
    ahead = jnp.bitwise_and(col - row, n - 1)
    reach = jnp.minimum(ahead, n - ahead)
    value = jnp.zeros((size, size), F32)
    for m, weight in enumerate(kinetic_weights):
        value = jnp.where(reach == m, weight, value)
    value = jnp.where(jnp.bitwise_xor(row, col) < n, value, 0.0)
    hi = value.astype(BF16)
    return hi, (value - hi.astype(F32)).astype(BF16)


def dot(a, b, dims=((1,), (0,))):
    return lax.dot_general(a, b, (dims, ((), ())), preferred_element_type=F32)


def plane_rows(x, ny):
    return slice(x * ny, (x + 1) * ny)


def partners(count):
    return [0, *reversed(range(1, count))]


def pieces_of(ref, index, count, rows, outs):
    for bits, out in zip(partners(count), outs):
        quarter = jnp.bitwise_xor(index, bits)
        begin = pl.multiple_of(quarter * rows, 8)
        out[...] = ref[:, pl.ds(begin, rows), :].astype(out.dtype)


def cast_kernel(count, psi_ref, half_ref, *outs):
    half_ref[...] = psi_ref[...].astype(BF16)
    rows = psi_ref.shape[1] // count
    pieces_of(psi_ref, lax.axis_index("band"), count, rows, outs)


def yz_part(psi, cz, cy):
    bands, ny, nz = psi.shape
    flat = psi.reshape(bands * ny, nz)
    hi = flat.astype(BF16)
    lo = (flat - hi.astype(F32)).astype(BF16)
    both = jnp.concatenate([hi, lo], axis=1)
    along_z = dot(both, cz[0]) + dot(hi, cz[1])
    size = cy[0].shape[0]
    along_y = []
    for begin in range(0, bands * ny, size):
        pair = dot(cy[0], both[begin : begin + size])
        along_y.append(pair[:, :nz] + pair[:, nz:] + dot(cy[1], hi[begin : begin + size]))
    return (along_z + jnp.concatenate(along_y, axis=0)).reshape(bands, ny, nz)


def same_cell(rows, cols):
    row = lax.broadcasted_iota(jnp.int32, (rows, cols), 0)
    col = lax.broadcasted_iota(jnp.int32, (rows, cols), 1)
    return jnp.where(jnp.bitwise_and(row - col, HALF - 1) == 0, 1.0, 0.0).astype(F32)


def table(proj_ref, a, p):
    npj, ny, nz = proj_ref.shape[1], proj_ref.shape[3], proj_ref.shape[4]
    halves = [
        proj_ref[a, :, p, h * HALF : (h + 1) * HALF, :].reshape(npj * HALF, nz)
        for h in range(ny // HALF)
    ]
    return jnp.concatenate(halves, axis=1)


def halves_along(value, axis):
    bands, ny, nz = value.shape
    parts = [value[:, h * HALF : (h + 1) * HALF].reshape(bands * HALF, nz) for h in range(ny // HALF)]
    return jnp.concatenate(parts, axis=axis)


def spread(weights, tables, nz):
    total = dot(weights, tables)
    rows = total.shape[0]
    halves = [
        total[:, h * nz : (h + 1) * nz].reshape(rows // HALF, HALF, nz)
        for h in range(total.shape[1] // nz)
    ]
    return jnp.concatenate(halves, axis=1)


def overlap(field_ref, planes, ny, table_ref):
    bands = field_ref.shape[0]
    left = [halves_along(field_ref[:, plane_rows(x, ny)], 1) for x in range(planes)]
    right = [table_ref[x] for x in range(planes)]
    d = dot(jnp.concatenate(left, axis=1), jnp.concatenate(right, axis=1), ((1,), (1,)))
    rows, cols = d.shape
    return (d * same_cell(rows, cols)).reshape(bands, HALF, cols).sum(axis=1)


def prepare_kernel(
    planes, first_ref, strength_ref, own_ref, proj_ref, near_ref, far_ref, e_ref, s_ref
):
    ny = own_ref.shape[1] // planes
    atoms, npj = proj_ref.shape[:2]
    me = lax.axis_index("space")
    for q in range(planes + BOX - 1):
        parts = []
        for a in range(atoms):
            p = q - (first_ref[me * atoms + a] - me * planes)
            inside = jnp.logical_and(p >= 0, p < BOX)
            part = table(proj_ref, a, jnp.clip(p, 0, BOX - 1))
            parts.append(part * jnp.where(inside, 1.0, 0.0).astype(BF16))
        whole = jnp.concatenate(parts, axis=0)
        if q < planes:
            near_ref[q] = whole
        else:
            far_ref[q - planes] = whole
    owner = lax.broadcasted_iota(jnp.int32, s_ref.shape, 1)
    scale = jnp.zeros(s_ref.shape, F32)
    for a in range(atoms):
        for j in range(npj):
            value = outer * strength_ref[j, me * atoms + a]
            scale = jnp.where(owner >= (a * npj + j) * HALF, value, scale)
    s_ref[...] = scale
    e_ref[...] = overlap(own_ref, planes, ny, near_ref)


def local_kernel(planes, psi_ref, g_ref, ahead_ref, edge_ref):
    bands, cells, nz = psi_ref.shape
    ny = cells // planes
    edge_ref[...] = psi_ref[:, plane_rows(planes - 1, ny)].astype(BF16)
    for x in range(planes - 1):
        total = None
        for m in range(x + 1, HALO + 1):
            term = kinetic_weights[m] * psi_ref[:, plane_rows(planes + x - m, ny)]
            total = term if total is None else total + term
        ahead_ref[:, plane_rows(x, ny)] = total
    cz_hi, cz_lo = circulant(nz, 1)
    cz = (jnp.concatenate([cz_hi, cz_hi], axis=0), cz_lo)
    cy = circulant(ny, bands // 2)
    for x in range(planes):
        here = plane_rows(x, ny)
        psi = psi_ref[:, here]
        total = yz_part(psi, cz, cy) + (kinetic_weights[0] - outer * center) * psi
        for m in range(1, HALO + 1):
            for target in (x + m, x - m):
                if 0 <= target < planes:
                    total = total + kinetic_weights[m] * psi_ref[:, plane_rows(target, ny)]
        g_ref[:, here] = total


def coefficient_kernel(planes, upper_ref, table_ref, e_ref, s_ref, ahead_ref, w_ref, next_ref):
    bands, cells, nz = upper_ref.shape
    ny = cells // planes
    reach = BOX - 1
    e = e_ref[...] + overlap(upper_ref, reach, ny, table_ref)
    cols = e.shape[1]
    tiles = -(-cols // nz)
    e = jnp.concatenate([e, jnp.zeros((bands, tiles * nz - cols), F32)], axis=1)
    e = jnp.concatenate([e[:, t * nz : (t + 1) * nz] for t in range(tiles)], axis=0)
    gi = lax.broadcasted_iota(jnp.int32, (nz, nz), 0)
    gj = lax.broadcasted_iota(jnp.int32, (nz, nz), 1)
    group = jnp.where(jnp.bitwise_xor(gi, gj) < HALF, 1.0, 0.0).astype(BF16)
    e_hi = e.astype(BF16)
    e_lo = (e - e_hi.astype(F32)).astype(BF16)
    coef = dot(e_hi, group) + dot(e_lo, group)
    coef = jnp.concatenate([coef[t * bands : (t + 1) * bands] for t in range(tiles)], axis=1)
    w = coef[:, :cols] * s_ref[...]
    rows = bands * HALF
    full = jnp.broadcast_to(w[:, None, :], (bands, HALF, cols)).reshape(rows, cols)
    weights = (full * same_cell(rows, cols)).astype(BF16)
    w_ref[...] = weights
    for q in range(reach):
        here = plane_rows(q, ny)
        block = spread(weights, table_ref[q], nz) + ahead_ref[:, here]
        next_ref[:, here] = block.astype(BF16)


def near_kernel(planes, unused, *refs):
    g_ref, psi_ref, prev_ref, pot_ref, w_ref, upper_ref, table_ref, out_ref = refs[unused:]
    bands, cells, nz = psi_ref.shape
    ny = cells // planes
    weights = w_ref[...]
    for x in range(planes):
        here = plane_rows(x, ny)
        total = g_ref[:, here] + spread(weights, table_ref[x], nz)
        total = total + (outer * pot_ref[here])[None] * psi_ref[:, here] - prev_ref[:, here]
        for m in range(planes - x, HALO + 1):
            value = upper_ref[:, plane_rows(x + m - planes, ny)].astype(F32)
            total = total + kinetic_weights[m] * value
        out_ref[:, here] = total


def complete(g_ref, arrived_ref, below_ref, out_ref):
    cut = arrived_ref.shape[1]
    out_ref[:, :cut] = (g_ref[:, :cut] + arrived_ref[...].astype(F32)).astype(out_ref.dtype)
    edge = kinetic_weights[HALO] * below_ref[...].astype(F32)
    out_ref[:, cut:] = (g_ref[:, cut:] + edge).astype(out_ref.dtype)


def finish_kernel(count, g_ref, arrived_ref, below_ref, *rest):
    outs, total = rest[:-1], rest[-1]
    complete(g_ref, arrived_ref, below_ref, total)
    rows = g_ref.shape[1] // count
    pieces_of(total, lax.axis_index("band"), count, rows, outs)


def output_kernel(g_ref, arrived_ref, below_ref, *rest):
    pieces, (out_ref, panel_ref) = rest[:-2], rest[-2:]
    complete(g_ref, arrived_ref, below_ref, out_ref)
    bands = g_ref.shape[0]
    for p, piece in enumerate(reversed(pieces)):
        panel_ref[p * bands : (p + 1) * bands] = piece[...]


def split_kernel(n_space, n_band, prod_ref, out_ref, held, pair):
    bands = prod_ref.shape[0] // n_band
    me = lax.axis_index("band")
    for p, bits in enumerate(partners(n_band)):
        begin = pl.multiple_of(jnp.bitwise_xor(me, bits) * bands, 8)
        held[pl.ds(begin, bands), :] = prod_ref[p * bands : (p + 1) * bands]
    rows = held.shape[0] // n_space
    for p, bits in enumerate(partners(n_band)):
        cols = [slice((h * n_band + p) * bands, (h * n_band + p + 1) * bands) for h in (0, 1)]
        pair[p] = jnp.concatenate([held[:, c] for c in cols], axis=1)
        owner = jnp.bitwise_xor(me, bits)
        lines = [pair[p, pl.ds(r, n_space, stride=rows), :] for r in range(rows)]
        packed = jnp.concatenate(lines, axis=1)
        for i in range(n_space):
            out_ref[i * n_band + owner] = packed[i : i + 1]


def last_kernel(got_ref, margin_ref, projection_ref):
    total = got_ref[...].sum(axis=0)
    rows, bands = margin_ref.shape
    for r in range(rows):
        begin = 2 * r * bands
        margin_ref[r : r + 1] = total[:, begin : begin + bands]
        projection_ref[r : r + 1] = total[:, begin + bands : begin + 2 * bands]


def cyclic(value, axis, steps):
    count = lax.axis_size(axis)
    return lax.ppermute(value, axis, [(i, (i + steps) % count) for i in range(count)])


def mirrored(value, axis, bits):
    count = lax.axis_size(axis)
    return lax.ppermute(value, axis, [(i, i ^ bits) for i in range(count)])


def exchanged(pieces):
    offsets = partners(len(pieces))
    return [mirrored(p, "band", bits) if bits else p for bits, p in zip(offsets, pieces)]


def struct(shape, kind=F32):
    return jax.ShapeDtypeStruct(shape, kind)


def call(kernel, name, out_shape, args, vmem=48, **extra):
    return pl.pallas_call(
        kernel, out_shape=out_shape, compiler_params=params(vmem * 2**20), name=name, **extra
    )(*args)


def shards(orbitals, previous, potential, projectors, strengths, atom_planes):
    bands, planes, ny, nz = orbitals.shape
    n_space = lax.axis_size("space")
    n_band = lax.axis_size("band")
    cells = planes * ny
    whole = (bands, cells, nz)
    quarter = (bands, cells // n_band, nz)
    psi = orbitals.reshape(whole)
    prev = previous.reshape(whole)
    pot = potential.reshape(cells, nz)

    vm = pl.BlockSpec(memory_space=pltpu.VMEM)
    sm = pl.BlockSpec(memory_space=pltpu.SMEM)
    anywhere = pl.BlockSpec(memory_space=pl.ANY)

    most = (bands, (planes - 1) * ny, nz)
    plane = (bands, ny, nz)
    half, *panel = call(
        partial(cast_kernel, n_band),
        "cast",
        (struct(whole, BF16),) + (struct(quarter, BF16),) * n_band,
        (psi,),
    )
    upper = cyclic(half, "space", -1)
    panel = exchanged(panel)
    g, ahead, edge = call(
        partial(local_kernel, planes),
        "local_part",
        (struct(whole), struct(most), struct(plane, BF16)),
        (psi,),
        cost_estimate=pl.CostEstimate(flops=10**9, bytes_accessed=2**20, transcendentals=0),
    )
    below = cyclic(edge, "space", 1)
    atoms, npj = projectors.shape[:2]
    cols = atoms * npj * HALF
    tables, far_tables, e, s = call(
        partial(prepare_kernel, planes),
        "prepare",
        (
            struct((planes, cols, ny // HALF * nz), BF16),
            struct((BOX - 1, cols, ny // HALF * nz), BF16),
            struct((bands, cols)),
            struct((1, cols)),
        ),
        (atom_planes, strengths.T, half, projectors),
        in_specs=[sm, sm, vm, vm],
        out_specs=(vm, vm, vm, vm),
        cost_estimate=pl.CostEstimate(flops=10**9, bytes_accessed=2**20, transcendentals=0),
    )
    w, beyond = call(
        partial(coefficient_kernel, planes),
        "coefficients",
        (struct((bands * HALF, cols), BF16), struct(most, BF16)),
        (upper, far_tables, e, s, ahead),
        cost_estimate=pl.CostEstimate(flops=10**9, bytes_accessed=2**20, transcendentals=0),
    )
    arrived = cyclic(beyond, "space", 1)
    g = call(
        partial(near_kernel, planes, 2),
        "near_part",
        struct(whole),
        (panel[2], panel[1], g, psi, prev, pot, w, upper, tables),
        in_specs=[anywhere] * 2 + [vm] * 7,
        out_specs=vm,
        cost_estimate=pl.CostEstimate(flops=2*10**10, bytes_accessed=4 * 2**20, transcendentals=0),
    )
    mine = call(
        partial(finish_kernel, n_band),
        "finish",
        (struct(quarter, BF16),) * n_band,
        (g, arrived, below),
        scratch_shapes=[pltpu.VMEM(whole, F32)],
    )
    mine = exchanged(mine)
    total_bands = n_band * bands
    filtered, panels = call(
        output_kernel,
        "output",
        (struct(whole, BF16), struct((total_bands, *quarter[1:]), BF16)),
        (g, arrived, below, *reversed(panel)),
    )
    left = jnp.concatenate(mine, axis=0).reshape(total_bands, -1)
    right = jnp.concatenate([left, panels.reshape(total_bands, -1)], axis=0)
    products = dot(left, right, ((1,), (1,))) * (1.0 / (cells * n_space * nz))
    out_rows = total_bands // n_space
    pieces = call(
        partial(split_kernel, n_space, n_band),
        "split",
        struct((n_space * n_band, 1, out_rows * 2 * bands)),
        (products,),
        scratch_shapes=[
            pltpu.VMEM(products.shape, F32),
            pltpu.VMEM((n_band, total_bands, 2 * bands), F32),
        ],
    )
    got = lax.all_to_all(pieces, ("space", "band"), 0, 0)
    margin, projection = call(
        last_kernel, "last_sum", (struct((out_rows, bands)), struct((out_rows, bands))), (got,)
    )
    return filtered.reshape(orbitals.shape), margin, projection


def solution(mesh):
    in_specs = (
        P("band", "space", None, None),
        P("band", "space", None, None),
        P("space", None, None),
        P("space", None, None, None, None),
        P(),
        P(),
    )
    out_specs = (P("band", "space", None, None), P("space", "band"), P("space", "band"))
    return jax.shard_map(shards, mesh=mesh, in_specs=in_specs, out_specs=out_specs, check_vma=False)
```

```python
from functools import partial

import jax
import jax.numpy as jnp
from jax import lax
from jax.experimental import pallas as pl
from jax.experimental.pallas import tpu as pltpu
from jax.sharding import PartitionSpec as P

HALO = 6
BOX = 6
NPJ = 9
HALF = 16

stencil_weights = (
    -5369.0 / 1800.0,
    12.0 / 7.0,
    -15.0 / 56.0,
    10.0 / 189.0,
    -1.0 / 112.0,
    2.0 / 1925.0,
    -1.0 / 16632.0,
)
center = 5.5
halfwidth = 5.5
outer = 2.0 / halfwidth
kinetic_weights = [-0.5 * outer * w for w in stencil_weights]

F32 = jnp.float32
BF16 = jnp.bfloat16


def params(vmem):
    return pltpu.CompilerParams(vmem_limit_bytes=vmem)


def circulant(n, blocks):
    size = n * blocks
    row = lax.broadcasted_iota(jnp.int32, (size, size), 0)
    col = lax.broadcasted_iota(jnp.int32, (size, size), 1)
    ahead = jnp.bitwise_and(col - row, n - 1)
    reach = jnp.minimum(ahead, n - ahead)
    value = jnp.zeros((size, size), F32)
    for m, weight in enumerate(kinetic_weights):
        value = jnp.where(reach == m, weight, value)
    value = jnp.where(jnp.bitwise_xor(row, col) < n, value, 0.0)
    hi = value.astype(BF16)
    return hi, (value - hi.astype(F32)).astype(BF16)


def dot(a, b, dims=((1,), (0,))):
    return lax.dot_general(a, b, (dims, ((), ())), preferred_element_type=F32)


def plane_rows(x, ny):
    return slice(x * ny, (x + 1) * ny)


def partners(count):
    return [0, *reversed(range(1, count))]


def pieces_of(ref, index, count, rows, outs):
    for bits, out in zip(partners(count), outs):
        quarter = jnp.bitwise_xor(index, bits)
        begin = pl.multiple_of(quarter * rows, 8)
        out[...] = ref[:, pl.ds(begin, rows), :].astype(out.dtype)


def cast_kernel(psi_ref, half_ref):
    half_ref[...] = psi_ref[...].astype(BF16)


def pieces_kernel(count, psi_ref, *outs):
    rows = psi_ref.shape[1] // count
    pieces_of(psi_ref, lax.axis_index("band"), count, rows, outs)


def yz_part(psi, cz, cy):
    bands, ny, nz = psi.shape
    flat = psi.reshape(bands * ny, nz)
    hi = flat.astype(BF16)
    lo = (flat - hi.astype(F32)).astype(BF16)
    both = jnp.concatenate([hi, lo], axis=1)
    along_z = dot(both, cz[0]) + dot(hi, cz[1])
    size = cy[0].shape[0]
    along_y = []
    for begin in range(0, bands * ny, size):
        pair = dot(cy[0], both[begin : begin + size])
        along_y.append(pair[:, :nz] + pair[:, nz:] + dot(cy[1], hi[begin : begin + size]))
    return (along_z + jnp.concatenate(along_y, axis=0)).reshape(bands, ny, nz)


def same_cell(rows, cols):
    row = lax.broadcasted_iota(jnp.int32, (rows, cols), 0)
    col = lax.broadcasted_iota(jnp.int32, (rows, cols), 1)
    return jnp.where(jnp.bitwise_and(row - col, HALF - 1) == 0, 1.0, 0.0).astype(F32)


def table(proj_ref, a, p):
    npj, ny, nz = proj_ref.shape[1], proj_ref.shape[3], proj_ref.shape[4]
    halves = [
        proj_ref[a, :, p, h * HALF : (h + 1) * HALF, :].reshape(npj * HALF, nz)
        for h in range(ny // HALF)
    ]
    return jnp.concatenate(halves, axis=1)


def halves_along(value, axis):
    bands, ny, nz = value.shape
    parts = [value[:, h * HALF : (h + 1) * HALF].reshape(bands * HALF, nz) for h in range(ny // HALF)]
    return jnp.concatenate(parts, axis=axis)


def spread(weights, tables, nz):
    total = dot(weights, tables)
    rows = total.shape[0]
    halves = [
        total[:, h * nz : (h + 1) * nz].reshape(rows // HALF, HALF, nz)
        for h in range(total.shape[1] // nz)
    ]
    return jnp.concatenate(halves, axis=1)


def overlap(field_ref, planes, ny, table_ref):
    bands = field_ref.shape[0]
    left = [halves_along(field_ref[:, plane_rows(x, ny)], 1) for x in range(planes)]
    right = [table_ref[x] for x in range(planes)]
    d = dot(jnp.concatenate(left, axis=1), jnp.concatenate(right, axis=1), ((1,), (1,)))
    rows, cols = d.shape
    return (d * same_cell(rows, cols)).reshape(bands, HALF, cols).sum(axis=1)


def prepare_kernel(
    planes, first_ref, strength_ref, own_ref, proj_ref, near_ref, far_ref, e_ref, s_ref
):
    ny = own_ref.shape[1] // planes
    atoms, npj = proj_ref.shape[:2]
    me = lax.axis_index("space")
    for q in range(planes + BOX - 1):
        parts = []
        for a in range(atoms):
            p = q - (first_ref[me * atoms + a] - me * planes)
            inside = jnp.logical_and(p >= 0, p < BOX)
            part = table(proj_ref, a, jnp.clip(p, 0, BOX - 1))
            parts.append(part * jnp.where(inside, 1.0, 0.0).astype(BF16))
        whole = jnp.concatenate(parts, axis=0)
        if q < planes:
            near_ref[q] = whole
        else:
            far_ref[q - planes] = whole
    owner = lax.broadcasted_iota(jnp.int32, s_ref.shape, 1)
    scale = jnp.zeros(s_ref.shape, F32)
    for a in range(atoms):
        for j in range(npj):
            value = outer * strength_ref[j, me * atoms + a]
            scale = jnp.where(owner >= (a * npj + j) * HALF, value, scale)
    s_ref[...] = scale
    e_ref[...] = overlap(own_ref, planes, ny, near_ref)


def ahead_kernel(planes, psi_ref, *refs):
    ahead_ref, edge_ref = refs[-2:]
    ny = psi_ref.shape[1] // planes
    edge_ref[...] = psi_ref[:, plane_rows(planes - 1, ny)].astype(BF16)
    for x in range(planes - 1):
        total = None
        for m in range(x + 1, HALO + 1):
            term = kinetic_weights[m] * psi_ref[:, plane_rows(planes + x - m, ny)]
            total = term if total is None else total + term
        ahead_ref[:, plane_rows(x, ny)] = total


def coefficient_kernel(planes, upper_ref, table_ref, e_ref, s_ref, ahead_ref, w_ref, next_ref):
    bands, cells, nz = upper_ref.shape
    ny = cells // planes
    reach = BOX - 1
    e = e_ref[...] + overlap(upper_ref, reach, ny, table_ref)
    cols = e.shape[1]
    tiles = -(-cols // nz)
    e = jnp.concatenate([e, jnp.zeros((bands, tiles * nz - cols), F32)], axis=1)
    e = jnp.concatenate([e[:, t * nz : (t + 1) * nz] for t in range(tiles)], axis=0)
    gi = lax.broadcasted_iota(jnp.int32, (nz, nz), 0)
    gj = lax.broadcasted_iota(jnp.int32, (nz, nz), 1)
    group = jnp.where(jnp.bitwise_xor(gi, gj) < HALF, 1.0, 0.0).astype(BF16)
    e_hi = e.astype(BF16)
    e_lo = (e - e_hi.astype(F32)).astype(BF16)
    coef = dot(e_hi, group) + dot(e_lo, group)
    coef = jnp.concatenate([coef[t * bands : (t + 1) * bands] for t in range(tiles)], axis=1)
    w = coef[:, :cols] * s_ref[...]
    rows = bands * HALF
    full = jnp.broadcast_to(w[:, None, :], (bands, HALF, cols)).reshape(rows, cols)
    weights = (full * same_cell(rows, cols)).astype(BF16)
    w_ref[...] = weights
    for q in range(reach):
        here = plane_rows(q, ny)
        block = spread(weights, table_ref[q], nz) + ahead_ref[:, here]
        next_ref[:, here] = block.astype(BF16)


def near_kernel(planes, psi_ref, prev_ref, pot_ref, w_ref, upper_ref, table_ref, out_ref):
    bands, cells, nz = psi_ref.shape
    ny = cells // planes
    weights = w_ref[...]
    cz_hi, cz_lo = circulant(nz, 1)
    cz = (jnp.concatenate([cz_hi, cz_hi], axis=0), cz_lo)
    cy = circulant(ny, bands // 2)
    for x in range(planes):
        here = plane_rows(x, ny)
        psi = psi_ref[:, here]
        total = yz_part(psi, cz, cy) + spread(weights, table_ref[x], nz)
        site = outer * pot_ref[here] + (kinetic_weights[0] - outer * center)
        total = total + site[None] * psi - prev_ref[:, here]
        for m in range(1, HALO + 1):
            for target in (x + m, x - m):
                if 0 <= target < planes:
                    total = total + kinetic_weights[m] * psi_ref[:, plane_rows(target, ny)]
                elif target >= planes:
                    value = upper_ref[:, plane_rows(target - planes, ny)].astype(F32)
                    total = total + kinetic_weights[m] * value
        out_ref[:, here] = total


def complete(g_ref, arrived_ref, below_ref, out_ref):
    cut = arrived_ref.shape[1]
    out_ref[:, :cut] = (g_ref[:, :cut] + arrived_ref[...].astype(F32)).astype(out_ref.dtype)
    edge = kinetic_weights[HALO] * below_ref[...].astype(F32)
    out_ref[:, cut:] = (g_ref[:, cut:] + edge).astype(out_ref.dtype)


def finish_kernel(count, g_ref, arrived_ref, below_ref, *rest):
    outs, total = rest[:-1], rest[-1]
    complete(g_ref, arrived_ref, below_ref, total)
    rows = g_ref.shape[1] // count
    pieces_of(total, lax.axis_index("band"), count, rows, outs)


def output_kernel(g_ref, arrived_ref, below_ref, *rest):
    pieces, (out_ref, panel_ref) = rest[:-2], rest[-2:]
    complete(g_ref, arrived_ref, below_ref, out_ref)
    bands = g_ref.shape[0]
    for p, piece in enumerate(reversed(pieces)):
        panel_ref[p * bands : (p + 1) * bands] = piece[...]


def split_kernel(n_space, n_band, prod_ref, out_ref, held, pair):
    bands = prod_ref.shape[0] // n_band
    me = lax.axis_index("band")
    for p, bits in enumerate(partners(n_band)):
        begin = pl.multiple_of(jnp.bitwise_xor(me, bits) * bands, 8)
        held[pl.ds(begin, bands), :] = prod_ref[p * bands : (p + 1) * bands]
    rows = held.shape[0] // n_space
    for p, bits in enumerate(partners(n_band)):
        cols = [slice((h * n_band + p) * bands, (h * n_band + p + 1) * bands) for h in (0, 1)]
        pair[p] = jnp.concatenate([held[:, c] for c in cols], axis=1)
        owner = jnp.bitwise_xor(me, bits)
        lines = [pair[p, pl.ds(r, n_space, stride=rows), :] for r in range(rows)]
        packed = jnp.concatenate(lines, axis=1)
        for i in range(n_space):
            out_ref[i * n_band + owner] = packed[i : i + 1]


def last_kernel(got_ref, margin_ref, projection_ref):
    total = got_ref[...].sum(axis=0)
    rows, bands = margin_ref.shape
    for r in range(rows):
        begin = 2 * r * bands
        margin_ref[r : r + 1] = total[:, begin : begin + bands]
        projection_ref[r : r + 1] = total[:, begin + bands : begin + 2 * bands]


def cyclic(value, axis, steps):
    count = lax.axis_size(axis)
    return lax.ppermute(value, axis, [(i, (i + steps) % count) for i in range(count)])


def mirrored(value, axis, bits):
    count = lax.axis_size(axis)
    return lax.ppermute(value, axis, [(i, i ^ bits) for i in range(count)])


def exchanged(pieces):
    offsets = partners(len(pieces))
    return [mirrored(p, "band", bits) if bits else p for bits, p in zip(offsets, pieces)]


def struct(shape, kind=F32):
    return jax.ShapeDtypeStruct(shape, kind)


def call(kernel, name, out_shape, args, vmem=48, **extra):
    return pl.pallas_call(
        kernel, out_shape=out_shape, compiler_params=params(vmem * 2**20), name=name, **extra
    )(*args)


def shards(orbitals, previous, potential, projectors, strengths, atom_planes):
    bands, planes, ny, nz = orbitals.shape
    n_space = lax.axis_size("space")
    n_band = lax.axis_size("band")
    cells = planes * ny
    whole = (bands, cells, nz)
    quarter = (bands, cells // n_band, nz)
    psi = orbitals.reshape(whole)
    prev = previous.reshape(whole)
    pot = potential.reshape(cells, nz)

    vm = pl.BlockSpec(memory_space=pltpu.VMEM)
    sm = pl.BlockSpec(memory_space=pltpu.SMEM)
    anywhere = pl.BlockSpec(memory_space=pl.ANY)

    most = (bands, (planes - 1) * ny, nz)
    plane = (bands, ny, nz)
    half = call(cast_kernel, "cast", struct(whole, BF16), (psi,))
    panel = call(
        partial(pieces_kernel, n_band),
        "pieces",
        (struct(quarter, BF16),) * n_band,
        (psi,),
        cost_estimate=pl.CostEstimate(flops=10**9, bytes_accessed=2**20, transcendentals=0),
    )
    upper = cyclic(half, "space", -1)
    panel = exchanged(panel)
    atoms, npj = projectors.shape[:2]
    cols = atoms * npj * HALF
    tables, far_tables, e, s = call(
        partial(prepare_kernel, planes),
        "prepare",
        (
            struct((planes, cols, ny // HALF * nz), BF16),
            struct((BOX - 1, cols, ny // HALF * nz), BF16),
            struct((bands, cols)),
            struct((1, cols)),
        ),
        (atom_planes, strengths.T, half, projectors),
        in_specs=[sm, sm, vm, vm],
        out_specs=(vm,) * 4,
        cost_estimate=pl.CostEstimate(flops=10**9, bytes_accessed=2**20, transcendentals=0),
    )
    ahead, edge = call(
        partial(ahead_kernel, planes),
        "ahead",
        (struct(most), struct(plane, BF16)),
        (psi, panel[3], s),
        in_specs=[vm, anywhere, anywhere],
        out_specs=(vm, vm),
        cost_estimate=pl.CostEstimate(flops=10**9, bytes_accessed=2**20, transcendentals=0),
    )
    below = cyclic(edge, "space", 1)
    w, beyond = call(
        partial(coefficient_kernel, planes),
        "coefficients",
        (struct((bands * HALF, cols), BF16), struct(most, BF16)),
        (upper, far_tables, e, s, ahead),
        cost_estimate=pl.CostEstimate(flops=10**9, bytes_accessed=2**20, transcendentals=0),
    )
    arrived = cyclic(beyond, "space", 1)
    g = call(
        partial(near_kernel, planes),
        "near_part",
        struct(whole),
        (psi, prev, pot, w, upper, tables),
        cost_estimate=pl.CostEstimate(flops=2*10**10, bytes_accessed=4 * 2**20, transcendentals=0),
    )
    mine = call(
        partial(finish_kernel, n_band),
        "finish",
        (struct(quarter, BF16),) * n_band,
        (g, arrived, below),
        scratch_shapes=[pltpu.VMEM(whole, F32)],
    )
    mine = exchanged(mine)
    total_bands = n_band * bands
    filtered, panels = call(
        output_kernel,
        "output",
        (struct(whole, BF16), struct((total_bands, *quarter[1:]), BF16)),
        (g, arrived, below, *reversed(panel)),
    )
    left = jnp.concatenate(mine, axis=0).reshape(total_bands, -1)
    right = jnp.concatenate([left, panels.reshape(total_bands, -1)], axis=0)
    products = dot(left, right, ((1,), (1,))) * (1.0 / (cells * n_space * nz))
    out_rows = total_bands // n_space
    pieces = call(
        partial(split_kernel, n_space, n_band),
        "split",
        struct((n_space * n_band, 1, out_rows * 2 * bands)),
        (products,),
        scratch_shapes=[
            pltpu.VMEM(products.shape, F32),
            pltpu.VMEM((n_band, total_bands, 2 * bands), F32),
        ],
    )
    got = lax.all_to_all(pieces, ("space", "band"), 0, 0)
    margin, projection = call(
        last_kernel, "last_sum", (struct((out_rows, bands)), struct((out_rows, bands))), (got,)
    )
    return filtered.reshape(orbitals.shape), margin, projection


def solution(mesh):
    in_specs = (
        P("band", "space", None, None),
        P("band", "space", None, None),
        P("space", None, None),
        P("space", None, None, None, None),
        P(),
        P(),
    )
    out_specs = (P("band", "space", None, None), P("space", "band"), P("space", "band"))
    return jax.shard_map(shards, mesh=mesh, in_specs=in_specs, out_specs=out_specs, check_vma=False)
```

```python
from functools import partial

import jax
import jax.numpy as jnp
from jax import lax
from jax.experimental import pallas as pl
from jax.experimental.pallas import tpu as pltpu
from jax.sharding import PartitionSpec as P

HALO = 6
BOX = 6
NPJ = 9
HALF = 16

stencil_weights = (
    -5369.0 / 1800.0,
    12.0 / 7.0,
    -15.0 / 56.0,
    10.0 / 189.0,
    -1.0 / 112.0,
    2.0 / 1925.0,
    -1.0 / 16632.0,
)
center = 5.5
halfwidth = 5.5
outer = 2.0 / halfwidth
kinetic_weights = [-0.5 * outer * w for w in stencil_weights]

F32 = jnp.float32
BF16 = jnp.bfloat16


def params(vmem):
    return pltpu.CompilerParams(vmem_limit_bytes=vmem)


def circulant(n, blocks):
    size = n * blocks
    row = lax.broadcasted_iota(jnp.int32, (size, size), 0)
    col = lax.broadcasted_iota(jnp.int32, (size, size), 1)
    ahead = jnp.bitwise_and(col - row, n - 1)
    reach = jnp.minimum(ahead, n - ahead)
    value = jnp.zeros((size, size), F32)
    for m, weight in enumerate(kinetic_weights):
        value = jnp.where(reach == m, weight, value)
    value = jnp.where(jnp.bitwise_xor(row, col) < n, value, 0.0)
    hi = value.astype(BF16)
    return hi, (value - hi.astype(F32)).astype(BF16)


def dot(a, b, dims=((1,), (0,))):
    return lax.dot_general(a, b, (dims, ((), ())), preferred_element_type=F32)


def plane_rows(x, ny):
    return slice(x * ny, (x + 1) * ny)


def partners(count):
    return [0, *reversed(range(1, count))]


def pieces_of(ref, index, count, rows, outs):
    for bits, out in zip(partners(count), outs):
        quarter = jnp.bitwise_xor(index, bits)
        begin = pl.multiple_of(quarter * rows, 8)
        out[...] = ref[:, pl.ds(begin, rows), :].astype(out.dtype)


def cast_kernel(psi_ref, half_ref):
    half_ref[...] = psi_ref[...].astype(BF16)


def pieces_kernel(count, psi_ref, *outs):
    rows = psi_ref.shape[1] // count
    pieces_of(psi_ref, lax.axis_index("band"), count, rows, outs)


def yz_part(psi, cz, cy):
    bands, ny, nz = psi.shape
    flat = psi.reshape(bands * ny, nz)
    hi = flat.astype(BF16)
    lo = (flat - hi.astype(F32)).astype(BF16)
    both = jnp.concatenate([hi, lo], axis=1)
    along_z = dot(both, cz[0]) + dot(hi, cz[1])
    size = cy[0].shape[0]
    along_y = []
    for begin in range(0, bands * ny, size):
        pair = dot(cy[0], both[begin : begin + size])
        along_y.append(pair[:, :nz] + pair[:, nz:] + dot(cy[1], hi[begin : begin + size]))
    return (along_z + jnp.concatenate(along_y, axis=0)).reshape(bands, ny, nz)


def same_cell(rows, cols):
    row = lax.broadcasted_iota(jnp.int32, (rows, cols), 0)
    col = lax.broadcasted_iota(jnp.int32, (rows, cols), 1)
    return jnp.where(jnp.bitwise_and(row - col, HALF - 1) == 0, 1.0, 0.0).astype(F32)


def table(proj_ref, a, p):
    npj, ny, nz = proj_ref.shape[1], proj_ref.shape[3], proj_ref.shape[4]
    halves = [
        proj_ref[a, :, p, h * HALF : (h + 1) * HALF, :].reshape(npj * HALF, nz)
        for h in range(ny // HALF)
    ]
    return jnp.concatenate(halves, axis=1)


def halves_along(value, axis):
    bands, ny, nz = value.shape
    parts = [value[:, h * HALF : (h + 1) * HALF].reshape(bands * HALF, nz) for h in range(ny // HALF)]
    return jnp.concatenate(parts, axis=axis)


def spread(weights, tables, nz):
    total = dot(weights, tables)
    rows = total.shape[0]
    halves = [
        total[:, h * nz : (h + 1) * nz].reshape(rows // HALF, HALF, nz)
        for h in range(total.shape[1] // nz)
    ]
    return jnp.concatenate(halves, axis=1)


def overlap(field_ref, planes, ny, table_ref):
    bands = field_ref.shape[0]
    left = [halves_along(field_ref[:, plane_rows(x, ny)], 1) for x in range(planes)]
    right = [table_ref[x] for x in range(planes)]
    d = dot(jnp.concatenate(left, axis=1), jnp.concatenate(right, axis=1), ((1,), (1,)))
    rows, cols = d.shape
    return (d * same_cell(rows, cols)).reshape(bands, HALF, cols).sum(axis=1)


def prepare_kernel(
    planes, first_ref, strength_ref, own_ref, proj_ref, near_ref, far_ref, e_ref, s_ref
):
    ny = own_ref.shape[1] // planes
    atoms, npj = proj_ref.shape[:2]
    me = lax.axis_index("space")
    for q in range(planes + BOX - 1):
        parts = []
        for a in range(atoms):
            p = q - (first_ref[me * atoms + a] - me * planes)
            inside = jnp.logical_and(p >= 0, p < BOX)
            part = table(proj_ref, a, jnp.clip(p, 0, BOX - 1))
            parts.append(part * jnp.where(inside, 1.0, 0.0).astype(BF16))
        whole = jnp.concatenate(parts, axis=0)
        if q < planes:
            near_ref[q] = whole
        else:
            far_ref[q - planes] = whole
    owner = lax.broadcasted_iota(jnp.int32, s_ref.shape, 1)
    scale = jnp.zeros(s_ref.shape, F32)
    for a in range(atoms):
        for j in range(npj):
            value = outer * strength_ref[j, me * atoms + a]
            scale = jnp.where(owner >= (a * npj + j) * HALF, value, scale)
    s_ref[...] = scale
    e_ref[...] = overlap(own_ref, planes, ny, near_ref)


def ahead_kernel(planes, psi_ref, *refs):
    ahead_ref, edge_ref = refs[-2:]
    ny = psi_ref.shape[1] // planes
    edge_ref[...] = psi_ref[:, plane_rows(planes - 1, ny)].astype(BF16)
    for x in range(planes - 1):
        total = None
        for m in range(x + 1, HALO + 1):
            term = kinetic_weights[m] * psi_ref[:, plane_rows(planes + x - m, ny)]
            total = term if total is None else total + term
        ahead_ref[:, plane_rows(x, ny)] = total


def coefficient_kernel(planes, upper_ref, table_ref, e_ref, s_ref, ahead_ref, w_ref, next_ref):
    bands, cells, nz = upper_ref.shape
    ny = cells // planes
    reach = BOX - 1
    e = e_ref[...] + overlap(upper_ref, reach, ny, table_ref)
    cols = e.shape[1]
    tiles = -(-cols // nz)
    e = jnp.concatenate([e, jnp.zeros((bands, tiles * nz - cols), F32)], axis=1)
    e = jnp.concatenate([e[:, t * nz : (t + 1) * nz] for t in range(tiles)], axis=0)
    gi = lax.broadcasted_iota(jnp.int32, (nz, nz), 0)
    gj = lax.broadcasted_iota(jnp.int32, (nz, nz), 1)
    group = jnp.where(jnp.bitwise_xor(gi, gj) < HALF, 1.0, 0.0).astype(BF16)
    e_hi = e.astype(BF16)
    e_lo = (e - e_hi.astype(F32)).astype(BF16)
    coef = dot(e_hi, group) + dot(e_lo, group)
    coef = jnp.concatenate([coef[t * bands : (t + 1) * bands] for t in range(tiles)], axis=1)
    w = coef[:, :cols] * s_ref[...]
    rows = bands * HALF
    full = jnp.broadcast_to(w[:, None, :], (bands, HALF, cols)).reshape(rows, cols)
    weights = (full * same_cell(rows, cols)).astype(BF16)
    w_ref[...] = weights
    for q in range(reach):
        here = plane_rows(q, ny)
        block = spread(weights, table_ref[q], nz) + ahead_ref[:, here]
        next_ref[:, here] = block.astype(BF16)


def near_kernel(planes, psi_ref, prev_ref, pot_ref, w_ref, upper_ref, table_ref, out_ref):
    bands, cells, nz = psi_ref.shape
    ny = cells // planes
    weights = w_ref[...]
    cz_hi, cz_lo = circulant(nz, 1)
    cz = (jnp.concatenate([cz_hi, cz_hi], axis=0), cz_lo)
    cy = circulant(ny, bands // 2)
    for x in range(planes):
        here = plane_rows(x, ny)
        psi = psi_ref[:, here]
        total = yz_part(psi, cz, cy) + spread(weights, table_ref[x], nz)
        site = outer * pot_ref[here] + (kinetic_weights[0] - outer * center)
        total = total + site[None] * psi - prev_ref[:, here]
        for m in range(1, HALO + 1):
            for target in (x + m, x - m):
                if 0 <= target < planes:
                    total = total + kinetic_weights[m] * psi_ref[:, plane_rows(target, ny)]
                elif target >= planes:
                    value = upper_ref[:, plane_rows(target - planes, ny)].astype(F32)
                    total = total + kinetic_weights[m] * value
        out_ref[:, here] = total


def complete(g_ref, arrived_ref, below_ref, out_ref):
    cut = arrived_ref.shape[1]
    out_ref[:, :cut] = (g_ref[:, :cut] + arrived_ref[...].astype(F32)).astype(out_ref.dtype)
    edge = kinetic_weights[HALO] * below_ref[...].astype(F32)
    out_ref[:, cut:] = (g_ref[:, cut:] + edge).astype(out_ref.dtype)


def finish_kernel(count, g_ref, arrived_ref, below_ref, *rest):
    outs, total = rest[:-1], rest[-1]
    complete(g_ref, arrived_ref, below_ref, total)
    rows = g_ref.shape[1] // count
    pieces_of(total, lax.axis_index("band"), count, rows, outs)


def output_kernel(g_ref, arrived_ref, below_ref, *rest):
    pieces, (out_ref, panel_ref) = rest[:-2], rest[-2:]
    complete(g_ref, arrived_ref, below_ref, out_ref)
    bands = g_ref.shape[0]
    for p, piece in enumerate(pieces):
        panel_ref[p * bands : (p + 1) * bands] = piece[...]


def split_kernel(n_space, n_band, prod_ref, out_ref, held, pair):
    bands = prod_ref.shape[0] // n_band
    me = lax.axis_index("band")
    for p, bits in enumerate(partners(n_band)):
        begin = pl.multiple_of(jnp.bitwise_xor(me, bits) * bands, 8)
        held[pl.ds(begin, bands), :] = prod_ref[p * bands : (p + 1) * bands]
    rows = held.shape[0] // n_space
    for p, bits in enumerate(partners(n_band)):
        cols = [slice((h * n_band + p) * bands, (h * n_band + p + 1) * bands) for h in (0, 1)]
        pair[p] = jnp.concatenate([held[:, c] for c in cols], axis=1)
        owner = jnp.bitwise_xor(me, bits)
        lines = [pair[p, pl.ds(r, n_space, stride=rows), :] for r in range(rows)]
        packed = jnp.concatenate(lines, axis=1)
        for i in range(n_space):
            out_ref[i * n_band + owner] = packed[i : i + 1]


def last_kernel(got_ref, margin_ref, projection_ref):
    total = got_ref[...].sum(axis=0)
    rows, bands = margin_ref.shape
    for r in range(rows):
        begin = 2 * r * bands
        margin_ref[r : r + 1] = total[:, begin : begin + bands]
        projection_ref[r : r + 1] = total[:, begin + bands : begin + 2 * bands]


def cyclic(value, axis, steps):
    count = lax.axis_size(axis)
    return lax.ppermute(value, axis, [(i, (i + steps) % count) for i in range(count)])


def mirrored(value, axis, bits):
    count = lax.axis_size(axis)
    return lax.ppermute(value, axis, [(i, i ^ bits) for i in range(count)])


def exchanged(pieces):
    offsets = partners(len(pieces))
    return [mirrored(p, "band", bits) if bits else p for bits, p in zip(offsets, pieces)]


def struct(shape, kind=F32):
    return jax.ShapeDtypeStruct(shape, kind)


def call(kernel, name, out_shape, args, vmem=48, **extra):
    return pl.pallas_call(
        kernel, out_shape=out_shape, compiler_params=params(vmem * 2**20), name=name, **extra
    )(*args)


def shards(orbitals, previous, potential, projectors, strengths, atom_planes):
    bands, planes, ny, nz = orbitals.shape
    n_space = lax.axis_size("space")
    n_band = lax.axis_size("band")
    cells = planes * ny
    whole = (bands, cells, nz)
    quarter = (bands, cells // n_band, nz)
    psi = orbitals.reshape(whole)
    prev = previous.reshape(whole)
    pot = potential.reshape(cells, nz)

    vm = pl.BlockSpec(memory_space=pltpu.VMEM)
    sm = pl.BlockSpec(memory_space=pltpu.SMEM)
    anywhere = pl.BlockSpec(memory_space=pl.ANY)

    most = (bands, (planes - 1) * ny, nz)
    plane = (bands, ny, nz)
    half = call(cast_kernel, "cast", struct(whole, BF16), (psi,))
    panel = call(
        partial(pieces_kernel, n_band),
        "pieces",
        (struct(quarter, BF16),) * n_band,
        (psi,),
        cost_estimate=pl.CostEstimate(flops=10**9, bytes_accessed=2**20, transcendentals=0),
    )
    upper = cyclic(half, "space", -1)
    panel = exchanged(panel)
    atoms, npj = projectors.shape[:2]
    cols = atoms * npj * HALF
    tables, far_tables, e, s = call(
        partial(prepare_kernel, planes),
        "prepare",
        (
            struct((planes, cols, ny // HALF * nz), BF16),
            struct((BOX - 1, cols, ny // HALF * nz), BF16),
            struct((bands, cols)),
            struct((1, cols)),
        ),
        (atom_planes, strengths.T, half, projectors),
        in_specs=[sm, sm, vm, vm],
        out_specs=(vm,) * 4,
        cost_estimate=pl.CostEstimate(flops=10**9, bytes_accessed=2**20, transcendentals=0),
    )
    ahead, edge = call(
        partial(ahead_kernel, planes),
        "ahead",
        (struct(most), struct(plane, BF16)),
        (psi, panel[3], s),
        in_specs=[vm, anywhere, anywhere],
        out_specs=(vm, vm),
        cost_estimate=pl.CostEstimate(flops=10**9, bytes_accessed=2**20, transcendentals=0),
    )
    below = cyclic(edge, "space", 1)
    w, beyond = call(
        partial(coefficient_kernel, planes),
        "coefficients",
        (struct((bands * HALF, cols), BF16), struct(most, BF16)),
        (upper, far_tables, e, s, ahead),
        cost_estimate=pl.CostEstimate(flops=10**9, bytes_accessed=2**20, transcendentals=0),
    )
    arrived = cyclic(beyond, "space", 1)
    g = call(
        partial(near_kernel, planes),
        "near_part",
        struct(whole),
        (psi, prev, pot, w, upper, tables),
        cost_estimate=pl.CostEstimate(flops=2*10**10, bytes_accessed=4 * 2**20, transcendentals=0),
    )
    mine = call(
        partial(finish_kernel, n_band),
        "finish",
        (struct(quarter, BF16),) * n_band,
        (g, arrived, below),
        scratch_shapes=[pltpu.VMEM(whole, F32)],
    )
    mine = exchanged(mine)
    total_bands = n_band * bands
    filtered, panels = call(
        output_kernel,
        "output",
        (struct(whole, BF16), struct((total_bands, *quarter[1:]), BF16)),
        (g, arrived, below, *panel),
    )
    left = jnp.concatenate(mine, axis=0).reshape(total_bands, -1)
    right = jnp.concatenate([left, panels.reshape(total_bands, -1)], axis=0)
    products = dot(left, right, ((1,), (1,))) * (1.0 / (cells * n_space * nz))
    out_rows = total_bands // n_space
    pieces = call(
        partial(split_kernel, n_space, n_band),
        "split",
        struct((n_space * n_band, 1, out_rows * 2 * bands)),
        (products,),
        scratch_shapes=[
            pltpu.VMEM(products.shape, F32),
            pltpu.VMEM((n_band, total_bands, 2 * bands), F32),
        ],
    )
    got = lax.all_to_all(pieces, ("space", "band"), 0, 0)
    margin, projection = call(
        last_kernel, "last_sum", (struct((out_rows, bands)), struct((out_rows, bands))), (got,)
    )
    return filtered.reshape(orbitals.shape), margin, projection


def solution(mesh):
    in_specs = (
        P("band", "space", None, None),
        P("band", "space", None, None),
        P("space", None, None),
        P("space", None, None, None, None),
        P(),
        P(),
    )
    out_specs = (P("band", "space", None, None), P("space", "band"), P("space", "band"))
    return jax.shard_map(shards, mesh=mesh, in_specs=in_specs, out_specs=out_specs, check_vma=False)
```

```python
from functools import partial

import jax
import jax.numpy as jnp
from jax import lax
from jax.experimental import pallas as pl
from jax.experimental.pallas import tpu as pltpu
from jax.sharding import PartitionSpec as P

HALO = 6
BOX = 6
NPJ = 9
HALF = 16

stencil_weights = (
    -5369.0 / 1800.0,
    12.0 / 7.0,
    -15.0 / 56.0,
    10.0 / 189.0,
    -1.0 / 112.0,
    2.0 / 1925.0,
    -1.0 / 16632.0,
)
center = 5.5
halfwidth = 5.5
outer = 2.0 / halfwidth
kinetic_weights = [-0.5 * outer * w for w in stencil_weights]

F32 = jnp.float32
BF16 = jnp.bfloat16


def params(vmem):
    return pltpu.CompilerParams(vmem_limit_bytes=vmem)


def circulant(n, blocks):
    size = n * blocks
    row = lax.broadcasted_iota(jnp.int32, (size, size), 0)
    col = lax.broadcasted_iota(jnp.int32, (size, size), 1)
    ahead = jnp.bitwise_and(col - row, n - 1)
    reach = jnp.minimum(ahead, n - ahead)
    value = jnp.zeros((size, size), F32)
    for m, weight in enumerate(kinetic_weights):
        value = jnp.where(reach == m, weight, value)
    value = jnp.where(jnp.bitwise_xor(row, col) < n, value, 0.0)
    hi = value.astype(BF16)
    return hi, (value - hi.astype(F32)).astype(BF16)


def dot(a, b, dims=((1,), (0,))):
    return lax.dot_general(a, b, (dims, ((), ())), preferred_element_type=F32)


def plane_rows(x, ny):
    return slice(x * ny, (x + 1) * ny)


def partners(count):
    return [0, *reversed(range(1, count))]


def pieces_of(ref, index, count, rows, outs):
    for bits, out in zip(partners(count), outs):
        quarter = jnp.bitwise_xor(index, bits)
        begin = pl.multiple_of(quarter * rows, 8)
        out[...] = ref[:, pl.ds(begin, rows), :].astype(out.dtype)


def cast_kernel(psi_ref, up_ref):
    up_ref[...] = psi_ref[:, : up_ref.shape[1]].astype(BF16)


def pieces_kernel(count, psi_ref, *outs):
    rows = psi_ref.shape[1] // count
    pieces_of(psi_ref, lax.axis_index("band"), count, rows, outs)


def yz_part(psi, cz, cy):
    bands, ny, nz = psi.shape
    flat = psi.reshape(bands * ny, nz)
    hi = flat.astype(BF16)
    lo = (flat - hi.astype(F32)).astype(BF16)
    both = jnp.concatenate([hi, lo], axis=1)
    along_z = dot(both, cz[0]) + dot(hi, cz[1])
    size = cy[0].shape[0]
    along_y = []
    for begin in range(0, bands * ny, size):
        pair = dot(cy[0], both[begin : begin + size])
        along_y.append(pair[:, :nz] + pair[:, nz:] + dot(cy[1], hi[begin : begin + size]))
    return (along_z + jnp.concatenate(along_y, axis=0)).reshape(bands, ny, nz)


def same_cell(rows, cols):
    row = lax.broadcasted_iota(jnp.int32, (rows, cols), 0)
    col = lax.broadcasted_iota(jnp.int32, (rows, cols), 1)
    return jnp.where(jnp.bitwise_and(row - col, HALF - 1) == 0, 1.0, 0.0).astype(F32)


def table(proj_ref, a, p):
    npj, ny, nz = proj_ref.shape[1], proj_ref.shape[3], proj_ref.shape[4]
    halves = [
        proj_ref[a, :, p, h * HALF : (h + 1) * HALF, :].reshape(npj * HALF, nz)
        for h in range(ny // HALF)
    ]
    return jnp.concatenate(halves, axis=1)


def halves_along(value, axis):
    bands, ny, nz = value.shape
    parts = [value[:, h * HALF : (h + 1) * HALF].reshape(bands * HALF, nz) for h in range(ny // HALF)]
    return jnp.concatenate(parts, axis=axis)


def spread(weights, tables, nz):
    total = dot(weights, tables)
    rows = total.shape[0]
    halves = [
        total[:, h * nz : (h + 1) * nz].reshape(rows // HALF, HALF, nz)
        for h in range(total.shape[1] // nz)
    ]
    return jnp.concatenate(halves, axis=1)


def overlap(field_ref, planes, ny, table_ref):
    bands = field_ref.shape[0]
    left = [halves_along(field_ref[:, plane_rows(x, ny)], 1) for x in range(planes)]
    right = [table_ref[x] for x in range(planes)]
    d = dot(jnp.concatenate(left, axis=1), jnp.concatenate(right, axis=1), ((1,), (1,)))
    rows, cols = d.shape
    return (d * same_cell(rows, cols)).reshape(bands, HALF, cols).sum(axis=1)


def prepare_kernel(
    planes, first_ref, strength_ref, own_ref, proj_ref, near_ref, far_ref, e_ref, s_ref
):
    ny = own_ref.shape[1] // planes
    atoms, npj = proj_ref.shape[:2]
    me = lax.axis_index("space")
    for q in range(planes + BOX - 1):
        parts = []
        for a in range(atoms):
            p = q - (first_ref[me * atoms + a] - me * planes)
            inside = jnp.logical_and(p >= 0, p < BOX)
            part = table(proj_ref, a, jnp.clip(p, 0, BOX - 1))
            parts.append(part * jnp.where(inside, 1.0, 0.0).astype(BF16))
        whole = jnp.concatenate(parts, axis=0)
        if q < planes:
            near_ref[q] = whole
        else:
            far_ref[q - planes] = whole
    owner = lax.broadcasted_iota(jnp.int32, s_ref.shape, 1)
    scale = jnp.zeros(s_ref.shape, F32)
    for a in range(atoms):
        for j in range(npj):
            value = outer * strength_ref[j, me * atoms + a]
            scale = jnp.where(owner >= (a * npj + j) * HALF, value, scale)
    s_ref[...] = scale
    e_ref[...] = overlap(own_ref, planes, ny, near_ref)


def ahead_kernel(planes, psi_ref, half_ref, ahead_ref, edge_ref):
    half_ref[...] = psi_ref[...].astype(BF16)
    ny = psi_ref.shape[1] // planes
    edge_ref[...] = psi_ref[:, plane_rows(planes - 1, ny)].astype(BF16)
    for x in range(planes - 1):
        total = None
        for m in range(x + 1, HALO + 1):
            term = kinetic_weights[m] * psi_ref[:, plane_rows(planes + x - m, ny)]
            total = term if total is None else total + term
        ahead_ref[:, plane_rows(x, ny)] = total


def coefficient_kernel(upper_ref, table_ref, e_ref, s_ref, ahead_ref, w_ref, next_ref):
    bands, cells, nz = upper_ref.shape
    reach = BOX - 1
    ny = cells // reach
    e = e_ref[...] + overlap(upper_ref, reach, ny, table_ref)
    cols = e.shape[1]
    tiles = -(-cols // nz)
    e = jnp.concatenate([e, jnp.zeros((bands, tiles * nz - cols), F32)], axis=1)
    e = jnp.concatenate([e[:, t * nz : (t + 1) * nz] for t in range(tiles)], axis=0)
    gi = lax.broadcasted_iota(jnp.int32, (nz, nz), 0)
    gj = lax.broadcasted_iota(jnp.int32, (nz, nz), 1)
    group = jnp.where(jnp.bitwise_xor(gi, gj) < HALF, 1.0, 0.0).astype(BF16)
    e_hi = e.astype(BF16)
    e_lo = (e - e_hi.astype(F32)).astype(BF16)
    coef = dot(e_hi, group) + dot(e_lo, group)
    coef = jnp.concatenate([coef[t * bands : (t + 1) * bands] for t in range(tiles)], axis=1)
    w = coef[:, :cols] * s_ref[...]
    rows = bands * HALF
    full = jnp.broadcast_to(w[:, None, :], (bands, HALF, cols)).reshape(rows, cols)
    weights = (full * same_cell(rows, cols)).astype(BF16)
    w_ref[...] = weights
    for q in range(reach):
        here = plane_rows(q, ny)
        block = spread(weights, table_ref[q], nz) + ahead_ref[:, here]
        next_ref[:, here] = block.astype(BF16)


def near_kernel(planes, psi_ref, prev_ref, pot_ref, w_ref, upper_ref, table_ref, out_ref):
    bands, cells, nz = psi_ref.shape
    ny = cells // planes
    weights = w_ref[...]
    cz_hi, cz_lo = circulant(nz, 1)
    cz = (jnp.concatenate([cz_hi, cz_hi], axis=0), cz_lo)
    cy = circulant(ny, bands // 2)
    for x in range(planes):
        here = plane_rows(x, ny)
        psi = psi_ref[:, here]
        total = yz_part(psi, cz, cy) + spread(weights, table_ref[x], nz)
        site = outer * pot_ref[here] + (kinetic_weights[0] - outer * center)
        total = total + site[None] * psi - prev_ref[:, here]
        for m in range(1, HALO + 1):
            for target in (x + m, x - m):
                if 0 <= target < planes:
                    total = total + kinetic_weights[m] * psi_ref[:, plane_rows(target, ny)]
                elif planes <= target < planes + BOX - 1:
                    value = upper_ref[:, plane_rows(target - planes, ny)].astype(F32)
                    total = total + kinetic_weights[m] * value
        out_ref[:, here] = total


def complete(g_ref, arrived_ref, below_ref, above_ref, out_ref):
    cut = arrived_ref.shape[1]
    out_ref[:, :cut] = (g_ref[:, :cut] + arrived_ref[...].astype(F32)).astype(out_ref.dtype)
    edge = kinetic_weights[HALO] * (below_ref[...].astype(F32) + above_ref[...].astype(F32))
    out_ref[:, cut:] = (g_ref[:, cut:] + edge).astype(out_ref.dtype)


def finish_kernel(count, g_ref, arrived_ref, below_ref, above_ref, *rest):
    outs, total = rest[:-1], rest[-1]
    complete(g_ref, arrived_ref, below_ref, above_ref, total)
    rows = g_ref.shape[1] // count
    pieces_of(total, lax.axis_index("band"), count, rows, outs)


def output_kernel(g_ref, arrived_ref, below_ref, above_ref, *rest):
    pieces, (out_ref, panel_ref) = rest[:-2], rest[-2:]
    complete(g_ref, arrived_ref, below_ref, above_ref, out_ref)
    bands = g_ref.shape[0]
    for p, piece in enumerate(pieces):
        panel_ref[p * bands : (p + 1) * bands] = piece[...]


def split_kernel(n_space, n_band, prod_ref, out_ref, held, pair):
    bands = prod_ref.shape[0] // n_band
    me = lax.axis_index("band")
    for p, bits in enumerate(partners(n_band)):
        begin = pl.multiple_of(jnp.bitwise_xor(me, bits) * bands, 8)
        held[pl.ds(begin, bands), :] = prod_ref[p * bands : (p + 1) * bands]
    rows = held.shape[0] // n_space
    for p, bits in enumerate(partners(n_band)):
        cols = [slice((h * n_band + p) * bands, (h * n_band + p + 1) * bands) for h in (0, 1)]
        pair[p] = jnp.concatenate([held[:, c] for c in cols], axis=1)
        owner = jnp.bitwise_xor(me, bits)
        lines = [pair[p, pl.ds(r, n_space, stride=rows), :] for r in range(rows)]
        packed = jnp.concatenate(lines, axis=1)
        for i in range(n_space):
            out_ref[i * n_band + owner] = packed[i : i + 1]


def last_kernel(got_ref, margin_ref, projection_ref):
    total = got_ref[...].sum(axis=0)
    rows, bands = margin_ref.shape
    for r in range(rows):
        begin = 2 * r * bands
        margin_ref[r : r + 1] = total[:, begin : begin + bands]
        projection_ref[r : r + 1] = total[:, begin + bands : begin + 2 * bands]


def cyclic(value, axis, steps):
    count = lax.axis_size(axis)
    return lax.ppermute(value, axis, [(i, (i + steps) % count) for i in range(count)])


def mirrored(value, axis, bits):
    count = lax.axis_size(axis)
    return lax.ppermute(value, axis, [(i, i ^ bits) for i in range(count)])


def exchanged(pieces):
    offsets = partners(len(pieces))
    return [mirrored(p, "band", bits) if bits else p for bits, p in zip(offsets, pieces)]


def struct(shape, kind=F32):
    return jax.ShapeDtypeStruct(shape, kind)


def call(kernel, name, out_shape, args, vmem=48, **extra):
    return pl.pallas_call(
        kernel, out_shape=out_shape, compiler_params=params(vmem * 2**20), name=name, **extra
    )(*args)


def shards(orbitals, previous, potential, projectors, strengths, atom_planes):
    bands, planes, ny, nz = orbitals.shape
    n_space = lax.axis_size("space")
    n_band = lax.axis_size("band")
    cells = planes * ny
    whole = (bands, cells, nz)
    quarter = (bands, cells // n_band, nz)
    psi = orbitals.reshape(whole)
    prev = previous.reshape(whole)
    pot = potential.reshape(cells, nz)

    vm = pl.BlockSpec(memory_space=pltpu.VMEM)
    sm = pl.BlockSpec(memory_space=pltpu.SMEM)
    anywhere = pl.BlockSpec(memory_space=pl.ANY)

    most = (bands, (planes - 1) * ny, nz)
    plane = (bands, ny, nz)
    up = call(cast_kernel, "cast", struct(most, BF16), (psi,))
    panel = call(
        partial(pieces_kernel, n_band),
        "pieces",
        (struct(quarter, BF16),) * n_band,
        (psi,),
        cost_estimate=pl.CostEstimate(flops=10**9, bytes_accessed=2**20, transcendentals=0),
    )
    upper = cyclic(up, "space", -1)
    panel = exchanged(panel)
    half, ahead, edge = call(
        partial(ahead_kernel, planes),
        "ahead",
        (struct(whole, BF16), struct(most), struct(plane, BF16)),
        (psi,),
        cost_estimate=pl.CostEstimate(flops=10**9, bytes_accessed=2**20, transcendentals=0),
    )
    below = cyclic(edge, "space", 1)
    above = cyclic(edge, "space", -1)
    atoms, npj = projectors.shape[:2]
    cols = atoms * npj * HALF
    tables, far_tables, e, s = call(
        partial(prepare_kernel, planes),
        "prepare",
        (
            struct((planes, cols, ny // HALF * nz), BF16),
            struct((BOX - 1, cols, ny // HALF * nz), BF16),
            struct((bands, cols)),
            struct((1, cols)),
        ),
        (atom_planes, strengths.T, half, projectors),
        in_specs=[sm, sm, vm, vm],
        out_specs=(vm,) * 4,
        cost_estimate=pl.CostEstimate(flops=10**9, bytes_accessed=2**20, transcendentals=0),
    )
    w, beyond = call(
        coefficient_kernel,
        "coefficients",
        (struct((bands * HALF, cols), BF16), struct(most, BF16)),
        (upper, far_tables, e, s, ahead),
        cost_estimate=pl.CostEstimate(flops=10**9, bytes_accessed=2**20, transcendentals=0),
    )
    arrived = cyclic(beyond, "space", 1)
    g = call(
        partial(near_kernel, planes),
        "near_part",
        struct(whole),
        (psi, prev, pot, w, upper, tables),
        cost_estimate=pl.CostEstimate(flops=2*10**10, bytes_accessed=4 * 2**20, transcendentals=0),
    )
    mine = call(
        partial(finish_kernel, n_band),
        "finish",
        (struct(quarter, BF16),) * n_band,
        (g, arrived, below, above),
        scratch_shapes=[pltpu.VMEM(whole, F32)],
    )
    mine = exchanged(mine)
    total_bands = n_band * bands
    filtered, panels = call(
        output_kernel,
        "output",
        (struct(whole, BF16), struct((total_bands, *quarter[1:]), BF16)),
        (g, arrived, below, above, *panel),
    )
    left = jnp.concatenate(mine, axis=0).reshape(total_bands, -1)
    right = jnp.concatenate([left, panels.reshape(total_bands, -1)], axis=0)
    products = dot(left, right, ((1,), (1,))) * (1.0 / (cells * n_space * nz))
    out_rows = total_bands // n_space
    pieces = call(
        partial(split_kernel, n_space, n_band),
        "split",
        struct((n_space * n_band, 1, out_rows * 2 * bands)),
        (products,),
        scratch_shapes=[
            pltpu.VMEM(products.shape, F32),
            pltpu.VMEM((n_band, total_bands, 2 * bands), F32),
        ],
    )
    got = lax.all_to_all(pieces, ("space", "band"), 0, 0)
    margin, projection = call(
        last_kernel, "last_sum", (struct((out_rows, bands)), struct((out_rows, bands))), (got,)
    )
    return filtered.reshape(orbitals.shape), margin, projection


def solution(mesh):
    in_specs = (
        P("band", "space", None, None),
        P("band", "space", None, None),
        P("space", None, None),
        P("space", None, None, None, None),
        P(),
        P(),
    )
    out_specs = (P("band", "space", None, None), P("space", "band"), P("space", "band"))
    return jax.shard_map(shards, mesh=mesh, in_specs=in_specs, out_specs=out_specs, check_vma=False)
```

```python
from functools import partial

import jax
import jax.numpy as jnp
from jax import lax
from jax.experimental import pallas as pl
from jax.experimental.pallas import tpu as pltpu
from jax.sharding import PartitionSpec as P

HALO = 6
BOX = 6
NPJ = 9
HALF = 16

stencil_weights = (
    -5369.0 / 1800.0,
    12.0 / 7.0,
    -15.0 / 56.0,
    10.0 / 189.0,
    -1.0 / 112.0,
    2.0 / 1925.0,
    -1.0 / 16632.0,
)
center = 5.5
halfwidth = 5.5
outer = 2.0 / halfwidth
kinetic_weights = [-0.5 * outer * w for w in stencil_weights]

F32 = jnp.float32
BF16 = jnp.bfloat16


def params(vmem):
    return pltpu.CompilerParams(vmem_limit_bytes=vmem)


def circulant(n, blocks):
    size = n * blocks
    row = lax.broadcasted_iota(jnp.int32, (size, size), 0)
    col = lax.broadcasted_iota(jnp.int32, (size, size), 1)
    ahead = jnp.bitwise_and(col - row, n - 1)
    reach = jnp.minimum(ahead, n - ahead)
    value = jnp.zeros((size, size), F32)
    for m, weight in enumerate(kinetic_weights):
        value = jnp.where(reach == m, weight, value)
    value = jnp.where(jnp.bitwise_xor(row, col) < n, value, 0.0)
    hi = value.astype(BF16)
    return hi, (value - hi.astype(F32)).astype(BF16)


def dot(a, b, dims=((1,), (0,))):
    return lax.dot_general(a, b, (dims, ((), ())), preferred_element_type=F32)


def plane_rows(x, ny):
    return slice(x * ny, (x + 1) * ny)


def partners(count):
    return [0, *reversed(range(1, count))]


def pieces_of(ref, index, count, rows, outs):
    for bits, out in zip(partners(count), outs):
        quarter = jnp.bitwise_xor(index, bits)
        begin = pl.multiple_of(quarter * rows, 8)
        out[...] = ref[:, pl.ds(begin, rows), :].astype(out.dtype)


def cast_kernel(psi_ref, half_ref):
    half_ref[...] = psi_ref[...].astype(BF16)


def pieces_kernel(count, psi_ref, *outs):
    rows = psi_ref.shape[1] // count
    pieces_of(psi_ref, lax.axis_index("band"), count, rows, outs)


def yz_part(psi, cz, cy):
    bands, ny, nz = psi.shape
    flat = psi.reshape(bands * ny, nz)
    hi = flat.astype(BF16)
    lo = (flat - hi.astype(F32)).astype(BF16)
    both = jnp.concatenate([hi, lo], axis=1)
    along_z = dot(both, cz[0]) + dot(hi, cz[1])
    size = cy[0].shape[0]
    along_y = []
    for begin in range(0, bands * ny, size):
        pair = dot(cy[0], both[begin : begin + size])
        along_y.append(pair[:, :nz] + pair[:, nz:] + dot(cy[1], hi[begin : begin + size]))
    return (along_z + jnp.concatenate(along_y, axis=0)).reshape(bands, ny, nz)


def same_cell(rows, cols):
    row = lax.broadcasted_iota(jnp.int32, (rows, cols), 0)
    col = lax.broadcasted_iota(jnp.int32, (rows, cols), 1)
    return jnp.where(jnp.bitwise_and(row - col, HALF - 1) == 0, 1.0, 0.0).astype(F32)


def table(proj_ref, a, p):
    npj, ny, nz = proj_ref.shape[1], proj_ref.shape[3], proj_ref.shape[4]
    halves = [
        proj_ref[a, :, p, h * HALF : (h + 1) * HALF, :].reshape(npj * HALF, nz)
        for h in range(ny // HALF)
    ]
    return jnp.concatenate(halves, axis=1)


def halves_along(value, axis):
    bands, ny, nz = value.shape
    parts = [value[:, h * HALF : (h + 1) * HALF].reshape(bands * HALF, nz) for h in range(ny // HALF)]
    return jnp.concatenate(parts, axis=axis)


def spread(weights, tables, nz):
    total = dot(weights, tables)
    rows = total.shape[0]
    halves = [
        total[:, h * nz : (h + 1) * nz].reshape(rows // HALF, HALF, nz)
        for h in range(total.shape[1] // nz)
    ]
    return jnp.concatenate(halves, axis=1)


def overlap(field_ref, planes, ny, table_ref):
    bands = field_ref.shape[0]
    left = [halves_along(field_ref[:, plane_rows(x, ny)], 1) for x in range(planes)]
    right = [table_ref[x] for x in range(planes)]
    d = dot(jnp.concatenate(left, axis=1), jnp.concatenate(right, axis=1), ((1,), (1,)))
    rows, cols = d.shape
    return (d * same_cell(rows, cols)).reshape(bands, HALF, cols).sum(axis=1)


def prepare_kernel(
    planes, first_ref, strength_ref, own_ref, proj_ref, near_ref, far_ref, e_ref, s_ref
):
    ny = own_ref.shape[1] // planes
    atoms, npj = proj_ref.shape[:2]
    me = lax.axis_index("space")
    for q in range(planes + BOX - 1):
        parts = []
        for a in range(atoms):
            p = q - (first_ref[me * atoms + a] - me * planes)
            inside = jnp.logical_and(p >= 0, p < BOX)
            part = table(proj_ref, a, jnp.clip(p, 0, BOX - 1))
            parts.append(part * jnp.where(inside, 1.0, 0.0).astype(BF16))
        whole = jnp.concatenate(parts, axis=0)
        if q < planes:
            near_ref[q] = whole
        else:
            far_ref[q - planes] = whole
    owner = lax.broadcasted_iota(jnp.int32, s_ref.shape, 1)
    scale = jnp.zeros(s_ref.shape, F32)
    for a in range(atoms):
        for j in range(npj):
            value = outer * strength_ref[j, me * atoms + a]
            scale = jnp.where(owner >= (a * npj + j) * HALF, value, scale)
    s_ref[...] = scale
    e_ref[...] = overlap(own_ref, planes, ny, near_ref)


def ahead_kernel(planes, psi_ref, ahead_ref, edge_ref):
    ny = psi_ref.shape[1] // planes
    edge_ref[...] = psi_ref[:, plane_rows(planes - 1, ny)].astype(BF16)
    for x in range(planes - 1):
        total = None
        for m in range(x + 1, HALO + 1):
            term = kinetic_weights[m] * psi_ref[:, plane_rows(planes + x - m, ny)]
            total = term if total is None else total + term
        ahead_ref[:, plane_rows(x, ny)] = total


def coefficient_kernel(planes, upper_ref, table_ref, e_ref, s_ref, ahead_ref, w_ref, next_ref):
    bands, cells, nz = upper_ref.shape
    ny = cells // planes
    reach = BOX - 1
    e = e_ref[...] + overlap(upper_ref, reach, ny, table_ref)
    cols = e.shape[1]
    tiles = -(-cols // nz)
    e = jnp.concatenate([e, jnp.zeros((bands, tiles * nz - cols), F32)], axis=1)
    e = jnp.concatenate([e[:, t * nz : (t + 1) * nz] for t in range(tiles)], axis=0)
    gi = lax.broadcasted_iota(jnp.int32, (nz, nz), 0)
    gj = lax.broadcasted_iota(jnp.int32, (nz, nz), 1)
    group = jnp.where(jnp.bitwise_xor(gi, gj) < HALF, 1.0, 0.0).astype(BF16)
    e_hi = e.astype(BF16)
    e_lo = (e - e_hi.astype(F32)).astype(BF16)
    coef = dot(e_hi, group) + dot(e_lo, group)
    coef = jnp.concatenate([coef[t * bands : (t + 1) * bands] for t in range(tiles)], axis=1)
    w = coef[:, :cols] * s_ref[...]
    rows = bands * HALF
    full = jnp.broadcast_to(w[:, None, :], (bands, HALF, cols)).reshape(rows, cols)
    weights = (full * same_cell(rows, cols)).astype(BF16)
    w_ref[...] = weights
    for q in range(reach):
        here = plane_rows(q, ny)
        block = spread(weights, table_ref[q], nz) + ahead_ref[:, here]
        next_ref[:, here] = block.astype(BF16)


def near_kernel(planes, psi_ref, prev_ref, pot_ref, w_ref, upper_ref, table_ref, out_ref):
    bands, cells, nz = psi_ref.shape
    ny = cells // planes
    weights = w_ref[...]
    cz_hi, cz_lo = circulant(nz, 1)
    cz = (jnp.concatenate([cz_hi, cz_hi], axis=0), cz_lo)
    cy = circulant(ny, bands // 2)
    for x in range(planes):
        here = plane_rows(x, ny)
        psi = psi_ref[:, here]
        total = yz_part(psi, cz, cy) + spread(weights, table_ref[x], nz)
        site = outer * pot_ref[here] + (kinetic_weights[0] - outer * center)
        total = total + site[None] * psi - prev_ref[:, here]
        for m in range(1, HALO + 1):
            for target in (x + m, x - m):
                if 0 <= target < planes:
                    total = total + kinetic_weights[m] * psi_ref[:, plane_rows(target, ny)]
                elif target >= planes:
                    value = upper_ref[:, plane_rows(target - planes, ny)].astype(F32)
                    total = total + kinetic_weights[m] * value
        out_ref[:, here] = total


def complete(g_ref, arrived_ref, below_ref, out_ref):
    cut = arrived_ref.shape[1]
    out_ref[:, :cut] = (g_ref[:, :cut] + arrived_ref[...].astype(F32)).astype(out_ref.dtype)
    edge = kinetic_weights[HALO] * below_ref[...].astype(F32)
    out_ref[:, cut:] = (g_ref[:, cut:] + edge).astype(out_ref.dtype)


def finish_kernel(count, g_ref, arrived_ref, below_ref, *rest):
    outs, total = rest[:-1], rest[-1]
    complete(g_ref, arrived_ref, below_ref, total)
    rows = g_ref.shape[1] // count
    pieces_of(total, lax.axis_index("band"), count, rows, outs)


def panel_order(count):
    return [count - 1, *range(1, count - 1), 0]


def output_kernel(g_ref, arrived_ref, below_ref, *rest):
    pieces, (out_ref, panel_ref) = rest[:-2], rest[-2:]
    complete(g_ref, arrived_ref, below_ref, out_ref)
    bands = g_ref.shape[0]
    for p, piece in zip(panel_order(len(pieces)), pieces):
        panel_ref[p * bands : (p + 1) * bands] = piece[...]


def split_kernel(n_space, n_band, prod_ref, out_ref, held, pair):
    bands = prod_ref.shape[0] // n_band
    me = lax.axis_index("band")
    for p, bits in enumerate(partners(n_band)):
        begin = pl.multiple_of(jnp.bitwise_xor(me, bits) * bands, 8)
        held[pl.ds(begin, bands), :] = prod_ref[p * bands : (p + 1) * bands]
    rows = held.shape[0] // n_space
    for p, bits in enumerate(partners(n_band)):
        cols = [slice((h * n_band + p) * bands, (h * n_band + p + 1) * bands) for h in (0, 1)]
        pair[p] = jnp.concatenate([held[:, c] for c in cols], axis=1)
        owner = jnp.bitwise_xor(me, bits)
        lines = [pair[p, pl.ds(r, n_space, stride=rows), :] for r in range(rows)]
        packed = jnp.concatenate(lines, axis=1)
        for i in range(n_space):
            out_ref[i * n_band + owner] = packed[i : i + 1]


def last_kernel(got_ref, margin_ref, projection_ref):
    total = got_ref[...].sum(axis=0)
    rows, bands = margin_ref.shape
    for r in range(rows):
        begin = 2 * r * bands
        margin_ref[r : r + 1] = total[:, begin : begin + bands]
        projection_ref[r : r + 1] = total[:, begin + bands : begin + 2 * bands]


def cyclic(value, axis, steps):
    count = lax.axis_size(axis)
    return lax.ppermute(value, axis, [(i, (i + steps) % count) for i in range(count)])


def mirrored(value, axis, bits):
    count = lax.axis_size(axis)
    return lax.ppermute(value, axis, [(i, i ^ bits) for i in range(count)])


def exchanged(pieces):
    offsets = partners(len(pieces))
    return [mirrored(p, "band", bits) if bits else p for bits, p in zip(offsets, pieces)]


def struct(shape, kind=F32):
    return jax.ShapeDtypeStruct(shape, kind)


def call(kernel, name, out_shape, args, vmem=48, **extra):
    return pl.pallas_call(
        kernel, out_shape=out_shape, compiler_params=params(vmem * 2**20), name=name, **extra
    )(*args)


def shards(orbitals, previous, potential, projectors, strengths, atom_planes):
    bands, planes, ny, nz = orbitals.shape
    n_space = lax.axis_size("space")
    n_band = lax.axis_size("band")
    cells = planes * ny
    whole = (bands, cells, nz)
    quarter = (bands, cells // n_band, nz)
    psi = orbitals.reshape(whole)
    prev = previous.reshape(whole)
    pot = potential.reshape(cells, nz)

    vm = pl.BlockSpec(memory_space=pltpu.VMEM)
    sm = pl.BlockSpec(memory_space=pltpu.SMEM)
    anywhere = pl.BlockSpec(memory_space=pl.ANY)

    most = (bands, (planes - 1) * ny, nz)
    plane = (bands, ny, nz)
    half = call(cast_kernel, "cast", struct(whole, BF16), (psi,))
    panel = call(
        partial(pieces_kernel, n_band),
        "pieces",
        (struct(quarter, BF16),) * n_band,
        (psi,),
        cost_estimate=pl.CostEstimate(flops=10**9, bytes_accessed=2**20, transcendentals=0),
    )
    upper = cyclic(half, "space", -1)
    panel = exchanged(panel)
    ahead, edge = call(
        partial(ahead_kernel, planes),
        "ahead",
        (struct(most), struct(plane, BF16)),
        (psi,),
        cost_estimate=pl.CostEstimate(flops=10**9, bytes_accessed=2**20, transcendentals=0),
    )
    below = cyclic(edge, "space", 1)
    atoms, npj = projectors.shape[:2]
    cols = atoms * npj * HALF
    tables, far_tables, e, s = call(
        partial(prepare_kernel, planes),
        "prepare",
        (
            struct((planes, cols, ny // HALF * nz), BF16),
            struct((BOX - 1, cols, ny // HALF * nz), BF16),
            struct((bands, cols)),
            struct((1, cols)),
        ),
        (atom_planes, strengths.T, half, projectors),
        in_specs=[sm, sm, vm, vm],
        out_specs=(vm,) * 4,
        cost_estimate=pl.CostEstimate(flops=10**9, bytes_accessed=2**20, transcendentals=0),
    )
    w, beyond = call(
        partial(coefficient_kernel, planes),
        "coefficients",
        (struct((bands * HALF, cols), BF16), struct(most, BF16)),
        (upper, far_tables, e, s, ahead),
        cost_estimate=pl.CostEstimate(flops=10**9, bytes_accessed=2**20, transcendentals=0),
    )
    arrived = cyclic(beyond, "space", 1)
    g = call(
        partial(near_kernel, planes),
        "near_part",
        struct(whole),
        (psi, prev, pot, w, upper, tables),
        cost_estimate=pl.CostEstimate(flops=2*10**10, bytes_accessed=4 * 2**20, transcendentals=0),
    )
    mine = call(
        partial(finish_kernel, n_band),
        "finish",
        (struct(quarter, BF16),) * n_band,
        (g, arrived, below),
        scratch_shapes=[pltpu.VMEM(whole, F32)],
    )
    mine = exchanged(mine)
    total_bands = n_band * bands
    filtered, panels = call(
        output_kernel,
        "output",
        (struct(whole, BF16), struct((total_bands, *quarter[1:]), BF16)),
        (g, arrived, below, *[panel[p] for p in panel_order(n_band)]),
    )
    left = jnp.concatenate(mine, axis=0).reshape(total_bands, -1)
    right = jnp.concatenate([left, panels.reshape(total_bands, -1)], axis=0)
    products = dot(left, right, ((1,), (1,))) * (1.0 / (cells * n_space * nz))
    out_rows = total_bands // n_space
    pieces = call(
        partial(split_kernel, n_space, n_band),
        "split",
        struct((n_space * n_band, 1, out_rows * 2 * bands)),
        (products,),
        scratch_shapes=[
            pltpu.VMEM(products.shape, F32),
            pltpu.VMEM((n_band, total_bands, 2 * bands), F32),
        ],
    )
    got = lax.all_to_all(pieces, ("space", "band"), 0, 0)
    margin, projection = call(
        last_kernel, "last_sum", (struct((out_rows, bands)), struct((out_rows, bands))), (got,)
    )
    return filtered.reshape(orbitals.shape), margin, projection


def solution(mesh):
    in_specs = (
        P("band", "space", None, None),
        P("band", "space", None, None),
        P("space", None, None),
        P("space", None, None, None, None),
        P(),
        P(),
    )
    out_specs = (P("band", "space", None, None), P("space", "band"), P("space", "band"))
    return jax.shard_map(shards, mesh=mesh, in_specs=in_specs, out_specs=out_specs, check_vma=False)
```

```python
from functools import partial

import jax
import jax.numpy as jnp
from jax import lax
from jax.experimental import pallas as pl
from jax.experimental.pallas import tpu as pltpu
from jax.sharding import PartitionSpec as P

HALO = 6
BOX = 6
NPJ = 9
HALF = 16

stencil_weights = (
    -5369.0 / 1800.0,
    12.0 / 7.0,
    -15.0 / 56.0,
    10.0 / 189.0,
    -1.0 / 112.0,
    2.0 / 1925.0,
    -1.0 / 16632.0,
)
center = 5.5
halfwidth = 5.5
outer = 2.0 / halfwidth
kinetic_weights = [-0.5 * outer * w for w in stencil_weights]

F32 = jnp.float32
BF16 = jnp.bfloat16


def params(vmem):
    return pltpu.CompilerParams(vmem_limit_bytes=vmem)


def circulant(n, blocks):
    size = n * blocks
    row = lax.broadcasted_iota(jnp.int32, (size, size), 0)
    col = lax.broadcasted_iota(jnp.int32, (size, size), 1)
    ahead = jnp.bitwise_and(col - row, n - 1)
    reach = jnp.minimum(ahead, n - ahead)
    value = jnp.zeros((size, size), F32)
    for m, weight in enumerate(kinetic_weights):
        value = jnp.where(reach == m, weight, value)
    value = jnp.where(jnp.bitwise_xor(row, col) < n, value, 0.0)
    hi = value.astype(BF16)
    return hi, (value - hi.astype(F32)).astype(BF16)


def dot(a, b, dims=((1,), (0,))):
    return lax.dot_general(a, b, (dims, ((), ())), preferred_element_type=F32)


def plane_rows(x, ny):
    return slice(x * ny, (x + 1) * ny)


def partners(count):
    return [0, *reversed(range(1, count))]


def pieces_of(ref, index, count, rows, outs):
    for bits, out in zip(partners(count), outs):
        quarter = jnp.bitwise_xor(index, bits)
        begin = pl.multiple_of(quarter * rows, 16 if rows % 16 == 0 else 8)
        out[...] = ref[:, pl.ds(begin, rows), :].astype(out.dtype)


def cast_kernel(psi_hbm, half_ref, psi_ref, sems):
    copies = [
        pltpu.make_async_copy(psi_hbm.at[b], psi_ref.at[b], sems.at[b])
        for b in range(psi_ref.shape[0])
    ]
    for copy in copies:
        copy.start()
    for b, copy in enumerate(copies):
        copy.wait()
        half_ref[b] = psi_ref[b].astype(BF16)


def pieces_kernel(count, psi_ref, *outs):
    rows = psi_ref.shape[1] // count
    pieces_of(psi_ref, lax.axis_index("band"), count, rows, outs)


def yz_part(psi, cz, cy):
    bands, ny, nz = psi.shape
    flat = psi.reshape(bands * ny, nz)
    hi = flat.astype(BF16)
    lo = (flat - hi.astype(F32)).astype(BF16)
    both = jnp.concatenate([hi, lo], axis=1)
    along_z = dot(both, cz[0]) + dot(hi, cz[1])
    size = cy[0].shape[0]
    along_y = []
    for begin in range(0, bands * ny, size):
        pair = dot(cy[0], both[begin : begin + size])
        along_y.append(pair[:, :nz] + pair[:, nz:] + dot(cy[1], hi[begin : begin + size]))
    return (along_z + jnp.concatenate(along_y, axis=0)).reshape(bands, ny, nz)


def same_cell(rows, cols):
    row = lax.broadcasted_iota(jnp.int32, (rows, cols), 0)
    col = lax.broadcasted_iota(jnp.int32, (rows, cols), 1)
    return jnp.where(jnp.bitwise_and(row - col, HALF - 1) == 0, 1.0, 0.0).astype(F32)


def table(proj_ref, a, p):
    npj, ny, nz = proj_ref.shape[1], proj_ref.shape[3], proj_ref.shape[4]
    halves = [
        proj_ref[a, :, p, h * HALF : (h + 1) * HALF, :].reshape(npj * HALF, nz)
        for h in range(ny // HALF)
    ]
    return jnp.concatenate(halves, axis=1)


def halves_along(value, axis):
    bands, ny, nz = value.shape
    parts = [value[:, h * HALF : (h + 1) * HALF].reshape(bands * HALF, nz) for h in range(ny // HALF)]
    return jnp.concatenate(parts, axis=axis)


def spread(weights, tables, nz):
    total = dot(weights, tables)
    rows = total.shape[0]
    halves = [
        total[:, h * nz : (h + 1) * nz].reshape(rows // HALF, HALF, nz)
        for h in range(total.shape[1] // nz)
    ]
    return jnp.concatenate(halves, axis=1)


def overlap(field_ref, planes, ny, table_ref):
    bands = field_ref.shape[0]
    left = [halves_along(field_ref[:, plane_rows(x, ny)], 1) for x in range(planes)]
    right = [table_ref[x] for x in range(planes)]
    d = dot(jnp.concatenate(left, axis=1), jnp.concatenate(right, axis=1), ((1,), (1,)))
    rows, cols = d.shape
    return (d * same_cell(rows, cols)).reshape(bands, HALF, cols).sum(axis=1)


def prepare_kernel(
    planes, first_ref, strength_ref, own_ref, proj_ref, near_ref, far_ref, e_ref, s_ref
):
    ny = own_ref.shape[1] // planes
    atoms, npj = proj_ref.shape[:2]
    me = lax.axis_index("space")
    for q in range(planes + BOX - 1):
        parts = []
        for a in range(atoms):
            p = q - (first_ref[me * atoms + a] - me * planes)
            inside = jnp.logical_and(p >= 0, p < BOX)
            part = table(proj_ref, a, jnp.clip(p, 0, BOX - 1))
            parts.append(part * jnp.where(inside, 1.0, 0.0).astype(BF16))
        whole = jnp.concatenate(parts, axis=0)
        if q < planes:
            near_ref[q] = whole
        else:
            far_ref[q - planes] = whole
    owner = lax.broadcasted_iota(jnp.int32, s_ref.shape, 1)
    scale = jnp.zeros(s_ref.shape, F32)
    for a in range(atoms):
        for j in range(npj):
            value = outer * strength_ref[j, me * atoms + a]
            scale = jnp.where(owner >= (a * npj + j) * HALF, value, scale)
    s_ref[...] = scale
    e_ref[...] = overlap(own_ref, planes, ny, near_ref)


def ahead_kernel(planes, psi_ref, ahead_ref):
    ny = psi_ref.shape[1] // planes
    for x in range(planes):
        total = None
        for m in range(x + 1, HALO + 1):
            term = kinetic_weights[m] * psi_ref[:, plane_rows(planes + x - m, ny)]
            total = term if total is None else total + term
        ahead_ref[:, plane_rows(x, ny)] = total


def coefficient_kernel(planes, upper_ref, table_ref, e_ref, s_ref, ahead_ref, w_ref, next_ref):
    bands, cells, nz = upper_ref.shape
    ny = cells // planes
    reach = BOX - 1
    e = e_ref[...] + overlap(upper_ref, reach, ny, table_ref)
    cols = e.shape[1]
    tiles = -(-cols // nz)
    e = jnp.concatenate([e, jnp.zeros((bands, tiles * nz - cols), F32)], axis=1)
    e = jnp.concatenate([e[:, t * nz : (t + 1) * nz] for t in range(tiles)], axis=0)
    gi = lax.broadcasted_iota(jnp.int32, (nz, nz), 0)
    gj = lax.broadcasted_iota(jnp.int32, (nz, nz), 1)
    group = jnp.where(jnp.bitwise_xor(gi, gj) < HALF, 1.0, 0.0).astype(BF16)
    e_hi = e.astype(BF16)
    e_lo = (e - e_hi.astype(F32)).astype(BF16)
    coef = dot(e_hi, group) + dot(e_lo, group)
    coef = jnp.concatenate([coef[t * bands : (t + 1) * bands] for t in range(tiles)], axis=1)
    w = coef[:, :cols] * s_ref[...]
    rows = bands * HALF
    full = jnp.broadcast_to(w[:, None, :], (bands, HALF, cols)).reshape(rows, cols)
    weights = (full * same_cell(rows, cols)).astype(BF16)
    w_ref[...] = weights
    for q in range(reach):
        here = plane_rows(q, ny)
        block = spread(weights, table_ref[q], nz) + ahead_ref[:, here]
        next_ref[:, here] = block.astype(BF16)
    rest = slice(reach * ny, planes * ny)
    next_ref[:, rest] = ahead_ref[:, rest].astype(BF16)


def near_kernel(planes, psi_ref, prev_ref, pot_ref, w_ref, upper_ref, table_ref, out_ref):
    bands, cells, nz = psi_ref.shape
    ny = cells // planes
    weights = w_ref[...]
    cz_hi, cz_lo = circulant(nz, 1)
    cz = (jnp.concatenate([cz_hi, cz_hi], axis=0), cz_lo)
    cy = circulant(ny, bands // 2)
    for x in range(planes):
        here = plane_rows(x, ny)
        psi = psi_ref[:, here]
        total = yz_part(psi, cz, cy) + spread(weights, table_ref[x], nz)
        site = outer * pot_ref[here] + (kinetic_weights[0] - outer * center)
        total = total + site[None] * psi - prev_ref[:, here]
        for m in range(1, HALO + 1):
            for target in (x + m, x - m):
                if 0 <= target < planes:
                    total = total + kinetic_weights[m] * psi_ref[:, plane_rows(target, ny)]
                elif target >= planes:
                    value = upper_ref[:, plane_rows(target - planes, ny)].astype(F32)
                    total = total + kinetic_weights[m] * value
        out_ref[:, here] = total


def finish_kernel(count, g_ref, arrived_ref, *rest):
    outs, total = rest[:-1], rest[-1]
    total[...] = g_ref[...] + arrived_ref[...].astype(F32)
    rows = g_ref.shape[1] // count
    pieces_of(total, lax.axis_index("band"), count, rows, outs)


def output_kernel(g_ref, arrived_ref, *rest):
    pieces, (out_ref, panel_ref) = rest[:-2], rest[-2:]
    out_ref[...] = (g_ref[...] + arrived_ref[...].astype(F32)).astype(BF16)
    bands = g_ref.shape[0]
    for p, piece in enumerate(pieces):
        panel_ref[p * bands : (p + 1) * bands] = piece[...]


def split_kernel(n_space, n_band, prod_ref, out_ref, held, pair):
    bands = prod_ref.shape[0] // n_band
    me = lax.axis_index("band")
    for p, bits in enumerate(partners(n_band)):
        begin = pl.multiple_of(jnp.bitwise_xor(me, bits) * bands, 8)
        held[pl.ds(begin, bands), :] = prod_ref[p * bands : (p + 1) * bands]
    rows = held.shape[0] // n_space
    for p, bits in enumerate(partners(n_band)):
        cols = [slice((h * n_band + p) * bands, (h * n_band + p + 1) * bands) for h in (0, 1)]
        pair[p] = jnp.concatenate([held[:, c] for c in cols], axis=1)
        owner = jnp.bitwise_xor(me, bits)
        lines = [pair[p, pl.ds(r, n_space, stride=rows), :] for r in range(rows)]
        packed = jnp.concatenate(lines, axis=1)
        for i in range(n_space):
            out_ref[i * n_band + owner] = packed[i : i + 1]


def last_kernel(got_ref, margin_ref, projection_ref):
    total = got_ref[...].sum(axis=0)
    rows, bands = margin_ref.shape
    for r in range(rows):
        begin = 2 * r * bands
        margin_ref[r : r + 1] = total[:, begin : begin + bands]
        projection_ref[r : r + 1] = total[:, begin + bands : begin + 2 * bands]


def cyclic(value, axis, steps):
    count = lax.axis_size(axis)
    return lax.ppermute(value, axis, [(i, (i + steps) % count) for i in range(count)])


def mirrored(value, axis, bits):
    count = lax.axis_size(axis)
    return lax.ppermute(value, axis, [(i, i ^ bits) for i in range(count)])


def exchanged(pieces):
    offsets = partners(len(pieces))
    return [mirrored(p, "band", bits) if bits else p for bits, p in zip(offsets, pieces)]


def struct(shape, kind=F32):
    return jax.ShapeDtypeStruct(shape, kind)


def call(kernel, name, out_shape, args, vmem=48, **extra):
    return pl.pallas_call(
        kernel, out_shape=out_shape, compiler_params=params(int(vmem * 2**20)), name=name, **extra
    )(*args)


def shards(orbitals, previous, potential, projectors, strengths, atom_planes):
    bands, planes, ny, nz = orbitals.shape
    n_space = lax.axis_size("space")
    n_band = lax.axis_size("band")
    cells = planes * ny
    whole = (bands, cells, nz)
    quarter = (bands, cells // n_band, nz)
    psi = orbitals.reshape(whole)
    prev = previous.reshape(whole)
    pot = potential.reshape(cells, nz)

    vm = pl.BlockSpec(memory_space=pltpu.VMEM)
    sm = pl.BlockSpec(memory_space=pltpu.SMEM)

    half = call(
        cast_kernel,
        "cast",
        struct(whole, BF16),
        (psi,),
        vmem=53.2,
        in_specs=[pl.BlockSpec(memory_space=pl.ANY)],
        out_specs=vm,
        scratch_shapes=[pltpu.VMEM(whole, F32), pltpu.SemaphoreType.DMA((bands,))],
    )
    panel = call(
        partial(pieces_kernel, n_band),
        "pieces",
        (struct(quarter, BF16),) * n_band,
        (half if quarter[1] % 16 == 0 else psi,),
        cost_estimate=pl.CostEstimate(flops=10**9, bytes_accessed=2**20, transcendentals=0),
    )
    upper = cyclic(half, "space", -1)
    panel = exchanged(panel)
    ahead = call(
        partial(ahead_kernel, planes),
        "ahead",
        struct(whole),
        (psi,),
        cost_estimate=pl.CostEstimate(flops=10**9, bytes_accessed=2**20, transcendentals=0),
    )
    atoms, npj = projectors.shape[:2]
    cols = atoms * npj * HALF
    tables, far_tables, e, s = call(
        partial(prepare_kernel, planes),
        "prepare",
        (
            struct((planes, cols, ny // HALF * nz), BF16),
            struct((BOX - 1, cols, ny // HALF * nz), BF16),
            struct((bands, cols)),
            struct((1, cols)),
        ),
        (atom_planes, strengths.T, half, projectors),
        in_specs=[sm, sm, vm, vm],
        out_specs=(vm,) * 4,
        cost_estimate=pl.CostEstimate(flops=10**9, bytes_accessed=2**20, transcendentals=0),
    )
    w, beyond = call(
        partial(coefficient_kernel, planes),
        "coefficients",
        (struct((bands * HALF, cols), BF16), struct(whole, BF16)),
        (upper, far_tables, e, s, ahead),
        cost_estimate=pl.CostEstimate(flops=10**9, bytes_accessed=2**20, transcendentals=0),
    )
    arrived = cyclic(beyond, "space", 1)
    g = call(
        partial(near_kernel, planes),
        "near_part",
        struct(whole),
        (psi, prev, pot, w, upper, tables),
        cost_estimate=pl.CostEstimate(flops=2*10**10, bytes_accessed=4 * 2**20, transcendentals=0),
    )
    mine = call(
        partial(finish_kernel, n_band),
        "finish",
        (struct(quarter, BF16),) * n_band,
        (g, arrived),
        scratch_shapes=[pltpu.VMEM(whole, F32)],
    )
    mine = exchanged(mine)
    total_bands = n_band * bands
    filtered, panels = call(
        output_kernel,
        "output",
        (struct(whole, BF16), struct((total_bands, *quarter[1:]), BF16)),
        (g, arrived, *panel),
    )
    left = jnp.concatenate(mine, axis=0).reshape(total_bands, -1)
    right = jnp.concatenate([left, panels.reshape(total_bands, -1)], axis=0)
    products = dot(left, right, ((1,), (1,))) * (1.0 / (cells * n_space * nz))
    out_rows = total_bands // n_space
    pieces = call(
        partial(split_kernel, n_space, n_band),
        "split",
        struct((n_space * n_band, 1, out_rows * 2 * bands)),
        (products,),
        scratch_shapes=[
            pltpu.VMEM(products.shape, F32),
            pltpu.VMEM((n_band, total_bands, 2 * bands), F32),
        ],
    )
    got = lax.all_to_all(pieces, ("space", "band"), 0, 0)
    margin, projection = call(
        last_kernel, "last_sum", (struct((out_rows, bands)), struct((out_rows, bands))), (got,)
    )
    return filtered.reshape(orbitals.shape), margin, projection


def solution(mesh):
    in_specs = (
        P("band", "space", None, None),
        P("band", "space", None, None),
        P("space", None, None),
        P("space", None, None, None, None),
        P(),
        P(),
    )
    out_specs = (P("band", "space", None, None), P("space", "band"), P("space", "band"))
    return jax.shard_map(shards, mesh=mesh, in_specs=in_specs, out_specs=out_specs, check_vma=False)
```

```python
from functools import partial

import jax
import jax.numpy as jnp
from jax import lax
from jax.experimental import pallas as pl
from jax.experimental.pallas import tpu as pltpu
from jax.sharding import PartitionSpec as P

HALO = 6
BOX = 6
NPJ = 9
HALF = 16

stencil_weights = (
    -5369.0 / 1800.0,
    12.0 / 7.0,
    -15.0 / 56.0,
    10.0 / 189.0,
    -1.0 / 112.0,
    2.0 / 1925.0,
    -1.0 / 16632.0,
)
center = 5.5
halfwidth = 5.5
outer = 2.0 / halfwidth
kinetic_weights = [-0.5 * outer * w for w in stencil_weights]

F32 = jnp.float32
BF16 = jnp.bfloat16


def params(vmem):
    return pltpu.CompilerParams(vmem_limit_bytes=vmem)


def circulant(n, blocks):
    size = n * blocks
    row = lax.broadcasted_iota(jnp.int32, (size, size), 0)
    col = lax.broadcasted_iota(jnp.int32, (size, size), 1)
    ahead = jnp.bitwise_and(col - row, n - 1)
    reach = jnp.minimum(ahead, n - ahead)
    value = jnp.zeros((size, size), F32)
    for m, weight in enumerate(kinetic_weights):
        value = jnp.where(reach == m, weight, value)
    value = jnp.where(jnp.bitwise_xor(row, col) < n, value, 0.0)
    hi = value.astype(BF16)
    return hi, (value - hi.astype(F32)).astype(BF16)


def dot(a, b, dims=((1,), (0,))):
    return lax.dot_general(a, b, (dims, ((), ())), preferred_element_type=F32)


def plane_rows(x, ny):
    return slice(x * ny, (x + 1) * ny)


def partners(count):
    return [0, *reversed(range(1, count))]


def pieces_of(ref, index, count, rows, outs):
    for bits, out in zip(partners(count), outs):
        quarter = jnp.bitwise_xor(index, bits)
        begin = pl.multiple_of(quarter * rows, 8)
        out[...] = ref[:, pl.ds(begin, rows), :].astype(out.dtype)


def cast_kernel(psi_ref, half_ref):
    half_ref[...] = psi_ref[...].astype(BF16)


def pieces_kernel(count, psi_ref, *outs):
    rows = psi_ref.shape[1] // count
    pieces_of(psi_ref, lax.axis_index("band"), count, rows, outs)


def yz_part(psi, cz, cy):
    bands, ny, nz = psi.shape
    flat = psi.reshape(bands * ny, nz)
    hi = flat.astype(BF16)
    lo = (flat - hi.astype(F32)).astype(BF16)
    both = jnp.concatenate([hi, lo], axis=1)
    along_z = dot(both, cz[0]) + dot(hi, cz[1])
    size = cy[0].shape[0]
    along_y = []
    for begin in range(0, bands * ny, size):
        pair = dot(cy[0], both[begin : begin + size])
        along_y.append(pair[:, :nz] + pair[:, nz:] + dot(cy[1], hi[begin : begin + size]))
    return (along_z + jnp.concatenate(along_y, axis=0)).reshape(bands, ny, nz)


def same_cell(rows, cols):
    row = lax.broadcasted_iota(jnp.int32, (rows, cols), 0)
    col = lax.broadcasted_iota(jnp.int32, (rows, cols), 1)
    return jnp.where(jnp.bitwise_and(row - col, HALF - 1) == 0, 1.0, 0.0).astype(F32)


def table(proj_ref, a, p):
    npj, ny, nz = proj_ref.shape[1], proj_ref.shape[3], proj_ref.shape[4]
    halves = [
        proj_ref[a, :, p, h * HALF : (h + 1) * HALF, :].reshape(npj * HALF, nz)
        for h in range(ny // HALF)
    ]
    return jnp.concatenate(halves, axis=1)


def halves_along(value, axis):
    bands, ny, nz = value.shape
    parts = [value[:, h * HALF : (h + 1) * HALF].reshape(bands * HALF, nz) for h in range(ny // HALF)]
    return jnp.concatenate(parts, axis=axis)


def spread(weights, tables, nz):
    total = dot(weights, tables)
    rows = total.shape[0]
    halves = [
        total[:, h * nz : (h + 1) * nz].reshape(rows // HALF, HALF, nz)
        for h in range(total.shape[1] // nz)
    ]
    return jnp.concatenate(halves, axis=1)


def overlap(field_ref, planes, ny, table_ref):
    bands = field_ref.shape[0]
    left = [halves_along(field_ref[:, plane_rows(x, ny)], 1) for x in range(planes)]
    right = [table_ref[x] for x in range(planes)]
    d = dot(jnp.concatenate(left, axis=1), jnp.concatenate(right, axis=1), ((1,), (1,)))
    rows, cols = d.shape
    return (d * same_cell(rows, cols)).reshape(bands, HALF, cols).sum(axis=1)


def prepare_kernel(
    planes, first_ref, strength_ref, own_ref, proj_ref, near_ref, far_ref, e_ref, s_ref
):
    ny = own_ref.shape[1] // planes
    atoms, npj = proj_ref.shape[:2]
    me = lax.axis_index("space")
    for q in range(planes + BOX - 1):
        parts = []
        for a in range(atoms):
            p = q - (first_ref[me * atoms + a] - me * planes)
            inside = jnp.logical_and(p >= 0, p < BOX)
            part = table(proj_ref, a, jnp.clip(p, 0, BOX - 1))
            parts.append(part * jnp.where(inside, 1.0, 0.0).astype(BF16))
        whole = jnp.concatenate(parts, axis=0)
        if q < planes:
            near_ref[q] = whole
        else:
            far_ref[q - planes] = whole
    owner = lax.broadcasted_iota(jnp.int32, s_ref.shape, 1)
    scale = jnp.zeros(s_ref.shape, F32)
    for a in range(atoms):
        for j in range(npj):
            value = outer * strength_ref[j, me * atoms + a]
            scale = jnp.where(owner >= (a * npj + j) * HALF, value, scale)
    s_ref[...] = scale
    e_ref[...] = overlap(own_ref, planes, ny, near_ref)


def ahead_kernel(planes, psi_ref, *refs):
    ahead_ref, edge_ref = refs[-2:]
    ny = psi_ref.shape[1] // planes
    edge_ref[...] = psi_ref[:, plane_rows(planes - 1, ny)].astype(BF16)
    for x in range(planes - 1):
        total = None
        for m in range(x + 1, HALO + 1):
            term = kinetic_weights[m] * psi_ref[:, plane_rows(planes + x - m, ny)]
            total = term if total is None else total + term
        ahead_ref[:, plane_rows(x, ny)] = total


def coefficient_kernel(planes, upper_ref, table_ref, e_ref, s_ref, ahead_ref, w_ref, next_ref):
    bands, cells, nz = upper_ref.shape
    ny = cells // planes
    reach = BOX - 1
    e = e_ref[...] + overlap(upper_ref, reach, ny, table_ref)
    cols = e.shape[1]
    tiles = -(-cols // nz)
    e = jnp.concatenate([e, jnp.zeros((bands, tiles * nz - cols), F32)], axis=1)
    e = jnp.concatenate([e[:, t * nz : (t + 1) * nz] for t in range(tiles)], axis=0)
    gi = lax.broadcasted_iota(jnp.int32, (nz, nz), 0)
    gj = lax.broadcasted_iota(jnp.int32, (nz, nz), 1)
    group = jnp.where(jnp.bitwise_xor(gi, gj) < HALF, 1.0, 0.0).astype(BF16)
    e_hi = e.astype(BF16)
    e_lo = (e - e_hi.astype(F32)).astype(BF16)
    coef = dot(e_hi, group) + dot(e_lo, group)
    coef = jnp.concatenate([coef[t * bands : (t + 1) * bands] for t in range(tiles)], axis=1)
    w = coef[:, :cols] * s_ref[...]
    rows = bands * HALF
    full = jnp.broadcast_to(w[:, None, :], (bands, HALF, cols)).reshape(rows, cols)
    weights = (full * same_cell(rows, cols)).astype(BF16)
    w_ref[...] = weights
    for q in range(reach):
        here = plane_rows(q, ny)
        block = spread(weights, table_ref[q], nz) + ahead_ref[:, here]
        next_ref[:, here] = block.astype(BF16)


def near_kernel(planes, psi_ref, prev_ref, pot_ref, w_ref, upper_ref, table_ref, out_ref):
    bands, cells, nz = psi_ref.shape
    ny = cells // planes
    weights = w_ref[...]
    cz_hi, cz_lo = circulant(nz, 1)
    cz = (jnp.concatenate([cz_hi, cz_hi], axis=0), cz_lo)
    cy = circulant(ny, bands // 2)
    for x in range(planes):
        here = plane_rows(x, ny)
        psi = psi_ref[:, here]
        total = yz_part(psi, cz, cy) + spread(weights, table_ref[x], nz)
        site = outer * pot_ref[here] + (kinetic_weights[0] - outer * center)
        total = total + site[None] * psi - prev_ref[:, here]
        for m in range(1, HALO + 1):
            for target in (x + m, x - m):
                if 0 <= target < planes:
                    total = total + kinetic_weights[m] * psi_ref[:, plane_rows(target, ny)]
                elif target >= planes:
                    value = upper_ref[:, plane_rows(target - planes, ny)].astype(F32)
                    total = total + kinetic_weights[m] * value
        out_ref[:, here] = total


def complete(g_ref, arrived_ref, below_ref, out_ref):
    cut = arrived_ref.shape[1]
    out_ref[:, :cut] = (g_ref[:, :cut] + arrived_ref[...].astype(F32)).astype(out_ref.dtype)
    edge = kinetic_weights[HALO] * below_ref[...].astype(F32)
    out_ref[:, cut:] = (g_ref[:, cut:] + edge).astype(out_ref.dtype)


def finish_kernel(count, g_ref, arrived_ref, below_ref, *rest):
    outs, total = rest[:-1], rest[-1]
    complete(g_ref, arrived_ref, below_ref, total)
    rows = g_ref.shape[1] // count
    pieces_of(total, lax.axis_index("band"), count, rows, outs)


def output_kernel(g_ref, arrived_ref, below_ref, *rest):
    pieces, (out_ref, panel_ref) = rest[:-2], rest[-2:]
    complete(g_ref, arrived_ref, below_ref, out_ref)
    bands = g_ref.shape[0]
    for p, piece in enumerate(reversed(pieces)):
        panel_ref[p * bands : (p + 1) * bands] = piece[...]


def split_kernel(n_space, n_band, prod_ref, keep_ref, give_ref, held, pair):
    bands = prod_ref.shape[0] // n_band
    me = lax.axis_index("band")
    parity = jnp.bitwise_and(lax.axis_index("space"), 1)
    for p, bits in enumerate(partners(n_band)):
        begin = pl.multiple_of(jnp.bitwise_xor(me, bits) * bands, 8)
        held[pl.ds(begin, bands), :] = prod_ref[p * bands : (p + 1) * bands]
    rows = held.shape[0] // n_space
    for p, bits in enumerate(partners(n_band)):
        cols = [slice((h * n_band + p) * bands, (h * n_band + p + 1) * bands) for h in (0, 1)]
        pair[p] = jnp.concatenate([held[:, c] for c in cols], axis=1)
        owner = jnp.bitwise_xor(me, bits)
        step = 2 * rows
        for ref, odd in ((keep_ref, parity), (give_ref, 1 - parity)):
            lines = [
                pair[p, pl.ds(odd * rows + r, n_space // 2, stride=step), :] for r in range(rows)
            ]
            packed = jnp.concatenate(lines, axis=1)
            for i in range(n_space // 2):
                ref[i * n_band + owner] = packed[i : i + 1]


def join_kernel(keep_ref, got_ref, out_ref):
    out_ref[...] = keep_ref[...] + got_ref[...]


def last_kernel(got_ref, margin_ref, projection_ref):
    total = got_ref[...].sum(axis=0)
    rows, bands = margin_ref.shape
    for r in range(rows):
        begin = 2 * r * bands
        margin_ref[r : r + 1] = total[:, begin : begin + bands]
        projection_ref[r : r + 1] = total[:, begin + bands : begin + 2 * bands]


def cyclic(value, axis, steps):
    count = lax.axis_size(axis)
    return lax.ppermute(value, axis, [(i, (i + steps) % count) for i in range(count)])


def mirrored(value, axis, bits):
    count = lax.axis_size(axis)
    return lax.ppermute(value, axis, [(i, i ^ bits) for i in range(count)])


def exchanged(pieces):
    offsets = partners(len(pieces))
    return [mirrored(p, "band", bits) if bits else p for bits, p in zip(offsets, pieces)]


def struct(shape, kind=F32):
    return jax.ShapeDtypeStruct(shape, kind)


def call(kernel, name, out_shape, args, vmem=48, **extra):
    return pl.pallas_call(
        kernel, out_shape=out_shape, compiler_params=params(vmem * 2**20), name=name, **extra
    )(*args)


def shards(orbitals, previous, potential, projectors, strengths, atom_planes):
    bands, planes, ny, nz = orbitals.shape
    n_space = lax.axis_size("space")
    n_band = lax.axis_size("band")
    cells = planes * ny
    whole = (bands, cells, nz)
    quarter = (bands, cells // n_band, nz)
    psi = orbitals.reshape(whole)
    prev = previous.reshape(whole)
    pot = potential.reshape(cells, nz)

    vm = pl.BlockSpec(memory_space=pltpu.VMEM)
    sm = pl.BlockSpec(memory_space=pltpu.SMEM)
    anywhere = pl.BlockSpec(memory_space=pl.ANY)

    most = (bands, (planes - 1) * ny, nz)
    plane = (bands, ny, nz)
    half = call(cast_kernel, "cast", struct(whole, BF16), (psi,))
    panel = call(
        partial(pieces_kernel, n_band),
        "pieces",
        (struct(quarter, BF16),) * n_band,
        (psi,),
        cost_estimate=pl.CostEstimate(flops=10**9, bytes_accessed=2**20, transcendentals=0),
    )
    upper = cyclic(half, "space", -1)
    panel = exchanged(panel)
    atoms, npj = projectors.shape[:2]
    cols = atoms * npj * HALF
    tables, far_tables, e, s = call(
        partial(prepare_kernel, planes),
        "prepare",
        (
            struct((planes, cols, ny // HALF * nz), BF16),
            struct((BOX - 1, cols, ny // HALF * nz), BF16),
            struct((bands, cols)),
            struct((1, cols)),
        ),
        (atom_planes, strengths.T, half, projectors),
        in_specs=[sm, sm, vm, vm],
        out_specs=(vm,) * 4,
        cost_estimate=pl.CostEstimate(flops=10**9, bytes_accessed=2**20, transcendentals=0),
    )
    ahead, edge = call(
        partial(ahead_kernel, planes),
        "ahead",
        (struct(most), struct(plane, BF16)),
        (psi, panel[3], s),
        in_specs=[vm, anywhere, anywhere],
        out_specs=(vm, vm),
        cost_estimate=pl.CostEstimate(flops=10**9, bytes_accessed=2**20, transcendentals=0),
    )
    below = cyclic(edge, "space", 1)
    w, beyond = call(
        partial(coefficient_kernel, planes),
        "coefficients",
        (struct((bands * HALF, cols), BF16), struct(most, BF16)),
        (upper, far_tables, e, s, ahead),
        cost_estimate=pl.CostEstimate(flops=10**9, bytes_accessed=2**20, transcendentals=0),
    )
    arrived = cyclic(beyond, "space", 1)
    g = call(
        partial(near_kernel, planes),
        "near_part",
        struct(whole),
        (psi, prev, pot, w, upper, tables),
        cost_estimate=pl.CostEstimate(flops=2*10**10, bytes_accessed=4 * 2**20, transcendentals=0),
    )
    mine = call(
        partial(finish_kernel, n_band),
        "finish",
        (struct(quarter, BF16),) * n_band,
        (g, arrived, below),
        scratch_shapes=[pltpu.VMEM(whole, F32)],
    )
    mine = exchanged(mine)
    total_bands = n_band * bands
    filtered, panels = call(
        output_kernel,
        "output",
        (struct(whole, BF16), struct((total_bands, *quarter[1:]), BF16)),
        (g, arrived, below, *reversed(panel)),
    )
    left = jnp.concatenate(mine, axis=0).reshape(total_bands, -1)
    right = jnp.concatenate([left, panels.reshape(total_bands, -1)], axis=0)
    products = dot(left, right, ((1,), (1,))) * (1.0 / (cells * n_space * nz))
    out_rows = total_bands // n_space
    half_pieces = struct((n_space // 2 * n_band, 1, out_rows * 2 * bands))
    keep, give = call(
        partial(split_kernel, n_space, n_band),
        "split",
        (half_pieces, half_pieces),
        (products,),
        scratch_shapes=[
            pltpu.VMEM(products.shape, F32),
            pltpu.VMEM((n_band, total_bands, 2 * bands), F32),
        ],
    )
    pieces = call(join_kernel, "join", half_pieces, (keep, mirrored(give, "space", 1)))
    got = lax.all_to_all(
        pieces,
        ("space", "band"),
        0,
        0,
        axis_index_groups=[
            [s * n_band + k for s in range(odd, n_space, 2) for k in range(n_band)] for odd in (0, 1)
        ],
    )
    margin, projection = call(
        last_kernel, "last_sum", (struct((out_rows, bands)), struct((out_rows, bands))), (got,)
    )
    return filtered.reshape(orbitals.shape), margin, projection


def solution(mesh):
    in_specs = (
        P("band", "space", None, None),
        P("band", "space", None, None),
        P("space", None, None),
        P("space", None, None, None, None),
        P(),
        P(),
    )
    out_specs = (P("band", "space", None, None), P("space", "band"), P("space", "band"))
    return jax.shard_map(shards, mesh=mesh, in_specs=in_specs, out_specs=out_specs, check_vma=False)
```

```python
from functools import partial

import jax
import jax.numpy as jnp
from jax import lax
from jax.experimental import pallas as pl
from jax.experimental.pallas import tpu as pltpu
from jax.sharding import PartitionSpec as P

HALO = 6
BOX = 6
NPJ = 9
HALF = 16

stencil_weights = (
    -5369.0 / 1800.0,
    12.0 / 7.0,
    -15.0 / 56.0,
    10.0 / 189.0,
    -1.0 / 112.0,
    2.0 / 1925.0,
    -1.0 / 16632.0,
)
center = 5.5
halfwidth = 5.5
outer = 2.0 / halfwidth
kinetic_weights = [-0.5 * outer * w for w in stencil_weights]

F32 = jnp.float32
BF16 = jnp.bfloat16


def params(vmem):
    return pltpu.CompilerParams(vmem_limit_bytes=vmem)


def circulant(n, blocks):
    size = n * blocks
    row = lax.broadcasted_iota(jnp.int32, (size, size), 0)
    col = lax.broadcasted_iota(jnp.int32, (size, size), 1)
    ahead = jnp.bitwise_and(col - row, n - 1)
    reach = jnp.minimum(ahead, n - ahead)
    value = jnp.zeros((size, size), F32)
    for m, weight in enumerate(kinetic_weights):
        value = jnp.where(reach == m, weight, value)
    value = jnp.where(jnp.bitwise_xor(row, col) < n, value, 0.0)
    hi = value.astype(BF16)
    return hi, (value - hi.astype(F32)).astype(BF16)


def dot(a, b, dims=((1,), (0,))):
    return lax.dot_general(a, b, (dims, ((), ())), preferred_element_type=F32)


def plane_rows(x, ny):
    return slice(x * ny, (x + 1) * ny)


def partners(count):
    return [0, *reversed(range(1, count))]


def pieces_of(ref, index, count, rows, outs):
    for bits, out in zip(partners(count), outs):
        quarter = jnp.bitwise_xor(index, bits)
        begin = pl.multiple_of(quarter * rows, 8)
        out[...] = ref[:, pl.ds(begin, rows), :].astype(out.dtype)


def cast_kernel(psi_ref, half_ref):
    half_ref[...] = psi_ref[...].astype(BF16)


def pieces_kernel(count, psi_ref, *outs):
    rows = psi_ref.shape[1] // count
    pieces_of(psi_ref, lax.axis_index("band"), count, rows, outs)


def yz_part(psi, cz, cy):
    bands, ny, nz = psi.shape
    flat = psi.reshape(bands * ny, nz)
    hi = flat.astype(BF16)
    lo = (flat - hi.astype(F32)).astype(BF16)
    both = jnp.concatenate([hi, lo], axis=1)
    along_z = dot(both, cz[0]) + dot(hi, cz[1])
    size = cy[0].shape[0]
    along_y = []
    for begin in range(0, bands * ny, size):
        pair = dot(cy[0], both[begin : begin + size])
        along_y.append(pair[:, :nz] + pair[:, nz:] + dot(cy[1], hi[begin : begin + size]))
    return (along_z + jnp.concatenate(along_y, axis=0)).reshape(bands, ny, nz)


def same_cell(rows, cols):
    row = lax.broadcasted_iota(jnp.int32, (rows, cols), 0)
    col = lax.broadcasted_iota(jnp.int32, (rows, cols), 1)
    return jnp.where(jnp.bitwise_and(row - col, HALF - 1) == 0, 1.0, 0.0).astype(F32)


def table(proj_ref, a, p):
    npj, ny, nz = proj_ref.shape[1], proj_ref.shape[3], proj_ref.shape[4]
    halves = [
        proj_ref[a, :, p, h * HALF : (h + 1) * HALF, :].reshape(npj * HALF, nz)
        for h in range(ny // HALF)
    ]
    return jnp.concatenate(halves, axis=1)


def halves_along(value, axis):
    bands, ny, nz = value.shape
    parts = [value[:, h * HALF : (h + 1) * HALF].reshape(bands * HALF, nz) for h in range(ny // HALF)]
    return jnp.concatenate(parts, axis=axis)


def spread(weights, tables, nz):
    total = dot(weights, tables)
    rows = total.shape[0]
    halves = [
        total[:, h * nz : (h + 1) * nz].reshape(rows // HALF, HALF, nz)
        for h in range(total.shape[1] // nz)
    ]
    return jnp.concatenate(halves, axis=1)


def plane_table(proj_ref, starts, q):
    parts = []
    for a, start in enumerate(starts):
        p = q - start
        inside = jnp.logical_and(p >= 0, p < BOX)
        part = table(proj_ref, a, jnp.clip(p, 0, BOX - 1))
        parts.append(part * jnp.where(inside, 1.0, 0.0).astype(BF16))
    return jnp.concatenate(parts, axis=0)


def box_starts(first_ref, atoms, planes):
    me = lax.axis_index("space")
    return [first_ref[me * atoms + a] - me * planes for a in range(atoms)]


def overlap(field_ref, tables, ny):
    bands = field_ref.shape[0]
    left = [halves_along(field_ref[:, plane_rows(x, ny)], 1) for x in range(len(tables))]
    d = dot(jnp.concatenate(left, axis=1), jnp.concatenate(tables, axis=1), ((1,), (1,)))
    rows, cols = d.shape
    return (d * same_cell(rows, cols)).reshape(bands, HALF, cols).sum(axis=1)


def prepare_kernel(planes, first_ref, strength_ref, own_ref, proj_ref, far_ref, e_ref, s_ref):
    ny = own_ref.shape[1] // planes
    atoms, npj = proj_ref.shape[:2]
    me = lax.axis_index("space")
    starts = box_starts(first_ref, atoms, planes)
    for q in range(BOX - 1):
        far_ref[q] = plane_table(proj_ref, starts, planes + q)
    owner = lax.broadcasted_iota(jnp.int32, s_ref.shape, 1)
    scale = jnp.zeros(s_ref.shape, F32)
    for a in range(atoms):
        for j in range(npj):
            value = outer * strength_ref[j, me * atoms + a]
            scale = jnp.where(owner >= (a * npj + j) * HALF, value, scale)
    s_ref[...] = scale
    e_ref[...] = overlap(own_ref, [plane_table(proj_ref, starts, q) for q in range(planes)], ny)


def ahead_kernel(planes, psi_ref, *refs):
    ahead_ref, edge_ref = refs[-2:]
    ny = psi_ref.shape[1] // planes
    edge_ref[...] = psi_ref[:, plane_rows(planes - 1, ny)].astype(BF16)
    for x in range(planes - 1):
        total = None
        for m in range(x + 1, HALO + 1):
            term = kinetic_weights[m] * psi_ref[:, plane_rows(planes + x - m, ny)]
            total = term if total is None else total + term
        ahead_ref[:, plane_rows(x, ny)] = total


def coefficient_kernel(planes, upper_ref, table_ref, e_ref, s_ref, ahead_ref, w_ref, next_ref):
    bands, cells, nz = upper_ref.shape
    ny = cells // planes
    reach = BOX - 1
    e = e_ref[...] + overlap(upper_ref, [table_ref[q] for q in range(reach)], ny)
    cols = e.shape[1]
    tiles = -(-cols // nz)
    e = jnp.concatenate([e, jnp.zeros((bands, tiles * nz - cols), F32)], axis=1)
    e = jnp.concatenate([e[:, t * nz : (t + 1) * nz] for t in range(tiles)], axis=0)
    gi = lax.broadcasted_iota(jnp.int32, (nz, nz), 0)
    gj = lax.broadcasted_iota(jnp.int32, (nz, nz), 1)
    group = jnp.where(jnp.bitwise_xor(gi, gj) < HALF, 1.0, 0.0).astype(BF16)
    e_hi = e.astype(BF16)
    e_lo = (e - e_hi.astype(F32)).astype(BF16)
    coef = dot(jnp.concatenate([e_hi, e_lo], axis=1), jnp.concatenate([group, group], axis=0))
    coef = jnp.concatenate([coef[t * bands : (t + 1) * bands] for t in range(tiles)], axis=1)
    w = coef[:, :cols] * s_ref[...]
    rows = bands * HALF
    full = jnp.broadcast_to(w[:, None, :], (bands, HALF, cols)).reshape(rows, cols)
    weights = (full * same_cell(rows, cols)).astype(BF16)
    w_ref[...] = weights
    for q in range(reach):
        here = plane_rows(q, ny)
        block = spread(weights, table_ref[q], nz) + ahead_ref[:, here]
        next_ref[:, here] = block.astype(BF16)


def near_kernel(
    planes, first_ref, psi_ref, prev_ref, pot_ref, w_ref, upper_ref, proj_ref, out_ref
):
    bands, cells, nz = psi_ref.shape
    ny = cells // planes
    weights = w_ref[...]
    starts = box_starts(first_ref, proj_ref.shape[0], planes)
    cz_hi, cz_lo = circulant(nz, 1)
    cz = (jnp.concatenate([cz_hi, cz_hi], axis=0), cz_lo)
    cy = circulant(ny, bands // 2)
    for x in range(planes):
        here = plane_rows(x, ny)
        psi = psi_ref[:, here]
        total = yz_part(psi, cz, cy) + spread(weights, plane_table(proj_ref, starts, x), nz)
        site = outer * pot_ref[here] + (kinetic_weights[0] - outer * center)
        total = total + site[None] * psi - prev_ref[:, here]
        for m in range(1, HALO + 1):
            for target in (x + m, x - m):
                if 0 <= target < planes:
                    total = total + kinetic_weights[m] * psi_ref[:, plane_rows(target, ny)]
                elif target >= planes:
                    value = upper_ref[:, plane_rows(target - planes, ny)].astype(F32)
                    total = total + kinetic_weights[m] * value
        out_ref[:, here] = total


def complete(g_ref, arrived_ref, below_ref, out_ref):
    cut = arrived_ref.shape[1]
    out_ref[:, :cut] = (g_ref[:, :cut] + arrived_ref[...].astype(F32)).astype(out_ref.dtype)
    edge = kinetic_weights[HALO] * below_ref[...].astype(F32)
    out_ref[:, cut:] = (g_ref[:, cut:] + edge).astype(out_ref.dtype)


def finish_kernel(count, g_ref, arrived_ref, below_ref, *rest):
    outs, total = rest[:-1], rest[-1]
    complete(g_ref, arrived_ref, below_ref, total)
    rows = g_ref.shape[1] // count
    pieces_of(total, lax.axis_index("band"), count, rows, outs)


def output_kernel(g_ref, arrived_ref, below_ref, *rest):
    pieces, (out_ref, panel_ref) = rest[:-2], rest[-2:]
    complete(g_ref, arrived_ref, below_ref, out_ref)
    bands = g_ref.shape[0]
    for p, piece in enumerate(reversed(pieces)):
        panel_ref[p * bands : (p + 1) * bands] = piece[...]


def split_kernel(n_space, n_band, prod_ref, out_ref, held, pair):
    bands = prod_ref.shape[0] // n_band
    me = lax.axis_index("band")
    for p, bits in enumerate(partners(n_band)):
        begin = pl.multiple_of(jnp.bitwise_xor(me, bits) * bands, 8)
        held[pl.ds(begin, bands), :] = prod_ref[p * bands : (p + 1) * bands]
    rows = held.shape[0] // n_space
    for p, bits in enumerate(partners(n_band)):
        cols = [slice((h * n_band + p) * bands, (h * n_band + p + 1) * bands) for h in (0, 1)]
        pair[p] = jnp.concatenate([held[:, c] for c in cols], axis=1)
        owner = jnp.bitwise_xor(me, bits)
        lines = [pair[p, pl.ds(r, n_space, stride=rows), :] for r in range(rows)]
        packed = jnp.concatenate(lines, axis=1)
        for i in range(n_space):
            out_ref[i * n_band + owner] = packed[i : i + 1]


def last_kernel(got_ref, margin_ref, projection_ref):
    total = got_ref[...].sum(axis=0)
    rows, bands = margin_ref.shape
    for r in range(rows):
        begin = 2 * r * bands
        margin_ref[r : r + 1] = total[:, begin : begin + bands]
        projection_ref[r : r + 1] = total[:, begin + bands : begin + 2 * bands]


def cyclic(value, axis, steps):
    count = lax.axis_size(axis)
    return lax.ppermute(value, axis, [(i, (i + steps) % count) for i in range(count)])


def mirrored(value, axis, bits):
    count = lax.axis_size(axis)
    return lax.ppermute(value, axis, [(i, i ^ bits) for i in range(count)])


def exchanged(pieces):
    offsets = partners(len(pieces))
    return [mirrored(p, "band", bits) if bits else p for bits, p in zip(offsets, pieces)]


def struct(shape, kind=F32):
    return jax.ShapeDtypeStruct(shape, kind)


def call(kernel, name, out_shape, args, vmem=48, **extra):
    return pl.pallas_call(
        kernel, out_shape=out_shape, compiler_params=params(vmem * 2**20), name=name, **extra
    )(*args)


def shards(orbitals, previous, potential, projectors, strengths, atom_planes):
    bands, planes, ny, nz = orbitals.shape
    n_space = lax.axis_size("space")
    n_band = lax.axis_size("band")
    cells = planes * ny
    whole = (bands, cells, nz)
    quarter = (bands, cells // n_band, nz)
    psi = orbitals.reshape(whole)
    prev = previous.reshape(whole)
    pot = potential.reshape(cells, nz)

    vm = pl.BlockSpec(memory_space=pltpu.VMEM)
    sm = pl.BlockSpec(memory_space=pltpu.SMEM)
    anywhere = pl.BlockSpec(memory_space=pl.ANY)

    most = (bands, (planes - 1) * ny, nz)
    plane = (bands, ny, nz)
    half = call(cast_kernel, "cast", struct(whole, BF16), (psi,))
    panel = call(
        partial(pieces_kernel, n_band),
        "pieces",
        (struct(quarter, BF16),) * n_band,
        (psi,),
        cost_estimate=pl.CostEstimate(flops=10**9, bytes_accessed=2**20, transcendentals=0),
    )
    upper = cyclic(half, "space", -1)
    panel = exchanged(panel)
    atoms, npj = projectors.shape[:2]
    cols = atoms * npj * HALF
    far_tables, e, s = call(
        partial(prepare_kernel, planes),
        "prepare",
        (
            struct((BOX - 1, cols, ny // HALF * nz), BF16),
            struct((bands, cols)),
            struct((1, cols)),
        ),
        (atom_planes, strengths.T, half, projectors),
        in_specs=[sm, sm, vm, vm],
        out_specs=(vm,) * 3,
        cost_estimate=pl.CostEstimate(flops=10**9, bytes_accessed=2**20, transcendentals=0),
    )
    ahead, edge = call(
        partial(ahead_kernel, planes),
        "ahead",
        (struct(most), struct(plane, BF16)),
        (psi, panel[3], s),
        in_specs=[vm, anywhere, anywhere],
        out_specs=(vm, vm),
        cost_estimate=pl.CostEstimate(flops=10**9, bytes_accessed=2**20, transcendentals=0),
    )
    below = cyclic(edge, "space", 1)
    w, beyond = call(
        partial(coefficient_kernel, planes),
        "coefficients",
        (struct((bands * HALF, cols), BF16), struct(most, BF16)),
        (upper, far_tables, e, s, ahead),
        cost_estimate=pl.CostEstimate(flops=10**9, bytes_accessed=2**20, transcendentals=0),
    )
    arrived = cyclic(beyond, "space", 1)
    g = call(
        partial(near_kernel, planes),
        "near_part",
        struct(whole),
        (atom_planes, psi, prev, pot, w, upper, projectors),
        in_specs=[sm] + [vm] * 6,
        out_specs=vm,
        cost_estimate=pl.CostEstimate(flops=2*10**10, bytes_accessed=4 * 2**20, transcendentals=0),
    )
    mine = call(
        partial(finish_kernel, n_band),
        "finish",
        (struct(quarter, BF16),) * n_band,
        (g, arrived, below),
        scratch_shapes=[pltpu.VMEM(whole, F32)],
    )
    mine = exchanged(mine)
    total_bands = n_band * bands
    filtered, panels = call(
        output_kernel,
        "output",
        (struct(whole, BF16), struct((total_bands, *quarter[1:]), BF16)),
        (g, arrived, below, *reversed(panel)),
    )
    left = jnp.concatenate(mine, axis=0).reshape(total_bands, -1)
    right = jnp.concatenate([left, panels.reshape(total_bands, -1)], axis=0)
    products = dot(left, right, ((1,), (1,))) * (1.0 / (cells * n_space * nz))
    out_rows = total_bands // n_space
    pieces = call(
        partial(split_kernel, n_space, n_band),
        "split",
        struct((n_space * n_band, 1, out_rows * 2 * bands)),
        (products,),
        scratch_shapes=[
            pltpu.VMEM(products.shape, F32),
            pltpu.VMEM((n_band, total_bands, 2 * bands), F32),
        ],
    )
    got = lax.all_to_all(pieces, ("space", "band"), 0, 0)
    margin, projection = call(
        last_kernel, "last_sum", (struct((out_rows, bands)), struct((out_rows, bands))), (got,)
    )
    return filtered.reshape(orbitals.shape), margin, projection


def solution(mesh):
    in_specs = (
        P("band", "space", None, None),
        P("band", "space", None, None),
        P("space", None, None),
        P("space", None, None, None, None),
        P(),
        P(),
    )
    out_specs = (P("band", "space", None, None), P("space", "band"), P("space", "band"))
    return jax.shard_map(shards, mesh=mesh, in_specs=in_specs, out_specs=out_specs, check_vma=False)
```

```python
from functools import partial

import jax
import jax.numpy as jnp
from jax import lax
from jax.experimental import pallas as pl
from jax.experimental.pallas import tpu as pltpu
from jax.sharding import PartitionSpec as P

HALO = 6
BOX = 6
NPJ = 9
HALF = 16

stencil_weights = (
    -5369.0 / 1800.0,
    12.0 / 7.0,
    -15.0 / 56.0,
    10.0 / 189.0,
    -1.0 / 112.0,
    2.0 / 1925.0,
    -1.0 / 16632.0,
)
center = 5.5
halfwidth = 5.5
outer = 2.0 / halfwidth
kinetic_weights = [-0.5 * outer * w for w in stencil_weights]

F32 = jnp.float32
BF16 = jnp.bfloat16


def params(vmem):
    return pltpu.CompilerParams(vmem_limit_bytes=vmem)


def circulant(n, blocks):
    size = n * blocks
    row = lax.broadcasted_iota(jnp.int32, (size, size), 0)
    col = lax.broadcasted_iota(jnp.int32, (size, size), 1)
    ahead = jnp.bitwise_and(col - row, n - 1)
    reach = jnp.minimum(ahead, n - ahead)
    value = jnp.zeros((size, size), F32)
    for m, weight in enumerate(kinetic_weights):
        value = jnp.where(reach == m, weight, value)
    value = jnp.where(jnp.bitwise_xor(row, col) < n, value, 0.0)
    hi = value.astype(BF16)
    return hi, (value - hi.astype(F32)).astype(BF16)


def dot(a, b, dims=((1,), (0,))):
    return lax.dot_general(a, b, (dims, ((), ())), preferred_element_type=F32)


def plane_rows(x, ny):
    return slice(x * ny, (x + 1) * ny)


def partners(count):
    return [0, *reversed(range(1, count))]


def pieces_of(ref, index, count, rows, outs):
    for bits, out in zip(partners(count), outs):
        quarter = jnp.bitwise_xor(index, bits)
        begin = pl.multiple_of(quarter * rows, 8)
        out[...] = ref[:, pl.ds(begin, rows), :].astype(out.dtype)


def cast_kernel(psi_ref, half_ref):
    half_ref[...] = psi_ref[...].astype(BF16)


def pieces_kernel(count, psi_ref, *outs):
    rows = psi_ref.shape[1] // count
    pieces_of(psi_ref, lax.axis_index("band"), count, rows, outs)


def yz_part(psi, cz, cy):
    bands, ny, nz = psi.shape
    flat = psi.reshape(bands * ny, nz)
    hi = flat.astype(BF16)
    lo = (flat - hi.astype(F32)).astype(BF16)
    both = jnp.concatenate([hi, lo], axis=1)
    along_z = dot(both, cz[0]) + dot(hi, cz[1])
    size = cy[0].shape[0]
    along_y = []
    for begin in range(0, bands * ny, size):
        pair = dot(cy[0], both[begin : begin + size])
        along_y.append(pair[:, :nz] + pair[:, nz:] + dot(cy[1], hi[begin : begin + size]))
    return (along_z + jnp.concatenate(along_y, axis=0)).reshape(bands, ny, nz)


def same_cell(rows, cols):
    row = lax.broadcasted_iota(jnp.int32, (rows, cols), 0)
    col = lax.broadcasted_iota(jnp.int32, (rows, cols), 1)
    return jnp.where(jnp.bitwise_and(row - col, HALF - 1) == 0, 1.0, 0.0).astype(F32)


def table(proj_ref, a, p):
    npj, ny, nz = proj_ref.shape[1], proj_ref.shape[3], proj_ref.shape[4]
    halves = [
        proj_ref[a, :, p, h * HALF : (h + 1) * HALF, :].reshape(npj * HALF, nz)
        for h in range(ny // HALF)
    ]
    return jnp.concatenate(halves, axis=1)


def halves_along(value, axis):
    bands, ny, nz = value.shape
    parts = [value[:, h * HALF : (h + 1) * HALF].reshape(bands * HALF, nz) for h in range(ny // HALF)]
    return jnp.concatenate(parts, axis=axis)


def spread(weights, tables, nz):
    total = dot(weights, tables)
    rows = total.shape[0]
    halves = [
        total[:, h * nz : (h + 1) * nz].reshape(rows // HALF, HALF, nz)
        for h in range(total.shape[1] // nz)
    ]
    return jnp.concatenate(halves, axis=1)


def plane_table(proj_ref, starts, q):
    parts = []
    for a, start in enumerate(starts):
        p = q - start
        inside = jnp.logical_and(p >= 0, p < BOX)
        part = table(proj_ref, a, jnp.clip(p, 0, BOX - 1))
        parts.append(part * jnp.where(inside, 1.0, 0.0).astype(BF16))
    return jnp.concatenate(parts, axis=0)


def box_starts(first_ref, atoms, planes):
    me = lax.axis_index("space")
    return [first_ref[me * atoms + a] - me * planes for a in range(atoms)]


def overlap(field_ref, tables, ny):
    left = [halves_along(field_ref[:, plane_rows(x, ny)], 1) for x in range(len(tables))]
    d = dot(jnp.concatenate(tables, axis=1), jnp.concatenate(left, axis=1), ((1,), (1,)))
    rows, cols = d.shape
    return (d * same_cell(rows, cols)).reshape(rows // HALF, HALF, cols).sum(axis=1)


def prepare_kernel(planes, first_ref, strength_ref, own_ref, proj_ref, far_ref, e_ref, s_ref):
    ny = own_ref.shape[1] // planes
    atoms, npj = proj_ref.shape[:2]
    me = lax.axis_index("space")
    starts = box_starts(first_ref, atoms, planes)
    for q in range(BOX - 1):
        far_ref[q] = plane_table(proj_ref, starts, planes + q)
    owner = lax.broadcasted_iota(jnp.int32, s_ref.shape, 1)
    scale = jnp.zeros(s_ref.shape, F32)
    for a in range(atoms):
        for j in range(npj):
            value = outer * strength_ref[j, me * atoms + a]
            scale = jnp.where(owner == a * npj + j, value, scale)
    s_ref[...] = scale
    e_ref[...] = overlap(own_ref, [plane_table(proj_ref, starts, q) for q in range(planes)], ny)


def ahead_kernel(planes, psi_ref, *refs):
    ahead_ref, edge_ref = refs[-2:]
    ny = psi_ref.shape[1] // planes
    edge_ref[...] = psi_ref[:, plane_rows(planes - 1, ny)].astype(BF16)
    for x in range(planes - 1):
        total = None
        for m in range(x + 1, HALO + 1):
            term = kinetic_weights[m] * psi_ref[:, plane_rows(planes + x - m, ny)]
            total = term if total is None else total + term
        ahead_ref[:, plane_rows(x, ny)] = total


def coefficient_kernel(planes, upper_ref, table_ref, e_ref, s_ref, ahead_ref, w_ref, next_ref):
    bands, cells, nz = upper_ref.shape
    ny = cells // planes
    reach = BOX - 1
    e = e_ref[...] + overlap(upper_ref, [table_ref[q] for q in range(reach)], ny)
    count, rows = e.shape
    wide = s_ref.shape[1]
    cols = count * HALF
    e = jnp.transpose(jnp.concatenate([e, jnp.zeros((wide - count, rows), F32)], axis=0))
    e_hi = e.astype(BF16)
    e_lo = (e - e_hi.astype(F32)).astype(BF16)
    gi = lax.broadcasted_iota(jnp.int32, (rows, rows), 0)
    gj = lax.broadcasted_iota(jnp.int32, (rows, rows), 1)
    group = jnp.where(jnp.bitwise_xor(gi, gj) < HALF, 1.0, 0.0).astype(BF16)
    coef = dot(jnp.concatenate([group, group], axis=1), jnp.concatenate([e_hi, e_lo], axis=0))
    w = (coef * s_ref[...]).astype(BF16)
    pi = lax.broadcasted_iota(jnp.int32, (wide, cols), 0)
    pj = lax.broadcasted_iota(jnp.int32, (wide, cols), 1)
    ahead = pj - pi * HALF
    repeat = jnp.where(jnp.logical_and(ahead >= 0, ahead < HALF), 1.0, 0.0).astype(BF16)
    weights = (dot(w, repeat) * same_cell(rows, cols)).astype(BF16)
    w_ref[...] = weights
    for q in range(reach):
        here = plane_rows(q, ny)
        block = spread(weights, table_ref[q], nz) + ahead_ref[:, here]
        next_ref[:, here] = block.astype(BF16)


def near_kernel(
    planes, first_ref, psi_ref, prev_ref, pot_ref, w_ref, upper_ref, proj_ref, out_ref
):
    bands, cells, nz = psi_ref.shape
    ny = cells // planes
    weights = w_ref[...]
    starts = box_starts(first_ref, proj_ref.shape[0], planes)
    cz_hi, cz_lo = circulant(nz, 1)
    cz = (jnp.concatenate([cz_hi, cz_hi], axis=0), cz_lo)
    cy = circulant(ny, bands // 2)
    for x in range(planes):
        here = plane_rows(x, ny)
        psi = psi_ref[:, here]
        total = yz_part(psi, cz, cy) + spread(weights, plane_table(proj_ref, starts, x), nz)
        site = outer * pot_ref[here] + (kinetic_weights[0] - outer * center)
        total = total + site[None] * psi - prev_ref[:, here]
        for m in range(1, HALO + 1):
            for target in (x + m, x - m):
                if 0 <= target < planes:
                    total = total + kinetic_weights[m] * psi_ref[:, plane_rows(target, ny)]
                elif target >= planes:
                    value = upper_ref[:, plane_rows(target - planes, ny)].astype(F32)
                    total = total + kinetic_weights[m] * value
        out_ref[:, here] = total


def complete(g_ref, arrived_ref, below_ref, out_ref):
    cut = arrived_ref.shape[1]
    out_ref[:, :cut] = (g_ref[:, :cut] + arrived_ref[...].astype(F32)).astype(out_ref.dtype)
    edge = kinetic_weights[HALO] * below_ref[...].astype(F32)
    out_ref[:, cut:] = (g_ref[:, cut:] + edge).astype(out_ref.dtype)


def finish_kernel(count, g_ref, arrived_ref, below_ref, *rest):
    outs, total = rest[:-1], rest[-1]
    complete(g_ref, arrived_ref, below_ref, total)
    rows = g_ref.shape[1] // count
    pieces_of(total, lax.axis_index("band"), count, rows, outs)


def output_kernel(g_ref, arrived_ref, below_ref, *rest):
    pieces, (out_ref, panel_ref) = rest[:-2], rest[-2:]
    complete(g_ref, arrived_ref, below_ref, out_ref)
    bands = g_ref.shape[0]
    for p, piece in enumerate(reversed(pieces)):
        panel_ref[p * bands : (p + 1) * bands] = piece[...]


def split_kernel(n_space, n_band, prod_ref, out_ref, held, pair):
    bands = prod_ref.shape[0] // n_band
    me = lax.axis_index("band")
    for p, bits in enumerate(partners(n_band)):
        begin = pl.multiple_of(jnp.bitwise_xor(me, bits) * bands, 8)
        held[pl.ds(begin, bands), :] = prod_ref[p * bands : (p + 1) * bands]
    rows = held.shape[0] // n_space
    for p, bits in enumerate(partners(n_band)):
        cols = [slice((h * n_band + p) * bands, (h * n_band + p + 1) * bands) for h in (0, 1)]
        pair[p] = jnp.concatenate([held[:, c] for c in cols], axis=1)
        owner = jnp.bitwise_xor(me, bits)
        lines = [pair[p, pl.ds(r, n_space, stride=rows), :] for r in range(rows)]
        packed = jnp.concatenate(lines, axis=1)
        for i in range(n_space):
            out_ref[i * n_band + owner] = packed[i : i + 1]


def last_kernel(got_ref, margin_ref, projection_ref):
    total = got_ref[...].sum(axis=0)
    rows, bands = margin_ref.shape
    for r in range(rows):
        begin = 2 * r * bands
        margin_ref[r : r + 1] = total[:, begin : begin + bands]
        projection_ref[r : r + 1] = total[:, begin + bands : begin + 2 * bands]


def cyclic(value, axis, steps):
    count = lax.axis_size(axis)
    return lax.ppermute(value, axis, [(i, (i + steps) % count) for i in range(count)])


def mirrored(value, axis, bits):
    count = lax.axis_size(axis)
    return lax.ppermute(value, axis, [(i, i ^ bits) for i in range(count)])


def exchanged(pieces):
    offsets = partners(len(pieces))
    return [mirrored(p, "band", bits) if bits else p for bits, p in zip(offsets, pieces)]


def struct(shape, kind=F32):
    return jax.ShapeDtypeStruct(shape, kind)


def call(kernel, name, out_shape, args, vmem=48, **extra):
    return pl.pallas_call(
        kernel, out_shape=out_shape, compiler_params=params(vmem * 2**20), name=name, **extra
    )(*args)


def shards(orbitals, previous, potential, projectors, strengths, atom_planes):
    bands, planes, ny, nz = orbitals.shape
    n_space = lax.axis_size("space")
    n_band = lax.axis_size("band")
    cells = planes * ny
    whole = (bands, cells, nz)
    quarter = (bands, cells // n_band, nz)
    psi = orbitals.reshape(whole)
    prev = previous.reshape(whole)
    pot = potential.reshape(cells, nz)

    vm = pl.BlockSpec(memory_space=pltpu.VMEM)
    sm = pl.BlockSpec(memory_space=pltpu.SMEM)
    anywhere = pl.BlockSpec(memory_space=pl.ANY)

    most = (bands, (planes - 1) * ny, nz)
    plane = (bands, ny, nz)
    half = call(cast_kernel, "cast", struct(whole, BF16), (psi,))
    panel = call(
        partial(pieces_kernel, n_band),
        "pieces",
        (struct(quarter, BF16),) * n_band,
        (psi,),
        cost_estimate=pl.CostEstimate(flops=10**9, bytes_accessed=2**20, transcendentals=0),
    )
    upper = cyclic(half, "space", -1)
    panel = exchanged(panel)
    atoms, npj = projectors.shape[:2]
    cols = atoms * npj * HALF
    far_tables, e, s = call(
        partial(prepare_kernel, planes),
        "prepare",
        (
            struct((BOX - 1, cols, ny // HALF * nz), BF16),
            struct((atoms * npj, bands * HALF)),
            struct((1, nz)),
        ),
        (atom_planes, strengths.T, half, projectors),
        in_specs=[sm, sm, vm, vm],
        out_specs=(vm,) * 3,
        cost_estimate=pl.CostEstimate(flops=10**9, bytes_accessed=2**20, transcendentals=0),
    )
    ahead, edge = call(
        partial(ahead_kernel, planes),
        "ahead",
        (struct(most), struct(plane, BF16)),
        (psi, panel[3], s),
        in_specs=[vm, anywhere, anywhere],
        out_specs=(vm, vm),
        cost_estimate=pl.CostEstimate(flops=10**9, bytes_accessed=2**20, transcendentals=0),
    )
    below = cyclic(edge, "space", 1)
    w, beyond = call(
        partial(coefficient_kernel, planes),
        "coefficients",
        (struct((bands * HALF, cols), BF16), struct(most, BF16)),
        (upper, far_tables, e, s, ahead),
        cost_estimate=pl.CostEstimate(flops=10**9, bytes_accessed=2**20, transcendentals=0),
    )
    arrived = cyclic(beyond, "space", 1)
    g = call(
        partial(near_kernel, planes),
        "near_part",
        struct(whole),
        (atom_planes, psi, prev, pot, w, upper, projectors),
        in_specs=[sm] + [vm] * 6,
        out_specs=vm,
        cost_estimate=pl.CostEstimate(flops=2*10**10, bytes_accessed=4 * 2**20, transcendentals=0),
    )
    mine = call(
        partial(finish_kernel, n_band),
        "finish",
        (struct(quarter, BF16),) * n_band,
        (g, arrived, below),
        scratch_shapes=[pltpu.VMEM(whole, F32)],
    )
    mine = exchanged(mine)
    total_bands = n_band * bands
    filtered, panels = call(
        output_kernel,
        "output",
        (struct(whole, BF16), struct((total_bands, *quarter[1:]), BF16)),
        (g, arrived, below, *reversed(panel)),
    )
    left = jnp.concatenate(mine, axis=0).reshape(total_bands, -1)
    right = jnp.concatenate([left, panels.reshape(total_bands, -1)], axis=0)
    products = dot(left, right, ((1,), (1,))) * (1.0 / (cells * n_space * nz))
    out_rows = total_bands // n_space
    pieces = call(
        partial(split_kernel, n_space, n_band),
        "split",
        struct((n_space * n_band, 1, out_rows * 2 * bands)),
        (products,),
        scratch_shapes=[
            pltpu.VMEM(products.shape, F32),
            pltpu.VMEM((n_band, total_bands, 2 * bands), F32),
        ],
    )
    got = lax.all_to_all(pieces, ("space", "band"), 0, 0)
    margin, projection = call(
        last_kernel, "last_sum", (struct((out_rows, bands)), struct((out_rows, bands))), (got,)
    )
    return filtered.reshape(orbitals.shape), margin, projection


def solution(mesh):
    in_specs = (
        P("band", "space", None, None),
        P("band", "space", None, None),
        P("space", None, None),
        P("space", None, None, None, None),
        P(),
        P(),
    )
    out_specs = (P("band", "space", None, None), P("space", "band"), P("space", "band"))
    return jax.shard_map(shards, mesh=mesh, in_specs=in_specs, out_specs=out_specs, check_vma=False)
```

```python
from functools import partial

import jax
import jax.numpy as jnp
from jax import lax
from jax.experimental import pallas as pl
from jax.experimental.pallas import tpu as pltpu
from jax.sharding import PartitionSpec as P

HALO = 6
BOX = 6
NPJ = 9
HALF = 16

stencil_weights = (
    -5369.0 / 1800.0,
    12.0 / 7.0,
    -15.0 / 56.0,
    10.0 / 189.0,
    -1.0 / 112.0,
    2.0 / 1925.0,
    -1.0 / 16632.0,
)
center = 5.5
halfwidth = 5.5
outer = 2.0 / halfwidth
kinetic_weights = [-0.5 * outer * w for w in stencil_weights]

F32 = jnp.float32
BF16 = jnp.bfloat16


def params(vmem):
    return pltpu.CompilerParams(vmem_limit_bytes=vmem)


def circulant(n, blocks):
    size = n * blocks
    row = lax.broadcasted_iota(jnp.int32, (size, size), 0)
    col = lax.broadcasted_iota(jnp.int32, (size, size), 1)
    ahead = jnp.bitwise_and(col - row, n - 1)
    reach = jnp.minimum(ahead, n - ahead)
    value = jnp.zeros((size, size), F32)
    for m, weight in enumerate(kinetic_weights):
        value = jnp.where(reach == m, weight, value)
    value = jnp.where(jnp.bitwise_xor(row, col) < n, value, 0.0)
    hi = value.astype(BF16)
    return hi, (value - hi.astype(F32)).astype(BF16)


def dot(a, b, dims=((1,), (0,))):
    return lax.dot_general(a, b, (dims, ((), ())), preferred_element_type=F32)


def plane_rows(x, ny):
    return slice(x * ny, (x + 1) * ny)


def partners(count):
    return [0, *reversed(range(1, count))]


def pieces_of(ref, index, count, rows, outs):
    for bits, out in zip(partners(count), outs):
        quarter = jnp.bitwise_xor(index, bits)
        begin = pl.multiple_of(quarter * rows, 8)
        out[...] = ref[:, pl.ds(begin, rows), :].astype(out.dtype)


def cast_kernel(psi_ref, half_ref):
    half_ref[...] = psi_ref[...].astype(BF16)


def pieces_kernel(count, psi_ref, *outs):
    rows = psi_ref.shape[1] // count
    pieces_of(psi_ref, lax.axis_index("band"), count, rows, outs)


def yz_part(psi, cz, cy):
    bands, ny, nz = psi.shape
    flat = psi.reshape(bands * ny, nz)
    hi = flat.astype(BF16)
    lo = (flat - hi.astype(F32)).astype(BF16)
    both = jnp.concatenate([hi, lo], axis=1)
    along_z = dot(both, cz[0]) + dot(hi, cz[1])
    size = cy[0].shape[0]
    along_y = []
    for begin in range(0, bands * ny, size):
        pair = dot(cy[0], both[begin : begin + size])
        along_y.append(pair[:, :nz] + pair[:, nz:] + dot(cy[1], hi[begin : begin + size]))
    return (along_z + jnp.concatenate(along_y, axis=0)).reshape(bands, ny, nz)


def same_cell(rows, cols):
    row = lax.broadcasted_iota(jnp.int32, (rows, cols), 0)
    col = lax.broadcasted_iota(jnp.int32, (rows, cols), 1)
    return jnp.where(jnp.bitwise_and(row - col, HALF - 1) == 0, 1.0, 0.0).astype(F32)


def table(proj_ref, a, p):
    npj, ny, nz = proj_ref.shape[1], proj_ref.shape[3], proj_ref.shape[4]
    halves = [
        proj_ref[a, :, p, h * HALF : (h + 1) * HALF, :].reshape(npj * HALF, nz)
        for h in range(ny // HALF)
    ]
    return jnp.concatenate(halves, axis=1)


def halves_along(value, axis):
    bands, ny, nz = value.shape
    parts = [value[:, h * HALF : (h + 1) * HALF].reshape(bands * HALF, nz) for h in range(ny // HALF)]
    return jnp.concatenate(parts, axis=axis)


def spread(weights, tables, nz):
    total = dot(weights, tables)
    rows = total.shape[0]
    halves = [
        total[:, h * nz : (h + 1) * nz].reshape(rows // HALF, HALF, nz)
        for h in range(total.shape[1] // nz)
    ]
    return jnp.concatenate(halves, axis=1)


def plane_table(proj_ref, starts, q):
    parts = []
    for a, start in enumerate(starts):
        p = q - start
        inside = jnp.logical_and(p >= 0, p < BOX)
        part = table(proj_ref, a, jnp.clip(p, 0, BOX - 1))
        parts.append(part * jnp.where(inside, 1.0, 0.0).astype(BF16))
    return jnp.concatenate(parts, axis=0)


def box_starts(first_ref, atoms, planes):
    me = lax.axis_index("space")
    return [first_ref[me * atoms + a] - me * planes for a in range(atoms)]


def overlap(field_ref, tables, ny):
    bands = field_ref.shape[0]
    left = [halves_along(field_ref[:, plane_rows(x, ny)], 1) for x in range(len(tables))]
    d = dot(jnp.concatenate(left, axis=1), jnp.concatenate(tables, axis=1), ((1,), (1,)))
    rows, cols = d.shape
    return (d * same_cell(rows, cols)).reshape(bands, HALF, cols).sum(axis=1)


def prepare_kernel(planes, first_ref, strength_ref, own_ref, proj_ref, far_ref, e_ref, s_ref):
    ny = own_ref.shape[1] // planes
    atoms, npj = proj_ref.shape[:2]
    me = lax.axis_index("space")
    starts = box_starts(first_ref, atoms, planes)
    for q in range(BOX - 1):
        far_ref[q] = plane_table(proj_ref, starts, planes + q)
    owner = lax.broadcasted_iota(jnp.int32, s_ref.shape, 1)
    scale = jnp.zeros(s_ref.shape, F32)
    for a in range(atoms):
        for j in range(npj):
            value = outer * strength_ref[j, me * atoms + a]
            scale = jnp.where(owner >= (a * npj + j) * HALF, value, scale)
    s_ref[...] = scale
    e_ref[...] = overlap(own_ref, [plane_table(proj_ref, starts, q) for q in range(planes)], ny)


def ahead_kernel(planes, psi_ref, ahead_ref, edge_ref):
    ny = psi_ref.shape[1] // planes
    edge_ref[...] = psi_ref[:, plane_rows(planes - 1, ny)].astype(BF16)
    for x in range(planes - 1):
        total = None
        for m in range(x + 1, HALO + 1):
            term = kinetic_weights[m] * psi_ref[:, plane_rows(planes + x - m, ny)]
            total = term if total is None else total + term
        ahead_ref[:, plane_rows(x, ny)] = total


def coefficient_kernel(planes, upper_ref, table_ref, e_ref, s_ref, ahead_ref, w_ref, next_ref):
    bands, cells, nz = upper_ref.shape
    ny = cells // planes
    reach = BOX - 1
    e = e_ref[...] + overlap(upper_ref, [table_ref[q] for q in range(reach)], ny)
    cols = e.shape[1]
    tiles = -(-cols // nz)
    e = jnp.concatenate([e, jnp.zeros((bands, tiles * nz - cols), F32)], axis=1)
    e = jnp.concatenate([e[:, t * nz : (t + 1) * nz] for t in range(tiles)], axis=0)
    gi = lax.broadcasted_iota(jnp.int32, (nz, nz), 0)
    gj = lax.broadcasted_iota(jnp.int32, (nz, nz), 1)
    group = jnp.where(jnp.bitwise_xor(gi, gj) < HALF, 1.0, 0.0).astype(BF16)
    e_hi = e.astype(BF16)
    e_lo = (e - e_hi.astype(F32)).astype(BF16)
    coef = dot(jnp.concatenate([e_hi, e_lo], axis=1), jnp.concatenate([group, group], axis=0))
    coef = jnp.concatenate([coef[t * bands : (t + 1) * bands] for t in range(tiles)], axis=1)
    w = coef[:, :cols] * s_ref[...]
    rows = bands * HALF
    full = jnp.broadcast_to(w[:, None, :], (bands, HALF, cols)).reshape(rows, cols)
    weights = (full * same_cell(rows, cols)).astype(BF16)
    w_ref[...] = weights
    for q in range(reach):
        here = plane_rows(q, ny)
        block = spread(weights, table_ref[q], nz) + ahead_ref[:, here]
        next_ref[:, here] = block.astype(BF16)


def near_kernel(planes, unused, first_ref, *refs):
    psi_ref, prev_ref, pot_ref, w_ref, upper_ref, proj_ref, out_ref = refs[unused:]
    bands, cells, nz = psi_ref.shape
    ny = cells // planes
    weights = w_ref[...]
    starts = box_starts(first_ref, proj_ref.shape[0], planes)
    cz_hi, cz_lo = circulant(nz, 1)
    cz = (jnp.concatenate([cz_hi, cz_hi], axis=0), cz_lo)
    cy = circulant(ny, bands // 2)
    for x in range(planes):
        here = plane_rows(x, ny)
        psi = psi_ref[:, here]
        total = yz_part(psi, cz, cy) + spread(weights, plane_table(proj_ref, starts, x), nz)
        site = outer * pot_ref[here] + (kinetic_weights[0] - outer * center)
        total = total + site[None] * psi - prev_ref[:, here]
        for m in range(1, HALO + 1):
            for target in (x + m, x - m):
                if 0 <= target < planes:
                    total = total + kinetic_weights[m] * psi_ref[:, plane_rows(target, ny)]
                elif target >= planes:
                    value = upper_ref[:, plane_rows(target - planes, ny)].astype(F32)
                    total = total + kinetic_weights[m] * value
        out_ref[:, here] = total


def complete(g_ref, arrived_ref, below_ref, out_ref):
    cut = arrived_ref.shape[1]
    out_ref[:, :cut] = (g_ref[:, :cut] + arrived_ref[...].astype(F32)).astype(out_ref.dtype)
    edge = kinetic_weights[HALO] * below_ref[...].astype(F32)
    out_ref[:, cut:] = (g_ref[:, cut:] + edge).astype(out_ref.dtype)


def finish_kernel(count, g_ref, arrived_ref, below_ref, *rest):
    outs, total = rest[:-1], rest[-1]
    complete(g_ref, arrived_ref, below_ref, total)
    rows = g_ref.shape[1] // count
    pieces_of(total, lax.axis_index("band"), count, rows, outs)


def panel_order(count):
    return [*range(1, count), 0]


def output_kernel(g_ref, arrived_ref, below_ref, *rest):
    pieces, (out_ref, panel_ref) = rest[:-2], rest[-2:]
    complete(g_ref, arrived_ref, below_ref, out_ref)
    bands = g_ref.shape[0]
    for p, piece in zip(panel_order(len(pieces)), pieces):
        panel_ref[p * bands : (p + 1) * bands] = piece[...]


def split_kernel(n_space, n_band, prod_ref, out_ref, held, pair):
    bands = prod_ref.shape[0] // n_band
    me = lax.axis_index("band")
    for p, bits in enumerate(partners(n_band)):
        begin = pl.multiple_of(jnp.bitwise_xor(me, bits) * bands, 8)
        held[pl.ds(begin, bands), :] = prod_ref[p * bands : (p + 1) * bands]
    rows = held.shape[0] // n_space
    for p, bits in enumerate(partners(n_band)):
        cols = [slice((h * n_band + p) * bands, (h * n_band + p + 1) * bands) for h in (0, 1)]
        pair[p] = jnp.concatenate([held[:, c] for c in cols], axis=1)
        owner = jnp.bitwise_xor(me, bits)
        lines = [pair[p, pl.ds(r, n_space, stride=rows), :] for r in range(rows)]
        packed = jnp.concatenate(lines, axis=1)
        for i in range(n_space):
            out_ref[i * n_band + owner] = packed[i : i + 1]


def last_kernel(got_ref, margin_ref, projection_ref):
    total = got_ref[...].sum(axis=0)
    rows, bands = margin_ref.shape
    for r in range(rows):
        begin = 2 * r * bands
        margin_ref[r : r + 1] = total[:, begin : begin + bands]
        projection_ref[r : r + 1] = total[:, begin + bands : begin + 2 * bands]


def cyclic(value, axis, steps):
    count = lax.axis_size(axis)
    return lax.ppermute(value, axis, [(i, (i + steps) % count) for i in range(count)])


def mirrored(value, axis, bits):
    count = lax.axis_size(axis)
    return lax.ppermute(value, axis, [(i, i ^ bits) for i in range(count)])


def exchanged(pieces):
    offsets = partners(len(pieces))
    return [mirrored(p, "band", bits) if bits else p for bits, p in zip(offsets, pieces)]


def struct(shape, kind=F32):
    return jax.ShapeDtypeStruct(shape, kind)


def call(kernel, name, out_shape, args, vmem=48, **extra):
    return pl.pallas_call(
        kernel, out_shape=out_shape, compiler_params=params(vmem * 2**20), name=name, **extra
    )(*args)


def shards(orbitals, previous, potential, projectors, strengths, atom_planes):
    bands, planes, ny, nz = orbitals.shape
    n_space = lax.axis_size("space")
    n_band = lax.axis_size("band")
    cells = planes * ny
    whole = (bands, cells, nz)
    quarter = (bands, cells // n_band, nz)
    psi = orbitals.reshape(whole)
    prev = previous.reshape(whole)
    pot = potential.reshape(cells, nz)

    vm = pl.BlockSpec(memory_space=pltpu.VMEM)
    sm = pl.BlockSpec(memory_space=pltpu.SMEM)
    anywhere = pl.BlockSpec(memory_space=pl.ANY)

    most = (bands, (planes - 1) * ny, nz)
    plane = (bands, ny, nz)
    half = call(cast_kernel, "cast", struct(whole, BF16), (psi,))
    panel = call(
        partial(pieces_kernel, n_band),
        "pieces",
        (struct(quarter, BF16),) * n_band,
        (psi,),
        cost_estimate=pl.CostEstimate(flops=10**9, bytes_accessed=2**20, transcendentals=0),
    )
    upper = cyclic(half, "space", -1)
    panel = exchanged(panel)
    ahead, edge = call(
        partial(ahead_kernel, planes),
        "ahead",
        (struct(most), struct(plane, BF16)),
        (psi,),
        cost_estimate=pl.CostEstimate(flops=10**9, bytes_accessed=2**20, transcendentals=0),
    )
    below = cyclic(edge, "space", 1)
    atoms, npj = projectors.shape[:2]
    cols = atoms * npj * HALF
    far_tables, e, s = call(
        partial(prepare_kernel, planes),
        "prepare",
        (
            struct((BOX - 1, cols, ny // HALF * nz), BF16),
            struct((bands, cols)),
            struct((1, cols)),
        ),
        (atom_planes, strengths.T, half, projectors),
        in_specs=[sm, sm, vm, vm],
        out_specs=(vm,) * 3,
        cost_estimate=pl.CostEstimate(flops=10**9, bytes_accessed=2**20, transcendentals=0),
    )
    w, beyond = call(
        partial(coefficient_kernel, planes),
        "coefficients",
        (struct((bands * HALF, cols), BF16), struct(most, BF16)),
        (upper, far_tables, e, s, ahead),
        cost_estimate=pl.CostEstimate(flops=10**9, bytes_accessed=2**20, transcendentals=0),
    )
    arrived = cyclic(beyond, "space", 1)
    g = call(
        partial(near_kernel, planes, 1),
        "near_part",
        struct(whole),
        (atom_planes, panel[1], psi, prev, pot, w, upper, projectors),
        in_specs=[sm] + [anywhere] * 1 + [vm] * 6,
        out_specs=vm,
        cost_estimate=pl.CostEstimate(flops=2*10**10, bytes_accessed=4 * 2**20, transcendentals=0),
    )
    mine = call(
        partial(finish_kernel, n_band),
        "finish",
        (struct(quarter, BF16),) * n_band,
        (g, arrived, below),
        scratch_shapes=[pltpu.VMEM(whole, F32)],
    )
    mine = exchanged(mine)
    total_bands = n_band * bands
    filtered, panels = call(
        output_kernel,
        "output",
        (struct(whole, BF16), struct((total_bands, *quarter[1:]), BF16)),
        (g, arrived, below, *[panel[p] for p in panel_order(n_band)]),
    )
    left = jnp.concatenate(mine, axis=0).reshape(total_bands, -1)
    right = jnp.concatenate([left, panels.reshape(total_bands, -1)], axis=0)
    products = dot(left, right, ((1,), (1,))) * (1.0 / (cells * n_space * nz))
    out_rows = total_bands // n_space
    pieces = call(
        partial(split_kernel, n_space, n_band),
        "split",
        struct((n_space * n_band, 1, out_rows * 2 * bands)),
        (products,),
        scratch_shapes=[
            pltpu.VMEM(products.shape, F32),
            pltpu.VMEM((n_band, total_bands, 2 * bands), F32),
        ],
    )
    got = lax.all_to_all(pieces, ("space", "band"), 0, 0)
    margin, projection = call(
        last_kernel, "last_sum", (struct((out_rows, bands)), struct((out_rows, bands))), (got,)
    )
    return filtered.reshape(orbitals.shape), margin, projection


def solution(mesh):
    in_specs = (
        P("band", "space", None, None),
        P("band", "space", None, None),
        P("space", None, None),
        P("space", None, None, None, None),
        P(),
        P(),
    )
    out_specs = (P("band", "space", None, None), P("space", "band"), P("space", "band"))
    return jax.shard_map(shards, mesh=mesh, in_specs=in_specs, out_specs=out_specs, check_vma=False)
```

```python
from functools import partial

import jax
import jax.numpy as jnp
from jax import lax
from jax.experimental import pallas as pl
from jax.experimental.pallas import tpu as pltpu
from jax.sharding import PartitionSpec as P

HALO = 6
BOX = 6
NPJ = 9
HALF = 16

stencil_weights = (
    -5369.0 / 1800.0,
    12.0 / 7.0,
    -15.0 / 56.0,
    10.0 / 189.0,
    -1.0 / 112.0,
    2.0 / 1925.0,
    -1.0 / 16632.0,
)
center = 5.5
halfwidth = 5.5
outer = 2.0 / halfwidth
kinetic_weights = [-0.5 * outer * w for w in stencil_weights]

F32 = jnp.float32
BF16 = jnp.bfloat16


def params(vmem):
    return pltpu.CompilerParams(vmem_limit_bytes=vmem)


def circulant(n, blocks):
    size = n * blocks
    row = lax.broadcasted_iota(jnp.int32, (size, size), 0)
    col = lax.broadcasted_iota(jnp.int32, (size, size), 1)
    ahead = jnp.bitwise_and(col - row, n - 1)
    reach = jnp.minimum(ahead, n - ahead)
    value = jnp.zeros((size, size), F32)
    for m, weight in enumerate(kinetic_weights):
        value = jnp.where(reach == m, weight, value)
    value = jnp.where(jnp.bitwise_xor(row, col) < n, value, 0.0)
    hi = value.astype(BF16)
    return hi, (value - hi.astype(F32)).astype(BF16)


def dot(a, b, dims=((1,), (0,))):
    return lax.dot_general(a, b, (dims, ((), ())), preferred_element_type=F32)


def plane_rows(x, ny):
    return slice(x * ny, (x + 1) * ny)


def partners(count):
    return [0, *range(count // 2, count), *range(1, count // 2)]


def pieces_of(ref, index, count, rows, outs):
    for bits, out in zip(partners(count), outs):
        quarter = jnp.bitwise_xor(index, bits)
        begin = pl.multiple_of(quarter * rows, 8)
        out[...] = ref[:, pl.ds(begin, rows), :].astype(out.dtype)


def cast_kernel(psi_ref, half_ref):
    half_ref[...] = psi_ref[...].astype(BF16)


def pieces_kernel(count, psi_ref, *outs):
    rows = psi_ref.shape[1] // count
    pieces_of(psi_ref, lax.axis_index("band"), count, rows, outs)


def yz_part(psi, cz, cy):
    bands, ny, nz = psi.shape
    flat = psi.reshape(bands * ny, nz)
    hi = flat.astype(BF16)
    lo = (flat - hi.astype(F32)).astype(BF16)
    both = jnp.concatenate([hi, lo], axis=1)
    along_z = dot(both, cz[0]) + dot(hi, cz[1])
    size = cy[0].shape[0]
    along_y = []
    for begin in range(0, bands * ny, size):
        pair = dot(cy[0], both[begin : begin + size])
        along_y.append(pair[:, :nz] + pair[:, nz:] + dot(cy[1], hi[begin : begin + size]))
    return (along_z + jnp.concatenate(along_y, axis=0)).reshape(bands, ny, nz)


def same_cell(rows, cols):
    row = lax.broadcasted_iota(jnp.int32, (rows, cols), 0)
    col = lax.broadcasted_iota(jnp.int32, (rows, cols), 1)
    return jnp.where(jnp.bitwise_and(row - col, HALF - 1) == 0, 1.0, 0.0).astype(F32)


def table(proj_ref, a, p):
    npj, ny, nz = proj_ref.shape[1], proj_ref.shape[3], proj_ref.shape[4]
    halves = [
        proj_ref[a, :, p, h * HALF : (h + 1) * HALF, :].reshape(npj * HALF, nz)
        for h in range(ny // HALF)
    ]
    return jnp.concatenate(halves, axis=1)


def halves_along(value, axis):
    bands, ny, nz = value.shape
    parts = [value[:, h * HALF : (h + 1) * HALF].reshape(bands * HALF, nz) for h in range(ny // HALF)]
    return jnp.concatenate(parts, axis=axis)


def spread(weights, tables, nz):
    total = dot(weights, tables)
    rows = total.shape[0]
    halves = [
        total[:, h * nz : (h + 1) * nz].reshape(rows // HALF, HALF, nz)
        for h in range(total.shape[1] // nz)
    ]
    return jnp.concatenate(halves, axis=1)


def plane_table(proj_ref, starts, q):
    parts = []
    for a, start in enumerate(starts):
        p = q - start
        inside = jnp.logical_and(p >= 0, p < BOX)
        part = table(proj_ref, a, jnp.clip(p, 0, BOX - 1))
        parts.append(part * jnp.where(inside, 1.0, 0.0).astype(BF16))
    return jnp.concatenate(parts, axis=0)


def box_starts(first_ref, atoms, planes):
    me = lax.axis_index("space")
    return [first_ref[me * atoms + a] - me * planes for a in range(atoms)]


def overlap(field_ref, tables, ny):
    bands = field_ref.shape[0]
    left = [halves_along(field_ref[:, plane_rows(x, ny)], 1) for x in range(len(tables))]
    d = dot(jnp.concatenate(left, axis=1), jnp.concatenate(tables, axis=1), ((1,), (1,)))
    rows, cols = d.shape
    return (d * same_cell(rows, cols)).reshape(bands, HALF, cols).sum(axis=1)


def prepare_kernel(planes, first_ref, strength_ref, own_ref, proj_ref, far_ref, e_ref, s_ref):
    ny = own_ref.shape[1] // planes
    atoms, npj = proj_ref.shape[:2]
    me = lax.axis_index("space")
    starts = box_starts(first_ref, atoms, planes)
    for q in range(BOX - 1):
        far_ref[q] = plane_table(proj_ref, starts, planes + q)
    owner = lax.broadcasted_iota(jnp.int32, s_ref.shape, 1)
    scale = jnp.zeros(s_ref.shape, F32)
    for a in range(atoms):
        for j in range(npj):
            value = outer * strength_ref[j, me * atoms + a]
            scale = jnp.where(owner >= (a * npj + j) * HALF, value, scale)
    s_ref[...] = scale
    e_ref[...] = overlap(own_ref, [plane_table(proj_ref, starts, q) for q in range(planes)], ny)


def ahead_kernel(planes, psi_ref, *refs):
    ahead_ref, edge_ref = refs[-2:]
    ny = psi_ref.shape[1] // planes
    edge_ref[...] = psi_ref[:, plane_rows(planes - 1, ny)].astype(BF16)
    for x in range(planes - 1):
        total = None
        for m in range(x + 1, HALO + 1):
            term = kinetic_weights[m] * psi_ref[:, plane_rows(planes + x - m, ny)]
            total = term if total is None else total + term
        ahead_ref[:, plane_rows(x, ny)] = total


def coefficient_kernel(planes, upper_ref, table_ref, e_ref, s_ref, ahead_ref, w_ref, next_ref):
    bands, cells, nz = upper_ref.shape
    ny = cells // planes
    reach = BOX - 1
    e = e_ref[...] + overlap(upper_ref, [table_ref[q] for q in range(reach)], ny)
    cols = e.shape[1]
    tiles = -(-cols // nz)
    e = jnp.concatenate([e, jnp.zeros((bands, tiles * nz - cols), F32)], axis=1)
    e = jnp.concatenate([e[:, t * nz : (t + 1) * nz] for t in range(tiles)], axis=0)
    gi = lax.broadcasted_iota(jnp.int32, (nz, nz), 0)
    gj = lax.broadcasted_iota(jnp.int32, (nz, nz), 1)
    group = jnp.where(jnp.bitwise_xor(gi, gj) < HALF, 1.0, 0.0).astype(BF16)
    e_hi = e.astype(BF16)
    e_lo = (e - e_hi.astype(F32)).astype(BF16)
    coef = dot(jnp.concatenate([e_hi, e_lo], axis=1), jnp.concatenate([group, group], axis=0))
    coef = jnp.concatenate([coef[t * bands : (t + 1) * bands] for t in range(tiles)], axis=1)
    w = coef[:, :cols] * s_ref[...]
    rows = bands * HALF
    full = jnp.broadcast_to(w[:, None, :], (bands, HALF, cols)).reshape(rows, cols)
    weights = (full * same_cell(rows, cols)).astype(BF16)
    w_ref[...] = weights
    for q in range(reach):
        here = plane_rows(q, ny)
        block = spread(weights, table_ref[q], nz) + ahead_ref[:, here]
        next_ref[:, here] = block.astype(BF16)


def near_kernel(
    planes, first_ref, psi_ref, prev_ref, pot_ref, w_ref, upper_ref, proj_ref, out_ref
):
    bands, cells, nz = psi_ref.shape
    ny = cells // planes
    weights = w_ref[...]
    starts = box_starts(first_ref, proj_ref.shape[0], planes)
    cz_hi, cz_lo = circulant(nz, 1)
    cz = (jnp.concatenate([cz_hi, cz_hi], axis=0), cz_lo)
    cy = circulant(ny, bands // 2)
    for x in range(planes):
        here = plane_rows(x, ny)
        psi = psi_ref[:, here]
        total = yz_part(psi, cz, cy) + spread(weights, plane_table(proj_ref, starts, x), nz)
        site = outer * pot_ref[here] + (kinetic_weights[0] - outer * center)
        total = total + site[None] * psi - prev_ref[:, here]
        for m in range(1, HALO + 1):
            for target in (x + m, x - m):
                if 0 <= target < planes:
                    total = total + kinetic_weights[m] * psi_ref[:, plane_rows(target, ny)]
                elif target >= planes:
                    value = upper_ref[:, plane_rows(target - planes, ny)].astype(F32)
                    total = total + kinetic_weights[m] * value
        out_ref[:, here] = total


def complete(g_ref, arrived_ref, below_ref, out_ref):
    cut = arrived_ref.shape[1]
    out_ref[:, :cut] = (g_ref[:, :cut] + arrived_ref[...].astype(F32)).astype(out_ref.dtype)
    edge = kinetic_weights[HALO] * below_ref[...].astype(F32)
    out_ref[:, cut:] = (g_ref[:, cut:] + edge).astype(out_ref.dtype)


def finish_kernel(count, g_ref, arrived_ref, below_ref, *rest):
    outs, total = rest[:-1], rest[-1]
    complete(g_ref, arrived_ref, below_ref, total)
    rows = g_ref.shape[1] // count
    pieces_of(total, lax.axis_index("band"), count, rows, outs)


def output_kernel(g_ref, arrived_ref, below_ref, *rest):
    pieces, (out_ref, panel_ref) = rest[:-2], rest[-2:]
    complete(g_ref, arrived_ref, below_ref, out_ref)
    bands = g_ref.shape[0]
    for p, piece in enumerate(reversed(pieces)):
        panel_ref[p * bands : (p + 1) * bands] = piece[...]


def split_kernel(n_space, n_band, prod_ref, out_ref, held, pair):
    bands = prod_ref.shape[0] // n_band
    me = lax.axis_index("band")
    for p, bits in enumerate(partners(n_band)):
        begin = pl.multiple_of(jnp.bitwise_xor(me, bits) * bands, 8)
        held[pl.ds(begin, bands), :] = prod_ref[p * bands : (p + 1) * bands]
    rows = held.shape[0] // n_space
    for p, bits in enumerate(partners(n_band)):
        cols = [slice((h * n_band + p) * bands, (h * n_band + p + 1) * bands) for h in (0, 1)]
        pair[p] = jnp.concatenate([held[:, c] for c in cols], axis=1)
        owner = jnp.bitwise_xor(me, bits)
        lines = [pair[p, pl.ds(r, n_space, stride=rows), :] for r in range(rows)]
        packed = jnp.concatenate(lines, axis=1)
        for i in range(n_space):
            out_ref[i * n_band + owner] = packed[i : i + 1]


def last_kernel(got_ref, margin_ref, projection_ref):
    total = got_ref[...].sum(axis=0)
    rows, bands = margin_ref.shape
    for r in range(rows):
        begin = 2 * r * bands
        margin_ref[r : r + 1] = total[:, begin : begin + bands]
        projection_ref[r : r + 1] = total[:, begin + bands : begin + 2 * bands]


def cyclic(value, axis, steps):
    count = lax.axis_size(axis)
    return lax.ppermute(value, axis, [(i, (i + steps) % count) for i in range(count)])


def mirrored(value, axis, bits):
    count = lax.axis_size(axis)
    return lax.ppermute(value, axis, [(i, i ^ bits) for i in range(count)])


def exchanged(pieces):
    offsets = partners(len(pieces))
    return [mirrored(p, "band", bits) if bits else p for bits, p in zip(offsets, pieces)]


def struct(shape, kind=F32):
    return jax.ShapeDtypeStruct(shape, kind)


def call(kernel, name, out_shape, args, vmem=48, **extra):
    return pl.pallas_call(
        kernel, out_shape=out_shape, compiler_params=params(vmem * 2**20), name=name, **extra
    )(*args)


def shards(orbitals, previous, potential, projectors, strengths, atom_planes):
    bands, planes, ny, nz = orbitals.shape
    n_space = lax.axis_size("space")
    n_band = lax.axis_size("band")
    cells = planes * ny
    whole = (bands, cells, nz)
    quarter = (bands, cells // n_band, nz)
    psi = orbitals.reshape(whole)
    prev = previous.reshape(whole)
    pot = potential.reshape(cells, nz)

    vm = pl.BlockSpec(memory_space=pltpu.VMEM)
    sm = pl.BlockSpec(memory_space=pltpu.SMEM)
    anywhere = pl.BlockSpec(memory_space=pl.ANY)

    most = (bands, (planes - 1) * ny, nz)
    plane = (bands, ny, nz)
    half = call(cast_kernel, "cast", struct(whole, BF16), (psi,))
    panel = call(
        partial(pieces_kernel, n_band),
        "pieces",
        (struct(quarter, BF16),) * n_band,
        (psi,),
        cost_estimate=pl.CostEstimate(flops=10**9, bytes_accessed=2**20, transcendentals=0),
    )
    upper = cyclic(half, "space", -1)
    panel = exchanged(panel)
    atoms, npj = projectors.shape[:2]
    cols = atoms * npj * HALF
    far_tables, e, s = call(
        partial(prepare_kernel, planes),
        "prepare",
        (
            struct((BOX - 1, cols, ny // HALF * nz), BF16),
            struct((bands, cols)),
            struct((1, cols)),
        ),
        (atom_planes, strengths.T, half, projectors),
        in_specs=[sm, sm, vm, vm],
        out_specs=(vm,) * 3,
        cost_estimate=pl.CostEstimate(flops=10**9, bytes_accessed=2**20, transcendentals=0),
    )
    ahead, edge = call(
        partial(ahead_kernel, planes),
        "ahead",
        (struct(most), struct(plane, BF16)),
        (psi, panel[3], s),
        in_specs=[vm, anywhere, anywhere],
        out_specs=(vm, vm),
        cost_estimate=pl.CostEstimate(flops=10**9, bytes_accessed=2**20, transcendentals=0),
    )
    below = cyclic(edge, "space", 1)
    w, beyond = call(
        partial(coefficient_kernel, planes),
        "coefficients",
        (struct((bands * HALF, cols), BF16), struct(most, BF16)),
        (upper, far_tables, e, s, ahead),
        cost_estimate=pl.CostEstimate(flops=10**9, bytes_accessed=2**20, transcendentals=0),
    )
    arrived = cyclic(beyond, "space", 1)
    g = call(
        partial(near_kernel, planes),
        "near_part",
        struct(whole),
        (atom_planes, psi, prev, pot, w, upper, projectors),
        in_specs=[sm] + [vm] * 6,
        out_specs=vm,
        cost_estimate=pl.CostEstimate(flops=2*10**10, bytes_accessed=4 * 2**20, transcendentals=0),
    )
    mine = call(
        partial(finish_kernel, n_band),
        "finish",
        (struct(quarter, BF16),) * n_band,
        (g, arrived, below),
        scratch_shapes=[pltpu.VMEM(whole, F32)],
    )
    mine = exchanged(mine)
    total_bands = n_band * bands
    filtered, panels = call(
        output_kernel,
        "output",
        (struct(whole, BF16), struct((total_bands, *quarter[1:]), BF16)),
        (g, arrived, below, *reversed(panel)),
    )
    left = jnp.concatenate(mine, axis=0).reshape(total_bands, -1)
    right = jnp.concatenate([left, panels.reshape(total_bands, -1)], axis=0)
    products = dot(left, right, ((1,), (1,))) * (1.0 / (cells * n_space * nz))
    out_rows = total_bands // n_space
    pieces = call(
        partial(split_kernel, n_space, n_band),
        "split",
        struct((n_space * n_band, 1, out_rows * 2 * bands)),
        (products,),
        scratch_shapes=[
            pltpu.VMEM(products.shape, F32),
            pltpu.VMEM((n_band, total_bands, 2 * bands), F32),
        ],
    )
    got = lax.all_to_all(pieces, ("space", "band"), 0, 0)
    margin, projection = call(
        last_kernel, "last_sum", (struct((out_rows, bands)), struct((out_rows, bands))), (got,)
    )
    return filtered.reshape(orbitals.shape), margin, projection


def solution(mesh):
    in_specs = (
        P("band", "space", None, None),
        P("band", "space", None, None),
        P("space", None, None),
        P("space", None, None, None, None),
        P(),
        P(),
    )
    out_specs = (P("band", "space", None, None), P("space", "band"), P("space", "band"))
    return jax.shard_map(shards, mesh=mesh, in_specs=in_specs, out_specs=out_specs, check_vma=False)
```

```python
from functools import partial

import jax
import jax.numpy as jnp
from jax import lax
from jax.experimental import pallas as pl
from jax.experimental.pallas import tpu as pltpu
from jax.sharding import PartitionSpec as P

HALO = 6
BOX = 6
NPJ = 9
HALF = 16

stencil_weights = (
    -5369.0 / 1800.0,
    12.0 / 7.0,
    -15.0 / 56.0,
    10.0 / 189.0,
    -1.0 / 112.0,
    2.0 / 1925.0,
    -1.0 / 16632.0,
)
center = 5.5
halfwidth = 5.5
outer = 2.0 / halfwidth
kinetic_weights = [-0.5 * outer * w for w in stencil_weights]

F32 = jnp.float32
BF16 = jnp.bfloat16


def params(vmem):
    return pltpu.CompilerParams(vmem_limit_bytes=vmem)


def circulant(n, blocks):
    size = n * blocks
    row = lax.broadcasted_iota(jnp.int32, (size, size), 0)
    col = lax.broadcasted_iota(jnp.int32, (size, size), 1)
    ahead = jnp.bitwise_and(col - row, n - 1)
    reach = jnp.minimum(ahead, n - ahead)
    value = jnp.zeros((size, size), F32)
    for m, weight in enumerate(kinetic_weights):
        value = jnp.where(reach == m, weight, value)
    value = jnp.where(jnp.bitwise_xor(row, col) < n, value, 0.0)
    hi = value.astype(BF16)
    return hi, (value - hi.astype(F32)).astype(BF16)


def dot(a, b, dims=((1,), (0,))):
    return lax.dot_general(a, b, (dims, ((), ())), preferred_element_type=F32)


def plane_rows(x, ny):
    return slice(x * ny, (x + 1) * ny)


def partners(count):
    return [0, *reversed(range(1, count))]


def pieces_of(ref, index, count, rows, outs):
    for bits, out in zip(partners(count), outs):
        quarter = jnp.bitwise_xor(index, bits)
        begin = pl.multiple_of(quarter * rows, 8)
        out[...] = ref[:, pl.ds(begin, rows), :].astype(out.dtype)


def cast_kernel(psi_ref, half_ref):
    half_ref[...] = psi_ref[...].astype(BF16)


def pieces_kernel(count, psi_ref, *outs):
    rows = psi_ref.shape[1] // count
    pieces_of(psi_ref, lax.axis_index("band"), count, rows, outs)


def yz_part(psi, cz, cy):
    bands, ny, nz = psi.shape
    flat = psi.reshape(bands * ny, nz)
    hi = flat.astype(BF16)
    lo = (flat - hi.astype(F32)).astype(BF16)
    both = jnp.concatenate([hi, lo], axis=1)
    along_z = dot(both, cz[0]) + dot(hi, cz[1])
    size = cy[0].shape[0]
    along_y = []
    for begin in range(0, bands * ny, size):
        pair = dot(cy[0], both[begin : begin + size])
        along_y.append(pair[:, :nz] + pair[:, nz:] + dot(cy[1], hi[begin : begin + size]))
    return (along_z + jnp.concatenate(along_y, axis=0)).reshape(bands, ny, nz)


def same_cell(rows, cols):
    row = lax.broadcasted_iota(jnp.int32, (rows, cols), 0)
    col = lax.broadcasted_iota(jnp.int32, (rows, cols), 1)
    return jnp.where(jnp.bitwise_and(row - col, HALF - 1) == 0, 1.0, 0.0).astype(F32)


def table(proj_ref, a, p):
    npj, ny, nz = proj_ref.shape[1], proj_ref.shape[3], proj_ref.shape[4]
    halves = [
        proj_ref[a, :, p, h * HALF : (h + 1) * HALF, :].reshape(npj * HALF, nz)
        for h in range(ny // HALF)
    ]
    return jnp.concatenate(halves, axis=1)


def halves_along(value, axis):
    bands, ny, nz = value.shape
    parts = [value[:, h * HALF : (h + 1) * HALF].reshape(bands * HALF, nz) for h in range(ny // HALF)]
    return jnp.concatenate(parts, axis=axis)


def spread(weights, tables, nz):
    total = dot(weights, tables)
    rows = total.shape[0]
    halves = [
        total[:, h * nz : (h + 1) * nz].reshape(rows // HALF, HALF, nz)
        for h in range(total.shape[1] // nz)
    ]
    return jnp.concatenate(halves, axis=1)


def plane_table(proj_ref, starts, q):
    parts = []
    for a, start in enumerate(starts):
        p = q - start
        inside = jnp.logical_and(p >= 0, p < BOX)
        part = table(proj_ref, a, jnp.clip(p, 0, BOX - 1))
        parts.append(part * jnp.where(inside, 1.0, 0.0).astype(BF16))
    return jnp.concatenate(parts, axis=0)


def box_starts(first_ref, atoms, planes):
    me = lax.axis_index("space")
    return [first_ref[me * atoms + a] - me * planes for a in range(atoms)]


def overlap(field_ref, tables, ny):
    bands = field_ref.shape[0]
    left = [halves_along(field_ref[:, plane_rows(x, ny)], 1) for x in range(len(tables))]
    d = dot(jnp.concatenate(left, axis=1), jnp.concatenate(tables, axis=1), ((1,), (1,)))
    rows, cols = d.shape
    return (d * same_cell(rows, cols)).reshape(bands, HALF, cols).sum(axis=1)


def prepare_kernel(planes, first_ref, strength_ref, own_ref, proj_ref, far_ref, e_ref, s_ref):
    ny = own_ref.shape[1] // planes
    atoms, npj = proj_ref.shape[:2]
    me = lax.axis_index("space")
    starts = box_starts(first_ref, atoms, planes)
    for q in range(BOX - 1):
        far_ref[q] = plane_table(proj_ref, starts, planes + q)
    owner = lax.broadcasted_iota(jnp.int32, s_ref.shape, 1)
    scale = jnp.zeros(s_ref.shape, F32)
    for a in range(atoms):
        for j in range(npj):
            value = outer * strength_ref[j, me * atoms + a]
            scale = jnp.where(owner >= (a * npj + j) * HALF, value, scale)
    s_ref[...] = scale
    e_ref[...] = overlap(own_ref, [plane_table(proj_ref, starts, q) for q in range(planes)], ny)


def ahead_kernel(planes, psi_ref, *refs):
    ahead_ref, edge_ref = refs[-2:]
    ny = psi_ref.shape[1] // planes
    edge_ref[...] = psi_ref[:, plane_rows(planes - 1, ny)].astype(BF16)
    for x in range(planes - 1):
        total = None
        for m in range(x + 1, HALO + 1):
            term = kinetic_weights[m] * psi_ref[:, plane_rows(planes + x - m, ny)]
            total = term if total is None else total + term
        ahead_ref[:, plane_rows(x, ny)] = total


def coefficient_kernel(planes, upper_ref, table_ref, e_ref, s_ref, ahead_ref, w_ref, next_ref):
    bands, cells, nz = upper_ref.shape
    ny = cells // planes
    reach = BOX - 1
    e = e_ref[...] + overlap(upper_ref, [table_ref[q] for q in range(reach)], ny)
    cols = e.shape[1]
    tiles = -(-cols // nz)
    e = jnp.concatenate([e, jnp.zeros((bands, tiles * nz - cols), F32)], axis=1)
    e = jnp.concatenate([e[:, t * nz : (t + 1) * nz] for t in range(tiles)], axis=0)
    gi = lax.broadcasted_iota(jnp.int32, (nz, nz), 0)
    gj = lax.broadcasted_iota(jnp.int32, (nz, nz), 1)
    group = jnp.where(jnp.bitwise_xor(gi, gj) < HALF, 1.0, 0.0).astype(BF16)
    e_hi = e.astype(BF16)
    e_lo = (e - e_hi.astype(F32)).astype(BF16)
    coef = dot(jnp.concatenate([e_hi, e_lo], axis=1), jnp.concatenate([group, group], axis=0))
    coef = jnp.concatenate([coef[t * bands : (t + 1) * bands] for t in range(tiles)], axis=1)
    w = coef[:, :cols] * s_ref[...]
    rows = bands * HALF
    full = jnp.broadcast_to(w[:, None, :], (bands, HALF, cols)).reshape(rows, cols)
    weights = (full * same_cell(rows, cols)).astype(BF16)
    w_ref[...] = weights
    for q in range(reach):
        here = plane_rows(q, ny)
        block = spread(weights, table_ref[q], nz) + ahead_ref[:, here]
        next_ref[:, here] = block.astype(BF16)


def near_kernel(
    planes, first_ref, psi_ref, prev_ref, pot_ref, w_ref, upper_ref, proj_ref, out_ref
):
    bands, cells, nz = psi_ref.shape
    ny = cells // planes
    weights = w_ref[...]
    starts = box_starts(first_ref, proj_ref.shape[0], planes)
    cz_hi, cz_lo = circulant(nz, 1)
    cz = (jnp.concatenate([cz_hi, cz_hi], axis=0), cz_lo)
    cy = circulant(ny, bands // 2)
    for x in range(planes):
        here = plane_rows(x, ny)
        psi = psi_ref[:, here]
        total = yz_part(psi, cz, cy) + spread(weights, plane_table(proj_ref, starts, x), nz)
        site = outer * pot_ref[here] + (kinetic_weights[0] - outer * center)
        total = total + site[None] * psi - prev_ref[:, here]
        for m in range(1, HALO + 1):
            for target in (x + m, x - m):
                if 0 <= target < planes:
                    total = total + kinetic_weights[m] * psi_ref[:, plane_rows(target, ny)]
                elif target >= planes:
                    value = upper_ref[:, plane_rows(target - planes, ny)].astype(F32)
                    total = total + kinetic_weights[m] * value
        out_ref[:, here] = total


def complete(g_ref, arrived_ref, below_ref, out_ref):
    cut = arrived_ref.shape[1]
    out_ref[:, :cut] = (g_ref[:, :cut] + arrived_ref[...].astype(F32)).astype(out_ref.dtype)
    edge = kinetic_weights[HALO] * below_ref[...].astype(F32)
    out_ref[:, cut:] = (g_ref[:, cut:] + edge).astype(out_ref.dtype)


def finish_kernel(count, g_ref, arrived_ref, below_ref, *rest):
    outs, total = rest[:-1], rest[-1]
    complete(g_ref, arrived_ref, below_ref, total)
    rows = g_ref.shape[1] // count
    pieces_of(total, lax.axis_index("band"), count, rows, outs)


def output_kernel(g_ref, arrived_ref, below_ref, *rest):
    pieces, (out_ref, panel_ref) = rest[:-2], rest[-2:]
    complete(g_ref, arrived_ref, below_ref, out_ref)
    bands = g_ref.shape[0]
    for p, piece in enumerate(reversed(pieces)):
        panel_ref[p * bands : (p + 1) * bands] = piece[...]


def split_kernel(n_space, n_band, prod_ref, out_ref, held, pair):
    bands = prod_ref.shape[0] // n_band
    me = lax.axis_index("band")
    for p, bits in enumerate(partners(n_band)):
        begin = pl.multiple_of(jnp.bitwise_xor(me, bits) * bands, 8)
        held[pl.ds(begin, bands), :] = prod_ref[p * bands : (p + 1) * bands]
    rows = held.shape[0] // n_space
    for p, bits in enumerate(partners(n_band)):
        cols = [slice((h * n_band + p) * bands, (h * n_band + p + 1) * bands) for h in (0, 1)]
        pair[p] = jnp.concatenate([held[:, c] for c in cols], axis=1)
        owner = jnp.bitwise_xor(me, bits)
        lines = [pair[p, pl.ds(r, n_space, stride=rows), :] for r in range(rows)]
        packed = jnp.concatenate(lines, axis=1)
        for i in range(n_space):
            out_ref[owner * n_space + i] = packed[i : i + 1]


def last_kernel(got_ref, margin_ref, projection_ref):
    total = got_ref[...].sum(axis=0)
    rows, bands = margin_ref.shape
    for r in range(rows):
        begin = 2 * r * bands
        margin_ref[r : r + 1] = total[:, begin : begin + bands]
        projection_ref[r : r + 1] = total[:, begin + bands : begin + 2 * bands]


def cyclic(value, axis, steps):
    count = lax.axis_size(axis)
    return lax.ppermute(value, axis, [(i, (i + steps) % count) for i in range(count)])


def mirrored(value, axis, bits):
    count = lax.axis_size(axis)
    return lax.ppermute(value, axis, [(i, i ^ bits) for i in range(count)])


def exchanged(pieces):
    offsets = partners(len(pieces))
    return [mirrored(p, "band", bits) if bits else p for bits, p in zip(offsets, pieces)]


def struct(shape, kind=F32):
    return jax.ShapeDtypeStruct(shape, kind)


def call(kernel, name, out_shape, args, vmem=48, **extra):
    return pl.pallas_call(
        kernel, out_shape=out_shape, compiler_params=params(vmem * 2**20), name=name, **extra
    )(*args)


def shards(orbitals, previous, potential, projectors, strengths, atom_planes):
    bands, planes, ny, nz = orbitals.shape
    n_space = lax.axis_size("space")
    n_band = lax.axis_size("band")
    cells = planes * ny
    whole = (bands, cells, nz)
    quarter = (bands, cells // n_band, nz)
    psi = orbitals.reshape(whole)
    prev = previous.reshape(whole)
    pot = potential.reshape(cells, nz)

    vm = pl.BlockSpec(memory_space=pltpu.VMEM)
    sm = pl.BlockSpec(memory_space=pltpu.SMEM)
    anywhere = pl.BlockSpec(memory_space=pl.ANY)

    most = (bands, (planes - 1) * ny, nz)
    plane = (bands, ny, nz)
    half = call(cast_kernel, "cast", struct(whole, BF16), (psi,))
    panel = call(
        partial(pieces_kernel, n_band),
        "pieces",
        (struct(quarter, BF16),) * n_band,
        (psi,),
        cost_estimate=pl.CostEstimate(flops=10**9, bytes_accessed=2**20, transcendentals=0),
    )
    upper = cyclic(half, "space", -1)
    panel = exchanged(panel)
    atoms, npj = projectors.shape[:2]
    cols = atoms * npj * HALF
    far_tables, e, s = call(
        partial(prepare_kernel, planes),
        "prepare",
        (
            struct((BOX - 1, cols, ny // HALF * nz), BF16),
            struct((bands, cols)),
            struct((1, cols)),
        ),
        (atom_planes, strengths.T, half, projectors),
        in_specs=[sm, sm, vm, vm],
        out_specs=(vm,) * 3,
        cost_estimate=pl.CostEstimate(flops=10**9, bytes_accessed=2**20, transcendentals=0),
    )
    ahead, edge = call(
        partial(ahead_kernel, planes),
        "ahead",
        (struct(most), struct(plane, BF16)),
        (psi, panel[3], s),
        in_specs=[vm, anywhere, anywhere],
        out_specs=(vm, vm),
        cost_estimate=pl.CostEstimate(flops=10**9, bytes_accessed=2**20, transcendentals=0),
    )
    below = cyclic(edge, "space", 1)
    w, beyond = call(
        partial(coefficient_kernel, planes),
        "coefficients",
        (struct((bands * HALF, cols), BF16), struct(most, BF16)),
        (upper, far_tables, e, s, ahead),
        cost_estimate=pl.CostEstimate(flops=10**9, bytes_accessed=2**20, transcendentals=0),
    )
    arrived = cyclic(beyond, "space", 1)
    g = call(
        partial(near_kernel, planes),
        "near_part",
        struct(whole),
        (atom_planes, psi, prev, pot, w, upper, projectors),
        in_specs=[sm] + [vm] * 6,
        out_specs=vm,
        cost_estimate=pl.CostEstimate(flops=2*10**10, bytes_accessed=4 * 2**20, transcendentals=0),
    )
    mine = call(
        partial(finish_kernel, n_band),
        "finish",
        (struct(quarter, BF16),) * n_band,
        (g, arrived, below),
        scratch_shapes=[pltpu.VMEM(whole, F32)],
    )
    mine = exchanged(mine)
    total_bands = n_band * bands
    filtered, panels = call(
        output_kernel,
        "output",
        (struct(whole, BF16), struct((total_bands, *quarter[1:]), BF16)),
        (g, arrived, below, *reversed(panel)),
    )
    left = jnp.concatenate(mine, axis=0).reshape(total_bands, -1)
    right = jnp.concatenate([left, panels.reshape(total_bands, -1)], axis=0)
    products = dot(left, right, ((1,), (1,))) * (1.0 / (cells * n_space * nz))
    out_rows = total_bands // n_space
    pieces = call(
        partial(split_kernel, n_space, n_band),
        "split",
        struct((n_space * n_band, 1, out_rows * 2 * bands)),
        (products,),
        scratch_shapes=[
            pltpu.VMEM(products.shape, F32),
            pltpu.VMEM((n_band, total_bands, 2 * bands), F32),
        ],
    )
    got = lax.all_to_all(pieces, ("band", "space"), 0, 0)
    margin, projection = call(
        last_kernel, "last_sum", (struct((out_rows, bands)), struct((out_rows, bands))), (got,)
    )
    return filtered.reshape(orbitals.shape), margin, projection


def solution(mesh):
    in_specs = (
        P("band", "space", None, None),
        P("band", "space", None, None),
        P("space", None, None),
        P("space", None, None, None, None),
        P(),
        P(),
    )
    out_specs = (P("band", "space", None, None), P("space", "band"), P("space", "band"))
    return jax.shard_map(shards, mesh=mesh, in_specs=in_specs, out_specs=out_specs, check_vma=False)
```

```python
from functools import partial

import jax
import jax.numpy as jnp
from jax import lax
from jax.experimental import pallas as pl
from jax.experimental.pallas import tpu as pltpu
from jax.sharding import PartitionSpec as P

HALO = 6
BOX = 6
NPJ = 9
HALF = 16

stencil_weights = (
    -5369.0 / 1800.0,
    12.0 / 7.0,
    -15.0 / 56.0,
    10.0 / 189.0,
    -1.0 / 112.0,
    2.0 / 1925.0,
    -1.0 / 16632.0,
)
center = 5.5
halfwidth = 5.5
outer = 2.0 / halfwidth
kinetic_weights = [-0.5 * outer * w for w in stencil_weights]

F32 = jnp.float32
BF16 = jnp.bfloat16


def params(vmem):
    return pltpu.CompilerParams(vmem_limit_bytes=vmem)


def circulant(n, blocks):
    size = n * blocks
    row = lax.broadcasted_iota(jnp.int32, (size, size), 0)
    col = lax.broadcasted_iota(jnp.int32, (size, size), 1)
    ahead = jnp.bitwise_and(col - row, n - 1)
    reach = jnp.minimum(ahead, n - ahead)
    value = jnp.zeros((size, size), F32)
    for m, weight in enumerate(kinetic_weights):
        value = jnp.where(reach == m, weight, value)
    value = jnp.where(jnp.bitwise_xor(row, col) < n, value, 0.0)
    hi = value.astype(BF16)
    return hi, (value - hi.astype(F32)).astype(BF16)


def dot(a, b, dims=((1,), (0,))):
    return lax.dot_general(a, b, (dims, ((), ())), preferred_element_type=F32)


def plane_rows(x, ny):
    return slice(x * ny, (x + 1) * ny)


def partners(count):
    return [0, *reversed(range(1, count))]


def pieces_of(ref, index, count, rows, outs):
    for bits, out in zip(partners(count), outs):
        quarter = jnp.bitwise_xor(index, bits)
        begin = pl.multiple_of(quarter * rows, 8)
        out[...] = ref[:, pl.ds(begin, rows), :].astype(out.dtype)


def cast_kernel(psi_ref, half_ref):
    half_ref[...] = psi_ref[...].astype(BF16)


def pieces_kernel(count, psi_ref, *outs):
    rows = psi_ref.shape[1] // count
    pieces_of(psi_ref, lax.axis_index("band"), count, rows, outs)


def yz_part(psi, cz, cy):
    bands, ny, nz = psi.shape
    flat = psi.reshape(bands * ny, nz)
    hi = flat.astype(BF16)
    lo = (flat - hi.astype(F32)).astype(BF16)
    both = jnp.concatenate([hi, lo], axis=1)
    along_z = dot(both, cz[0]) + dot(hi, cz[1])
    size = cy[0].shape[0]
    along_y = []
    for begin in range(0, bands * ny, size):
        pair = dot(cy[0], both[begin : begin + size])
        along_y.append(pair[:, :nz] + pair[:, nz:] + dot(cy[1], hi[begin : begin + size]))
    return (along_z + jnp.concatenate(along_y, axis=0)).reshape(bands, ny, nz)


def same_cell(rows, cols):
    row = lax.broadcasted_iota(jnp.int32, (rows, cols), 0)
    col = lax.broadcasted_iota(jnp.int32, (rows, cols), 1)
    return jnp.where(jnp.bitwise_and(row - col, HALF - 1) == 0, 1.0, 0.0).astype(F32)


def table(proj_ref, a, p):
    npj, ny, nz = proj_ref.shape[1], proj_ref.shape[3], proj_ref.shape[4]
    halves = [
        proj_ref[a, :, p, h * HALF : (h + 1) * HALF, :].reshape(npj * HALF, nz)
        for h in range(ny // HALF)
    ]
    return jnp.concatenate(halves, axis=1)


def halves_along(value, axis):
    bands, ny, nz = value.shape
    parts = [value[:, h * HALF : (h + 1) * HALF].reshape(bands * HALF, nz) for h in range(ny // HALF)]
    return jnp.concatenate(parts, axis=axis)


def spread(weights, tables, nz):
    total = dot(weights, tables)
    rows = total.shape[0]
    halves = [
        total[:, h * nz : (h + 1) * nz].reshape(rows // HALF, HALF, nz)
        for h in range(total.shape[1] // nz)
    ]
    return jnp.concatenate(halves, axis=1)


def overlap(field_ref, planes, ny, table_ref):
    bands = field_ref.shape[0]
    left = [halves_along(field_ref[:, plane_rows(x, ny)], 1) for x in range(planes)]
    right = [table_ref[x] for x in range(planes)]
    d = dot(jnp.concatenate(left, axis=1), jnp.concatenate(right, axis=1), ((1,), (1,)))
    rows, cols = d.shape
    return (d * same_cell(rows, cols)).reshape(bands, HALF, cols).sum(axis=1)


def prepare_kernel(
    planes, first_ref, strength_ref, own_ref, proj_ref, near_ref, far_ref, e_ref, s_ref
):
    ny = own_ref.shape[1] // planes
    atoms, npj = proj_ref.shape[:2]
    me = lax.axis_index("space")
    for q in range(planes + BOX - 1):
        parts = []
        for a in range(atoms):
            p = q - (first_ref[me * atoms + a] - me * planes)
            inside = jnp.logical_and(p >= 0, p < BOX)
            part = table(proj_ref, a, jnp.clip(p, 0, BOX - 1))
            parts.append(part * jnp.where(inside, 1.0, 0.0).astype(BF16))
        whole = jnp.concatenate(parts, axis=0)
        if q < planes:
            near_ref[q] = whole
        else:
            far_ref[q - planes] = whole
    owner = lax.broadcasted_iota(jnp.int32, s_ref.shape, 1)
    scale = jnp.zeros(s_ref.shape, F32)
    for a in range(atoms):
        for j in range(npj):
            value = outer * strength_ref[j, me * atoms + a]
            scale = jnp.where(owner >= (a * npj + j) * HALF, value, scale)
    s_ref[...] = scale
    e_ref[...] = overlap(own_ref, planes, ny, near_ref)


def ahead_kernel(planes, psi_ref, *refs):
    ahead_ref, edge_ref = refs[-2:]
    ny = psi_ref.shape[1] // planes
    edge_ref[...] = psi_ref[:, plane_rows(planes - 1, ny)].astype(BF16)
    for x in range(planes - 1):
        total = None
        for m in range(x + 1, HALO + 1):
            term = kinetic_weights[m] * psi_ref[:, plane_rows(planes + x - m, ny)]
            total = term if total is None else total + term
        ahead_ref[:, plane_rows(x, ny)] = total


def coefficient_kernel(planes, upper_ref, table_ref, e_ref, s_ref, ahead_ref, w_ref, next_ref):
    bands, cells, nz = upper_ref.shape
    ny = cells // planes
    reach = BOX - 1
    e = e_ref[...] + overlap(upper_ref, reach, ny, table_ref)
    cols = e.shape[1]
    tiles = -(-cols // nz)
    e = jnp.concatenate([e, jnp.zeros((bands, tiles * nz - cols), F32)], axis=1)
    e = jnp.concatenate([e[:, t * nz : (t + 1) * nz] for t in range(tiles)], axis=0)
    gi = lax.broadcasted_iota(jnp.int32, (nz, nz), 0)
    gj = lax.broadcasted_iota(jnp.int32, (nz, nz), 1)
    group = jnp.where(jnp.bitwise_xor(gi, gj) < HALF, 1.0, 0.0).astype(BF16)
    e_hi = e.astype(BF16)
    e_lo = (e - e_hi.astype(F32)).astype(BF16)
    coef = dot(e_hi, group) + dot(e_lo, group)
    coef = jnp.concatenate([coef[t * bands : (t + 1) * bands] for t in range(tiles)], axis=1)
    w = coef[:, :cols] * s_ref[...]
    rows = bands * HALF
    full = jnp.broadcast_to(w[:, None, :], (bands, HALF, cols)).reshape(rows, cols)
    weights = (full * same_cell(rows, cols)).astype(BF16)
    w_ref[...] = weights
    for q in range(reach):
        here = plane_rows(q, ny)
        block = spread(weights, table_ref[q], nz) + ahead_ref[:, here]
        next_ref[:, here] = block.astype(BF16)


def near_kernel(planes, psi_ref, prev_ref, pot_ref, w_ref, upper_ref, table_ref, out_ref):
    bands, cells, nz = psi_ref.shape
    ny = cells // planes
    weights = w_ref[...]
    cz_hi, cz_lo = circulant(nz, 1)
    cz = (jnp.concatenate([cz_hi, cz_hi], axis=0), cz_lo)
    cy = circulant(ny, bands // 2)
    for x in range(planes):
        here = plane_rows(x, ny)
        psi = psi_ref[:, here]
        total = yz_part(psi, cz, cy) + spread(weights, table_ref[x], nz)
        site = outer * pot_ref[here] + (kinetic_weights[0] - outer * center)
        total = total + site[None] * psi - prev_ref[:, here]
        for m in range(1, HALO + 1):
            for target in (x + m, x - m):
                if 0 <= target < planes:
                    total = total + kinetic_weights[m] * psi_ref[:, plane_rows(target, ny)]
                elif target >= planes:
                    value = upper_ref[:, plane_rows(target - planes, ny)].astype(F32)
                    total = total + kinetic_weights[m] * value
        out_ref[:, here] = total


def complete(g_ref, arrived_ref, below_ref, out_ref):
    cut = arrived_ref.shape[1]
    out_ref[:, :cut] = (g_ref[:, :cut] + arrived_ref[...].astype(F32)).astype(out_ref.dtype)
    edge = kinetic_weights[HALO] * below_ref[...].astype(F32)
    out_ref[:, cut:] = (g_ref[:, cut:] + edge).astype(out_ref.dtype)


def finish_kernel(count, g_ref, arrived_ref, below_ref, *rest):
    outs, total = rest[:-1], rest[-1]
    complete(g_ref, arrived_ref, below_ref, total)
    rows = g_ref.shape[1] // count
    pieces_of(total, lax.axis_index("band"), count, rows, outs)


def output_kernel(g_ref, arrived_ref, below_ref, *rest):
    pieces, (out_ref, panel_ref) = rest[:-2], rest[-2:]
    complete(g_ref, arrived_ref, below_ref, out_ref)
    bands = g_ref.shape[0]
    for p, piece in enumerate(reversed(pieces)):
        panel_ref[p * bands : (p + 1) * bands] = piece[...]


def split_kernel(n_space, n_band, prod_ref, out_ref, held, pair):
    bands = prod_ref.shape[0] // n_band
    me = lax.axis_index("band")
    for p, bits in enumerate(partners(n_band)):
        begin = pl.multiple_of(jnp.bitwise_xor(me, bits) * bands, 8)
        held[pl.ds(begin, bands), :] = prod_ref[p * bands : (p + 1) * bands]
    rows = held.shape[0] // n_space
    for p, bits in enumerate(partners(n_band)):
        cols = [slice((h * n_band + p) * bands, (h * n_band + p + 1) * bands) for h in (0, 1)]
        pair[p] = jnp.concatenate([held[:, c] for c in cols], axis=1)
        owner = jnp.bitwise_xor(me, bits)
        lines = [pair[p, pl.ds(r, n_space, stride=rows), :] for r in range(rows)]
        packed = jnp.concatenate(lines, axis=1)
        for i in range(n_space):
            out_ref[i * n_band + owner] = packed[i : i + 1]


def last_kernel(got_ref, margin_ref, projection_ref):
    total = got_ref[...].sum(axis=0)
    rows, bands = margin_ref.shape
    for r in range(rows):
        begin = 2 * r * bands
        margin_ref[r : r + 1] = total[:, begin : begin + bands]
        projection_ref[r : r + 1] = total[:, begin + bands : begin + 2 * bands]


def cyclic(value, axis, steps):
    count = lax.axis_size(axis)
    return lax.ppermute(value, axis, [(i, (i + steps) % count) for i in range(count)])


def mirrored(value, axis, bits):
    count = lax.axis_size(axis)
    return lax.ppermute(value, axis, [(i, i ^ bits) for i in range(count)])


def exchanged(pieces):
    offsets = partners(len(pieces))
    return [mirrored(p, "band", bits) if bits else p for bits, p in zip(offsets, pieces)]


def struct(shape, kind=F32):
    return jax.ShapeDtypeStruct(shape, kind)


def call(kernel, name, out_shape, args, vmem=48, **extra):
    return pl.pallas_call(
        kernel, out_shape=out_shape, compiler_params=params(vmem * 2**20), name=name, **extra
    )(*args)


def shards(orbitals, previous, potential, projectors, strengths, atom_planes):
    bands, planes, ny, nz = orbitals.shape
    n_space = lax.axis_size("space")
    n_band = lax.axis_size("band")
    cells = planes * ny
    whole = (bands, cells, nz)
    quarter = (bands, cells // n_band, nz)
    psi = orbitals.reshape(whole)
    prev = previous.reshape(whole)
    pot = potential.reshape(cells, nz)

    vm = pl.BlockSpec(memory_space=pltpu.VMEM)
    sm = pl.BlockSpec(memory_space=pltpu.SMEM)
    anywhere = pl.BlockSpec(memory_space=pl.ANY)

    most = (bands, (planes - 1) * ny, nz)
    plane = (bands, ny, nz)
    half = call(cast_kernel, "cast", struct(whole, BF16), (psi,))
    panel = call(
        partial(pieces_kernel, n_band),
        "pieces",
        (struct(quarter, BF16),) * n_band,
        (psi,),
        cost_estimate=pl.CostEstimate(flops=10**9, bytes_accessed=2**20, transcendentals=0),
    )
    upper = cyclic(half, "space", -1)
    panel = exchanged(panel)
    atoms, npj = projectors.shape[:2]
    cols = atoms * npj * HALF
    tables, far_tables, e, s = call(
        partial(prepare_kernel, planes),
        "prepare",
        (
            struct((planes, cols, ny // HALF * nz), BF16),
            struct((BOX - 1, cols, ny // HALF * nz), BF16),
            struct((bands, cols)),
            struct((1, cols)),
        ),
        (atom_planes, strengths.T, half, projectors),
        in_specs=[sm, sm, vm, vm],
        out_specs=(vm,) * 4,
        cost_estimate=pl.CostEstimate(flops=10**9, bytes_accessed=2**20, transcendentals=0),
    )
    ahead, edge = call(
        partial(ahead_kernel, planes),
        "ahead",
        (struct(most), struct(plane, BF16)),
        (psi, panel[3], s),
        in_specs=[vm, anywhere, anywhere],
        out_specs=(vm, vm),
        cost_estimate=pl.CostEstimate(flops=10**9, bytes_accessed=2**20, transcendentals=0),
    )
    below = cyclic(edge, "space", 1)
    w, beyond = call(
        partial(coefficient_kernel, planes),
        "coefficients",
        (struct((bands * HALF, cols), BF16), struct(most, BF16)),
        (upper, far_tables, e, s, ahead),
        cost_estimate=pl.CostEstimate(flops=10**9, bytes_accessed=2**20, transcendentals=0),
    )
    arrived = cyclic(beyond, "space", 1)
    g = call(
        partial(near_kernel, planes),
        "near_part",
        struct(whole),
        (psi, prev, pot, w, upper, tables),
        cost_estimate=pl.CostEstimate(flops=2*10**10, bytes_accessed=4 * 2**20, transcendentals=0),
    )
    mine = call(
        partial(finish_kernel, n_band),
        "finish",
        (struct(quarter, BF16),) * n_band,
        (g, arrived, below),
        scratch_shapes=[pltpu.VMEM(whole, F32)],
    )
    mine = exchanged(mine)
    total_bands = n_band * bands
    filtered, panels = call(
        output_kernel,
        "output",
        (struct(whole, BF16), struct((total_bands, *quarter[1:]), BF16)),
        (g, arrived, below, *reversed(panel)),
    )
    left = jnp.concatenate(mine, axis=0).reshape(total_bands, -1)
    filtered, rows = lax.optimization_barrier((filtered, panels.reshape(total_bands, -1)))
    right = jnp.concatenate([left, rows], axis=0)
    products = dot(left, right, ((1,), (1,))) * (1.0 / (cells * n_space * nz))
    out_rows = total_bands // n_space
    pieces = call(
        partial(split_kernel, n_space, n_band),
        "split",
        struct((n_space * n_band, 1, out_rows * 2 * bands)),
        (products,),
        scratch_shapes=[
            pltpu.VMEM(products.shape, F32),
            pltpu.VMEM((n_band, total_bands, 2 * bands), F32),
        ],
    )
    got = lax.all_to_all(pieces, ("space", "band"), 0, 0)
    margin, projection = call(
        last_kernel, "last_sum", (struct((out_rows, bands)), struct((out_rows, bands))), (got,)
    )
    return filtered.reshape(orbitals.shape), margin, projection


def solution(mesh):
    in_specs = (
        P("band", "space", None, None),
        P("band", "space", None, None),
        P("space", None, None),
        P("space", None, None, None, None),
        P(),
        P(),
    )
    out_specs = (P("band", "space", None, None), P("space", "band"), P("space", "band"))
    return jax.shard_map(shards, mesh=mesh, in_specs=in_specs, out_specs=out_specs, check_vma=False)
```

```python
from functools import partial

import jax
import jax.numpy as jnp
from jax import lax
from jax.experimental import pallas as pl
from jax.experimental.pallas import tpu as pltpu
from jax.sharding import PartitionSpec as P

HALO = 6
BOX = 6
NPJ = 9
HALF = 16

stencil_weights = (
    -5369.0 / 1800.0,
    12.0 / 7.0,
    -15.0 / 56.0,
    10.0 / 189.0,
    -1.0 / 112.0,
    2.0 / 1925.0,
    -1.0 / 16632.0,
)
center = 5.5
halfwidth = 5.5
outer = 2.0 / halfwidth
kinetic_weights = [-0.5 * outer * w for w in stencil_weights]

F32 = jnp.float32
BF16 = jnp.bfloat16


def params(vmem):
    return pltpu.CompilerParams(vmem_limit_bytes=vmem)


def circulant(n, blocks):
    size = n * blocks
    row = lax.broadcasted_iota(jnp.int32, (size, size), 0)
    col = lax.broadcasted_iota(jnp.int32, (size, size), 1)
    ahead = jnp.bitwise_and(col - row, n - 1)
    reach = jnp.minimum(ahead, n - ahead)
    value = jnp.zeros((size, size), F32)
    for m, weight in enumerate(kinetic_weights):
        value = jnp.where(reach == m, weight, value)
    value = jnp.where(jnp.bitwise_xor(row, col) < n, value, 0.0)
    hi = value.astype(BF16)
    return hi, (value - hi.astype(F32)).astype(BF16)


def dot(a, b, dims=((1,), (0,))):
    return lax.dot_general(a, b, (dims, ((), ())), preferred_element_type=F32)


def plane_rows(x, ny):
    return slice(x * ny, (x + 1) * ny)


def partners(count):
    return [0, *reversed(range(1, count))]


def pieces_of(ref, index, count, rows, outs):
    for bits, out in zip(partners(count), outs):
        quarter = jnp.bitwise_xor(index, bits)
        begin = pl.multiple_of(quarter * rows, 16 if rows % 16 == 0 else 8)
        out[...] = ref[:, pl.ds(begin, rows), :].astype(out.dtype)


def pieces_kernel(count, psi_ref, *outs):
    rows = psi_ref.shape[1] // count
    pieces_of(psi_ref, lax.axis_index("band"), count, rows, outs)


def yz_part(psi, cz, cy):
    bands, ny, nz = psi.shape
    flat = psi.reshape(bands * ny, nz)
    hi = flat.astype(BF16)
    lo = (flat - hi.astype(F32)).astype(BF16)
    both = jnp.concatenate([hi, lo], axis=1)
    along_z = dot(both, cz[0]) + dot(hi, cz[1])
    size = cy[0].shape[0]
    along_y = []
    for begin in range(0, bands * ny, size):
        pair = dot(cy[0], both[begin : begin + size])
        along_y.append(pair[:, :nz] + pair[:, nz:] + dot(cy[1], hi[begin : begin + size]))
    return (along_z + jnp.concatenate(along_y, axis=0)).reshape(bands, ny, nz)


def same_cell(rows, cols):
    row = lax.broadcasted_iota(jnp.int32, (rows, cols), 0)
    col = lax.broadcasted_iota(jnp.int32, (rows, cols), 1)
    return jnp.where(jnp.bitwise_and(row - col, HALF - 1) == 0, 1.0, 0.0).astype(F32)


def table(proj_ref, a, p):
    npj, ny, nz = proj_ref.shape[1], proj_ref.shape[3], proj_ref.shape[4]
    halves = [
        proj_ref[a, :, p, h * HALF : (h + 1) * HALF, :].reshape(npj * HALF, nz)
        for h in range(ny // HALF)
    ]
    return jnp.concatenate(halves, axis=1)


def halves_along(value, axis):
    bands, ny, nz = value.shape
    parts = [value[:, h * HALF : (h + 1) * HALF].reshape(bands * HALF, nz) for h in range(ny // HALF)]
    return jnp.concatenate(parts, axis=axis)


def spread(weights, tables, nz):
    total = dot(weights, tables)
    rows = total.shape[0]
    halves = [
        total[:, h * nz : (h + 1) * nz].reshape(rows // HALF, HALF, nz)
        for h in range(total.shape[1] // nz)
    ]
    return jnp.concatenate(halves, axis=1)


def overlap(field_ref, planes, ny, table_ref):
    bands = field_ref.shape[0]
    left = [halves_along(field_ref[:, plane_rows(x, ny)], 1) for x in range(planes)]
    right = [table_ref[x] for x in range(planes)]
    d = dot(jnp.concatenate(left, axis=1), jnp.concatenate(right, axis=1), ((1,), (1,)))
    rows, cols = d.shape
    return (d * same_cell(rows, cols)).reshape(bands, HALF, cols).sum(axis=1)


def prepare_kernel(
    planes, first_ref, strength_ref, own_ref, proj_ref, near_ref, far_ref, e_ref, s_ref
):
    ny = own_ref.shape[1] // planes
    atoms, npj = proj_ref.shape[:2]
    me = lax.axis_index("space")
    for q in range(planes + BOX - 1):
        parts = []
        for a in range(atoms):
            p = q - (first_ref[me * atoms + a] - me * planes)
            inside = jnp.logical_and(p >= 0, p < BOX)
            part = table(proj_ref, a, jnp.clip(p, 0, BOX - 1))
            parts.append(part * jnp.where(inside, 1.0, 0.0).astype(BF16))
        whole = jnp.concatenate(parts, axis=0)
        if q < planes:
            near_ref[q] = whole
        else:
            far_ref[q - planes] = whole
    owner = lax.broadcasted_iota(jnp.int32, s_ref.shape, 1)
    scale = jnp.zeros(s_ref.shape, F32)
    for a in range(atoms):
        for j in range(npj):
            value = outer * strength_ref[j, me * atoms + a]
            scale = jnp.where(owner >= (a * npj + j) * HALF, value, scale)
    s_ref[...] = scale
    e_ref[...] = overlap(own_ref, planes, ny, near_ref)


def ahead_kernel(planes, psi_ref, *refs):
    ahead_ref, edge_ref = refs[-2:]
    ny = psi_ref.shape[1] // planes
    edge_ref[...] = psi_ref[:, plane_rows(planes - 1, ny)].astype(BF16)
    for x in range(planes - 1):
        total = None
        for m in range(x + 1, HALO + 1):
            term = kinetic_weights[m] * psi_ref[:, plane_rows(planes + x - m, ny)]
            total = term if total is None else total + term
        ahead_ref[:, plane_rows(x, ny)] = total


def coefficient_kernel(planes, upper_ref, table_ref, e_ref, s_ref, ahead_ref, w_ref, next_ref):
    bands, cells, nz = upper_ref.shape
    ny = cells // planes
    reach = BOX - 1
    e = e_ref[...] + overlap(upper_ref, reach, ny, table_ref)
    cols = e.shape[1]
    tiles = -(-cols // nz)
    e = jnp.concatenate([e, jnp.zeros((bands, tiles * nz - cols), F32)], axis=1)
    e = jnp.concatenate([e[:, t * nz : (t + 1) * nz] for t in range(tiles)], axis=0)
    gi = lax.broadcasted_iota(jnp.int32, (nz, nz), 0)
    gj = lax.broadcasted_iota(jnp.int32, (nz, nz), 1)
    group = jnp.where(jnp.bitwise_xor(gi, gj) < HALF, 1.0, 0.0).astype(BF16)
    e_hi = e.astype(BF16)
    e_lo = (e - e_hi.astype(F32)).astype(BF16)
    coef = dot(e_hi, group) + dot(e_lo, group)
    coef = jnp.concatenate([coef[t * bands : (t + 1) * bands] for t in range(tiles)], axis=1)
    w = coef[:, :cols] * s_ref[...]
    rows = bands * HALF
    full = jnp.broadcast_to(w[:, None, :], (bands, HALF, cols)).reshape(rows, cols)
    weights = (full * same_cell(rows, cols)).astype(BF16)
    w_ref[...] = weights
    for q in range(reach):
        here = plane_rows(q, ny)
        block = spread(weights, table_ref[q], nz) + ahead_ref[:, here]
        next_ref[:, here] = block.astype(BF16)


def near_kernel(planes, psi_ref, prev_ref, pot_ref, w_ref, upper_ref, table_ref, out_ref):
    bands, cells, nz = psi_ref.shape
    ny = cells // planes
    weights = w_ref[...]
    cz_hi, cz_lo = circulant(nz, 1)
    cz = (jnp.concatenate([cz_hi, cz_hi], axis=0), cz_lo)
    cy = circulant(ny, bands // 2)
    for x in range(planes):
        here = plane_rows(x, ny)
        psi = psi_ref[:, here]
        total = yz_part(psi, cz, cy) + spread(weights, table_ref[x], nz)
        site = outer * pot_ref[here] + (kinetic_weights[0] - outer * center)
        total = total + site[None] * psi - prev_ref[:, here]
        for m in range(1, HALO + 1):
            for target in (x + m, x - m):
                if 0 <= target < planes:
                    total = total + kinetic_weights[m] * psi_ref[:, plane_rows(target, ny)]
                elif target >= planes:
                    value = upper_ref[:, plane_rows(target - planes, ny)].astype(F32)
                    total = total + kinetic_weights[m] * value
        out_ref[:, here] = total


def complete(g_ref, arrived_ref, below_ref, out_ref):
    cut = arrived_ref.shape[1]
    out_ref[:, :cut] = (g_ref[:, :cut] + arrived_ref[...].astype(F32)).astype(out_ref.dtype)
    edge = kinetic_weights[HALO] * below_ref[...].astype(F32)
    out_ref[:, cut:] = (g_ref[:, cut:] + edge).astype(out_ref.dtype)


def finish_kernel(count, g_ref, arrived_ref, below_ref, *rest):
    outs, total = rest[:-1], rest[-1]
    complete(g_ref, arrived_ref, below_ref, total)
    rows = g_ref.shape[1] // count
    pieces_of(total, lax.axis_index("band"), count, rows, outs)


def output_kernel(g_ref, arrived_ref, below_ref, *rest):
    pieces, (out_ref, panel_ref) = rest[:-2], rest[-2:]
    complete(g_ref, arrived_ref, below_ref, out_ref)
    bands = g_ref.shape[0]
    for p, piece in enumerate(reversed(pieces)):
        panel_ref[p * bands : (p + 1) * bands] = piece[...]


def split_kernel(n_space, n_band, prod_ref, out_ref, held, pair):
    bands = prod_ref.shape[0] // n_band
    me = lax.axis_index("band")
    for p, bits in enumerate(partners(n_band)):
        begin = pl.multiple_of(jnp.bitwise_xor(me, bits) * bands, 8)
        held[pl.ds(begin, bands), :] = prod_ref[p * bands : (p + 1) * bands]
    rows = held.shape[0] // n_space
    for p, bits in enumerate(partners(n_band)):
        cols = [slice((h * n_band + p) * bands, (h * n_band + p + 1) * bands) for h in (0, 1)]
        pair[p] = jnp.concatenate([held[:, c] for c in cols], axis=1)
        owner = jnp.bitwise_xor(me, bits)
        lines = [pair[p, pl.ds(r, n_space, stride=rows), :] for r in range(rows)]
        packed = jnp.concatenate(lines, axis=1)
        for i in range(n_space):
            out_ref[i * n_band + owner] = packed[i : i + 1]


def last_kernel(got_ref, margin_ref, projection_ref):
    total = got_ref[...].sum(axis=0)
    rows, bands = margin_ref.shape
    for r in range(rows):
        begin = 2 * r * bands
        margin_ref[r : r + 1] = total[:, begin : begin + bands]
        projection_ref[r : r + 1] = total[:, begin + bands : begin + 2 * bands]


def cyclic(value, axis, steps):
    count = lax.axis_size(axis)
    return lax.ppermute(value, axis, [(i, (i + steps) % count) for i in range(count)])


def mirrored(value, axis, bits):
    count = lax.axis_size(axis)
    return lax.ppermute(value, axis, [(i, i ^ bits) for i in range(count)])


def exchanged(pieces):
    offsets = partners(len(pieces))
    return [mirrored(p, "band", bits) if bits else p for bits, p in zip(offsets, pieces)]


def struct(shape, kind=F32):
    return jax.ShapeDtypeStruct(shape, kind)


def call(kernel, name, out_shape, args, vmem=48, **extra):
    return pl.pallas_call(
        kernel, out_shape=out_shape, compiler_params=params(vmem * 2**20), name=name, **extra
    )(*args)


def shards(orbitals, previous, potential, projectors, strengths, atom_planes):
    bands, planes, ny, nz = orbitals.shape
    n_space = lax.axis_size("space")
    n_band = lax.axis_size("band")
    cells = planes * ny
    whole = (bands, cells, nz)
    quarter = (bands, cells // n_band, nz)
    psi = orbitals.reshape(whole)
    prev = previous.reshape(whole)
    pot = potential.reshape(cells, nz)

    vm = pl.BlockSpec(memory_space=pltpu.VMEM)
    sm = pl.BlockSpec(memory_space=pltpu.SMEM)
    anywhere = pl.BlockSpec(memory_space=pl.ANY)

    most = (bands, (planes - 1) * ny, nz)
    plane = (bands, ny, nz)
    half = psi.astype(BF16)
    panel = call(
        partial(pieces_kernel, n_band),
        "pieces",
        (struct(quarter, BF16),) * n_band,
        (half if quarter[1] % 16 == 0 else psi,),
        cost_estimate=pl.CostEstimate(flops=10**9, bytes_accessed=2**20, transcendentals=0),
    )
    upper = cyclic(half, "space", -1)
    panel = exchanged(panel)
    atoms, npj = projectors.shape[:2]
    cols = atoms * npj * HALF
    tables, far_tables, e, s = call(
        partial(prepare_kernel, planes),
        "prepare",
        (
            struct((planes, cols, ny // HALF * nz), BF16),
            struct((BOX - 1, cols, ny // HALF * nz), BF16),
            struct((bands, cols)),
            struct((1, cols)),
        ),
        (atom_planes, strengths.T, half, projectors),
        in_specs=[sm, sm, vm, vm],
        out_specs=(vm,) * 4,
        cost_estimate=pl.CostEstimate(flops=10**9, bytes_accessed=2**20, transcendentals=0),
    )
    ahead, edge = call(
        partial(ahead_kernel, planes),
        "ahead",
        (struct(most), struct(plane, BF16)),
        (psi, panel[3], s),
        in_specs=[vm, anywhere, anywhere],
        out_specs=(vm, vm),
        cost_estimate=pl.CostEstimate(flops=10**9, bytes_accessed=2**20, transcendentals=0),
    )
    below = cyclic(edge, "space", 1)
    w, beyond = call(
        partial(coefficient_kernel, planes),
        "coefficients",
        (struct((bands * HALF, cols), BF16), struct(most, BF16)),
        (upper, far_tables, e, s, ahead),
        cost_estimate=pl.CostEstimate(flops=10**9, bytes_accessed=2**20, transcendentals=0),
    )
    arrived = cyclic(beyond, "space", 1)
    g = call(
        partial(near_kernel, planes),
        "near_part",
        struct(whole),
        (psi, prev, pot, w, upper, tables),
        cost_estimate=pl.CostEstimate(flops=2*10**10, bytes_accessed=4 * 2**20, transcendentals=0),
    )
    mine = call(
        partial(finish_kernel, n_band),
        "finish",
        (struct(quarter, BF16),) * n_band,
        (g, arrived, below),
        scratch_shapes=[pltpu.VMEM(whole, F32)],
    )
    mine = exchanged(mine)
    total_bands = n_band * bands
    filtered, panels = call(
        output_kernel,
        "output",
        (struct(whole, BF16), struct((total_bands, *quarter[1:]), BF16)),
        (g, arrived, below, *reversed(panel)),
    )
    left = jnp.concatenate(mine, axis=0).reshape(total_bands, -1)
    filtered, rows = lax.optimization_barrier((filtered, panels.reshape(total_bands, -1)))
    right = jnp.concatenate([left, rows], axis=0)
    products = dot(left, right, ((1,), (1,))) * (1.0 / (cells * n_space * nz))
    out_rows = total_bands // n_space
    pieces = call(
        partial(split_kernel, n_space, n_band),
        "split",
        struct((n_space * n_band, 1, out_rows * 2 * bands)),
        (products,),
        scratch_shapes=[
            pltpu.VMEM(products.shape, F32),
            pltpu.VMEM((n_band, total_bands, 2 * bands), F32),
        ],
    )
    got = lax.all_to_all(pieces, ("space", "band"), 0, 0)
    margin, projection = call(
        last_kernel, "last_sum", (struct((out_rows, bands)), struct((out_rows, bands))), (got,)
    )
    return filtered.reshape(orbitals.shape), margin, projection


def solution(mesh):
    in_specs = (
        P("band", "space", None, None),
        P("band", "space", None, None),
        P("space", None, None),
        P("space", None, None, None, None),
        P(),
        P(),
    )
    out_specs = (P("band", "space", None, None), P("space", "band"), P("space", "band"))
    return jax.shard_map(shards, mesh=mesh, in_specs=in_specs, out_specs=out_specs, check_vma=False)
```

```python
from functools import partial

import jax
import jax.numpy as jnp
from jax import lax
from jax.experimental import pallas as pl
from jax.experimental.pallas import tpu as pltpu
from jax.sharding import PartitionSpec as P

HALO = 6
BOX = 6
NPJ = 9
HALF = 16

stencil_weights = (
    -5369.0 / 1800.0,
    12.0 / 7.0,
    -15.0 / 56.0,
    10.0 / 189.0,
    -1.0 / 112.0,
    2.0 / 1925.0,
    -1.0 / 16632.0,
)
center = 5.5
halfwidth = 5.5
outer = 2.0 / halfwidth
kinetic_weights = [-0.5 * outer * w for w in stencil_weights]

F32 = jnp.float32
BF16 = jnp.bfloat16


def params(vmem):
    return pltpu.CompilerParams(vmem_limit_bytes=vmem)


def circulant(n, blocks):
    size = n * blocks
    row = lax.broadcasted_iota(jnp.int32, (size, size), 0)
    col = lax.broadcasted_iota(jnp.int32, (size, size), 1)
    ahead = jnp.bitwise_and(col - row, n - 1)
    reach = jnp.minimum(ahead, n - ahead)
    value = jnp.zeros((size, size), F32)
    for m, weight in enumerate(kinetic_weights):
        value = jnp.where(reach == m, weight, value)
    value = jnp.where(jnp.bitwise_xor(row, col) < n, value, 0.0)
    hi = value.astype(BF16)
    return hi, (value - hi.astype(F32)).astype(BF16)


def dot(a, b, dims=((1,), (0,))):
    return lax.dot_general(a, b, (dims, ((), ())), preferred_element_type=F32)


def plane_rows(x, ny):
    return slice(x * ny, (x + 1) * ny)


def partners(count):
    return [0, *reversed(range(1, count))]


def pieces_of(ref, index, count, rows, outs):
    for bits, out in zip(partners(count), outs):
        quarter = jnp.bitwise_xor(index, bits)
        begin = pl.multiple_of(quarter * rows, 8)
        out[...] = ref[:, pl.ds(begin, rows), :].astype(out.dtype)


def cast_kernel(psi_ref, half_ref):
    half_ref[...] = psi_ref[...].astype(BF16)


def pieces_kernel(count, psi_ref, *outs):
    rows = psi_ref.shape[1] // count
    pieces_of(psi_ref, lax.axis_index("band"), count, rows, outs)


def yz_part(psi, cz, cy):
    bands, ny, nz = psi.shape
    flat = psi.reshape(bands * ny, nz)
    hi = flat.astype(BF16)
    lo = (flat - hi.astype(F32)).astype(BF16)
    both = jnp.concatenate([hi, lo], axis=1)
    along_z = dot(both, cz[0]) + dot(hi, cz[1])
    size = cy[0].shape[0]
    along_y = []
    for begin in range(0, bands * ny, size):
        pair = dot(cy[0], both[begin : begin + size])
        along_y.append(pair[:, :nz] + pair[:, nz:] + dot(cy[1], hi[begin : begin + size]))
    return (along_z + jnp.concatenate(along_y, axis=0)).reshape(bands, ny, nz)


def same_cell(rows, cols):
    row = lax.broadcasted_iota(jnp.int32, (rows, cols), 0)
    col = lax.broadcasted_iota(jnp.int32, (rows, cols), 1)
    return jnp.where(jnp.bitwise_and(row - col, HALF - 1) == 0, 1.0, 0.0).astype(F32)


def table(proj_ref, a, p):
    npj, ny, nz = proj_ref.shape[1], proj_ref.shape[3], proj_ref.shape[4]
    halves = [
        proj_ref[a, :, p, h * HALF : (h + 1) * HALF, :].reshape(npj * HALF, nz)
        for h in range(ny // HALF)
    ]
    return jnp.concatenate(halves, axis=1)


def halves_along(value, axis):
    bands, ny, nz = value.shape
    parts = [value[:, h * HALF : (h + 1) * HALF].reshape(bands * HALF, nz) for h in range(ny // HALF)]
    return jnp.concatenate(parts, axis=axis)


def spread(weights, tables, nz):
    total = dot(weights, tables)
    rows = total.shape[0]
    halves = [
        total[:, h * nz : (h + 1) * nz].reshape(rows // HALF, HALF, nz)
        for h in range(total.shape[1] // nz)
    ]
    return jnp.concatenate(halves, axis=1)


def plane_table(proj_ref, starts, q):
    parts = []
    for a, start in enumerate(starts):
        p = q - start
        inside = jnp.logical_and(p >= 0, p < BOX)
        part = table(proj_ref, a, jnp.clip(p, 0, BOX - 1))
        parts.append(part * jnp.where(inside, 1.0, 0.0).astype(BF16))
    return jnp.concatenate(parts, axis=0)


def box_starts(first_ref, atoms, planes):
    me = lax.axis_index("space")
    return [first_ref[me * atoms + a] - me * planes for a in range(atoms)]


def overlap(field_ref, tables, ny):
    bands = field_ref.shape[0]
    left = [halves_along(field_ref[:, plane_rows(x, ny)], 1) for x in range(len(tables))]
    d = dot(jnp.concatenate(left, axis=1), jnp.concatenate(tables, axis=1), ((1,), (1,)))
    rows, cols = d.shape
    return (d * same_cell(rows, cols)).reshape(bands, HALF, cols).sum(axis=1)


def prepare_kernel(planes, first_ref, strength_ref, own_ref, proj_ref, far_ref, e_ref, s_ref):
    ny = own_ref.shape[1] // planes
    atoms, npj = proj_ref.shape[:2]
    me = lax.axis_index("space")
    starts = box_starts(first_ref, atoms, planes)
    for q in range(BOX - 1):
        far_ref[q] = plane_table(proj_ref, starts, planes + q)
    owner = lax.broadcasted_iota(jnp.int32, s_ref.shape, 1)
    scale = jnp.zeros(s_ref.shape, F32)
    for a in range(atoms):
        for j in range(npj):
            value = outer * strength_ref[j, me * atoms + a]
            scale = jnp.where(owner >= (a * npj + j) * HALF, value, scale)
    s_ref[...] = scale
    e_ref[...] = overlap(own_ref, [plane_table(proj_ref, starts, q) for q in range(planes)], ny)


def ahead_kernel(planes, psi_ref, *refs):
    ahead_ref, edge_ref = refs[-2:]
    ny = psi_ref.shape[1] // planes
    edge_ref[...] = psi_ref[:, plane_rows(planes - 1, ny)].astype(BF16)
    for x in range(planes - 1):
        total = None
        for m in range(x + 1, HALO + 1):
            term = kinetic_weights[m] * psi_ref[:, plane_rows(planes + x - m, ny)]
            total = term if total is None else total + term
        ahead_ref[:, plane_rows(x, ny)] = total


def coefficient_kernel(planes, upper_ref, table_ref, e_ref, s_ref, ahead_ref, w_ref, next_ref):
    bands, cells, nz = upper_ref.shape
    ny = cells // planes
    reach = BOX - 1
    e = e_ref[...] + overlap(upper_ref, [table_ref[q] for q in range(reach)], ny)
    cols = e.shape[1]
    tiles = -(-cols // nz)
    e = jnp.concatenate([e, jnp.zeros((bands, tiles * nz - cols), F32)], axis=1)
    e = jnp.concatenate([e[:, t * nz : (t + 1) * nz] for t in range(tiles)], axis=0)
    gi = lax.broadcasted_iota(jnp.int32, (nz, nz), 0)
    gj = lax.broadcasted_iota(jnp.int32, (nz, nz), 1)
    group = jnp.where(jnp.bitwise_xor(gi, gj) < HALF, 1.0, 0.0).astype(BF16)
    e_hi = e.astype(BF16)
    e_lo = (e - e_hi.astype(F32)).astype(BF16)
    coef = dot(jnp.concatenate([e_hi, e_lo], axis=1), jnp.concatenate([group, group], axis=0))
    coef = jnp.concatenate([coef[t * bands : (t + 1) * bands] for t in range(tiles)], axis=1)
    w = coef[:, :cols] * s_ref[...]
    rows = bands * HALF
    full = jnp.broadcast_to(w[:, None, :], (bands, HALF, cols)).reshape(rows, cols)
    weights = (full * same_cell(rows, cols)).astype(BF16)
    w_ref[...] = weights
    for q in range(reach):
        here = plane_rows(q, ny)
        block = spread(weights, table_ref[q], nz) + ahead_ref[:, here]
        next_ref[:, here] = block.astype(BF16)


def near_kernel(
    planes, first_ref, psi_ref, prev_ref, pot_ref, w_ref, upper_ref, proj_ref, out_ref
):
    bands, cells, nz = psi_ref.shape
    ny = cells // planes
    weights = w_ref[...]
    starts = box_starts(first_ref, proj_ref.shape[0], planes)
    cz_hi, cz_lo = circulant(nz, 1)
    cz = (jnp.concatenate([cz_hi, cz_hi], axis=0), cz_lo)
    cy = circulant(ny, bands // 2)
    for x in range(planes):
        here = plane_rows(x, ny)
        psi = psi_ref[:, here]
        total = yz_part(psi, cz, cy) + spread(weights, plane_table(proj_ref, starts, x), nz)
        site = outer * pot_ref[here] + (kinetic_weights[0] - outer * center)
        total = total + site[None] * psi - prev_ref[:, here]
        for m in range(1, HALO + 1):
            for target in (x + m, x - m):
                if 0 <= target < planes:
                    total = total + kinetic_weights[m] * psi_ref[:, plane_rows(target, ny)]
                elif target >= planes:
                    value = upper_ref[:, plane_rows(target - planes, ny)].astype(F32)
                    total = total + kinetic_weights[m] * value
        out_ref[:, here] = total


def complete(g_ref, arrived_ref, below_ref, out_ref):
    cut = arrived_ref.shape[1]
    out_ref[:, :cut] = (g_ref[:, :cut] + arrived_ref[...].astype(F32)).astype(out_ref.dtype)
    edge = kinetic_weights[HALO] * below_ref[...].astype(F32)
    out_ref[:, cut:] = (g_ref[:, cut:] + edge).astype(out_ref.dtype)


def finish_kernel(count, g_ref, arrived_ref, below_ref, *rest):
    outs, total = rest[:-1], rest[-1]
    complete(g_ref, arrived_ref, below_ref, total)
    rows = g_ref.shape[1] // count
    pieces_of(total, lax.axis_index("band"), count, rows, outs)


def output_kernel(g_ref, arrived_ref, below_ref, *rest):
    pieces, (out_ref, panel_ref) = rest[:-2], rest[-2:]
    complete(g_ref, arrived_ref, below_ref, out_ref)
    bands = g_ref.shape[0]
    for p, piece in enumerate(reversed(pieces)):
        panel_ref[p * bands : (p + 1) * bands] = piece[...]


def split_kernel(n_space, n_band, prod_ref, out_ref, held, pair):
    bands = prod_ref.shape[0] // n_band
    me = lax.axis_index("band")
    for p, bits in enumerate(partners(n_band)):
        begin = pl.multiple_of(jnp.bitwise_xor(me, bits) * bands, 8)
        held[pl.ds(begin, bands), :] = prod_ref[p * bands : (p + 1) * bands]
    rows = held.shape[0] // n_space
    for p, bits in enumerate(partners(n_band)):
        cols = [slice((h * n_band + p) * bands, (h * n_band + p + 1) * bands) for h in (0, 1)]
        pair[p] = jnp.concatenate([held[:, c] for c in cols], axis=1)
        owner = jnp.bitwise_xor(me, bits)
        lines = [pair[p, pl.ds(r, n_space, stride=rows), :] for r in range(rows)]
        packed = jnp.concatenate(lines, axis=1)
        for i in range(n_space):
            out_ref[i * n_band + owner] = packed[i : i + 1]


def last_kernel(got_ref, margin_ref, projection_ref):
    total = got_ref[...].sum(axis=0)
    rows, bands = margin_ref.shape
    for r in range(rows):
        begin = 2 * r * bands
        margin_ref[r : r + 1] = total[:, begin : begin + bands]
        projection_ref[r : r + 1] = total[:, begin + bands : begin + 2 * bands]


def cyclic(value, axis, steps):
    count = lax.axis_size(axis)
    return lax.ppermute(value, axis, [(i, (i + steps) % count) for i in range(count)])


def mirrored(value, axis, bits):
    count = lax.axis_size(axis)
    return lax.ppermute(value, axis, [(i, i ^ bits) for i in range(count)])


def exchanged(pieces):
    offsets = partners(len(pieces))
    return [mirrored(p, "band", bits) if bits else p for bits, p in zip(offsets, pieces)]


def struct(shape, kind=F32):
    return jax.ShapeDtypeStruct(shape, kind)


def call(kernel, name, out_shape, args, vmem=48, **extra):
    return pl.pallas_call(
        kernel, out_shape=out_shape, compiler_params=params(vmem * 2**20), name=name, **extra
    )(*args)


def shards(orbitals, previous, potential, projectors, strengths, atom_planes):
    bands, planes, ny, nz = orbitals.shape
    n_space = lax.axis_size("space")
    n_band = lax.axis_size("band")
    cells = planes * ny
    whole = (bands, cells, nz)
    quarter = (bands, cells // n_band, nz)
    psi = orbitals.reshape(whole)
    prev = previous.reshape(whole)
    pot = potential.reshape(cells, nz)

    vm = pl.BlockSpec(memory_space=pltpu.VMEM)
    sm = pl.BlockSpec(memory_space=pltpu.SMEM)
    anywhere = pl.BlockSpec(memory_space=pl.ANY)

    most = (bands, (planes - 1) * ny, nz)
    plane = (bands, ny, nz)
    half = call(cast_kernel, "cast", struct(whole, BF16), (psi,))
    panel = call(
        partial(pieces_kernel, n_band),
        "pieces",
        (struct(quarter, BF16),) * n_band,
        (psi,),
        cost_estimate=pl.CostEstimate(flops=10**9, bytes_accessed=2**20, transcendentals=0),
    )
    upper = cyclic(half, "space", -1)
    panel = exchanged(panel)
    atoms, npj = projectors.shape[:2]
    cols = atoms * npj * HALF
    far_tables, e, s = call(
        partial(prepare_kernel, planes),
        "prepare",
        (
            struct((BOX - 1, cols, ny // HALF * nz), BF16),
            struct((bands, cols)),
            struct((1, cols)),
        ),
        (atom_planes, strengths.T, half, projectors),
        in_specs=[sm, sm, vm, vm],
        out_specs=(vm,) * 3,
        cost_estimate=pl.CostEstimate(flops=10**9, bytes_accessed=2**20, transcendentals=0),
    )
    ahead, edge = call(
        partial(ahead_kernel, planes),
        "ahead",
        (struct(most), struct(plane, BF16)),
        (psi, panel[3], s),
        in_specs=[vm, anywhere, anywhere],
        out_specs=(vm, vm),
        cost_estimate=pl.CostEstimate(flops=10**9, bytes_accessed=2**20, transcendentals=0),
    )
    below = cyclic(edge, "space", 1)
    w, beyond = call(
        partial(coefficient_kernel, planes),
        "coefficients",
        (struct((bands * HALF, cols), BF16), struct(most, BF16)),
        (upper, far_tables, e, s, ahead),
        cost_estimate=pl.CostEstimate(flops=10**9, bytes_accessed=2**20, transcendentals=0),
    )
    arrived = cyclic(beyond, "space", 1)
    g = call(
        partial(near_kernel, planes),
        "near_part",
        struct(whole),
        (atom_planes, psi, prev, pot, w, upper, projectors),
        in_specs=[sm] + [vm] * 6,
        out_specs=vm,
        cost_estimate=pl.CostEstimate(flops=2*10**10, bytes_accessed=4 * 2**20, transcendentals=0),
    )
    mine = call(
        partial(finish_kernel, n_band),
        "finish",
        (struct(quarter, BF16),) * n_band,
        (g, arrived, below),
        scratch_shapes=[pltpu.VMEM(whole, F32)],
    )
    mine = exchanged(mine)
    total_bands = n_band * bands
    filtered, panels = call(
        output_kernel,
        "output",
        (struct(whole, BF16), struct((total_bands, *quarter[1:]), BF16)),
        (g, arrived, below, *reversed(panel)),
    )
    left = jnp.concatenate(mine, axis=0).reshape(total_bands, -1)
    filtered, rows = lax.optimization_barrier((filtered, panels.reshape(total_bands, -1)))
    right = jnp.concatenate([left, rows], axis=0)
    products = dot(left, right, ((1,), (1,))) * (1.0 / (cells * n_space * nz))
    out_rows = total_bands // n_space
    pieces = call(
        partial(split_kernel, n_space, n_band),
        "split",
        struct((n_space * n_band, 1, out_rows * 2 * bands)),
        (products,),
        scratch_shapes=[
            pltpu.VMEM(products.shape, F32),
            pltpu.VMEM((n_band, total_bands, 2 * bands), F32),
        ],
    )
    got = lax.all_to_all(pieces, ("space", "band"), 0, 0)
    margin, projection = call(
        last_kernel, "last_sum", (struct((out_rows, bands)), struct((out_rows, bands))), (got,)
    )
    return filtered.reshape(orbitals.shape), margin, projection


def solution(mesh):
    in_specs = (
        P("band", "space", None, None),
        P("band", "space", None, None),
        P("space", None, None),
        P("space", None, None, None, None),
        P(),
        P(),
    )
    out_specs = (P("band", "space", None, None), P("space", "band"), P("space", "band"))
    return jax.shard_map(shards, mesh=mesh, in_specs=in_specs, out_specs=out_specs, check_vma=False)
```
